32 devices in a mesh: seq: 4 (over x, core), fsdp: 8 (over z, y).
Axes of the slice: x: 2, y: 2, z: 4, core: 2. Of those that a mesh axis runs over, the one named last changes fastest.
Arguments:
- hidden_in: bfloat16 [2, 4096, 2048], P(None, ('seq', 'fsdp')), may hold values from -6 to 6
- out_cotangent: bfloat16 [2, 4096, 2048], P(None, ('seq', 'fsdp')), may hold values from -6 to 6
- positions: int32 [2, 4096], replicated, may hold values from 0 to 4095, as said below
- block_mask: int32 [2, 16, 16], replicated, may hold values from 0 to 1, as said below
- norm_gain: bfloat16 [2048], P('fsdp'), may hold values from 0.5 to 1.5
- norm_bias: bfloat16 [2048], P('fsdp'), may hold values from -3 to 3
- qkv_weight: bfloat16 [2048, 2304], P('fsdp'), may hold values from -0.125 to 0.125
- proj_weight: bfloat16 [2048, 2048], P('fsdp'), may hold values from -3 to 3
- mlp_gain: bfloat16 [2048], P('fsdp'), may hold values from 0.5 to 1.5
- mlp_bias: bfloat16 [2048], P('fsdp'), may hold values from -3 to 3
- fc_weight: bfloat16 [2048, 8192], P('fsdp'), may hold values from -0.125 to 0.125
- down_weight: bfloat16 [8192, 2048], P('fsdp'), may hold values from -0.0625 to 0.0625
Outputs:
- hidden_out: bfloat16 [2, 4096, 2048], P(None, ('seq', 'fsdp'))
- grad_input: bfloat16 [2, 4096, 2048], P(None, ('seq', 'fsdp'))
- grad_norm_gain: float32 [2048], P('fsdp')
- grad_norm_bias: float32 [2048], P('fsdp')
- grad_qkv: float32 [2048, 2304], P('fsdp')
- grad_proj: float32 [2048, 2048], P('fsdp')
- grad_mlp_gain: float32 [2048], P('fsdp')
- grad_mlp_bias: float32 [2048], P('fsdp')
- grad_fc: float32 [2048, 8192], P('fsdp')
- grad_down: float32 [8192, 2048], P('fsdp')
The draws below stay inside these ranges and needn't reach their ends.
Inputs may be any that keep to these rules, and one draw needn't show every extreme that they name: In each sequence positions start at 0, and each next entry is either 0 (a new packed document begins) or one more than the entry before it. One of the 2 sequences, which one drawn from the seed, is a single document of 4096 tokens; in the others no document is longer than 2048 tokens, and the first one has exactly that length. block_mask[b, i, j] is 1 where i = j and 0 where j > i.
All inputs are finite; a program needn't handle non-finite values.
Results may differ from the reference program's by a relative error of at most 0.019.
Values may be sent and summed in bfloat16 or wider, within the bound.
A program may use at most 448 MiB of HBM per device.

```python
import jax
import jax.numpy as jnp
from jax import lax

D = 2048
HEADS = 16
HD = 128
FF = 8192
QKV = 2304
MB = 2
MB_TOK = 128
BLOCK = 256
SEQ_LEN = 4096
NBLK = 16


def draw_positions(key, part):
    longest = 16 * MB_TOK
    marks = jax.random.randint(key, (MB, SEQ_LEN), 0, longest)
    index = jnp.broadcast_to(jnp.arange(SEQ_LEN, dtype=jnp.int32), (MB, SEQ_LEN))
    begins = (marks == 0) & (index >= longest) | (index % longest == 0)
    chosen = jax.random.randint(jax.random.fold_in(key, 7), (), 0, MB)
    rowid = jnp.arange(MB, dtype=jnp.int32)[:, None]
    begins = jnp.where(rowid == chosen, index == 0, begins)
    starts = jnp.where(begins, index, 0)
    return (index - lax.cummax(starts, axis=1)).astype(jnp.int32)


def draw_block_mask(key, part):
    coins = jax.random.randint(key, (MB, NBLK, NBLK), 0, 4)
    rowid = jnp.arange(NBLK, dtype=jnp.int32)[:, None]
    colid = jnp.arange(NBLK, dtype=jnp.int32)[None, :]
    keep = (colid < rowid) & (coins != 0) | (colid == rowid)
    return keep.astype(jnp.int32)


def block_levels(own_key, extent, shards, low, high):
    gain, own = 1.0, jax.random.fold_in(own_key, 6)
    for position, parts in shards:
        draws = jnp.exp(jax.random.uniform(jax.random.fold_in(own, position), (parts,), jnp.float32, low / len(shards), high / len(shards)))
        gain = gain * jnp.repeat(draws, extent[position] // parts).reshape([-1 if axis == position else 1 for axis in range(len(extent))])
    return gain


def scatter_about(stream_key, shape, width, most, shards=(), kind=jnp.bfloat16):
    array = width * jax.random.normal(stream_key, shape, jnp.float32)
    if shards:
        array = array * block_levels(stream_key, shape, shards, -0.22, 0.18)
    return jnp.clip(array, -most, most).astype(kind)


def setup_inputs(seed: int = 0) -> dict:
    splits = jax.random.split(jax.random.key(seed), 13)
    hidden_in = scatter_about(splits[0], (MB, SEQ_LEN, D), 1.0, 6.0, ((1, 32),))
    out_cotangent = scatter_about(splits[1], (MB, SEQ_LEN, D), 1.0, 6.0, ((1, 32),))
    positions = draw_positions(jax.random.fold_in(splits[12], 71), 0)
    block_mask = draw_block_mask(jax.random.fold_in(splits[12], 71), 0)
    norm_gain = jnp.clip(1.0 + 0.1 * jax.random.normal(splits[4], (D,), jnp.float32), 0.5, 1.5).astype(jnp.bfloat16)
    norm_bias = scatter_about(splits[5], (D,), 0.5, 3.0, ((0, 8),))
    qkv_weight = scatter_about(splits[6], (D, QKV), D ** -0.5, 0.125, ((0, 8),))
    proj_weight = scatter_about(splits[7], (D, D), (max(D // 512, 1)) ** -0.5, 3.0, ((0, 8),))
    mlp_gain = jnp.clip(1.0 + 0.1 * jax.random.normal(splits[8], (D,), jnp.float32), 0.5, 1.5).astype(jnp.bfloat16)
    mlp_bias = scatter_about(splits[9], (D,), 0.5, 3.0, ((0, 8),))
    fc_weight = scatter_about(splits[10], (D, FF), D ** -0.5, 0.125, ((0, 8),))
    down_weight = scatter_about(splits[11], (FF, D), FF ** -0.5, 0.0625, ((0, 8),))
    return {"hidden_in": hidden_in, "out_cotangent": out_cotangent, "positions": positions, "block_mask": block_mask, "norm_gain": norm_gain, "norm_bias": norm_bias, "qkv_weight": qkv_weight, "proj_weight": proj_weight, "mlp_gain": mlp_gain, "mlp_bias": mlp_bias, "fc_weight": fc_weight, "down_weight": down_weight}


EPS = 1e-05
NEG_FILL = -1e+30

@jax.custom_vjp
def low(v):
    return lax.optimization_barrier(v.astype(jnp.bfloat16)).astype(jnp.float32)

@jax.custom_vjp
def low_back(v):
    return v

def low_keep(v):
    return (low(v), None)

def low_pass(kept, grad):
    return (grad,)

def back_keep(v):
    return (v, None)

def back_low(kept, grad):
    return (low(grad),)
low.defvjp(low_keep, low_pass)
low_back.defvjp(back_keep, back_low)

def matmul(left, right):
    return jnp.dot(left, right, precision=lax.Precision.HIGHEST, preferred_element_type=jnp.float32)

def layer_norm(values):
    mean = lax.optimization_barrier(jnp.mean(values, axis=-1, keepdims=True))
    center = values - mean
    return center * lax.rsqrt(lax.optimization_barrier(jnp.mean(center * center, axis=-1, keepdims=True)) + EPS)

def attention(queries, keys, values, places, mask_table):
    count = SEQ_LEN // BLOCK
    blocks = queries.reshape(count, BLOCK, HEADS, HD)
    starts = jnp.arange(count, dtype=jnp.int32) * BLOCK
    key_index = jnp.arange(SEQ_LEN, dtype=jnp.int32)
    scale = HD ** (-0.5)

    @jax.checkpoint
    def one_block(item):
        block, start = item
        tokens = start + jnp.arange(BLOCK, dtype=jnp.int32)
        first_keys = tokens - places[tokens]
        marks = mask_table[tokens // BLOCK][:, key_index // BLOCK]
        allowed = (marks == 1) & (key_index[None, :] <= tokens[:, None]) & (key_index[None, :] >= first_keys[:, None])
        scores = low_back(jnp.einsum('qhd,kd->hqk', block, keys, precision=lax.Precision.HIGHEST) * scale)
        scores = jnp.where(allowed[None], scores, NEG_FILL)
        weights = low(jax.nn.softmax(scores, axis=-1))
        return jnp.einsum('hqk,kd->qhd', weights, values, precision=lax.Precision.HIGHEST)
    return lax.map(one_block, (blocks, starts)).reshape(SEQ_LEN, D)

def layer_forward(inputs, places, mask_table, params):
    norm_gain, norm_bias, qkv_weight, proj_weight, mlp_gain, mlp_bias, fc_weight, down_weight = params
    normed_one = layer_norm(inputs)
    attn_in = low(normed_one * norm_gain + norm_bias)
    projected = matmul(attn_in, qkv_weight)
    queries = low_back(low(projected[:, :D]))
    keys = low_back(low(projected[:, D:D + HD]))
    values = low_back(low(projected[:, D + HD:]))
    heads = attention(queries.reshape(SEQ_LEN, HEADS, HD), keys, values, places, mask_table)
    heads = low_back(low(heads))
    resid = inputs + low_back(matmul(heads, proj_weight))
    normed_two = layer_norm(resid)
    mlp_in = low(normed_two * mlp_gain + mlp_bias)
    pre_act = low_back(matmul(mlp_in, fc_weight))
    activ = low(jax.nn.gelu(pre_act, approximate=True))
    return resid + matmul(activ, down_weight)

def reference(hidden_in, out_cotangent, positions, block_mask, norm_gain, norm_bias, qkv_weight, proj_weight, mlp_gain, mlp_bias, fc_weight, down_weight):
    params = tuple((p.astype(jnp.float32) for p in (norm_gain, norm_bias, qkv_weight, proj_weight, mlp_gain, mlp_bias, fc_weight, down_weight)))

    def one_sequence(carry, item):
        inputs, cotangent, places, mask_table = item

        def forward(values, *weights):
            return layer_forward(values, places, mask_table, weights)
        result, pullback = jax.vjp(forward, inputs.astype(jnp.float32), *params)
        grads = pullback(cotangent.astype(jnp.float32))
        carry = tuple((c + g for c, g in zip(carry, grads[1:])))
        return (carry, (result.astype(jnp.bfloat16), grads[0].astype(jnp.bfloat16)))
    zeros = tuple((jnp.zeros_like(p) for p in params))
    totals, (results, input_grads) = lax.scan(one_sequence, zeros, (hidden_in, out_cotangent, positions, block_mask))
    return (results, input_grads, totals[0], totals[1], totals[2], totals[3], totals[4], totals[5], totals[6], totals[7])
```

```python
import functools
import math

import jax
import jax.numpy as jnp
from jax import lax
from jax.experimental import pallas as pl
from jax.experimental.pallas import tpu as pltpu
from jax.sharding import PartitionSpec as P

HEADS = 16
HD = 128
MB = 2
BLOCK = 256
EPS = 1e-05
NEG_FILL = -1e30
SCALE = HD ** (-0.5)
LOG2E = math.log2(math.e)
BF = jnp.bfloat16
F32 = jnp.float32


def dot_rows(left, right):
    return lax.dot_general(left, right, (((0,), (0,)), ((), ())), preferred_element_type=F32)


def dot_cols(left, right):
    return lax.dot_general(left, right, (((1,), (1,)), ((), ())), preferred_element_type=F32)


def dot_plain(left, right):
    return lax.dot_general(left, right, (((1,), (0,)), ((), ())), preferred_element_type=F32)


def tie(value, after):
    return lax.optimization_barrier((value, after))[0]


def core_swap(value):
    return lax.ppermute(value, "seq", [(s, s ^ 1) for s in range(4)])


def chip_swap(value):
    return lax.ppermute(value, "seq", [(s, s ^ 2) for s in range(4)])


def seq_gather(value):
    across = chip_swap(value)
    pair = core_swap(value)
    pair_across = core_swap(across)
    return jnp.stack([value, pair, across, pair_across])


def seq_scatter(parts):
    far = core_swap(parts[3].astype(BF))
    near = core_swap(parts[1].astype(BF))
    across = chip_swap((parts[2] + far.astype(F32)).astype(BF))
    return parts[0] + near.astype(F32) + across.astype(F32)


def ring_order(count):
    return [2 * i for i in range(count // 2)] + [2 * i + 1 for i in reversed(range(count // 2))]


class Ring:
    def __init__(self, count):
        order = ring_order(count)
        self.count = count
        self.up = [(order[i], order[(i + 1) % count]) for i in range(count)]
        self.down = [(order[(i + 1) % count], order[i]) for i in range(count)]
        place = lax.axis_index("fsdp")
        half = count // 2
        self.place = place
        self.at = jnp.where(place % 2 == 0, place // 2, count - 1 - place // 2)

    def owner(self, step):
        count, half = self.count, self.count // 2
        at = lax.rem(self.at + (step + count), count)
        return jnp.where(at < half, 2 * at, 2 * (count - 1 - at) + 1)

    def gather(self, value):
        count = self.count
        rows = value.shape[0]
        out = jnp.zeros((count,) + value.shape, value.dtype)
        put = lambda out, piece, owner, row: lax.dynamic_update_slice(
            out, piece[None], (owner, row) + (0,) * (value.ndim - 1)
        )
        out = put(out, value, self.place, 0)
        low = high = value
        for step in range(1, count // 2):
            low = lax.ppermute(low, "fsdp", self.up)
            high = lax.ppermute(high, "fsdp", self.down)
            out = put(out, low, self.owner(-step), 0)
            out = put(out, high, self.owner(step), 0)
        half = rows // 2
        low = lax.ppermute(low[:half], "fsdp", self.up)
        high = lax.ppermute(high[half:], "fsdp", self.down)
        out = put(out, low, self.owner(-(count // 2)), 0)
        return put(out, high, self.owner(count // 2), half)

    def scatter(self, chunk):
        count = self.count
        middle = chunk(self.owner(count // 2))
        half = middle.shape[0] // 2
        up = middle[:half].astype(BF)
        down = middle[half:].astype(BF)
        for step in range(count // 2 - 1, -1, -1):
            up = lax.ppermute(up, "fsdp", self.up).astype(F32)
            down = lax.ppermute(down, "fsdp", self.down).astype(F32)
            if step == count // 2 - 1:
                mine = chunk(self.owner(step))
                up = jnp.concatenate([mine[:half] + up, mine[half:]], axis=0)
                mine = chunk(self.owner(-step))
                down = jnp.concatenate([mine[:half], mine[half:] + down], axis=0)
            elif step:
                up = chunk(self.owner(step)) + up
                down = chunk(self.owner(-step)) + down
            else:
                return chunk(self.place) + up + down
            up = up.astype(BF)
            down = down.astype(BF)


def attend_kernel(tables, q_ref, kv_ref, first_ref, out_ref, log_ref, stack, high, total, result, *, heads, blocks):
    batch, piece = pl.program_id(0), pl.program_id(1)
    count = q_ref.shape[2]
    base = (batch * pl.num_programs(1) + piece) * (blocks + 4)
    chunk, low_tile, high_tile = tables[base], tables[base + 1], tables[base + 2]
    for h in range(heads):
        stack[h * count : (h + 1) * count, :] = q_ref[0, 0, :, h * HD : (h + 1) * HD]
    high[...] = jnp.full_like(high, NEG_FILL)
    total[...] = jnp.zeros_like(total)
    result[...] = jnp.zeros_like(result)
    tokens = chunk * count + lax.broadcasted_iota(jnp.int32, (1, count), 1)
    first = first_ref[0, 0]

    def step(tile, carry):
        @pl.when(tables[base + 4 + tile] != 0)
        def _():
            part = kv_ref[pl.ds(2 * tile, 2), 0].reshape(BLOCK, 2 * HD)
            keys, values = part[:, :HD], part[:, HD:]
            scores = dot_cols(keys, stack[...])
            index = tile * BLOCK + lax.broadcasted_iota(jnp.int32, (BLOCK, count), 0)
            allowed = (index <= tokens) & (index >= first)
            weights, scales = [], []
            for h in range(heads):
                lanes = slice(h * count, (h + 1) * count)
                score = jnp.where(allowed, scores[:, lanes] * (SCALE * LOG2E), NEG_FILL)
                old = high[:, lanes]
                new = jnp.maximum(old, jnp.max(score, axis=0, keepdims=True))
                weight = jnp.exp2(score - new)
                scale = jnp.exp2(old - new)
                high[:, lanes] = new
                total[:, lanes] = total[:, lanes] * scale + jnp.sum(weight, axis=0, keepdims=True)
                weights.append(weight.astype(BF))
                scales.append(scale)
            added = dot_rows(values, jnp.concatenate(weights, axis=1))
            result[...] = result[...] * jnp.concatenate(scales, axis=1) + added

        return carry

    lax.fori_loop(low_tile, high_tile, step, 0)
    final = result[...] / total[...]
    logs = high[...] + jnp.log2(total[...])
    for h in range(heads):
        lanes = slice(h * count, (h + 1) * count)
        out_ref[0, 0, :, h * HD : (h + 1) * HD] = final[:, lanes].T.astype(BF)
        log_ref[0, 0, h : h + 1, :] = logs[:, lanes]


def attend_back_kernel(
    tables,
    q_ref,
    kv_ref,
    first_ref,
    out_ref,
    log_ref,
    grad_ref,
    dq_ref,
    dkv_ref,
    stack,
    grads,
    logs,
    deltas,
    dq_sum,
    dkv_sum,
    *,
    heads,
    blocks,
):
    batch, piece = pl.program_id(0), pl.program_id(1)
    count = q_ref.shape[2]
    base = (batch * pl.num_programs(1) + piece) * (blocks + 4)
    chunk, low_tile, high_tile = tables[base], tables[base + 1], tables[base + 2]

    @pl.when(piece == 0)
    def _():
        dkv_sum[...] = jnp.zeros_like(dkv_sum)

    for h in range(heads):
        rows = slice(h * count, (h + 1) * count)
        cols = slice(h * HD, (h + 1) * HD)
        stack[rows, :] = q_ref[0, 0, :, cols]
        grad = grad_ref[0, 0, :, cols]
        grads[rows, :] = grad
        product = grad.astype(F32) * out_ref[0, 0, :, cols].astype(F32)
        deltas[:, rows] = jnp.sum(product.T, axis=0, keepdims=True)
        logs[:, rows] = log_ref[0, 0, h : h + 1, :]
    dq_sum[...] = jnp.zeros_like(dq_sum)
    tokens = chunk * count + lax.broadcasted_iota(jnp.int32, (1, count), 1)
    first = first_ref[0, 0]

    def step(tile, carry):
        @pl.when(tables[base + 4 + tile] != 0)
        def _():
            part = kv_ref[pl.ds(2 * tile, 2), 0].reshape(BLOCK, 2 * HD)
            keys, values = part[:, :HD], part[:, HD:]
            scores = dot_cols(keys, stack[...])
            pulls = dot_cols(values, grads[...])
            index = tile * BLOCK + lax.broadcasted_iota(jnp.int32, (BLOCK, count), 0)
            allowed = (index <= tokens) & (index >= first)
            weights, score_grads = [], []
            for h in range(heads):
                lanes = slice(h * count, (h + 1) * count)
                score = jnp.where(allowed, scores[:, lanes] * (SCALE * LOG2E), NEG_FILL)
                weight = jnp.exp2(score - logs[:, lanes])
                weights.append(weight.astype(BF))
                score_grads.append((weight * (pulls[:, lanes] - deltas[:, lanes])).astype(BF))
            weight = jnp.concatenate(weights, axis=1)
            score_grad = jnp.concatenate(score_grads, axis=1)
            dv = dot_plain(weight, grads[...])
            dk = dot_plain(score_grad, stack[...])
            dq_sum[...] += dot_rows(keys, score_grad)
            both = jnp.concatenate([dk, dv], axis=1).reshape(2, BLOCK // 2, 2 * HD)
            dkv_sum[pl.ds(2 * tile, 2)] += both

        return carry

    lax.fori_loop(low_tile, high_tile, step, 0)
    for h in range(heads):
        lanes = slice(h * count, (h + 1) * count)
        dq_ref[0, 0, :, h * HD : (h + 1) * HD] = (dq_sum[:, lanes] * SCALE).T.astype(BF)

    @pl.when(piece == pl.num_programs(1) - 1)
    def _():
        dkv_ref[:, 0, :, :HD] = (dkv_sum[:, :, :HD] * SCALE).astype(BF)
        dkv_ref[:, 0, :, HD:] = dkv_sum[:, :, HD:].astype(BF)


def attend(tables, first, queries, key_values, blocks):
    pieces, batches, count, width = queries.shape
    heads = width // HD
    chunks = key_values.shape[0]
    row_spec = pl.BlockSpec((1, 1, count, width), lambda b, i, t: (i, b, 0, 0))
    kv_spec = pl.BlockSpec((chunks, 1, count, 2 * HD), lambda b, i, t: (0, b, 0, 0))
    first_spec = pl.BlockSpec((1, 1, 1, count), lambda b, i, t: (i, b, 0, 0))
    log_spec = pl.BlockSpec((1, 1, heads, count), lambda b, i, t: (i, b, 0, 0))
    rows = heads * count
    return pl.pallas_call(
        functools.partial(attend_kernel, heads=heads, blocks=blocks),
        out_shape=(
            jax.ShapeDtypeStruct(queries.shape, BF),
            jax.ShapeDtypeStruct((pieces, batches, heads, count), F32),
        ),
        grid_spec=pltpu.PrefetchScalarGridSpec(
            num_scalar_prefetch=1,
            grid=(batches, pieces),
            in_specs=[row_spec, kv_spec, first_spec],
            out_specs=[row_spec, log_spec],
            scratch_shapes=[
                pltpu.VMEM((rows, HD), BF),
                pltpu.VMEM((1, rows), F32),
                pltpu.VMEM((1, rows), F32),
                pltpu.VMEM((HD, rows), F32),
            ],
        ),
        compiler_params=pltpu.CompilerParams(vmem_limit_bytes=40 << 20),
        cost_estimate=pl.CostEstimate(flops=4 * rows * HD * chunks * count * pieces, bytes_accessed=16 << 20, transcendentals=rows * chunks * count * pieces),
        name="attend",
    )(tables, queries, key_values, first)


def attend_back(tables, first, queries, key_values, out, logs, grads, blocks):
    pieces, batches, count, width = queries.shape
    heads = width // HD
    chunks = key_values.shape[0]
    row_spec = pl.BlockSpec((1, 1, count, width), lambda b, i, t: (i, b, 0, 0))
    kv_spec = pl.BlockSpec((chunks, 1, count, 2 * HD), lambda b, i, t: (0, b, 0, 0))
    first_spec = pl.BlockSpec((1, 1, 1, count), lambda b, i, t: (i, b, 0, 0))
    log_spec = pl.BlockSpec((1, 1, heads, count), lambda b, i, t: (i, b, 0, 0))
    rows = heads * count
    return pl.pallas_call(
        functools.partial(attend_back_kernel, heads=heads, blocks=blocks),
        out_shape=(
            jax.ShapeDtypeStruct(queries.shape, BF),
            jax.ShapeDtypeStruct(key_values.shape, BF),
        ),
        grid_spec=pltpu.PrefetchScalarGridSpec(
            num_scalar_prefetch=1,
            grid=(batches, pieces),
            in_specs=[row_spec, kv_spec, first_spec, row_spec, log_spec, row_spec],
            out_specs=[row_spec, kv_spec],
            scratch_shapes=[
                pltpu.VMEM((rows, HD), BF),
                pltpu.VMEM((rows, HD), BF),
                pltpu.VMEM((1, rows), F32),
                pltpu.VMEM((1, rows), F32),
                pltpu.VMEM((HD, rows), F32),
                pltpu.VMEM((chunks, count, 2 * HD), F32),
            ],
        ),
        compiler_params=pltpu.CompilerParams(vmem_limit_bytes=60 << 20),
        cost_estimate=pl.CostEstimate(flops=10 * rows * HD * chunks * count * pieces, bytes_accessed=32 << 20, transcendentals=rows * chunks * count * pieces),
        name="attend_back",
    )(tables, queries, key_values, first, out, logs, grads)


def layer_norm(values):
    mean = jnp.mean(values, axis=-1, keepdims=True)
    center = values - mean
    inverse = lax.rsqrt(jnp.mean(center * center, axis=-1, keepdims=True) + EPS)
    return center * inverse, inverse


def norm_back(grad, normed, inverse):
    return inverse * (
        grad
        - jnp.mean(grad, axis=-1, keepdims=True)
        - normed * jnp.mean(grad * normed, axis=-1, keepdims=True)
    )


def gelu_tanh(values):
    return jax.nn.gelu(values, approximate=True)


def shards(
    hidden_in,
    out_cotangent,
    positions,
    block_mask,
    norm_gain,
    norm_bias,
    qkv_weight,
    proj_weight,
    mlp_gain,
    mlp_bias,
    fc_weight,
    down_weight,
):
    seq_count = lax.axis_size("seq")
    fsdp_count = lax.axis_size("fsdp")
    s = lax.axis_index("seq")
    f = lax.axis_index("fsdp")
    ring = Ring(fsdp_count)
    count = hidden_in.shape[1]
    width = hidden_in.shape[2]
    length = positions.shape[1]
    blocks = length // BLOCK
    shard = qkv_weight.shape[0]
    ff = fc_weight.shape[1]
    ff_shard = down_weight.shape[0]
    heads_here = HEADS // seq_count
    head_cols = heads_here * HD
    quarter = ff_shard // seq_count
    tokens_here = MB * count
    group = seq_count * tokens_here

    chunk_ids = jnp.stack([(s ^ i) * fsdp_count + f for i in range(seq_count)]).astype(jnp.int32)
    token_ids = chunk_ids[:, None] * count + jnp.arange(count, dtype=jnp.int32)[None]
    first = token_ids[:, None, :] - jnp.stack(
        [lax.dynamic_slice_in_dim(positions, chunk_ids[i] * count, count, 1) for i in range(seq_count)]
    )
    first = first[:, :, None, :]
    high_tiles = (chunk_ids * count + count - 1) // BLOCK + 1
    tables = jnp.concatenate(
        [
            jnp.broadcast_to(chunk_ids[None, :, None], (MB, seq_count, 1)),
            (first[:, :, 0, :1] // BLOCK).transpose(1, 0, 2),
            jnp.broadcast_to(high_tiles[None, :, None], (MB, seq_count, 1)),
            jnp.zeros((MB, seq_count, 1), jnp.int32),
            jnp.stack([block_mask[:, (chunk_ids[i] * count) // BLOCK] for i in range(seq_count)], axis=1),
        ],
        axis=2,
    ).reshape(-1)

    vectors = jnp.stack([norm_gain, norm_bias, mlp_gain, mlp_bias])
    own_qkv = jnp.concatenate(
        [lax.dynamic_slice_in_dim(qkv_weight, s * head_cols, head_cols, 1), qkv_weight[:, width:]], axis=1
    )
    qkv_cols = own_qkv.shape[1]
    span = 16
    padded = jnp.pad(vectors, ((0, span - 4), (0, qkv_cols - shard)))
    qkv_ring = ring.gather(jnp.concatenate([own_qkv, padded], axis=0))
    hidden_all = seq_gather(hidden_in)
    qkv_full = qkv_ring[:, :shard].reshape(width, qkv_cols)
    vectors = qkv_ring[:, shard : shard + 4, :shard].transpose(1, 0, 2).reshape(4, width).astype(F32)
    gain_one, bias_one, gain_two, bias_two = vectors[0], vectors[1], vectors[2], vectors[3]

    part = shard // seq_count
    pairs = [
        (j * fsdp_count + q * (fsdp_count // seq_count) + t // seq_count, q * fsdp_count + t)
        for q in range(seq_count)
        for t in range(fsdp_count)
        for j in [t % seq_count]
    ]
    back_pairs = [(b, a) for a, b in pairs]
    own_proj = lax.ppermute(
        lax.dynamic_slice_in_dim(proj_weight, s * part, part, 0), ("seq", "fsdp"), pairs
    )

    rows_all = hidden_all.reshape(group, width).astype(F32)
    normed_all, _ = layer_norm(rows_all)
    attn_in = (normed_all * gain_one + bias_one).astype(BF)
    own_attn_in = attn_in[:tokens_here]
    key_values = dot_plain(own_attn_in, qkv_full[:, head_cols:]).astype(BF)
    kv_ring = ring.gather(key_values)
    kv_rel = seq_gather(kv_ring)
    kv_all = jnp.zeros((seq_count,) + kv_ring.shape, BF)
    for i in range(seq_count):
        kv_all = lax.dynamic_update_slice(kv_all, kv_rel[i][None], (s ^ i, 0, 0, 0))
    kv_all = kv_all.reshape(seq_count * fsdp_count, MB, count, 2 * HD)
    queries = dot_plain(attn_in, qkv_full[:, :head_cols]).astype(BF).reshape(seq_count, MB, count, head_cols)

    own_proj = tie(own_proj, kv_ring)
    proj_full = ring.gather(own_proj).reshape(head_cols, width)
    fc_own = lax.dynamic_slice_in_dim(
        fc_weight.reshape(shard, fsdp_count, seq_count, quarter), s, 1, 2
    ).reshape(shard, fsdp_count * quarter)
    fc_own = tie(fc_own, proj_full)
    fc_full = ring.gather(fc_own).reshape(width, fsdp_count * quarter)
    down_own = lax.dynamic_slice_in_dim(down_weight, s * quarter, quarter, 0)
    down_own = tie(down_own, fc_full)
    down_full = ring.gather(down_own).reshape(fsdp_count * quarter, width)
    cotangent_all = seq_gather(tie(out_cotangent, hidden_all)).reshape(group, width)

    heads_out, logs = attend(tables, first, queries, kv_all, blocks)
    heads_rows = heads_out.reshape(group, head_cols)

    def partial_sums(left, right):
        return [
            dot_plain(left[i * tokens_here : (i + 1) * tokens_here], right) for i in range(seq_count)
        ]

    hidden_own = hidden_in.reshape(tokens_here, width).astype(F32)
    cotangent = out_cotangent.reshape(tokens_here, width)
    resid = hidden_own + seq_scatter(partial_sums(heads_rows, proj_full))
    normed_two, inverse_two = layer_norm(resid)
    mlp_in_own = (normed_two * gain_two + bias_two).astype(BF)
    mlp_in = seq_gather(mlp_in_own).reshape(group, width)
    pre_act = dot_plain(mlp_in, fc_full)
    activ, gelu_pull = jax.vjp(gelu_tanh, pre_act)
    activ = activ.astype(BF)
    activ_grad = dot_cols(cotangent_all, down_full)
    pre_grad = gelu_pull(activ_grad)[0].astype(BF)
    fc_turned = fc_full
    mlp_in_grad = seq_scatter(
        [
            dot_cols(pre_grad[i * tokens_here : (i + 1) * tokens_here], fc_turned)
            for i in range(seq_count)
        ]
    )
    result = (resid + seq_scatter(partial_sums(activ, down_full))).astype(BF)

    mlp_gain_part = jnp.sum(mlp_in_grad * normed_two, axis=0)
    mlp_bias_part = jnp.sum(mlp_in_grad, axis=0)
    resid_grad = cotangent.astype(F32) + norm_back(mlp_in_grad * gain_two, normed_two, inverse_two)
    branch_own = resid_grad.astype(BF)
    branch = seq_gather(branch_own).reshape(group, width)
    heads_grad = dot_cols(branch, proj_full).astype(BF).reshape(seq_count, MB, count, head_cols)

    down_sum = dot_rows(activ, cotangent_all).reshape(fsdp_count, quarter, width)
    down_grad = ring.scatter(lambda t: lax.dynamic_index_in_dim(down_sum, t, 0, keepdims=False)).astype(BF)
    fc_sum = dot_rows(mlp_in, pre_grad).reshape(fsdp_count, shard, fsdp_count * quarter)
    fc_sum = tie(fc_sum, down_grad)
    fc_grad = ring.scatter(lambda t: lax.dynamic_index_in_dim(fc_sum, t, 0, keepdims=False)).astype(BF)
    proj_sum = dot_rows(heads_rows, branch).reshape(fsdp_count, part, width)
    proj_sum = tie(proj_sum, fc_grad)
    proj_grad = ring.scatter(lambda t: lax.dynamic_index_in_dim(proj_sum, t, 0, keepdims=False)).astype(BF)
    proj_grad = lax.ppermute(proj_grad, ("seq", "fsdp"), back_pairs)

    query_grads, kv_grads = attend_back(
        tables, first, queries, kv_all, heads_out, logs, heads_grad, blocks
    )
    query_rows = query_grads.reshape(group, head_cols)
    query_sum = dot_rows(attn_in, query_rows).reshape(fsdp_count, shard, head_cols)
    query_weight_grad = ring.scatter(
        lambda t: lax.dynamic_index_in_dim(query_sum, t, 0, keepdims=False)
    ).astype(BF)
    attn_in_grad = seq_scatter(
        [
            dot_cols(query_rows[i * tokens_here : (i + 1) * tokens_here], qkv_full[:, :head_cols])
            for i in range(seq_count)
        ]
    )
    kv_grads = kv_grads.reshape(seq_count, fsdp_count, tokens_here, 2 * HD)
    kv_seq = seq_scatter(
        [
            lax.dynamic_index_in_dim(kv_grads, s ^ i, 0, keepdims=False).astype(F32)
            for i in range(seq_count)
        ]
    )
    kv_own = ring.scatter(lambda t: lax.dynamic_index_in_dim(kv_seq, t, 0, keepdims=False)).astype(BF)
    attn_in_grad = attn_in_grad + dot_cols(kv_own, qkv_full[:, head_cols:])
    normed_one, inverse_one = layer_norm(hidden_own)
    norm_gain_part = jnp.sum(attn_in_grad * normed_one, axis=0)
    norm_bias_part = jnp.sum(attn_in_grad, axis=0)
    grad_input = (resid_grad + norm_back(attn_in_grad * gain_one, normed_one, inverse_one)).astype(BF)

    kv_sum = dot_rows(own_attn_in, kv_own).reshape(fsdp_count, shard, 2 * HD)
    vector_sum = jnp.stack([norm_gain_part, norm_bias_part, mlp_gain_part, mlp_bias_part])
    vector_sum = vector_sum.reshape(4, fsdp_count, shard).transpose(1, 0, 2)
    tail_cols = max(2 * HD, shard)
    kv_sum = jnp.pad(kv_sum, ((0, 0), (0, 0), (0, tail_cols - 2 * HD)))
    vector_sum = jnp.pad(vector_sum, ((0, 0), (0, span - 4), (0, tail_cols - shard)))
    tail_sum = jnp.concatenate([kv_sum, vector_sum], axis=1)
    tail = ring.scatter(lambda t: lax.dynamic_index_in_dim(tail_sum, t, 0, keepdims=False)).astype(BF)
    tail = tail.astype(F32) + core_swap(tail).astype(F32)
    tail = tail.astype(BF)
    tail = tail.astype(F32) + chip_swap(tail).astype(F32)
    kv_weight_grad = tail[:shard, : 2 * HD]
    vector_grads = tail[shard : shard + 4, :shard]

    def spread(piece, axis):
        pieces = seq_gather(piece)
        shape = piece.shape[:axis] + (seq_count,) + piece.shape[axis:]
        out = jnp.zeros(shape, F32)
        for i in range(seq_count):
            start = [0] * len(shape)
            start[axis] = s ^ i
            out = lax.dynamic_update_slice(out, jnp.expand_dims(pieces[i], axis).astype(F32), start)
        return out

    grad_down = spread(down_grad, 0).reshape(ff_shard, width)
    grad_fc = spread(fc_grad.reshape(shard, fsdp_count, quarter), 2).reshape(shard, ff)
    grad_proj = spread(proj_grad, 0).reshape(shard, width)
    grad_query = spread(query_weight_grad, 1).reshape(shard, width)
    grad_qkv = jnp.concatenate([grad_query, kv_weight_grad], axis=1)
    return (
        result.reshape(hidden_in.shape),
        grad_input.reshape(hidden_in.shape),
        vector_grads[0],
        vector_grads[1],
        grad_qkv,
        grad_proj,
        vector_grads[2],
        vector_grads[3],
        grad_fc,
        grad_down,
    )


def solution(mesh):
    rows = P(None, ("seq", "fsdp"), None)
    vector = P("fsdp")
    matrix = P("fsdp", None)
    in_specs = (rows, rows, P(), P(), vector, vector, matrix, matrix, vector, vector, matrix, matrix)
    out_specs = (rows, rows, vector, vector, matrix, matrix, vector, vector, matrix, matrix)
    return jax.shard_map(shards, mesh=mesh, in_specs=in_specs, out_specs=out_specs, check_vma=False)
```

```python
import functools
import math

import jax
import jax.numpy as jnp
from jax import lax
from jax.experimental import pallas as pl
from jax.experimental.pallas import tpu as pltpu
from jax.sharding import PartitionSpec as P

HEADS = 16
HD = 128
MB = 2
BLOCK = 256
EPS = 1e-05
NEG_FILL = -1e30
SCALE = HD ** (-0.5)
LOG2E = math.log2(math.e)
BF = jnp.bfloat16
F32 = jnp.float32


def dot_rows(left, right):
    return lax.dot_general(left, right, (((0,), (0,)), ((), ())), preferred_element_type=F32)


def dot_cols(left, right):
    return lax.dot_general(left, right, (((1,), (1,)), ((), ())), preferred_element_type=F32)


def dot_plain(left, right):
    return lax.dot_general(left, right, (((1,), (0,)), ((), ())), preferred_element_type=F32)


def tie(value, after):
    return lax.optimization_barrier((value, after))[0]


def core_swap(value):
    return lax.ppermute(value, "seq", [(s, s ^ 1) for s in range(4)])


def chip_swap(value):
    return lax.ppermute(value, "seq", [(s, s ^ 2) for s in range(4)])


def seq_gather(value):
    across = chip_swap(value)
    pair = core_swap(value)
    pair_across = core_swap(across)
    return [value, pair, across, pair_across]


def seq_scatter(parts):
    far = core_swap(parts[3].astype(BF))
    near = core_swap(parts[1].astype(BF))
    across = chip_swap((parts[2] + far.astype(F32)).astype(BF))
    return parts[0] + near.astype(F32) + across.astype(F32)


def ring_order(count):
    return [2 * i for i in range(count // 2)] + [2 * i + 1 for i in reversed(range(count // 2))]


class Ring:
    def __init__(self, count):
        order = ring_order(count)
        self.count = count
        self.up = [(order[i], order[(i + 1) % count]) for i in range(count)]
        self.down = [(order[(i + 1) % count], order[i]) for i in range(count)]
        place = lax.axis_index("fsdp")
        half = count // 2
        self.place = place
        self.at = jnp.where(place % 2 == 0, place // 2, count - 1 - place // 2)

    def owner(self, step):
        count, half = self.count, self.count // 2
        at = lax.rem(self.at + (step + count), count)
        return jnp.where(at < half, 2 * at, 2 * (count - 1 - at) + 1)

    def gather(self, value, out):
        count = self.count
        half = value.shape[0] // 2

        def put(piece, owner, row):
            return lax.dynamic_update_slice(out, piece[None], (owner, row) + (0,) * (value.ndim - 1))

        low = high = value
        for step in range(1, count // 2 + 1):
            last = step == count // 2
            if last:
                low, high = low[:half], high[half:]
            low = lax.ppermute(low, "fsdp", self.up)
            high = lax.ppermute(high, "fsdp", self.down)
            low, high = yield low, high
            out = put(low, self.owner(-step), 0)
            out = put(high, self.owner(step), half if last else 0)
        return out

    def steps(self):
        half = self.count // 2
        return [half] + [sign * n for n in range(half - 1, 0, -1) for sign in (1, -1)] + [0]

    def order(self):
        return jnp.stack([self.owner(n) for n in self.steps()]).astype(jnp.int32)

    def scatter(self, chunk):
        count = self.count
        middle = chunk(count // 2)
        half = middle.shape[0] // 2
        up = middle[:half].astype(BF)
        down = middle[half:].astype(BF)
        for step in range(count // 2 - 1, -1, -1):
            up = lax.ppermute(up, "fsdp", self.up)
            down = lax.ppermute(down, "fsdp", self.down)
            up, down = yield up, down
            up, down = up.astype(F32), down.astype(F32)
            if step == count // 2 - 1:
                mine = chunk(step)
                up = jnp.concatenate([mine[:half] + up, mine[half:]], axis=0)
                mine = chunk(-step)
                down = jnp.concatenate([mine[:half], mine[half:] + down], axis=0)
            elif step:
                up = chunk(step) + up
                down = chunk(-step) + down
            else:
                return chunk(0) + up + down
            up = up.astype(BF)
            down = down.astype(BF)


class Flow:
    def __init__(self, ring, steps):
        self.ring, self.steps, self.result = ring, steps, None
        self.pending = next(steps)

    def advance(self, values=()):
        for _ in range(max(1, self.ring.count // 8)):
            if self.result is None:
                self.pending, values = lax.optimization_barrier((self.pending, values))
                try:
                    self.pending = self.steps.send(self.pending)
                except StopIteration as end:
                    self.result = end.value
        return values

    def finish(self):
        while self.result is None:
            self.advance()
        return self.result


def attend_kernel(tables, q_ref, kv_ref, first_ref, out_ref, log_ref, stack, high, total, result, *, heads, blocks):
    batch, piece = pl.program_id(0), pl.program_id(1)
    count = q_ref.shape[2]
    base = (batch * pl.num_programs(1) + piece) * (blocks + 4)
    chunk, low_tile, high_tile = tables[base], tables[base + 1], tables[base + 2]
    for h in range(heads):
        stack[h * count : (h + 1) * count, :] = q_ref[0, 0, :, h * HD : (h + 1) * HD]
    high[...] = jnp.full_like(high, NEG_FILL)
    total[...] = jnp.zeros_like(total)
    result[...] = jnp.zeros_like(result)
    tokens = chunk * count + lax.broadcasted_iota(jnp.int32, (1, count), 1)
    first = first_ref[0, 0]

    def step(tile, carry):
        @pl.when(tables[base + 4 + tile] != 0)
        def _():
            part = kv_ref[pl.ds(2 * tile, 2), 0].reshape(BLOCK, 2 * HD)
            keys, values = part[:, :HD], part[:, HD:]
            scores = dot_cols(keys, stack[...])
            index = tile * BLOCK + lax.broadcasted_iota(jnp.int32, (BLOCK, count), 0)
            allowed = (index <= tokens) & (index >= first)
            weights, scales = [], []
            for h in range(heads):
                lanes = slice(h * count, (h + 1) * count)
                score = jnp.where(allowed, scores[:, lanes] * (SCALE * LOG2E), NEG_FILL)
                old = high[:, lanes]
                new = jnp.maximum(old, jnp.max(score, axis=0, keepdims=True))
                weight = jnp.exp2(score - new)
                scale = jnp.exp2(old - new)
                high[:, lanes] = new
                total[:, lanes] = total[:, lanes] * scale + jnp.sum(weight, axis=0, keepdims=True)
                weights.append(weight.astype(BF))
                scales.append(scale)
            added = dot_rows(values, jnp.concatenate(weights, axis=1))
            result[...] = result[...] * jnp.concatenate(scales, axis=1) + added

        return carry

    lax.fori_loop(low_tile, high_tile, step, 0)
    final = result[...] / total[...]
    logs = high[...] + jnp.log2(total[...])
    for h in range(heads):
        lanes = slice(h * count, (h + 1) * count)
        out_ref[0, 0, :, h * HD : (h + 1) * HD] = final[:, lanes].T.astype(BF)
        log_ref[0, 0, h : h + 1, :] = logs[:, lanes]


def attend_back_kernel(
    tables,
    q_ref,
    kv_ref,
    first_ref,
    out_ref,
    log_ref,
    grad_ref,
    dq_ref,
    dkv_ref,
    stack,
    grads,
    logs,
    deltas,
    dq_sum,
    dkv_sum,
    *,
    heads,
    blocks,
):
    batch, piece = pl.program_id(0), pl.program_id(1)
    count = q_ref.shape[2]
    base = (batch * pl.num_programs(1) + piece) * (blocks + 4)
    chunk, low_tile, high_tile = tables[base], tables[base + 1], tables[base + 2]

    @pl.when(piece == 0)
    def _():
        dkv_sum[...] = jnp.zeros_like(dkv_sum)

    for h in range(heads):
        rows = slice(h * count, (h + 1) * count)
        cols = slice(h * HD, (h + 1) * HD)
        stack[rows, :] = q_ref[0, 0, :, cols]
        grad = grad_ref[0, 0, :, cols]
        grads[rows, :] = grad
        product = grad.astype(F32) * out_ref[0, 0, :, cols].astype(F32)
        deltas[:, rows] = jnp.sum(product.T, axis=0, keepdims=True)
        logs[:, rows] = log_ref[0, 0, h : h + 1, :]
    dq_sum[...] = jnp.zeros_like(dq_sum)
    tokens = chunk * count + lax.broadcasted_iota(jnp.int32, (1, count), 1)
    first = first_ref[0, 0]

    def step(tile, carry):
        @pl.when(tables[base + 4 + tile] != 0)
        def _():
            part = kv_ref[pl.ds(2 * tile, 2), 0].reshape(BLOCK, 2 * HD)
            keys, values = part[:, :HD], part[:, HD:]
            scores = dot_cols(keys, stack[...])
            pulls = dot_cols(values, grads[...])
            index = tile * BLOCK + lax.broadcasted_iota(jnp.int32, (BLOCK, count), 0)
            allowed = (index <= tokens) & (index >= first)
            weights, score_grads = [], []
            for h in range(heads):
                lanes = slice(h * count, (h + 1) * count)
                score = jnp.where(allowed, scores[:, lanes] * (SCALE * LOG2E), NEG_FILL)
                weight = jnp.exp2(score - logs[:, lanes])
                weights.append(weight.astype(BF))
                score_grads.append((weight * (pulls[:, lanes] - deltas[:, lanes])).astype(BF))
            weight = jnp.concatenate(weights, axis=1)
            score_grad = jnp.concatenate(score_grads, axis=1)
            dv = dot_plain(weight, grads[...])
            dk = dot_plain(score_grad, stack[...])
            dq_sum[...] += dot_rows(keys, score_grad)
            both = jnp.concatenate([dk, dv], axis=1).reshape(2, BLOCK // 2, 2 * HD)
            dkv_sum[pl.ds(2 * tile, 2)] += both

        return carry

    lax.fori_loop(low_tile, high_tile, step, 0)
    for h in range(heads):
        lanes = slice(h * count, (h + 1) * count)
        dq_ref[0, 0, :, h * HD : (h + 1) * HD] = (dq_sum[:, lanes] * SCALE).T.astype(BF)

    @pl.when(piece == pl.num_programs(1) - 1)
    def _():
        dkv_ref[:, 0, :, :HD] = (dkv_sum[:, :, :HD] * SCALE).astype(BF)
        dkv_ref[:, 0, :, HD:] = dkv_sum[:, :, HD:].astype(BF)


def attend(tables, first, queries, key_values, blocks):
    pieces, batches, count, width = queries.shape
    heads = width // HD
    chunks = key_values.shape[0]
    row_spec = pl.BlockSpec((1, 1, count, width), lambda b, i, t: (i, b, 0, 0))
    kv_spec = pl.BlockSpec((chunks, 1, count, 2 * HD), lambda b, i, t: (0, b, 0, 0))
    first_spec = pl.BlockSpec((1, 1, 1, count), lambda b, i, t: (i, b, 0, 0))
    log_spec = pl.BlockSpec((1, 1, heads, count), lambda b, i, t: (i, b, 0, 0))
    rows = heads * count
    return pl.pallas_call(
        functools.partial(attend_kernel, heads=heads, blocks=blocks),
        out_shape=(
            jax.ShapeDtypeStruct(queries.shape, BF),
            jax.ShapeDtypeStruct((pieces, batches, heads, count), F32),
        ),
        grid_spec=pltpu.PrefetchScalarGridSpec(
            num_scalar_prefetch=1,
            grid=(batches, pieces),
            in_specs=[row_spec, kv_spec, first_spec],
            out_specs=[row_spec, log_spec],
            scratch_shapes=[
                pltpu.VMEM((rows, HD), BF),
                pltpu.VMEM((1, rows), F32),
                pltpu.VMEM((1, rows), F32),
                pltpu.VMEM((HD, rows), F32),
            ],
        ),
        compiler_params=pltpu.CompilerParams(vmem_limit_bytes=40 << 20),
        cost_estimate=pl.CostEstimate(flops=4 * rows * HD * chunks * count * pieces, bytes_accessed=16 << 20, transcendentals=rows * chunks * count * pieces),
        name="attend",
    )(tables, queries, key_values, first)


def attend_back(tables, first, queries, key_values, out, logs, grads, blocks):
    pieces, batches, count, width = queries.shape
    heads = width // HD
    chunks = key_values.shape[0]
    row_spec = pl.BlockSpec((1, 1, count, width), lambda b, i, t: (i, b, 0, 0))
    kv_spec = pl.BlockSpec((chunks, 1, count, 2 * HD), lambda b, i, t: (0, b, 0, 0))
    first_spec = pl.BlockSpec((1, 1, 1, count), lambda b, i, t: (i, b, 0, 0))
    log_spec = pl.BlockSpec((1, 1, heads, count), lambda b, i, t: (i, b, 0, 0))
    rows = heads * count
    return pl.pallas_call(
        functools.partial(attend_back_kernel, heads=heads, blocks=blocks),
        out_shape=(
            jax.ShapeDtypeStruct(queries.shape, BF),
            jax.ShapeDtypeStruct(key_values.shape, BF),
        ),
        grid_spec=pltpu.PrefetchScalarGridSpec(
            num_scalar_prefetch=1,
            grid=(batches, pieces),
            in_specs=[row_spec, kv_spec, first_spec, row_spec, log_spec, row_spec],
            out_specs=[row_spec, kv_spec],
            scratch_shapes=[
                pltpu.VMEM((rows, HD), BF),
                pltpu.VMEM((rows, HD), BF),
                pltpu.VMEM((1, rows), F32),
                pltpu.VMEM((1, rows), F32),
                pltpu.VMEM((HD, rows), F32),
                pltpu.VMEM((chunks, count, 2 * HD), F32),
            ],
        ),
        compiler_params=pltpu.CompilerParams(vmem_limit_bytes=60 << 20),
        cost_estimate=pl.CostEstimate(flops=10 * rows * HD * chunks * count * pieces, bytes_accessed=32 << 20, transcendentals=rows * chunks * count * pieces),
        name="attend_back",
    )(tables, queries, key_values, first, out, logs, grads)


def neighbours(count):
    s, f = lax.axis_index("seq"), lax.axis_index("fsdp")
    half = count // 2
    at = jnp.where(lax.rem(f, 2) == 0, f // 2, count - 1 - f // 2)

    def owner(step):
        place = lax.rem(at + (step + count), count)
        return jnp.where(place < half, 2 * place, 2 * (count - 1 - place) + 1)

    chip = lax.rem(s + 2, 4)
    core = s + 1 - 2 * lax.rem(s, 2)
    return s, f, owner, (s, owner(1)), (s, owner(-1)), (chip, f), (core, f)


def greet(*devices):
    barrier = pltpu.get_barrier_semaphore()
    for device in devices:
        pl.semaphore_signal(barrier, inc=1, device_id=device, device_id_type=pl.DeviceIdType.MESH)
    pl.semaphore_wait(barrier, len(devices))


def send(source, target, sems, index, device):
    copy = pltpu.make_async_remote_copy(
        src_ref=source,
        dst_ref=target,
        send_sem=sems.at[(0,) + index],
        recv_sem=sems.at[(1,) + index],
        device_id=device,
        device_id_type=pl.DeviceIdType.MESH,
    )
    copy.start()
    return copy


class KernelRing:
    def __init__(self, count, own, slots, sems, owner, up, down):
        self.count, self.own, self.slots, self.sems = count, own, slots, sems
        self.owner, self.up, self.down = owner, up, down
        self.copies = {}

    def start(self, step):
        half = self.slots.shape[1] // 2
        for way, device in enumerate((self.up, self.down)):
            slot = self.slots.at[self.owner((1 - step) if way == 0 else (step - 1))]
            source = self.own if step == 1 else slot
            if step == self.count // 2:
                rows = pl.ds(way * half, half)
                source, slot = source.at[rows], slot.at[rows]
            self.copies[way, step] = send(source, slot, self.sems, (way, step - 1), device)

    def arrived(self, step):
        self.copies[0, step].wait_recv()
        self.copies[1, step].wait_recv()

    def finish(self):
        for copy in self.copies.values():
            copy.wait_send()


def opening_kernel(
    hidden,
    kv_own,
    q_own,
    proj_own,
    hidden_out,
    kvw_out,
    qw_out,
    proj_out,
    kv_out,
    weights,
    mine,
    hid_chip,
    hid_core,
    kvw_sems,
    q_sems,
    proj_sems,
    kv_sems,
    kv_chip,
    kv_core,
    kv_far,
    local,
    *,
    count,
    shard,
):
    s, f, owner, up, down, chip, core = neighbours(count)
    greet(up, down, chip, core)
    steps = count // 2
    rings = [
        KernelRing(count, own, slots, sems, owner, up, down)
        for own, slots, sems in ((kv_own, kvw_out, kvw_sems), (q_own, qw_out, q_sems), (proj_own, proj_out, proj_sems))
    ]
    kvw, qw, proj = rings
    kvw.start(1)
    rows = hidden.shape[0] // 2
    halves = [pl.ds(i * rows, rows) for i in range(2)]
    across = [send(hidden.at[half], hidden_out.at[2, half], hid_chip, (i,), chip) for i, half in enumerate(halves)]
    pair = [send(hidden, hidden_out.at[1], hid_core, (2,), core)]
    stays = [
        pltpu.make_async_copy(source, target, local.at[i])
        for i, (source, target) in enumerate(
            (
                (hidden, hidden_out.at[0]),
                (kv_own, kvw_out.at[f]),
                (q_own, qw_out.at[f]),
                (proj_own, proj_out.at[f]),
            )
        )
    ]
    for copy in stays:
        copy.start()
    values = hidden[...].astype(F32)
    mean = jnp.mean(values, axis=-1, keepdims=True)
    center = values - mean
    inverse = lax.rsqrt(jnp.mean(center * center, axis=-1, keepdims=True) + EPS)
    for step in range(2, steps + 1):
        kvw.arrived(step - 1)
        kvw.start(step)
    qw.start(1)
    kvw.arrived(steps)
    stays[1].wait()
    load = pltpu.make_async_copy(kvw_out, weights, local.at[4])
    load.start()
    load.wait()
    total = jnp.zeros((hidden.shape[0], kvw_out.shape[2]), F32)
    for t in range(count):
        cols = slice(t * shard, (t + 1) * shard)
        normed = (hidden[:, cols].astype(F32) - mean) * inverse
        gain = weights[t, shard : shard + 1, :shard].astype(F32)
        bias = weights[t, shard + 1 : shard + 2, :shard].astype(F32)
        total += dot_plain((normed * gain + bias).astype(BF), weights[t, :shard, :])
    mine[...] = total.astype(BF)

    spread = KernelRing(count, mine, kv_out.at[s], kv_sems, owner, up, down)
    spread.start(1)
    keep = pltpu.make_async_copy(mine, kv_out.at[s, f], local.at[5])
    keep.start()
    kv_across, kv_pair = [], []

    def pass_on(source, place):
        index = (len(kv_across),)
        kv_across.append((place, send(source, kv_out.at[s, place], kv_chip, index, chip)))
        kv_pair.append(send(source, kv_out.at[s, place], kv_core, index, core))

    pass_on(mine, f)
    for i, half in enumerate(halves):
        across[i].wait_recv()
        pair.append(send(hidden_out.at[2, half], hidden_out.at[2 + 1, half], hid_core, (i,), core))
    for step in range(1, steps + 1):
        spread.arrived(step)
        qw.arrived(step)
        if step < steps:
            spread.start(step + 1)
            qw.start(step + 1)
            for place in (owner(-step), owner(step)):
                pass_on(kv_out.at[s, place], place)
        else:
            pass_on(kv_out.at[s, owner(steps)], owner(steps))
        if step == 1:
            proj.start(1)
        else:
            proj.arrived(step - 1)
            proj.start(step)
    other = lax.rem(s + 2, 4)
    far = []
    for i, (place, copy) in enumerate(kv_across):
        copy.wait_recv()
        slot = kv_out.at[other, place]
        far.append(send(slot, slot, kv_far, (i,), core))
    proj.arrived(steps)
    for ring in rings + [spread]:
        ring.finish()
    for copy in [keep, stays[0], stays[2], stays[3]]:
        copy.wait()
    for copy in across + [copy for _, copy in kv_across]:
        copy.wait_send()
    for copy in pair + kv_pair + far:
        copy.wait()


def opening(hidden, kv_own, q_own, proj_own, fsdp_count, shard):
    count, width = hidden.shape
    dma = pltpu.SemaphoreType.DMA
    ring = dma((2, 2, fsdp_count // 2))
    anywhere = pl.BlockSpec(memory_space=pl.ANY)
    inside = pl.BlockSpec(memory_space=pltpu.VMEM)
    return pl.pallas_call(
        functools.partial(opening_kernel, count=fsdp_count, shard=shard),
        out_shape=(
            jax.ShapeDtypeStruct((4,) + hidden.shape, BF),
            jax.ShapeDtypeStruct((fsdp_count,) + kv_own.shape, BF),
            jax.ShapeDtypeStruct((fsdp_count,) + q_own.shape, BF),
            jax.ShapeDtypeStruct((fsdp_count,) + proj_own.shape, BF),
            jax.ShapeDtypeStruct((4, fsdp_count, count, 2 * HD), BF),
        ),
        in_specs=[inside, anywhere, anywhere, anywhere],
        out_specs=(anywhere,) * 5,
        scratch_shapes=[
            pltpu.VMEM((fsdp_count,) + kv_own.shape, BF),
            pltpu.VMEM((count, 2 * HD), BF),
            dma((2, 2)),
            dma((2, 3)),
            ring,
            ring,
            ring,
            ring,
            dma((2, fsdp_count)),
            dma((2, fsdp_count)),
            dma((2, fsdp_count)),
            dma((6,)),
        ],
        compiler_params=pltpu.CompilerParams(
            collective_id=1, has_side_effects=True, vmem_limit_bytes=40 << 20
        ),
        name="opening",
    )(hidden, kv_own, q_own, proj_own)


def pack_kernel(place, fc_ref, down_ref, own_ref, all_ref):
    rows = fc_ref.shape[0]
    own_ref[:rows] = fc_ref[...]
    own_ref[rows:] = down_ref[...]
    all_ref[0] = own_ref[...]


def pack(place, fc_weight, down_weight, parts, quarter):
    rows, width = fc_weight.shape[0], down_weight.shape[1]
    if quarter % 128:
        fc_own = lax.dynamic_slice_in_dim(fc_weight.reshape(rows, parts, 4, quarter), place[0], 1, 2)
        down_own = lax.dynamic_slice_in_dim(down_weight, place[0] * quarter, quarter, 0)
        own = jnp.concatenate([fc_own.reshape(rows, parts * quarter), down_own], axis=0)
        return own, lax.dynamic_update_slice(jnp.zeros((parts,) + own.shape, BF), own[None], (place[1], 0, 0))
    return pl.pallas_call(
        pack_kernel,
        out_shape=(
            jax.ShapeDtypeStruct((rows + quarter, width), BF),
            jax.ShapeDtypeStruct((parts, rows + quarter, width), BF),
        ),
        grid_spec=pltpu.PrefetchScalarGridSpec(
            num_scalar_prefetch=1,
            grid=(parts,),
            in_specs=[
                pl.BlockSpec((rows, quarter), lambda g, p: (0, g * 4 + p[0])),
                pl.BlockSpec((quarter, quarter), lambda g, p: (p[0], g)),
            ],
            out_specs=(
                pl.BlockSpec((rows + quarter, quarter), lambda g, p: (0, g)),
                pl.BlockSpec((1, rows + quarter, quarter), lambda g, p: (p[1], 0, g)),
            ),
        ),
        compiler_params=pltpu.CompilerParams(vmem_limit_bytes=30 << 20),
        name="pack",
    )(place, fc_weight, down_weight)


GELU_A = math.sqrt(2 / math.pi)
GELU_B = 0.044715


def middle_kernel(rows_ref, cot_ref, fc_ref, down_ref, activ_ref, pre_ref, grad_ref, total, *, step):
    tile = pl.program_id(0)
    fc = fc_ref[...].reshape(-1, fc_ref.shape[2])
    down = down_ref[...].reshape(-1, down_ref.shape[2])

    @pl.when(tile == 0)
    def _():
        total[...] = jnp.zeros_like(total)

    for at in range(0, rows_ref.shape[0], step):
        part = slice(at, at + step)
        value = dot_plain(rows_ref[part], fc)
        pull = dot_cols(cot_ref[part], down)
        square = value * value
        bend = jnp.tanh(GELU_A * value * (1.0 + GELU_B * square))
        half = 0.5 * (1.0 + bend)
        activ_ref[part] = (value * half).astype(BF)
        slope = half + 0.5 * value * (1.0 - bend * bend) * (GELU_A * (1.0 + 3.0 * GELU_B * square))
        grad = (pull * slope).astype(BF)
        pre_ref[part] = grad
        total[part] += dot_cols(grad, fc)

    @pl.when(tile == pl.num_programs(0) - 1)
    def _():
        grad_ref[...] = total[...].astype(BF)


def middle(rows, cot, weights, shard, tile):
    count, width = rows.shape
    parts, quarter = weights.shape[0], weights.shape[1] - shard
    hidden = parts * quarter
    per = tile // quarter
    whole = pl.BlockSpec((count, width), lambda n: (0, 0), pipeline_mode=pl.Buffered(1))
    cols = pl.BlockSpec((count, tile), lambda n: (0, n))
    return pl.pallas_call(
        functools.partial(middle_kernel, step=256),
        out_shape=(
            jax.ShapeDtypeStruct((count, hidden), BF),
            jax.ShapeDtypeStruct((count, hidden), BF),
            jax.ShapeDtypeStruct((count, width), BF),
        ),
        grid=(hidden // tile,),
        in_specs=[
            whole,
            whole,
            pl.BlockSpec((parts, shard, tile), lambda n: (0, 0, n)),
            pl.BlockSpec((per, quarter, width), lambda n: (n, 1, 0)),
        ],
        out_specs=(cols, cols, pl.BlockSpec((count, width), lambda n: (0, 0))),
        scratch_shapes=[pltpu.VMEM((count, width), F32)],
        compiler_params=pltpu.CompilerParams(vmem_limit_bytes=60 << 20),
        name="middle",
    )(rows, cot, weights, weights)


def turned_kernel(order, left_ref, right_ref, left_two_ref, right_two_ref, out_ref):
    rows = left_ref.shape[1]
    out_ref[0, :rows] = dot_rows(left_ref[...], right_ref[...]).astype(BF)
    out_ref[0, rows:] = dot_rows(left_two_ref[...], right_two_ref[...]).astype(BF)


def turned(order, left, right, left_two, right_two, shard):
    count, width = right.shape
    chunks = order.shape[0]
    if shard % 128:
        one = dot_rows(left, right).astype(BF).reshape(-1, shard, width)
        two = dot_rows(left_two, right_two).astype(BF).reshape(-1, shard, width)
        both = jnp.concatenate([one, two], axis=1)
        return jnp.stack([lax.dynamic_index_in_dim(both, order[i], 0, False) for i in range(chunks)])
    whole = pl.BlockSpec((count, width), lambda n, o: (0, 0), pipeline_mode=pl.Buffered(1))
    cols = pl.BlockSpec((count, shard), lambda n, o: (0, o[n]))
    return pl.pallas_call(
        turned_kernel,
        out_shape=jax.ShapeDtypeStruct((chunks, 2 * shard, width), BF),
        grid_spec=pltpu.PrefetchScalarGridSpec(
            num_scalar_prefetch=1,
            grid=(chunks,),
            in_specs=[cols, whole, cols, whole],
            out_specs=pl.BlockSpec((1, 2 * shard, width), lambda n, o: (n, 0, 0)),
        ),
        compiler_params=pltpu.CompilerParams(vmem_limit_bytes=60 << 20),
        name="turned",
    )(order, left, right, left_two, right_two)


def lower_kernel(rows_ref, down_ref, out_ref):
    down = down_ref[...].reshape(-1, down_ref.shape[2])
    out_ref[...] = dot_plain(rows_ref[...], down).astype(BF)


def lower(rows, weights, shard, tile):
    count = rows.shape[0]
    parts, quarter, width = weights.shape[0], weights.shape[1] - shard, weights.shape[2]
    return pl.pallas_call(
        lower_kernel,
        out_shape=jax.ShapeDtypeStruct((count, width), BF),
        grid=(width // tile,),
        in_specs=[
            pl.BlockSpec(rows.shape, lambda n: (0, 0), pipeline_mode=pl.Buffered(1)),
            pl.BlockSpec((parts, quarter, tile), lambda n: (0, 1, n)),
        ],
        out_specs=pl.BlockSpec((count, tile), lambda n: (0, n)),
        compiler_params=pltpu.CompilerParams(vmem_limit_bytes=60 << 20),
        name="lower",
    )(rows, weights)


def rows_kernel(place, *refs):
    *ins, out = refs
    rows = ins[0].shape[0]
    for i, ref in enumerate(ins):
        out[pl.ds(pl.multiple_of((place[0] ^ i) * rows, rows), rows), :] = ref[...].astype(F32)


def stack_rows(place, pieces, tile):
    rows, width = pieces[0].shape
    return pl.pallas_call(
        rows_kernel,
        out_shape=jax.ShapeDtypeStruct((len(pieces) * rows, width), F32),
        grid_spec=pltpu.PrefetchScalarGridSpec(
            num_scalar_prefetch=1,
            grid=(width // tile,),
            in_specs=[pl.BlockSpec((rows, tile), lambda n, p: (0, n))] * len(pieces),
            out_specs=pl.BlockSpec((len(pieces) * rows, tile), lambda n, p: (0, n)),
        ),
        compiler_params=pltpu.CompilerParams(vmem_limit_bytes=40 << 20),
        name="stack_rows",
    )(place, *pieces)


def cols_kernel(place, *refs):
    *ins, out = refs
    cols = ins[0].shape[1]
    for i, ref in enumerate(ins):
        out[:, pl.ds(pl.multiple_of((place[0] ^ i) * cols, cols), cols)] = ref[...].astype(F32)


def stack_cols(place, pieces, cols):
    rows, width = pieces[0].shape
    count = len(pieces)
    if cols % 128:
        ordered = jnp.stack([lax.dynamic_index_in_dim(jnp.stack(pieces), place[0] ^ i, 0, False) for i in range(count)])
        ordered = ordered.reshape(count, rows, width // cols, cols).transpose(1, 2, 0, 3)
        return ordered.reshape(rows, count * width).astype(F32)
    return pl.pallas_call(
        cols_kernel,
        out_shape=jax.ShapeDtypeStruct((rows, count * width), F32),
        grid_spec=pltpu.PrefetchScalarGridSpec(
            num_scalar_prefetch=1,
            grid=(width // cols,),
            in_specs=[pl.BlockSpec((rows, cols), lambda n, p: (0, n))] * count,
            out_specs=pl.BlockSpec((rows, count * cols), lambda n, p: (0, n)),
        ),
        compiler_params=pltpu.CompilerParams(vmem_limit_bytes=40 << 20),
        name="stack_cols",
    )(place, *pieces)


def layer_norm(values):
    mean = jnp.mean(values, axis=-1, keepdims=True)
    center = values - mean
    inverse = lax.rsqrt(jnp.mean(center * center, axis=-1, keepdims=True) + EPS)
    return center * inverse, inverse


def norm_back(grad, normed, inverse):
    return inverse * (
        grad
        - jnp.mean(grad, axis=-1, keepdims=True)
        - normed * jnp.mean(grad * normed, axis=-1, keepdims=True)
    )


def gelu_tanh(values):
    return jax.nn.gelu(values, approximate=True)


def shards(
    hidden_in,
    out_cotangent,
    positions,
    block_mask,
    norm_gain,
    norm_bias,
    qkv_weight,
    proj_weight,
    mlp_gain,
    mlp_bias,
    fc_weight,
    down_weight,
):
    seq_count = lax.axis_size("seq")
    fsdp_count = lax.axis_size("fsdp")
    s = lax.axis_index("seq")
    f = lax.axis_index("fsdp")
    ring = Ring(fsdp_count)
    count = hidden_in.shape[1]
    width = hidden_in.shape[2]
    length = positions.shape[1]
    blocks = length // BLOCK
    shard = qkv_weight.shape[0]
    ff = fc_weight.shape[1]
    ff_shard = down_weight.shape[0]
    heads_here = HEADS // seq_count
    head_cols = heads_here * HD
    quarter = ff_shard // seq_count
    tokens_here = MB * count
    group = seq_count * tokens_here

    chunk_ids = jnp.stack([(s ^ i) * fsdp_count + f for i in range(seq_count)]).astype(jnp.int32)
    token_ids = chunk_ids[:, None] * count + jnp.arange(count, dtype=jnp.int32)[None]
    first = token_ids[:, None, :] - jnp.stack(
        [lax.dynamic_slice_in_dim(positions, chunk_ids[i] * count, count, 1) for i in range(seq_count)]
    )
    first = first[:, :, None, :]
    high_tiles = (chunk_ids * count + count - 1) // BLOCK + 1
    tables = jnp.concatenate(
        [
            jnp.broadcast_to(chunk_ids[None, :, None], (MB, seq_count, 1)),
            (first[:, :, 0, :1] // BLOCK).transpose(1, 0, 2),
            jnp.broadcast_to(high_tiles[None, :, None], (MB, seq_count, 1)),
            jnp.zeros((MB, seq_count, 1), jnp.int32),
            jnp.stack([block_mask[:, (chunk_ids[i] * count) // BLOCK] for i in range(seq_count)], axis=1),
        ],
        axis=2,
    ).reshape(-1)

    place = jnp.stack([s, f]).astype(jnp.int32)
    ff_own, ff_slots = pack(place, fc_weight, down_weight, fsdp_count, quarter)
    flow = Flow(ring, ring.gather(ff_own, ff_slots))

    part = shard // seq_count
    pairs = [
        (j * fsdp_count + q * (fsdp_count // seq_count) + t // seq_count, q * fsdp_count + t)
        for q in range(seq_count)
        for t in range(fsdp_count)
        for j in [t % seq_count]
    ]
    back_pairs = [(b, a) for a, b in pairs]
    own_proj = lax.ppermute(
        lax.dynamic_slice_in_dim(proj_weight, s * part, part, 0), ("seq", "fsdp"), pairs
    )

    span = 32
    vectors = jnp.stack([norm_gain, norm_bias, mlp_gain, mlp_bias])
    padded = jnp.pad(vectors, ((0, span - 4), (0, 2 * HD - shard)))
    own_kv = jnp.concatenate([qkv_weight[:, width:], padded], axis=0)
    own_q = lax.dynamic_slice_in_dim(qkv_weight, s * head_cols, head_cols, 1)
    opened = opening(hidden_in.reshape(tokens_here, width), own_kv, own_q, own_proj, fsdp_count, shard)
    hidden_all, kv_ring, q_ring, proj_ring, kv_all = flow.advance(opened)
    kv_weight = kv_ring[:, :shard].reshape(width, 2 * HD)
    vectors = kv_ring[:, shard : shard + 4, :shard].transpose(1, 0, 2).reshape(4, width).astype(F32)
    gain_one, bias_one, gain_two, bias_two = vectors[0], vectors[1], vectors[2], vectors[3]
    q_weight = q_ring.reshape(width, head_cols)
    proj_full = proj_ring.reshape(head_cols, width)
    kv_all = kv_all.reshape(seq_count * fsdp_count, MB, count, 2 * HD)
    normed_all, _ = layer_norm(hidden_all.reshape(group, width).astype(F32))
    attn_in = (normed_all * gain_one + bias_one).astype(BF)
    own_attn_in = attn_in[:tokens_here]
    queries = dot_plain(attn_in, q_weight).astype(BF).reshape(seq_count, MB, count, head_cols)
    cotangent = out_cotangent.reshape(tokens_here, width)
    cotangent_all = jnp.concatenate(seq_gather(tie(cotangent, queries)), axis=0)

    heads_out, logs = attend(tables, first, queries, kv_all, blocks)
    heads_rows = heads_out.reshape(group, head_cols)

    def pieces(rows):
        return [rows[i * tokens_here : (i + 1) * tokens_here] for i in range(seq_count)]

    hidden_own = hidden_in.reshape(tokens_here, width).astype(F32)
    resid = hidden_own + seq_scatter([dot_plain(piece, proj_full) for piece in pieces(heads_rows)])
    resid, cotangent_all = flow.advance((resid, cotangent_all))
    normed_two, inverse_two = layer_norm(resid)
    mlp_in_own = (normed_two * gain_two + bias_two).astype(BF)
    mlp_in = flow.advance(jnp.concatenate(seq_gather(mlp_in_own), axis=0))
    weights = flow.finish()
    activ, pre_grad, mlp_in_part = middle(mlp_in, cotangent_all, weights, shard, BLOCK)
    mlp_in_grad = seq_scatter([piece.astype(F32) for piece in pieces(mlp_in_part)])

    order = ring.order()
    early = 3
    ff_early = turned(order[:early], mlp_in, pre_grad, activ, cotangent_all, shard)
    ff_late = turned(order[early:], mlp_in, pre_grad, activ, cotangent_all, shard)
    steps = ring.steps()

    def ff_chunk(n):
        at = steps.index(n)
        return (ff_early[at] if at < early else ff_late[at - early]).astype(F32)

    flow = Flow(ring, ring.scatter(ff_chunk))
    lowered = lower(activ, weights, shard, BLOCK)
    mlp_in_grad, lowered = flow.advance((mlp_in_grad, lowered))

    mlp_gain_part = jnp.sum(mlp_in_grad * normed_two, axis=0)
    mlp_bias_part = jnp.sum(mlp_in_grad, axis=0)
    resid_grad = cotangent.astype(F32) + norm_back(mlp_in_grad * gain_two, normed_two, inverse_two)
    branch_own = resid_grad.astype(BF)
    branch, lowered = flow.advance((jnp.concatenate(seq_gather(branch_own), axis=0), lowered))
    result = (resid + seq_scatter([piece.astype(F32) for piece in pieces(lowered)])).astype(BF)
    heads_grad = dot_cols(branch, proj_full).astype(BF).reshape(seq_count, MB, count, head_cols)
    query_grads, kv_grads = attend_back(
        tables, first, queries, kv_all, heads_out, logs, heads_grad, blocks
    )
    query_grads, kv_grads, result = flow.advance((query_grads, kv_grads, result))
    query_rows = query_grads.reshape(group, head_cols)

    proj_sum = dot_rows(heads_rows, branch).astype(BF).reshape(fsdp_count, part, width)
    query_sum = dot_rows(attn_in, query_rows).astype(BF).reshape(fsdp_count, shard, head_cols)
    folds = width // head_cols
    query_sum = (
        query_sum.reshape(fsdp_count, folds, shard // folds, head_cols)
        .transpose(0, 2, 1, 3)
        .reshape(fsdp_count, shard // folds, width)
    )
    attn_sum = jnp.concatenate([proj_sum, query_sum], axis=1)
    attn_flow = Flow(
        ring,
        ring.scatter(
            lambda n: lax.dynamic_index_in_dim(attn_sum, ring.owner(n), 0, keepdims=False).astype(F32)
        ),
    )
    attn_grad = attn_flow.finish().astype(BF)
    proj_grad = lax.ppermute(attn_grad[:part], ("seq", "fsdp"), back_pairs)
    query_weight_grad = (
        attn_grad[part:].reshape(shard // folds, folds, head_cols).transpose(1, 0, 2).reshape(shard, head_cols)
    )

    attn_in_grad = seq_scatter(
        [dot_cols(piece, q_weight) for piece in pieces(query_rows)]
    )
    kv_grads = kv_grads.reshape(seq_count, fsdp_count, tokens_here, 2 * HD)
    kv_seq = seq_scatter(
        [
            lax.dynamic_index_in_dim(kv_grads, s ^ i, 0, keepdims=False).astype(F32)
            for i in range(seq_count)
        ]
    )
    kv_seq = flow.advance(kv_seq)
    ff_grad = flow.finish().astype(BF)
    kv_flow = Flow(
        ring,
        ring.scatter(lambda n: lax.dynamic_index_in_dim(kv_seq, ring.owner(n), 0, keepdims=False)),
    )
    kv_own = kv_flow.finish().astype(BF)
    attn_in_grad = attn_in_grad + dot_cols(kv_own, kv_weight)
    normed_one, inverse_one = layer_norm(hidden_own)
    norm_gain_part = jnp.sum(attn_in_grad * normed_one, axis=0)
    norm_bias_part = jnp.sum(attn_in_grad, axis=0)
    grad_input = (resid_grad + norm_back(attn_in_grad * gain_one, normed_one, inverse_one)).astype(BF)

    kv_sum = dot_rows(own_attn_in, kv_own).reshape(fsdp_count, shard, 2 * HD)
    vector_sum = jnp.stack([norm_gain_part, norm_bias_part, mlp_gain_part, mlp_bias_part])
    vector_sum = vector_sum.reshape(4, fsdp_count, shard).transpose(1, 0, 2)
    tail_cols = max(2 * HD, shard)
    kv_sum = jnp.pad(kv_sum, ((0, 0), (0, 0), (0, tail_cols - 2 * HD)))
    vector_sum = jnp.pad(vector_sum, ((0, 0), (0, span - 4), (0, tail_cols - shard)))
    tail_sum = jnp.concatenate([kv_sum, vector_sum], axis=1)
    tail_flow = Flow(
        ring,
        ring.scatter(lambda n: lax.dynamic_index_in_dim(tail_sum, ring.owner(n), 0, keepdims=False)),
    )
    tail = tail_flow.finish().astype(BF)
    tail = tail.astype(F32) + core_swap(tail).astype(F32)
    tail = tail.astype(BF)
    tail = tail.astype(F32) + chip_swap(tail).astype(F32)
    kv_weight_grad = tail[:shard, : 2 * HD]
    vector_grads = tail[shard : shard + 4, :shard]

    ff_pieces = seq_gather(ff_grad)
    grad_fc = stack_cols(place, [piece[:shard] for piece in ff_pieces], quarter)
    grad_down = stack_rows(place, [piece[shard:] for piece in ff_pieces], BLOCK)
    grad_proj = stack_rows(place, seq_gather(proj_grad), BLOCK)
    grad_query = stack_cols(place, seq_gather(query_weight_grad), head_cols)
    grad_qkv = jnp.concatenate([grad_query, kv_weight_grad], axis=1)
    return (
        result.reshape(hidden_in.shape),
        grad_input.reshape(hidden_in.shape),
        vector_grads[0],
        vector_grads[1],
        grad_qkv,
        grad_proj,
        vector_grads[2],
        vector_grads[3],
        grad_fc,
        grad_down,
    )


def solution(mesh):
    rows = P(None, ("seq", "fsdp"), None)
    vector = P("fsdp")
    matrix = P("fsdp", None)
    in_specs = (rows, rows, P(), P(), vector, vector, matrix, matrix, vector, vector, matrix, matrix)
    out_specs = (rows, rows, vector, vector, matrix, matrix, vector, vector, matrix, matrix)
    return jax.shard_map(shards, mesh=mesh, in_specs=in_specs, out_specs=out_specs, check_vma=False)
```

```python
import functools
import math

import jax
import jax.numpy as jnp
from jax import lax
from jax.experimental import pallas as pl
from jax.experimental.pallas import tpu as pltpu
from jax.sharding import PartitionSpec as P

HEADS = 16
HD = 128
MB = 2
BLOCK = 256
EPS = 1e-05
NEG_FILL = -1e30
SCALE = HD ** (-0.5)
LOG2E = math.log2(math.e)
BF = jnp.bfloat16
COST = pl.CostEstimate(flops=0, bytes_accessed=0, transcendentals=0)
F32 = jnp.float32


def dot_rows(left, right):
    return lax.dot_general(left, right, (((0,), (0,)), ((), ())), preferred_element_type=F32)


def dot_cols(left, right):
    return lax.dot_general(left, right, (((1,), (1,)), ((), ())), preferred_element_type=F32)


def dot_plain(left, right):
    return lax.dot_general(left, right, (((1,), (0,)), ((), ())), preferred_element_type=F32)


def tie(value, after):
    return lax.optimization_barrier((value, after))[0]


def core_swap(value):
    return lax.ppermute(value, "seq", [(s, s ^ 1) for s in range(4)])


def chip_swap(value):
    return lax.ppermute(value, "seq", [(s, s ^ 2) for s in range(4)])


def seq_gather(value):
    across = chip_swap(value)
    pair = core_swap(value)
    pair_across = core_swap(across)
    return [value, pair, across, pair_across]


def seq_scatter(parts):
    far = core_swap(parts[3].astype(BF))
    near = core_swap(parts[1].astype(BF))
    across = chip_swap((parts[2] + far.astype(F32)).astype(BF))
    return parts[0] + near.astype(F32) + across.astype(F32)


def ring_order(count):
    return [2 * i for i in range(count // 2)] + [2 * i + 1 for i in reversed(range(count // 2))]


class Ring:
    def __init__(self, count):
        order = ring_order(count)
        self.count = count
        self.up = [(order[i], order[(i + 1) % count]) for i in range(count)]
        self.down = [(order[(i + 1) % count], order[i]) for i in range(count)]
        place = lax.axis_index("fsdp")
        half = count // 2
        self.place = place
        self.at = jnp.where(place % 2 == 0, place // 2, count - 1 - place // 2)

    def owner(self, step):
        count, half = self.count, self.count // 2
        at = lax.rem(self.at + (step + count), count)
        return jnp.where(at < half, 2 * at, 2 * (count - 1 - at) + 1)

    def gather(self, value, out):
        count = self.count
        half = value.shape[0] // 2

        def put(piece, owner, row):
            return lax.dynamic_update_slice(out, piece[None], (owner, row) + (0,) * (value.ndim - 1))

        low = high = value
        for step in range(1, count // 2 + 1):
            last = step == count // 2
            if last:
                low, high = low[:half], high[half:]
            low = lax.ppermute(low, "fsdp", self.up)
            high = lax.ppermute(high, "fsdp", self.down)
            low, high = yield low, high
            out = put(low, self.owner(-step), 0)
            out = put(high, self.owner(step), half if last else 0)
        return out

    def steps(self):
        half = self.count // 2
        return [half] + [sign * n for n in range(half - 1, 0, -1) for sign in (1, -1)] + [0]

    def order(self):
        return jnp.stack([self.owner(n) for n in self.steps()]).astype(jnp.int32)

    def scatter(self, chunk, last=True):
        count = self.count
        middle = chunk(count // 2)
        half = middle.shape[0] // 2
        up = middle[:half].astype(BF)
        down = middle[half:].astype(BF)
        for step in range(count // 2 - 1, -1, -1):
            if step == 0 and not last:
                return up, down
            up = lax.ppermute(up, "fsdp", self.up)
            down = lax.ppermute(down, "fsdp", self.down)
            up, down = yield up, down
            up, down = up.astype(F32), down.astype(F32)
            if step == count // 2 - 1:
                mine = chunk(step)
                up = jnp.concatenate([mine[:half] + up, mine[half:]], axis=0)
                mine = chunk(-step)
                down = jnp.concatenate([mine[:half], mine[half:] + down], axis=0)
            elif step:
                up = chunk(step) + up
                down = chunk(-step) + down
            else:
                return chunk(0) + up + down
            up = up.astype(BF)
            down = down.astype(BF)


class Flow:
    def __init__(self, ring, steps):
        self.ring, self.steps, self.result = ring, steps, None
        self.pending = next(steps)

    def advance(self, values=()):
        for _ in range(max(1, self.ring.count // 8)):
            if self.result is None:
                self.pending, values = lax.optimization_barrier((self.pending, values))
                try:
                    self.pending = self.steps.send(self.pending)
                except StopIteration as end:
                    self.result = end.value
        return values

    def finish(self):
        while self.result is None:
            self.advance()
        return self.result


def attend_kernel(tables, q_ref, kv_ref, first_ref, out_ref, log_ref, stack, high, total, result, *, heads, blocks):
    batch, piece = pl.program_id(0), pl.program_id(1)
    count = q_ref.shape[2]
    base = (batch * pl.num_programs(1) + piece) * (blocks + 4)
    chunk, low_tile, high_tile = tables[base], tables[base + 1], tables[base + 2]
    for h in range(heads):
        stack[h * count : (h + 1) * count, :] = q_ref[0, 0, :, h * HD : (h + 1) * HD]
    high[...] = jnp.full_like(high, NEG_FILL)
    total[...] = jnp.zeros_like(total)
    result[...] = jnp.zeros_like(result)
    tokens = chunk * count + lax.broadcasted_iota(jnp.int32, (1, count), 1)
    first = first_ref[0, 0]

    def step(tile, carry):
        @pl.when(tables[base + 4 + tile] != 0)
        def _():
            part = kv_ref[pl.ds(2 * tile, 2), 0].reshape(BLOCK, 2 * HD)
            keys, values = part[:, :HD], part[:, HD:]
            scores = dot_cols(keys, stack[...])
            index = tile * BLOCK + lax.broadcasted_iota(jnp.int32, (BLOCK, count), 0)
            allowed = (index <= tokens) & (index >= first)
            weights, scales = [], []
            for h in range(heads):
                lanes = slice(h * count, (h + 1) * count)
                score = jnp.where(allowed, scores[:, lanes] * (SCALE * LOG2E), NEG_FILL)
                old = high[:, lanes]
                new = jnp.maximum(old, jnp.max(score, axis=0, keepdims=True))
                weight = jnp.exp2(score - new)
                scale = jnp.exp2(old - new)
                high[:, lanes] = new
                total[:, lanes] = total[:, lanes] * scale + jnp.sum(weight, axis=0, keepdims=True)
                weights.append(weight.astype(BF))
                scales.append(scale)
            added = dot_rows(values, jnp.concatenate(weights, axis=1))
            result[...] = result[...] * jnp.concatenate(scales, axis=1) + added

        return carry

    lax.fori_loop(low_tile, high_tile, step, 0)
    final = result[...] / total[...]
    logs = high[...] + jnp.log2(total[...])
    for h in range(heads):
        lanes = slice(h * count, (h + 1) * count)
        out_ref[0, 0, :, h * HD : (h + 1) * HD] = final[:, lanes].T.astype(BF)
        log_ref[0, 0, h : h + 1, :] = logs[:, lanes]


def attend_back_kernel(
    tables,
    q_ref,
    kv_ref,
    first_ref,
    out_ref,
    log_ref,
    grad_ref,
    dq_ref,
    dkv_ref,
    stack,
    grads,
    logs,
    deltas,
    dq_sum,
    dkv_sum,
    *,
    heads,
    blocks,
):
    batch, piece = pl.program_id(0), pl.program_id(1)
    count = q_ref.shape[2]
    base = (batch * pl.num_programs(1) + piece) * (blocks + 4)
    chunk, low_tile, high_tile = tables[base], tables[base + 1], tables[base + 2]

    @pl.when(piece == 0)
    def _():
        dkv_sum[...] = jnp.zeros_like(dkv_sum)

    for h in range(heads):
        rows = slice(h * count, (h + 1) * count)
        cols = slice(h * HD, (h + 1) * HD)
        stack[rows, :] = q_ref[0, 0, :, cols]
        grad = grad_ref[0, 0, :, cols]
        grads[rows, :] = grad
        product = grad.astype(F32) * out_ref[0, 0, :, cols].astype(F32)
        deltas[:, rows] = jnp.sum(product.T, axis=0, keepdims=True)
        logs[:, rows] = log_ref[0, 0, h : h + 1, :]
    dq_sum[...] = jnp.zeros_like(dq_sum)
    tokens = chunk * count + lax.broadcasted_iota(jnp.int32, (1, count), 1)
    first = first_ref[0, 0]

    def step(tile, carry):
        @pl.when(tables[base + 4 + tile] != 0)
        def _():
            part = kv_ref[pl.ds(2 * tile, 2), 0].reshape(BLOCK, 2 * HD)
            keys, values = part[:, :HD], part[:, HD:]
            scores = dot_cols(keys, stack[...])
            pulls = dot_cols(values, grads[...])
            index = tile * BLOCK + lax.broadcasted_iota(jnp.int32, (BLOCK, count), 0)
            allowed = (index <= tokens) & (index >= first)
            weights, score_grads = [], []
            for h in range(heads):
                lanes = slice(h * count, (h + 1) * count)
                score = jnp.where(allowed, scores[:, lanes] * (SCALE * LOG2E), NEG_FILL)
                weight = jnp.exp2(score - logs[:, lanes])
                weights.append(weight.astype(BF))
                score_grads.append((weight * (pulls[:, lanes] - deltas[:, lanes])).astype(BF))
            weight = jnp.concatenate(weights, axis=1)
            score_grad = jnp.concatenate(score_grads, axis=1)
            dv = dot_plain(weight, grads[...])
            dk = dot_plain(score_grad, stack[...])
            dq_sum[...] += dot_rows(keys, score_grad)
            both = jnp.concatenate([dk, dv], axis=1).reshape(2, BLOCK // 2, 2 * HD)
            dkv_sum[pl.ds(2 * tile, 2)] += both

        return carry

    lax.fori_loop(low_tile, high_tile, step, 0)
    for h in range(heads):
        lanes = slice(h * count, (h + 1) * count)
        dq_ref[0, 0, :, h * HD : (h + 1) * HD] = (dq_sum[:, lanes] * SCALE).T.astype(BF)

    @pl.when(piece == pl.num_programs(1) - 1)
    def _():
        dkv_ref[:, 0, :, :HD] = (dkv_sum[:, :, :HD] * SCALE).astype(BF)
        dkv_ref[:, 0, :, HD:] = dkv_sum[:, :, HD:].astype(BF)


def attend(tables, first, queries, key_values, blocks):
    pieces, batches, count, width = queries.shape
    heads = width // HD
    chunks = key_values.shape[0]
    row_spec = pl.BlockSpec((1, 1, count, width), lambda b, i, t: (i, b, 0, 0))
    kv_spec = pl.BlockSpec((chunks, 1, count, 2 * HD), lambda b, i, t: (0, b, 0, 0))
    first_spec = pl.BlockSpec((1, 1, 1, count), lambda b, i, t: (i, b, 0, 0))
    log_spec = pl.BlockSpec((1, 1, heads, count), lambda b, i, t: (i, b, 0, 0))
    rows = heads * count
    return pl.pallas_call(
        functools.partial(attend_kernel, heads=heads, blocks=blocks),
        out_shape=(
            jax.ShapeDtypeStruct(queries.shape, BF),
            jax.ShapeDtypeStruct((pieces, batches, heads, count), F32),
        ),
        grid_spec=pltpu.PrefetchScalarGridSpec(
            num_scalar_prefetch=1,
            grid=(batches, pieces),
            in_specs=[row_spec, kv_spec, first_spec],
            out_specs=[row_spec, log_spec],
            scratch_shapes=[
                pltpu.VMEM((rows, HD), BF),
                pltpu.VMEM((1, rows), F32),
                pltpu.VMEM((1, rows), F32),
                pltpu.VMEM((HD, rows), F32),
            ],
        ),
        compiler_params=pltpu.CompilerParams(vmem_limit_bytes=40 << 20),
        cost_estimate=COST,
        name="attend",
    )(tables, queries, key_values, first)


def attend_back(tables, first, queries, key_values, out, logs, grads, blocks):
    pieces, batches, count, width = queries.shape
    heads = width // HD
    chunks = key_values.shape[0]
    row_spec = pl.BlockSpec((1, 1, count, width), lambda b, i, t: (i, b, 0, 0))
    kv_spec = pl.BlockSpec((chunks, 1, count, 2 * HD), lambda b, i, t: (0, b, 0, 0))
    first_spec = pl.BlockSpec((1, 1, 1, count), lambda b, i, t: (i, b, 0, 0))
    log_spec = pl.BlockSpec((1, 1, heads, count), lambda b, i, t: (i, b, 0, 0))
    rows = heads * count
    return pl.pallas_call(
        functools.partial(attend_back_kernel, heads=heads, blocks=blocks),
        out_shape=(
            jax.ShapeDtypeStruct(queries.shape, BF),
            jax.ShapeDtypeStruct(key_values.shape, BF),
        ),
        grid_spec=pltpu.PrefetchScalarGridSpec(
            num_scalar_prefetch=1,
            grid=(batches, pieces),
            in_specs=[row_spec, kv_spec, first_spec, row_spec, log_spec, row_spec],
            out_specs=[row_spec, kv_spec],
            scratch_shapes=[
                pltpu.VMEM((rows, HD), BF),
                pltpu.VMEM((rows, HD), BF),
                pltpu.VMEM((1, rows), F32),
                pltpu.VMEM((1, rows), F32),
                pltpu.VMEM((HD, rows), F32),
                pltpu.VMEM((chunks, count, 2 * HD), F32),
            ],
        ),
        compiler_params=pltpu.CompilerParams(vmem_limit_bytes=60 << 20),
        cost_estimate=COST,
        name="attend_back",
    )(tables, queries, key_values, first, out, logs, grads)


def neighbours(count):
    s, f = lax.axis_index("seq"), lax.axis_index("fsdp")
    half = count // 2
    at = jnp.where(lax.rem(f, 2) == 0, f // 2, count - 1 - f // 2)

    def owner(step):
        place = lax.rem(at + (step + count), count)
        return jnp.where(place < half, 2 * place, 2 * (count - 1 - place) + 1)

    chip = lax.rem(s + 2, 4)
    core = s + 1 - 2 * lax.rem(s, 2)
    return s, f, owner, (s, owner(1)), (s, owner(-1)), (chip, f), (core, f)


def greet(*devices):
    barrier = pltpu.get_barrier_semaphore()
    for device in devices:
        pl.semaphore_signal(barrier, inc=1, device_id=device, device_id_type=pl.DeviceIdType.MESH)
    pl.semaphore_wait(barrier, len(devices))


def send(source, target, sems, index, device):
    copy = pltpu.make_async_remote_copy(
        src_ref=source,
        dst_ref=target,
        send_sem=sems.at[(0,) + index],
        recv_sem=sems.at[(1,) + index],
        device_id=device,
        device_id_type=pl.DeviceIdType.MESH,
    )
    copy.start()
    return copy


class KernelRing:
    def __init__(self, count, own, slots, sems, owner, up, down):
        self.count, self.own, self.slots, self.sems = count, own, slots, sems
        self.owner, self.up, self.down = owner, up, down
        self.copies = {}

    def start(self, step):
        half = self.slots.shape[1] // 2
        for way, device in enumerate((self.up, self.down)):
            slot = self.slots.at[self.owner((1 - step) if way == 0 else (step - 1))]
            source = self.own if step == 1 else slot
            if step == self.count // 2:
                rows = pl.ds(way * half, half)
                source, slot = source.at[rows], slot.at[rows]
            self.copies[way, step] = send(source, slot, self.sems, (way, step - 1), device)

    def arrived(self, step):
        self.copies[0, step].wait_recv()
        self.copies[1, step].wait_recv()

    def finish(self):
        for copy in self.copies.values():
            copy.wait_send()


def opening_kernel(
    hidden,
    kv_own,
    q_own,
    proj_own,
    hidden_out,
    kvw_out,
    qw_out,
    proj_out,
    kv_out,
    weights,
    mine,
    hid_chip,
    hid_core,
    kvw_sems,
    q_sems,
    proj_sems,
    kv_sems,
    kv_chip,
    kv_core,
    kv_far,
    local,
    *,
    count,
    shard,
):
    s, f, owner, up, down, chip, core = neighbours(count)
    greet(up, down, chip, core)
    steps = count // 2
    rings = [
        KernelRing(count, own, slots, sems, owner, up, down)
        for own, slots, sems in ((kv_own, kvw_out, kvw_sems), (q_own, qw_out, q_sems), (proj_own, proj_out, proj_sems))
    ]
    kvw, qw, proj = rings
    kvw.start(1)
    rows = hidden.shape[0] // 2
    halves = [pl.ds(i * rows, rows) for i in range(2)]
    across = [send(hidden.at[half], hidden_out.at[2, half], hid_chip, (i,), chip) for i, half in enumerate(halves)]
    pair = [send(hidden, hidden_out.at[1], hid_core, (2,), core)]
    stays = [
        pltpu.make_async_copy(source, target, local.at[i])
        for i, (source, target) in enumerate(
            (
                (hidden, hidden_out.at[0]),
                (kv_own, kvw_out.at[f]),
                (q_own, qw_out.at[f]),
                (proj_own, proj_out.at[f]),
            )
        )
    ]
    for copy in stays:
        copy.start()
    values = hidden[...].astype(F32)
    mean = jnp.mean(values, axis=-1, keepdims=True)
    center = values - mean
    inverse = lax.rsqrt(jnp.mean(center * center, axis=-1, keepdims=True) + EPS)
    for step in range(2, steps + 1):
        kvw.arrived(step - 1)
        kvw.start(step)
    qw.start(1)
    kvw.arrived(steps)
    stays[1].wait()
    load = pltpu.make_async_copy(kvw_out, weights, local.at[4])
    load.start()
    load.wait()
    total = jnp.zeros((hidden.shape[0], kvw_out.shape[2]), F32)
    for t in range(count):
        cols = slice(t * shard, (t + 1) * shard)
        normed = (hidden[:, cols].astype(F32) - mean) * inverse
        gain = weights[t, shard : shard + 1, :shard].astype(F32)
        bias = weights[t, shard + 1 : shard + 2, :shard].astype(F32)
        total += dot_plain((normed * gain + bias).astype(BF), weights[t, :shard, :])
    mine[...] = total.astype(BF)

    spread = KernelRing(count, mine, kv_out.at[s], kv_sems, owner, up, down)
    spread.start(1)
    keep = pltpu.make_async_copy(mine, kv_out.at[s, f], local.at[5])
    keep.start()
    kv_across, kv_pair = [], []

    def pass_on(source, place):
        index = (len(kv_across),)
        kv_across.append((place, send(source, kv_out.at[s, place], kv_chip, index, chip)))
        kv_pair.append(send(source, kv_out.at[s, place], kv_core, index, core))

    pass_on(mine, f)
    for i, half in enumerate(halves):
        across[i].wait_recv()
        pair.append(send(hidden_out.at[2, half], hidden_out.at[2 + 1, half], hid_core, (i,), core))
    for step in range(1, steps + 1):
        spread.arrived(step)
        qw.arrived(step)
        if step < steps:
            spread.start(step + 1)
            qw.start(step + 1)
            for place in (owner(-step), owner(step)):
                pass_on(kv_out.at[s, place], place)
        else:
            pass_on(kv_out.at[s, owner(steps)], owner(steps))
        if step == 1:
            proj.start(1)
        else:
            proj.arrived(step - 1)
            proj.start(step)
    other = lax.rem(s + 2, 4)
    far = []
    for i, (place, copy) in enumerate(kv_across):
        copy.wait_recv()
        slot = kv_out.at[other, place]
        far.append(send(slot, slot, kv_far, (i,), core))
    proj.arrived(steps)
    for ring in rings + [spread]:
        ring.finish()
    for copy in [keep, stays[0], stays[2], stays[3]]:
        copy.wait()
    for copy in across + [copy for _, copy in kv_across]:
        copy.wait_send()
    for copy in pair + kv_pair + far:
        copy.wait()


def opening(hidden, kv_own, q_own, proj_own, fsdp_count, shard):
    count, width = hidden.shape
    dma = pltpu.SemaphoreType.DMA
    ring = dma((2, 2, fsdp_count // 2))
    anywhere = pl.BlockSpec(memory_space=pl.ANY)
    inside = pl.BlockSpec(memory_space=pltpu.VMEM)
    return pl.pallas_call(
        functools.partial(opening_kernel, count=fsdp_count, shard=shard),
        out_shape=(
            jax.ShapeDtypeStruct((4,) + hidden.shape, BF),
            jax.ShapeDtypeStruct((fsdp_count,) + kv_own.shape, BF),
            jax.ShapeDtypeStruct((fsdp_count,) + q_own.shape, BF),
            jax.ShapeDtypeStruct((fsdp_count,) + proj_own.shape, BF),
            jax.ShapeDtypeStruct((4, fsdp_count, count, 2 * HD), BF),
        ),
        in_specs=[inside, anywhere, anywhere, anywhere],
        out_specs=(anywhere,) * 5,
        scratch_shapes=[
            pltpu.VMEM((fsdp_count,) + kv_own.shape, BF),
            pltpu.VMEM((count, 2 * HD), BF),
            dma((2, 2)),
            dma((2, 3)),
            ring,
            ring,
            ring,
            ring,
            dma((2, fsdp_count)),
            dma((2, fsdp_count)),
            dma((2, fsdp_count)),
            dma((6,)),
        ],
        compiler_params=pltpu.CompilerParams(
            collective_id=1, has_side_effects=True, vmem_limit_bytes=40 << 20
        ),
        cost_estimate=COST,
        name="opening",
    )(hidden, kv_own, q_own, proj_own)


def pack_kernel(place, fc_ref, down_ref, own_ref, all_ref):
    rows = fc_ref.shape[0]
    own_ref[:rows] = fc_ref[...]
    own_ref[rows:] = down_ref[...]
    all_ref[0] = own_ref[...]


def pack(place, fc_weight, down_weight, parts, quarter):
    rows, width = fc_weight.shape[0], down_weight.shape[1]
    if quarter % 128:
        fc_own = lax.dynamic_slice_in_dim(fc_weight.reshape(rows, parts, 4, quarter), place[0], 1, 2)
        down_own = lax.dynamic_slice_in_dim(down_weight, place[0] * quarter, quarter, 0)
        own = jnp.concatenate([fc_own.reshape(rows, parts * quarter), down_own], axis=0)
        return own, lax.dynamic_update_slice(jnp.zeros((parts,) + own.shape, BF), own[None], (place[1], 0, 0))
    return pl.pallas_call(
        pack_kernel,
        out_shape=(
            jax.ShapeDtypeStruct((rows + quarter, width), BF),
            jax.ShapeDtypeStruct((parts, rows + quarter, width), BF),
        ),
        grid_spec=pltpu.PrefetchScalarGridSpec(
            num_scalar_prefetch=1,
            grid=(parts,),
            in_specs=[
                pl.BlockSpec((rows, quarter), lambda g, p: (0, g * 4 + p[0])),
                pl.BlockSpec((quarter, quarter), lambda g, p: (p[0], g)),
            ],
            out_specs=(
                pl.BlockSpec((rows + quarter, quarter), lambda g, p: (0, g)),
                pl.BlockSpec((1, rows + quarter, quarter), lambda g, p: (p[1], 0, g)),
            ),
        ),
        compiler_params=pltpu.CompilerParams(vmem_limit_bytes=30 << 20),
        cost_estimate=COST,
        name="pack",
    )(place, fc_weight, down_weight)


GELU_A = math.sqrt(2 / math.pi)
GELU_B = 0.044715


def middle_kernel(rows_ref, cot_ref, fc_ref, down_ref, activ_ref, pre_ref, grad_ref, total, *, step):
    tile = pl.program_id(0)
    fc = fc_ref[...].reshape(-1, fc_ref.shape[2])
    down = down_ref[...].reshape(-1, down_ref.shape[2])

    @pl.when(tile == 0)
    def _():
        total[...] = jnp.zeros_like(total)

    for at in range(0, rows_ref.shape[0], step):
        part = slice(at, at + step)
        value = dot_plain(rows_ref[part], fc)
        pull = dot_cols(cot_ref[part], down)
        square = value * value
        bend = jnp.tanh(GELU_A * value * (1.0 + GELU_B * square))
        half = 0.5 * (1.0 + bend)
        activ_ref[part] = (value * half).astype(BF)
        slope = half + 0.5 * value * (1.0 - bend * bend) * (GELU_A * (1.0 + 3.0 * GELU_B * square))
        grad = (pull * slope).astype(BF)
        pre_ref[part] = grad
        total[part] += dot_cols(grad, fc)

    @pl.when(tile == pl.num_programs(0) - 1)
    def _():
        grad_ref[...] = total[...].astype(BF)


def middle(rows, cot, weights, shard, tile):
    count, width = rows.shape
    parts, quarter = weights.shape[0], weights.shape[1] - shard
    hidden = parts * quarter
    per = tile // quarter
    whole = pl.BlockSpec((count, width), lambda n: (0, 0), pipeline_mode=pl.Buffered(1))
    cols = pl.BlockSpec((count, tile), lambda n: (0, n))
    return pl.pallas_call(
        functools.partial(middle_kernel, step=256),
        out_shape=(
            jax.ShapeDtypeStruct((count, hidden), BF),
            jax.ShapeDtypeStruct((count, hidden), BF),
            jax.ShapeDtypeStruct((count, width), BF),
        ),
        grid=(hidden // tile,),
        in_specs=[
            whole,
            whole,
            pl.BlockSpec((parts, shard, tile), lambda n: (0, 0, n)),
            pl.BlockSpec((per, quarter, width), lambda n: (n, 1, 0)),
        ],
        out_specs=(cols, cols, pl.BlockSpec((count, width), lambda n: (0, 0))),
        scratch_shapes=[pltpu.VMEM((count, width), F32)],
        compiler_params=pltpu.CompilerParams(vmem_limit_bytes=60 << 20),
        cost_estimate=COST,
        name="middle",
    )(rows, cot, weights, weights)


def turned_kernel(order, left_ref, right_ref, left_two_ref, right_two_ref, out_ref):
    rows = left_ref.shape[1]
    out_ref[0, :rows] = dot_rows(left_ref[...], right_ref[...]).astype(BF)
    out_ref[0, rows:] = dot_rows(left_two_ref[...], right_two_ref[...]).astype(BF)


def turned(order, left, right, left_two, right_two, shard):
    count, width = right.shape
    chunks = order.shape[0]
    if shard % 128:
        one = dot_rows(left, right).astype(BF).reshape(-1, shard, width)
        two = dot_rows(left_two, right_two).astype(BF).reshape(-1, shard, width)
        both = jnp.concatenate([one, two], axis=1)
        return jnp.stack([lax.dynamic_index_in_dim(both, order[i], 0, False) for i in range(chunks)])
    whole = pl.BlockSpec((count, width), lambda n, o: (0, 0), pipeline_mode=pl.Buffered(1))
    cols = pl.BlockSpec((count, shard), lambda n, o: (0, o[n]))
    return pl.pallas_call(
        turned_kernel,
        out_shape=jax.ShapeDtypeStruct((chunks, 2 * shard, width), BF),
        grid_spec=pltpu.PrefetchScalarGridSpec(
            num_scalar_prefetch=1,
            grid=(chunks,),
            in_specs=[cols, whole, cols, whole],
            out_specs=pl.BlockSpec((1, 2 * shard, width), lambda n, o: (n, 0, 0)),
        ),
        compiler_params=pltpu.CompilerParams(vmem_limit_bytes=60 << 20),
        cost_estimate=COST,
        name="turned",
    )(order, left, right, left_two, right_two)


def lower_kernel(rows_ref, down_ref, out_ref):
    down = down_ref[...].reshape(-1, down_ref.shape[2])
    out_ref[...] = dot_plain(rows_ref[...], down).astype(BF)


def lower(rows, weights, shard, tile):
    count = rows.shape[0]
    parts, quarter, width = weights.shape[0], weights.shape[1] - shard, weights.shape[2]
    return pl.pallas_call(
        lower_kernel,
        out_shape=jax.ShapeDtypeStruct((count, width), BF),
        grid=(width // tile,),
        in_specs=[
            pl.BlockSpec(rows.shape, lambda n: (0, 0), pipeline_mode=pl.Buffered(1)),
            pl.BlockSpec((parts, quarter, tile), lambda n: (0, 1, n)),
        ],
        out_specs=pl.BlockSpec((count, tile), lambda n: (0, n)),
        compiler_params=pltpu.CompilerParams(vmem_limit_bytes=60 << 20),
        cost_estimate=COST,
        name="lower",
    )(rows, weights)


class KernelScatter:
    def __init__(self, count, chunk, outs, ins, sems, up, down):
        self.steps, self.chunk, self.outs, self.ins, self.sems = count // 2, chunk, outs, ins, sems
        self.devices = (up, down)
        self.half = outs.shape[2] // 2
        self.copies = {}

    def start(self, step):
        half = self.half
        for way, sign in ((0, 1), (1, -1)):
            mine = self.chunk(sign * (self.steps - step))
            if step > 1:
                self.copies[way, step - 2].wait_send()
            out, into = self.outs.at[way, step % 2], self.ins.at[way, step]
            rows = slice(way * half, (way + 1) * half)
            rest = slice((1 - way) * half, (2 - way) * half)
            if step == 0:
                out, into = out.at[pl.ds(0, half)], into.at[pl.ds(0, half)]
                out[...] = mine[rows].astype(BF)
            elif step == 1:
                out[rows] = (mine[rows] + self.ins[way, 0, :half].astype(F32)).astype(BF)
                out[rest] = mine[rest].astype(BF)
            else:
                out[...] = (mine + self.ins[way, step - 1].astype(F32)).astype(BF)
            self.copies[way, step] = send(out, into, self.sems, (way, step), self.devices[way])

    def arrived(self, step):
        self.copies[0, step].wait_recv()
        self.copies[1, step].wait_recv()

    def total(self):
        last = self.steps - 1
        return self.chunk(0) + self.ins[0, last].astype(F32) + self.ins[1, last].astype(F32)

    def finish(self):
        for (_, step), copy in self.copies.items():
            if step >= self.steps - 2:
                copy.wait_send()


def closing_kernel(
    kv_parts,
    query_rows,
    q_weight,
    attn_parts,
    ff_up,
    ff_down,
    ff_last,
    resid_grad,
    hidden,
    kv_weight,
    attn_in,
    mlp_vectors,
    grad_out,
    attn_out,
    ff_out,
    tail_out,
    kv_here,
    kv_near,
    kv_far,
    kv_chip_in,
    kv_outs,
    kv_ins,
    q_far_out,
    q_far,
    q_near,
    q_chip_in,
    q_here,
    attn_here,
    attn_outs,
    attn_ins,
    ff_here,
    ff_ins,
    ff_sum,
    kv_total,
    tail_here,
    tail_outs,
    tail_ins,
    swap_out,
    swap_in,
    local,
    kv_core_sems,
    kv_chip_sems,
    kv_sems,
    q_core_sems,
    q_chip_sems,
    attn_sems,
    ff_sems,
    ff_chip_sems,
    ff_core_sems,
    tail_sems,
    swap_sems,
    *,
    count,
    shard,
):
    s, f, owner, up, down, chip, core = neighbours(count)
    steps = count // 2
    order = [steps] + [sign * n for n in range(steps - 1, 0, -1) for sign in (1, -1)] + [0]
    other, sibling = lax.rem(s + 2, 4), core[0]
    far = lax.rem(sibling + 2, 4)
    tokens = hidden.shape[0]
    greet(up, down, chip, core)

    kv_pair = [
        send(kv_parts.at[far], kv_far, kv_core_sems, (0,), core),
        send(kv_parts.at[sibling], kv_near, kv_core_sems, (1,), core),
    ]
    loads = [
        pltpu.make_async_copy(kv_parts.at[other], kv_here.at[1], local.at[0]),
        pltpu.make_async_copy(kv_parts.at[s], kv_here.at[0], local.at[1]),
        pltpu.make_async_copy(attn_parts, attn_here, local.at[2]),
        pltpu.make_async_copy(ff_last, ff_here, local.at[3]),
    ]
    for copy in loads:
        copy.start()
    ff_rows = ff_last.shape[0] // 2
    ff_parts = [pl.ds(i * ff_rows, ff_rows) for i in range(2)]
    ff_ring = []

    def ff_start(i):
        for way, (source, device) in enumerate(((ff_up, up), (ff_down, down))):
            copy = send(source.at[ff_parts[i]], ff_ins.at[way, ff_parts[i]], ff_sems, (way, i), device)
            ff_ring.append(copy)

    ff_start(0)

    def query_part(i):
        return dot_cols(query_rows[i * tokens : (i + 1) * tokens], q_weight[...])

    q_far_out[...] = query_part(3).astype(BF)
    q_pair = [send(q_far_out, q_far, q_core_sems, (0,), core)]
    grad_out[...] = query_part(1).astype(BF)
    loads[0].wait()
    kv_pair[0].wait_recv()
    kv_across = {}
    for i, n in enumerate(order):
        place = owner(n)
        kv_here[1, place] = (kv_here[1, place].astype(F32) + kv_far[place].astype(F32)).astype(BF)
        kv_across[n] = send(kv_here.at[1, place], kv_chip_in.at[i], kv_chip_sems, (i,), chip)
    part = query_part(2)
    q_pair[0].wait()
    q_chip_out = q_far_out
    q_chip_out[...] = (part + q_far[...].astype(F32)).astype(BF)
    rows = tokens // 2
    q_halves = [pl.ds(i * rows, rows) for i in range(2)]
    q_across = [
        send(q_chip_out.at[half], q_chip_in.at[half], q_chip_sems, (i,), chip) for i, half in enumerate(q_halves)
    ]
    q_pair.append(send(grad_out, q_near, q_core_sems, (1,), core))
    q_here[...] = query_part(0)
    loads[1].wait()
    kv_pair[1].wait_recv()

    def kv_chunk(n):
        n = steps if n == -steps else n
        place = owner(n)
        here = kv_here[0, place].astype(F32) + kv_near[place].astype(F32)
        return here + kv_chip_in[order.index(n)].astype(F32)

    kv = KernelScatter(count, kv_chunk, kv_outs, kv_ins, kv_sems, up, down)
    for step in range(steps):
        for n in {steps - step, -(steps - step)} & set(order):
            kv_across[n].wait_recv()
        if step:
            kv.arrived(step - 1)
        kv.start(step)
    ff_start(1)
    loads[2].wait()

    def attn_chunk(n):
        return attn_here[order.index(steps if n == -steps else n)].astype(F32)

    attn = KernelScatter(count, attn_chunk, attn_outs, attn_ins, attn_sems, up, down)
    attn.start(0)

    loads[3].wait()
    ff_pair, ff_across = [], []

    def ff_close(i):
        rows = ff_parts[i]
        for copy in ff_ring[2 * i : 2 * i + 2]:
            copy.wait_recv()
        arrived = ff_ins[0, rows].astype(F32) + ff_ins[1, rows].astype(F32)
        ff_sum[rows] = (ff_here[rows].astype(F32) + arrived).astype(BF)
        ff_across.append(send(ff_sum.at[rows], ff_out.at[2, rows], ff_chip_sems, (i,), chip))
        ff_pair.append(send(ff_sum.at[rows], ff_out.at[1, rows], ff_core_sems, (i,), core))

    ff_close(0)
    kv_across[0].wait_recv()
    kv.arrived(steps - 1)
    kv_total[...] = kv.total().astype(BF)

    q_pair[1].wait()
    for copy in q_across:
        copy.wait_recv()
    q_here[...] += q_near[...].astype(F32) + q_chip_in[...].astype(F32)
    for t in range(count):
        cols = slice(t * shard, (t + 1) * shard)
        q_here[:, cols] += dot_cols(kv_total[...], kv_weight[t, :shard, :])
    gain = jnp.concatenate([kv_weight[t, shard : shard + 1, :shard] for t in range(count)], axis=1).astype(F32)
    block = 64
    gain_grad = jnp.zeros((1, hidden.shape[1]), F32)
    bias_grad = jnp.zeros((1, hidden.shape[1]), F32)
    for at in range(0, tokens, block):
        here = slice(at, at + block)
        normed, inverse = layer_norm(hidden[here].astype(F32))
        grad = q_here[here]
        gain_grad += jnp.sum(grad * normed, axis=0, keepdims=True)
        bias_grad += jnp.sum(grad, axis=0, keepdims=True)
        grad_out[here] = (resid_grad[here] + norm_back(grad * gain, normed, inverse)).astype(BF)

    tail_here[...] = jnp.zeros_like(tail_here)
    vectors = (gain_grad, bias_grad, mlp_vectors[0:1], mlp_vectors[1:2])
    for t in range(count):
        cols = slice(t * shard, (t + 1) * shard)
        tail_here[t, :shard, :] = dot_rows(attn_in[:, cols], kv_total[...])
        for j, vector in enumerate(vectors):
            tail_here[t, shard + j : shard + j + 1, :shard] = vector[:, cols]
    tail = KernelScatter(count, lambda n: tail_here[owner(n)], tail_outs, tail_ins, tail_sems, up, down)
    for step in range(steps):
        if step:
            tail.arrived(step - 1)
        tail.start(step)
        if step == 0:
            ff_close(1)
        attn.arrived(step)
        if step < steps - 1:
            attn.start(step + 1)
    attn_out[...] = attn.total().astype(BF)
    tail.arrived(steps - 1)
    total = tail.total()
    swap_out[0] = total.astype(BF)
    swaps = [send(swap_out.at[0], swap_in.at[0], swap_sems, (0,), core)]
    for i, rows in enumerate(ff_parts):
        ff_across[i].wait_recv()
        ff_pair.append(send(ff_out.at[2, rows], ff_out.at[3, rows], ff_core_sems, (2 + i,), core))
    keep = pltpu.make_async_copy(ff_sum, ff_out.at[0], local.at[4])
    keep.start()
    swaps[0].wait_recv()
    swap_out[1] = (swap_out[0].astype(F32) + swap_in[0].astype(F32)).astype(BF)
    swaps.append(send(swap_out.at[1], swap_in.at[1], swap_sems, (1,), chip))
    swaps[1].wait_recv()
    tail_out[...] = swap_out[1].astype(F32) + swap_in[1].astype(F32)
    keep.wait()
    for ring in (kv, attn, tail):
        ring.finish()
    for copy in kv_pair + q_across + list(kv_across.values()) + ff_ring + ff_across + swaps:
        copy.wait_send()
    for copy in ff_pair:
        copy.wait()


def closing(kv_parts, query_rows, q_weight, attn_parts, ff_flow, resid_grad, hidden, kv_weight, attn_in, mlp_vectors, shard):
    ff_up, ff_down, ff_last = ff_flow
    fsdp_count, tokens, kv_cols = kv_parts.shape[1:]
    width = hidden.shape[1]
    steps = fsdp_count // 2
    dma = pltpu.SemaphoreType.DMA
    anywhere = pl.BlockSpec(memory_space=pl.ANY)
    inside = pl.BlockSpec(memory_space=pltpu.VMEM)
    attn_shape = attn_parts.shape[1:]
    tail_shape = kv_weight.shape[1:]
    wide = pltpu.VMEM((tokens, width), BF)
    kv_all = pltpu.VMEM((fsdp_count, tokens, kv_cols), BF)

    def ring(shape):
        return pltpu.VMEM((2, steps) + tuple(shape), BF)

    def pair(shape):
        return pltpu.VMEM((2, 2) + tuple(shape), BF)

    ring_sems = dma((2, 2, steps))
    return pl.pallas_call(
        functools.partial(closing_kernel, count=fsdp_count, shard=shard),
        out_shape=(
            jax.ShapeDtypeStruct((tokens, width), BF),
            jax.ShapeDtypeStruct(attn_shape, BF),
            jax.ShapeDtypeStruct((4,) + ff_last.shape, BF),
            jax.ShapeDtypeStruct(tail_shape, F32),
        ),
        in_specs=[anywhere, inside, inside, anywhere, anywhere, anywhere, anywhere] + [inside] * 5,
        out_specs=(inside, inside, anywhere, inside),
        scratch_shapes=[
            pltpu.VMEM((2, fsdp_count, tokens, kv_cols), BF),
            kv_all,
            kv_all,
            kv_all,
            pair((tokens, kv_cols)),
            ring((tokens, kv_cols)),
            wide,
            wide,
            wide,
            wide,
            pltpu.VMEM((tokens, width), F32),
            pltpu.VMEM(attn_parts.shape, BF),
            pair(attn_shape),
            ring(attn_shape),
            pltpu.VMEM(ff_last.shape, BF),
            pltpu.VMEM((2,) + ff_last.shape, BF),
            pltpu.VMEM(ff_last.shape, BF),
            pltpu.VMEM((tokens, kv_cols), BF),
            pltpu.VMEM((fsdp_count,) + tail_shape, F32),
            pair(tail_shape),
            ring(tail_shape),
            pltpu.VMEM((2,) + tail_shape, BF),
            pltpu.VMEM((2,) + tail_shape, BF),
            dma((5,)),
            dma((2, 2)),
            dma((2, fsdp_count)),
            ring_sems,
            dma((2, 2)),
            dma((2, 2)),
            ring_sems,
            dma((2, 2, 2)),
            dma((2, 2)),
            dma((2, 4)),
            ring_sems,
            dma((2, 2)),
        ],
        compiler_params=pltpu.CompilerParams(
            collective_id=2, has_side_effects=True, vmem_limit_bytes=61 << 20
        ),
        cost_estimate=COST,
        name="closing",
    )(
        kv_parts,
        query_rows,
        q_weight,
        attn_parts,
        ff_up,
        ff_down,
        ff_last,
        resid_grad,
        hidden,
        kv_weight,
        attn_in,
        mlp_vectors,
    )


def attn_turned_kernel(order, rows_ref, query_ref, proj_ref, out_ref):
    part, cols = proj_ref.shape[0], query_ref.shape[1]
    grad = dot_rows(rows_ref[...], query_ref[...]).astype(BF)
    lines = out_ref.shape[1] - part
    out_ref[0, :part] = proj_ref[...]
    for k in range(grad.shape[0] // lines):
        out_ref[0, part:, k * cols : (k + 1) * cols] = grad[k * lines : (k + 1) * lines]


def attn_turned(order, rows, query_rows, proj_sum, shard):
    count, width = rows.shape
    cols = query_rows.shape[1]
    chunks = order.shape[0]
    part = proj_sum.shape[0] // chunks
    folds = width // cols
    lines = shard // folds
    if shard % 128:
        grad = dot_rows(rows, query_rows).astype(BF).reshape(chunks, folds, lines, cols)
        grad = grad.transpose(0, 2, 1, 3).reshape(chunks, lines, width)
        both = jnp.concatenate([proj_sum.reshape(chunks, part, width), grad], axis=1)
        return jnp.stack([lax.dynamic_index_in_dim(both, order[i], 0, False) for i in range(chunks)])
    return pl.pallas_call(
        attn_turned_kernel,
        out_shape=jax.ShapeDtypeStruct((chunks, part + lines, width), BF),
        grid_spec=pltpu.PrefetchScalarGridSpec(
            num_scalar_prefetch=1,
            grid=(chunks,),
            in_specs=[
                pl.BlockSpec((count, shard), lambda n, o: (0, o[n])),
                pl.BlockSpec((count, cols), lambda n, o: (0, 0)),
                pl.BlockSpec((part, width), lambda n, o: (o[n], 0)),
            ],
            out_specs=pl.BlockSpec((1, part + lines, width), lambda n, o: (n, 0, 0)),
        ),
        compiler_params=pltpu.CompilerParams(vmem_limit_bytes=30 << 20),
        cost_estimate=COST,
        name="attn_turned",
    )(order, rows, query_rows, proj_sum)


def rows_kernel(place, *refs):
    *ins, out = refs
    rows = ins[0].shape[0]
    for i, ref in enumerate(ins):
        out[pl.ds(pl.multiple_of((place[0] ^ i) * rows, rows), rows), :] = ref[...].astype(F32)


def stack_rows(place, pieces, tile):
    rows, width = pieces[0].shape
    return pl.pallas_call(
        rows_kernel,
        out_shape=jax.ShapeDtypeStruct((len(pieces) * rows, width), F32),
        grid_spec=pltpu.PrefetchScalarGridSpec(
            num_scalar_prefetch=1,
            grid=(width // tile,),
            in_specs=[pl.BlockSpec((rows, tile), lambda n, p: (0, n))] * len(pieces),
            out_specs=pl.BlockSpec((len(pieces) * rows, tile), lambda n, p: (0, n)),
        ),
        compiler_params=pltpu.CompilerParams(vmem_limit_bytes=40 << 20),
        cost_estimate=COST,
        name="stack_rows",
    )(place, *pieces)


def cols_kernel(place, *refs):
    *ins, out = refs
    cols = ins[0].shape[1]
    for i, ref in enumerate(ins):
        out[:, pl.ds(pl.multiple_of((place[0] ^ i) * cols, cols), cols)] = ref[...].astype(F32)


def stack_cols(place, pieces, cols):
    rows, width = pieces[0].shape
    count = len(pieces)
    if cols % 128:
        ordered = jnp.stack([lax.dynamic_index_in_dim(jnp.stack(pieces), place[0] ^ i, 0, False) for i in range(count)])
        ordered = ordered.reshape(count, rows, width // cols, cols).transpose(1, 2, 0, 3)
        return ordered.reshape(rows, count * width).astype(F32)
    return pl.pallas_call(
        cols_kernel,
        out_shape=jax.ShapeDtypeStruct((rows, count * width), F32),
        grid_spec=pltpu.PrefetchScalarGridSpec(
            num_scalar_prefetch=1,
            grid=(width // cols,),
            in_specs=[pl.BlockSpec((rows, cols), lambda n, p: (0, n))] * count,
            out_specs=pl.BlockSpec((rows, count * cols), lambda n, p: (0, n)),
        ),
        compiler_params=pltpu.CompilerParams(vmem_limit_bytes=40 << 20),
        cost_estimate=COST,
        name="stack_cols",
    )(place, *pieces)


def layer_norm(values):
    mean = jnp.mean(values, axis=-1, keepdims=True)
    center = values - mean
    inverse = lax.rsqrt(jnp.mean(center * center, axis=-1, keepdims=True) + EPS)
    return center * inverse, inverse


def norm_back(grad, normed, inverse):
    return inverse * (
        grad
        - jnp.mean(grad, axis=-1, keepdims=True)
        - normed * jnp.mean(grad * normed, axis=-1, keepdims=True)
    )


def gelu_tanh(values):
    return jax.nn.gelu(values, approximate=True)


def shards(
    hidden_in,
    out_cotangent,
    positions,
    block_mask,
    norm_gain,
    norm_bias,
    qkv_weight,
    proj_weight,
    mlp_gain,
    mlp_bias,
    fc_weight,
    down_weight,
):
    seq_count = lax.axis_size("seq")
    fsdp_count = lax.axis_size("fsdp")
    s = lax.axis_index("seq")
    f = lax.axis_index("fsdp")
    ring = Ring(fsdp_count)
    count = hidden_in.shape[1]
    width = hidden_in.shape[2]
    length = positions.shape[1]
    blocks = length // BLOCK
    shard = qkv_weight.shape[0]
    ff = fc_weight.shape[1]
    ff_shard = down_weight.shape[0]
    heads_here = HEADS // seq_count
    head_cols = heads_here * HD
    quarter = ff_shard // seq_count
    tokens_here = MB * count
    group = seq_count * tokens_here

    chunk_ids = jnp.stack([(s ^ i) * fsdp_count + f for i in range(seq_count)]).astype(jnp.int32)
    token_ids = chunk_ids[:, None] * count + jnp.arange(count, dtype=jnp.int32)[None]
    first = token_ids[:, None, :] - jnp.stack(
        [lax.dynamic_slice_in_dim(positions, chunk_ids[i] * count, count, 1) for i in range(seq_count)]
    )
    first = first[:, :, None, :]
    high_tiles = (chunk_ids * count + count - 1) // BLOCK + 1
    tables = jnp.concatenate(
        [
            jnp.broadcast_to(chunk_ids[None, :, None], (MB, seq_count, 1)),
            (first[:, :, 0, :1] // BLOCK).transpose(1, 0, 2),
            jnp.broadcast_to(high_tiles[None, :, None], (MB, seq_count, 1)),
            jnp.zeros((MB, seq_count, 1), jnp.int32),
            jnp.stack([block_mask[:, (chunk_ids[i] * count) // BLOCK] for i in range(seq_count)], axis=1),
        ],
        axis=2,
    ).reshape(-1)

    place = jnp.stack([s, f]).astype(jnp.int32)
    ff_own, ff_slots = pack(place, fc_weight, down_weight, fsdp_count, quarter)
    flow = Flow(ring, ring.gather(ff_own, ff_slots))

    part = shard // seq_count
    pairs = [
        (j * fsdp_count + q * (fsdp_count // seq_count) + t // seq_count, q * fsdp_count + t)
        for q in range(seq_count)
        for t in range(fsdp_count)
        for j in [t % seq_count]
    ]
    back_pairs = [(b, a) for a, b in pairs]
    own_proj = lax.ppermute(
        lax.dynamic_slice_in_dim(proj_weight, s * part, part, 0), ("seq", "fsdp"), pairs
    )

    span = 32
    vectors = jnp.stack([norm_gain, norm_bias, mlp_gain, mlp_bias])
    padded = jnp.pad(vectors, ((0, span - 4), (0, 2 * HD - shard)))
    own_kv = jnp.concatenate([qkv_weight[:, width:], padded], axis=0)
    own_q = lax.dynamic_slice_in_dim(qkv_weight, s * head_cols, head_cols, 1)
    opened = opening(hidden_in.reshape(tokens_here, width), own_kv, own_q, own_proj, fsdp_count, shard)
    hidden_all, kv_ring, q_ring, proj_ring, kv_all = flow.advance(opened)
    kv_weight = kv_ring[:, :shard].reshape(width, 2 * HD)
    vectors = kv_ring[:, shard : shard + 4, :shard].transpose(1, 0, 2).reshape(4, width).astype(F32)
    gain_one, bias_one, gain_two, bias_two = vectors[0], vectors[1], vectors[2], vectors[3]
    q_weight = q_ring.reshape(width, head_cols)
    proj_full = proj_ring.reshape(head_cols, width)
    kv_all = kv_all.reshape(seq_count * fsdp_count, MB, count, 2 * HD)
    normed_all, _ = layer_norm(hidden_all.reshape(group, width).astype(F32))
    attn_in = (normed_all * gain_one + bias_one).astype(BF)
    own_attn_in = attn_in[:tokens_here]
    queries = dot_plain(attn_in, q_weight).astype(BF).reshape(seq_count, MB, count, head_cols)
    cotangent = out_cotangent.reshape(tokens_here, width)
    cotangent_all = jnp.concatenate(seq_gather(tie(cotangent, queries)), axis=0)

    heads_out, logs = attend(tables, first, queries, kv_all, blocks)
    heads_rows = heads_out.reshape(group, head_cols)

    def pieces(rows):
        return [rows[i * tokens_here : (i + 1) * tokens_here] for i in range(seq_count)]

    hidden_own = hidden_in.reshape(tokens_here, width).astype(F32)
    resid = hidden_own + seq_scatter([dot_plain(piece, proj_full) for piece in pieces(heads_rows)])
    resid, cotangent_all = flow.advance((resid, cotangent_all))
    normed_two, inverse_two = layer_norm(resid)
    mlp_in_own = (normed_two * gain_two + bias_two).astype(BF)
    mlp_in = flow.advance(jnp.concatenate(seq_gather(mlp_in_own), axis=0))
    weights = flow.finish()
    activ, pre_grad, mlp_in_part = middle(mlp_in, cotangent_all, weights, shard, BLOCK)
    mlp_in_grad = seq_scatter([piece.astype(F32) for piece in pieces(mlp_in_part)])

    order = ring.order()
    early = 3
    ff_early = turned(order[:early], mlp_in, pre_grad, activ, cotangent_all, shard)
    ff_late = turned(order[early:], mlp_in, pre_grad, activ, cotangent_all, shard)
    steps = ring.steps()

    def ff_chunk(n):
        at = steps.index(n)
        return (ff_early[at] if at < early else ff_late[at - early]).astype(F32)

    flow = Flow(ring, ring.scatter(ff_chunk, last=False))
    mlp_in_grad, ff_late, activ_later = flow.advance((mlp_in_grad, ff_late, activ))
    lowered = lower(activ_later, weights, shard, BLOCK)

    mlp_gain_part = jnp.sum(mlp_in_grad * normed_two, axis=0)
    mlp_bias_part = jnp.sum(mlp_in_grad, axis=0)
    resid_grad = cotangent.astype(F32) + norm_back(mlp_in_grad * gain_two, normed_two, inverse_two)
    branch_own = resid_grad.astype(BF)
    branch, lowered = flow.advance((jnp.concatenate(seq_gather(branch_own), axis=0), lowered))
    result = (resid + seq_scatter([piece.astype(F32) for piece in pieces(lowered)])).astype(BF)
    heads_grad = dot_cols(branch, proj_full).astype(BF).reshape(seq_count, MB, count, head_cols)
    query_grads, kv_grads = attend_back(
        tables, first, queries, kv_all, heads_out, logs, heads_grad, blocks
    )
    query_grads, kv_grads, result = flow.advance((query_grads, kv_grads, result))
    query_rows = query_grads.reshape(group, head_cols)

    proj_sum = dot_rows(heads_rows, branch).astype(BF)
    attn_parts = attn_turned(order, attn_in, query_rows, proj_sum, shard)
    ff_up, ff_down = flow.finish()
    grad_input, attn_grad, ff_all, tail = closing(
        kv_grads.reshape(seq_count, fsdp_count, tokens_here, 2 * HD),
        query_rows,
        q_weight,
        attn_parts,
        (ff_up, ff_down, ff_late[-1]),
        resid_grad,
        hidden_in.reshape(tokens_here, width),
        kv_ring,
        own_attn_in,
        jnp.stack([mlp_gain_part, mlp_bias_part]),
        shard,
    )
    kv_weight_grad = tail[:shard, : 2 * HD]
    vector_grads = tail[shard : shard + 4, :shard]
    folds = width // head_cols
    proj_grad = lax.ppermute(attn_grad[:part], ("seq", "fsdp"), back_pairs)
    query_weight_grad = (
        attn_grad[part:].reshape(shard // folds, folds, head_cols).transpose(1, 0, 2).reshape(shard, head_cols)
    )
    ff_pieces = [ff_all[i] for i in range(seq_count)]
    grad_fc = stack_cols(place, [piece[:shard] for piece in ff_pieces], quarter)
    grad_down = stack_rows(place, [piece[shard:] for piece in ff_pieces], BLOCK)
    grad_proj = stack_rows(place, seq_gather(proj_grad), BLOCK)
    grad_query = stack_cols(place, seq_gather(query_weight_grad), head_cols)
    grad_qkv = jnp.concatenate([grad_query, kv_weight_grad], axis=1)
    return (
        result.reshape(hidden_in.shape),
        grad_input.reshape(hidden_in.shape),
        vector_grads[0],
        vector_grads[1],
        grad_qkv,
        grad_proj,
        vector_grads[2],
        vector_grads[3],
        grad_fc,
        grad_down,
    )


def solution(mesh):
    rows = P(None, ("seq", "fsdp"), None)
    vector = P("fsdp")
    matrix = P("fsdp", None)
    in_specs = (rows, rows, P(), P(), vector, vector, matrix, matrix, vector, vector, matrix, matrix)
    out_specs = (rows, rows, vector, vector, matrix, matrix, vector, vector, matrix, matrix)
    return jax.shard_map(shards, mesh=mesh, in_specs=in_specs, out_specs=out_specs, check_vma=False)
```

```python
import functools
import math

import jax
import jax.numpy as jnp
from jax import lax
from jax.experimental import pallas as pl
from jax.experimental.pallas import tpu as pltpu
from jax.sharding import PartitionSpec as P

HEADS = 16
HD = 128
MB = 2
BLOCK = 256
EPS = 1e-05
NEG_FILL = -1e30
SCALE = HD ** (-0.5)
LOG2E = math.log2(math.e)
BF = jnp.bfloat16
COST = pl.CostEstimate(flops=0, bytes_accessed=0, transcendentals=0)
F32 = jnp.float32


def dot_rows(left, right):
    return lax.dot_general(left, right, (((0,), (0,)), ((), ())), preferred_element_type=F32)


def dot_cols(left, right):
    return lax.dot_general(left, right, (((1,), (1,)), ((), ())), preferred_element_type=F32)


def dot_plain(left, right):
    return lax.dot_general(left, right, (((1,), (0,)), ((), ())), preferred_element_type=F32)


def ring_order(count):
    return [2 * i for i in range(count // 2)] + [2 * i + 1 for i in reversed(range(count // 2))]


class Ring:
    def __init__(self, count):
        order = ring_order(count)
        self.count = count
        self.up = [(order[i], order[(i + 1) % count]) for i in range(count)]
        self.down = [(order[(i + 1) % count], order[i]) for i in range(count)]
        place = lax.axis_index("fsdp")
        half = count // 2
        self.place = place
        self.at = jnp.where(place % 2 == 0, place // 2, count - 1 - place // 2)

    def owner(self, step):
        count, half = self.count, self.count // 2
        at = lax.rem(self.at + (step + count), count)
        return jnp.where(at < half, 2 * at, 2 * (count - 1 - at) + 1)

    def steps(self):
        half = self.count // 2
        return [half] + [sign * n for n in range(half - 1, 0, -1) for sign in (1, -1)] + [0]

    def order(self):
        return jnp.stack([self.owner(n) for n in self.steps()]).astype(jnp.int32)

    def scatter(self, up, down, chunk):
        for step in range(self.count // 2 - 3, 0, -1):
            up = lax.ppermute(up, "fsdp", self.up)
            down = lax.ppermute(down, "fsdp", self.down)
            up, down = yield up, down
            up = (chunk(step).astype(F32) + up.astype(F32)).astype(BF)
            down = (chunk(-step).astype(F32) + down.astype(F32)).astype(BF)
        return up, down


class Flow:
    def __init__(self, ring, steps):
        self.ring, self.steps, self.result = ring, steps, None
        self.pending = next(steps)

    def advance(self, values=()):
        for _ in range(max(1, self.ring.count // 8)):
            if self.result is None:
                self.pending, values = lax.optimization_barrier((self.pending, values))
                try:
                    self.pending = self.steps.send(self.pending)
                except StopIteration as end:
                    self.result = end.value
        return values

    def finish(self):
        while self.result is None:
            self.advance()
        return self.result


def attend_kernel(tables, q_ref, kv_ref, first_ref, out_ref, log_ref, stack, high, total, result, *, heads, blocks):
    batch, piece = pl.program_id(0), pl.program_id(1)
    count = q_ref.shape[2]
    base = (batch * pl.num_programs(1) + piece) * (blocks + 4)
    chunk, low_tile, high_tile = tables[base], tables[base + 1], tables[base + 2]
    for h in range(heads):
        stack[h * count : (h + 1) * count, :] = q_ref[0, 0, :, h * HD : (h + 1) * HD]
    high[...] = jnp.full_like(high, NEG_FILL)
    total[...] = jnp.zeros_like(total)
    result[...] = jnp.zeros_like(result)
    tokens = chunk * count + lax.broadcasted_iota(jnp.int32, (1, count), 1)
    first = first_ref[0, 0]

    def step(tile, carry):
        @pl.when(tables[base + 4 + tile] != 0)
        def _():
            part = kv_ref[pl.ds(2 * tile, 2), 0].reshape(BLOCK, 2 * HD)
            keys, values = part[:, :HD], part[:, HD:]
            scores = dot_cols(keys, stack[...])
            index = tile * BLOCK + lax.broadcasted_iota(jnp.int32, (BLOCK, count), 0)
            allowed = (index <= tokens) & (index >= first)
            weights, scales = [], []
            for h in range(heads):
                lanes = slice(h * count, (h + 1) * count)
                score = jnp.where(allowed, scores[:, lanes] * (SCALE * LOG2E), NEG_FILL)
                old = high[:, lanes]
                new = jnp.maximum(old, jnp.max(score, axis=0, keepdims=True))
                weight = jnp.exp2(score - new)
                scale = jnp.exp2(old - new)
                high[:, lanes] = new
                total[:, lanes] = total[:, lanes] * scale + jnp.sum(weight, axis=0, keepdims=True)
                weights.append(weight.astype(BF))
                scales.append(scale)
            added = dot_rows(values, jnp.concatenate(weights, axis=1))
            result[...] = result[...] * jnp.concatenate(scales, axis=1) + added

        return carry

    lax.fori_loop(low_tile, high_tile, step, 0)
    final = result[...] / total[...]
    logs = high[...] + jnp.log2(total[...])
    for h in range(heads):
        lanes = slice(h * count, (h + 1) * count)
        out_ref[0, 0, :, h * HD : (h + 1) * HD] = final[:, lanes].T.astype(BF)
        log_ref[0, 0, h : h + 1, :] = logs[:, lanes]


def attend_back_kernel(
    tables,
    q_ref,
    kv_ref,
    first_ref,
    out_ref,
    log_ref,
    grad_ref,
    dq_ref,
    dkv_ref,
    stack,
    grads,
    logs,
    deltas,
    dq_sum,
    dkv_sum,
    *,
    heads,
    blocks,
):
    batch, piece = pl.program_id(0), pl.program_id(1)
    count = q_ref.shape[2]
    base = (batch * pl.num_programs(1) + piece) * (blocks + 4)
    chunk, low_tile, high_tile = tables[base], tables[base + 1], tables[base + 2]

    @pl.when(piece == 0)
    def _():
        dkv_sum[...] = jnp.zeros_like(dkv_sum)

    for h in range(heads):
        rows = slice(h * count, (h + 1) * count)
        cols = slice(h * HD, (h + 1) * HD)
        stack[rows, :] = q_ref[0, 0, :, cols]
        grad = grad_ref[0, 0, :, cols]
        grads[rows, :] = grad
        product = grad.astype(F32) * out_ref[0, 0, :, cols].astype(F32)
        deltas[:, rows] = jnp.sum(product.T, axis=0, keepdims=True)
        logs[:, rows] = log_ref[0, 0, h : h + 1, :]
    dq_sum[...] = jnp.zeros_like(dq_sum)
    tokens = chunk * count + lax.broadcasted_iota(jnp.int32, (1, count), 1)
    first = first_ref[0, 0]

    def step(tile, carry):
        @pl.when(tables[base + 4 + tile] != 0)
        def _():
            part = kv_ref[pl.ds(2 * tile, 2), 0].reshape(BLOCK, 2 * HD)
            keys, values = part[:, :HD], part[:, HD:]
            scores = dot_cols(keys, stack[...])
            pulls = dot_cols(values, grads[...])
            index = tile * BLOCK + lax.broadcasted_iota(jnp.int32, (BLOCK, count), 0)
            allowed = (index <= tokens) & (index >= first)
            weights, score_grads = [], []
            for h in range(heads):
                lanes = slice(h * count, (h + 1) * count)
                score = jnp.where(allowed, scores[:, lanes] * (SCALE * LOG2E), NEG_FILL)
                weight = jnp.exp2(score - logs[:, lanes])
                weights.append(weight.astype(BF))
                score_grads.append((weight * (pulls[:, lanes] - deltas[:, lanes])).astype(BF))
            weight = jnp.concatenate(weights, axis=1)
            score_grad = jnp.concatenate(score_grads, axis=1)
            dv = dot_plain(weight, grads[...])
            dk = dot_plain(score_grad, stack[...])
            dq_sum[...] += dot_rows(keys, score_grad)
            both = jnp.concatenate([dk, dv], axis=1).reshape(2, BLOCK // 2, 2 * HD)
            dkv_sum[pl.ds(2 * tile, 2)] += both

        return carry

    lax.fori_loop(low_tile, high_tile, step, 0)
    for h in range(heads):
        lanes = slice(h * count, (h + 1) * count)
        dq_ref[0, 0, :, h * HD : (h + 1) * HD] = (dq_sum[:, lanes] * SCALE).T.astype(BF)

    @pl.when(piece == pl.num_programs(1) - 1)
    def _():
        dkv_ref[:, 0, :, :HD] = (dkv_sum[:, :, :HD] * SCALE).astype(BF)
        dkv_ref[:, 0, :, HD:] = dkv_sum[:, :, HD:].astype(BF)


def attend(tables, first, queries, key_values, blocks):
    pieces, batches, count, width = queries.shape
    heads = width // HD
    chunks = key_values.shape[0]
    row_spec = pl.BlockSpec((1, 1, count, width), lambda b, i, t: (i, b, 0, 0))
    kv_spec = pl.BlockSpec((chunks, 1, count, 2 * HD), lambda b, i, t: (0, b, 0, 0))
    first_spec = pl.BlockSpec((1, 1, 1, count), lambda b, i, t: (i, b, 0, 0))
    log_spec = pl.BlockSpec((1, 1, heads, count), lambda b, i, t: (i, b, 0, 0))
    rows = heads * count
    return pl.pallas_call(
        functools.partial(attend_kernel, heads=heads, blocks=blocks),
        out_shape=(
            jax.ShapeDtypeStruct(queries.shape, BF),
            jax.ShapeDtypeStruct((pieces, batches, heads, count), F32),
        ),
        grid_spec=pltpu.PrefetchScalarGridSpec(
            num_scalar_prefetch=1,
            grid=(batches, pieces),
            in_specs=[row_spec, kv_spec, first_spec],
            out_specs=[row_spec, log_spec],
            scratch_shapes=[
                pltpu.VMEM((rows, HD), BF),
                pltpu.VMEM((1, rows), F32),
                pltpu.VMEM((1, rows), F32),
                pltpu.VMEM((HD, rows), F32),
            ],
        ),
        compiler_params=pltpu.CompilerParams(vmem_limit_bytes=40 << 20),
        cost_estimate=COST,
        name="attend",
    )(tables, queries, key_values, first)


def attend_back(tables, first, queries, key_values, out, logs, grads, blocks):
    pieces, batches, count, width = queries.shape
    heads = width // HD
    chunks = key_values.shape[0]
    row_spec = pl.BlockSpec((1, 1, count, width), lambda b, i, t: (i, b, 0, 0))
    kv_spec = pl.BlockSpec((chunks, 1, count, 2 * HD), lambda b, i, t: (0, b, 0, 0))
    first_spec = pl.BlockSpec((1, 1, 1, count), lambda b, i, t: (i, b, 0, 0))
    log_spec = pl.BlockSpec((1, 1, heads, count), lambda b, i, t: (i, b, 0, 0))
    rows = heads * count
    return pl.pallas_call(
        functools.partial(attend_back_kernel, heads=heads, blocks=blocks),
        out_shape=(
            jax.ShapeDtypeStruct(queries.shape, BF),
            jax.ShapeDtypeStruct(key_values.shape, BF),
        ),
        grid_spec=pltpu.PrefetchScalarGridSpec(
            num_scalar_prefetch=1,
            grid=(batches, pieces),
            in_specs=[row_spec, kv_spec, first_spec, row_spec, log_spec, row_spec],
            out_specs=[row_spec, kv_spec],
            scratch_shapes=[
                pltpu.VMEM((rows, HD), BF),
                pltpu.VMEM((rows, HD), BF),
                pltpu.VMEM((1, rows), F32),
                pltpu.VMEM((1, rows), F32),
                pltpu.VMEM((HD, rows), F32),
                pltpu.VMEM((chunks, count, 2 * HD), F32),
            ],
        ),
        compiler_params=pltpu.CompilerParams(vmem_limit_bytes=60 << 20),
        cost_estimate=COST,
        name="attend_back",
    )(tables, queries, key_values, first, out, logs, grads)


def neighbours(count):
    s, f = lax.axis_index("seq"), lax.axis_index("fsdp")
    half = count // 2
    at = jnp.where(lax.rem(f, 2) == 0, f // 2, count - 1 - f // 2)

    def owner(step):
        place = lax.rem(at + (step + count), count)
        return jnp.where(place < half, 2 * place, 2 * (count - 1 - place) + 1)

    chip = lax.rem(s + 2, 4)
    core = s + 1 - 2 * lax.rem(s, 2)
    return s, f, owner, (s, owner(1)), (s, owner(-1)), (chip, f), (core, f)


def greet(*devices):
    barrier = pltpu.get_barrier_semaphore()
    for device in devices:
        pl.semaphore_signal(barrier, inc=1, device_id=device, device_id_type=pl.DeviceIdType.MESH)
    pl.semaphore_wait(barrier, len(devices))


def met(device, s, f):
    return (device[0] == s) & (device[1] == f)


def greet_also(devices, sources, own, s, f):
    barrier = pltpu.get_barrier_semaphore()
    for device in devices:
        pl.semaphore_signal(barrier, inc=1, device_id=device, device_id_type=pl.DeviceIdType.MESH)
    for device in sources:

        @pl.when(jnp.logical_not(met(device, s, f)))
        def _():
            pl.semaphore_signal(barrier, inc=1, device_id=device, device_id_type=pl.DeviceIdType.MESH)

    pl.semaphore_wait(barrier, len(devices) + len(sources) - own)


class Maybe:
    def __init__(self, source, target, landing, send_sem, recv_sem, landing_sem, local_sem, device, sender, s, f):
        self.here, self.from_here = met(device, s, f), met(sender, s, f)
        kind = dict(device_id_type=pl.DeviceIdType.MESH)
        self.copy = pltpu.make_async_remote_copy(source, target, send_sem, recv_sem, device_id=device, **kind)
        self.into = pltpu.make_async_remote_copy(source, landing, send_sem, landing_sem, device_id=device, **kind)
        self.stay = pltpu.make_async_copy(source, target, local_sem)

        @pl.when(self.here)
        def _():
            self.stay.start()

        @pl.when(jnp.logical_not(self.here))
        def _():
            self.copy.start()

    def arrived(self):
        @pl.when(jnp.logical_not(self.from_here))
        def _():
            self.into.wait_recv()

    def left(self):
        @pl.when(self.here)
        def _():
            self.stay.wait()

        @pl.when(jnp.logical_not(self.here))
        def _():
            self.copy.wait_send()


def send(source, target, sems, index, device):
    copy = pltpu.make_async_remote_copy(
        src_ref=source,
        dst_ref=target,
        send_sem=sems.at[(0,) + index],
        recv_sem=sems.at[(1,) + index],
        device_id=device,
        device_id_type=pl.DeviceIdType.MESH,
    )
    copy.start()
    return copy


class KernelRing:
    def __init__(self, count, own, slots, sems, owner, up, down):
        self.count, self.own, self.slots, self.sems = count, own, slots, sems
        self.owner, self.up, self.down = owner, up, down
        self.copies = {}

    def start(self, step):
        half = self.slots.shape[1] // 2
        for way, device in enumerate((self.up, self.down)):
            slot = self.slots.at[self.owner((1 - step) if way == 0 else (step - 1))]
            source = self.own if step == 1 else slot
            if step == self.count // 2:
                rows = pl.ds(way * half, half)
                source, slot = source.at[rows], slot.at[rows]
            self.copies[way, step] = send(source, slot, self.sems, (way, step - 1), device)

    def arrived(self, step):
        self.copies[0, step].wait_recv()
        self.copies[1, step].wait_recv()

    def finish(self):
        for copy in self.copies.values():
            copy.wait_send()


def opening_kernel(
    hidden,
    kv_own,
    qkv_weight,
    proj_weight,
    fc_weight,
    cot,
    hidden_out,
    kvw_out,
    qw_out,
    proj_out,
    kv_out,
    fc_out,
    cot_out,
    weights,
    mine,
    hid_chip,
    hid_core,
    kvw_sems,
    q_sems,
    proj_sems,
    kv_sems,
    kv_chip,
    kv_core,
    kv_far,
    fc_sems,
    cot_sems,
    move_sems,
    cut_sems,
    local,
    *,
    count,
    shard,
):
    s, f, owner, up, down, chip, core = neighbours(count)
    steps = count // 2
    per = count // 4
    target = (f // per, 4 * lax.rem(f, per) + s)
    source = (lax.rem(f, 4), s * per + f // 4)
    own_goes = met(target, s, f).astype(jnp.int32)
    greet_also((up, down, chip, core), (source,), own_goes, s, f)
    part = proj_out.shape[1]
    q_cols = qw_out.shape[2]
    q_own = qkv_weight.at[:, pl.ds(pl.multiple_of(s * q_cols, q_cols), q_cols)]
    proj_own, fc_own = proj_out.at[f], fc_out.at[f]
    rings = [
        KernelRing(count, own, slots, sems, owner, up, down)
        for own, slots, sems in (
            (kv_own, kvw_out, kvw_sems),
            (q_own, qw_out, q_sems),
            (proj_own, proj_out, proj_sems),
            (fc_own, fc_out, fc_sems),
        )
    ]
    kvw, qw, proj, fc = rings
    kvw.start(1)
    moved = Maybe(
        proj_weight.at[pl.ds(pl.multiple_of(s * part, part), part)],
        proj_out.at[target[1]],
        proj_own,
        move_sems.at[0],
        move_sems.at[1],
        move_sems.at[1],
        move_sems.at[2],
        target,
        source,
        s,
        f,
    )
    if fc_weight.shape[1] == fc_out.shape[2]:
        cuts = [pltpu.make_async_copy(fc_weight, fc_own, cut_sems.at[0])]
    else:
        cols = fc_out.shape[2] // count
        cuts = [
            pltpu.make_async_copy(
                fc_weight.at[:, pl.ds(pl.multiple_of((g * 4 + s) * cols, cols), cols)],
                fc_own.at[:, pl.ds(g * cols, cols)],
                cut_sems.at[g],
            )
            for g in range(count)
        ]
    for copy in cuts:
        copy.start()
    rows = hidden.shape[0] // 2
    halves = [pl.ds(i * rows, rows) for i in range(2)]
    across = [send(hidden.at[half], hidden_out.at[2, half], hid_chip, (i,), chip) for i, half in enumerate(halves)]
    pair = [send(hidden, hidden_out.at[1], hid_core, (2,), core)]
    stays = [
        pltpu.make_async_copy(source, target, local.at[i])
        for i, (source, target) in enumerate(
            (
                (hidden, hidden_out.at[0]),
                (kv_own, kvw_out.at[f]),
                (q_own, qw_out.at[f]),
                (cot, cot_out.at[0]),
            )
        )
    ]
    for copy in stays:
        copy.start()
    values = hidden[...].astype(F32)
    mean = jnp.mean(values, axis=-1, keepdims=True)
    center = values - mean
    inverse = lax.rsqrt(jnp.mean(center * center, axis=-1, keepdims=True) + EPS)
    for step in range(2, steps + 1):
        kvw.arrived(step - 1)
        kvw.start(step)
    qw.start(1)
    for copy in cuts:
        copy.wait()
    fc.start(1)
    kvw.arrived(steps)
    stays[1].wait()
    load = pltpu.make_async_copy(kvw_out, weights, local.at[6])
    load.start()
    load.wait()
    total = jnp.zeros((hidden.shape[0], kvw_out.shape[2]), F32)
    for t in range(count):
        cols = slice(t * shard, (t + 1) * shard)
        normed = (hidden[:, cols].astype(F32) - mean) * inverse
        gain = weights[t, shard : shard + 1, :shard].astype(F32)
        bias = weights[t, shard + 1 : shard + 2, :shard].astype(F32)
        total += dot_plain((normed * gain + bias).astype(BF), weights[t, :shard, :])
    mine[...] = total.astype(BF)

    spread = KernelRing(count, mine, kv_out.at[s], kv_sems, owner, up, down)
    spread.start(1)
    keep = pltpu.make_async_copy(mine, kv_out.at[s, f], local.at[7])
    keep.start()
    kv_across, kv_pair = [], []

    def pass_on(source, place):
        index = (len(kv_across),)
        kv_across.append((place, send(source, kv_out.at[s, place], kv_chip, index, chip)))
        kv_pair.append(send(source, kv_out.at[s, place], kv_core, index, core))

    pass_on(mine, f)
    for i, half in enumerate(halves):
        across[i].wait_recv()
        pair.append(send(hidden_out.at[2, half], hidden_out.at[2 + 1, half], hid_core, (i,), core))
    for step in range(1, steps + 1):
        spread.arrived(step)
        qw.arrived(step)
        if step < steps:
            spread.start(step + 1)
            qw.start(step + 1)
            for place in (owner(-step), owner(step)):
                pass_on(kv_out.at[s, place], place)
        else:
            pass_on(kv_out.at[s, owner(steps)], owner(steps))
        if step == 1:
            moved.arrived()
            moved.left()
            proj.start(1)
            cot_across = send(cot, cot_out.at[2], cot_sems, (0,), chip)
            cot_pair = send(cot, cot_out.at[1], cot_sems, (1,), core)
        else:
            proj.arrived(step - 1)
            proj.start(step)
        fc.arrived(step)
        if step < steps:
            fc.start(step + 1)
    other = lax.rem(s + 2, 4)
    far = []
    for i, (place, copy) in enumerate(kv_across):
        copy.wait_recv()
        slot = kv_out.at[other, place]
        far.append(send(slot, slot, kv_far, (i,), core))
    cot_across.wait()
    cot_far = send(cot_out.at[2], cot_out.at[3], cot_sems, (2,), core)
    proj.arrived(steps)
    for ring in rings + [spread]:
        ring.finish()
    for copy in [keep, cot_pair, cot_far, stays[0]] + stays[2:]:
        copy.wait()
    for copy in across + [copy for _, copy in kv_across]:
        copy.wait_send()
    for copy in pair + kv_pair + far:
        copy.wait()


def opening(hidden, kv_own, qkv_weight, proj_weight, fc_weight, cot, fsdp_count, q_cols):
    count, width = hidden.shape
    shard = qkv_weight.shape[0]
    dma = pltpu.SemaphoreType.DMA
    ring = dma((2, 2, fsdp_count // 2))
    anywhere = pl.BlockSpec(memory_space=pltpu.HBM)
    inside = pl.BlockSpec(memory_space=pltpu.VMEM)
    return pl.pallas_call(
        functools.partial(opening_kernel, count=fsdp_count, shard=shard),
        out_shape=(
            jax.ShapeDtypeStruct((4,) + hidden.shape, BF),
            jax.ShapeDtypeStruct((fsdp_count,) + kv_own.shape, BF),
            jax.ShapeDtypeStruct((fsdp_count, shard, q_cols), BF),
            jax.ShapeDtypeStruct((fsdp_count, shard // 4, width), BF),
            jax.ShapeDtypeStruct((4, fsdp_count, count, 2 * HD), BF),
            jax.ShapeDtypeStruct((fsdp_count, shard, width), BF),
            jax.ShapeDtypeStruct((4,) + hidden.shape, BF),
        ),
        in_specs=[inside] + [anywhere] * 5,
        out_specs=(anywhere,) * 7,
        scratch_shapes=[
            pltpu.VMEM((fsdp_count,) + kv_own.shape, BF),
            pltpu.VMEM((count, 2 * HD), BF),
            dma((2, 2)),
            dma((2, 3)),
            ring,
            ring,
            ring,
            ring,
            dma((2, fsdp_count)),
            dma((2, fsdp_count)),
            dma((2, fsdp_count)),
            ring,
            dma((2, 3)),
            dma((3,)),
            dma((fsdp_count,)),
            dma((8,)),
        ],
        compiler_params=pltpu.CompilerParams(
            collective_id=1, has_side_effects=True, vmem_limit_bytes=40 << 20
        ),
        cost_estimate=COST,
        name="opening",
    )(hidden, kv_own, qkv_weight, proj_weight, fc_weight, cot)


GELU_A = math.sqrt(2 / math.pi)
GELU_B = 0.044715


def middle_kernel(rows_ref, cot_ref, fc_ref, down_ref, activ_ref, pre_ref, grad_ref, total, *, step):
    tile = pl.program_id(0)
    fc = fc_ref[...].reshape(-1, fc_ref.shape[2])
    down = down_ref[...].reshape(-1, down_ref.shape[2])

    @pl.when(tile == 0)
    def _():
        total[...] = jnp.zeros_like(total)

    for at in range(0, rows_ref.shape[0], step):
        part = slice(at, at + step)
        value = dot_plain(rows_ref[part], fc)
        pull = dot_cols(cot_ref[part], down)
        square = value * value
        bend = jnp.tanh(GELU_A * value * (1.0 + GELU_B * square))
        half = 0.5 * (1.0 + bend)
        activ_ref[part] = (value * half).astype(BF)
        slope = half + 0.5 * value * (1.0 - bend * bend) * (GELU_A * (1.0 + 3.0 * GELU_B * square))
        grad = (pull * slope).astype(BF)
        pre_ref[part] = grad
        total[part] += dot_cols(grad, fc)

    @pl.when(tile == pl.num_programs(0) - 1)
    def _():
        grad_ref[...] = total[...].astype(BF)


def middle(rows, cot, fc_all, down_all, tile):
    count, width = rows.shape
    parts, shard = fc_all.shape[:2]
    quarter = down_all.shape[1]
    hidden = parts * quarter
    per = tile // quarter
    whole = pl.BlockSpec((count, width), lambda n: (0, 0), pipeline_mode=pl.Buffered(1))
    cols = pl.BlockSpec((count, tile), lambda n: (0, n))
    return pl.pallas_call(
        functools.partial(middle_kernel, step=256),
        out_shape=(
            jax.ShapeDtypeStruct((count, hidden), BF),
            jax.ShapeDtypeStruct((count, hidden), BF),
            jax.ShapeDtypeStruct((count, width), BF),
        ),
        grid=(hidden // tile,),
        in_specs=[
            whole,
            whole,
            pl.BlockSpec((parts, shard, tile), lambda n: (0, 0, n)),
            pl.BlockSpec((per, quarter, width), lambda n: (n, 0, 0)),
        ],
        out_specs=(cols, cols, pl.BlockSpec((count, width), lambda n: (0, 0))),
        scratch_shapes=[pltpu.VMEM((count, width), F32)],
        compiler_params=pltpu.CompilerParams(vmem_limit_bytes=60 << 20),
        cost_estimate=COST,
        name="middle",
    )(rows, cot, fc_all, down_all)


def bridge_kernel(
    heads,
    proj,
    hidden,
    vectors,
    down_own,
    mlp_out,
    resid_out,
    down_out,
    far_out,
    far,
    near_out,
    near,
    chip_in,
    mine,
    pair_sems,
    chip_sems,
    spread_chip,
    spread_core,
    down_sems,
    local,
    *,
    count,
):
    s, f, owner, up, down, chip, core = neighbours(count)
    greet(up, down, chip, core)
    steps = count // 2
    tokens = hidden.shape[0]
    ring = KernelRing(count, down_own, down_out, down_sems, owner, up, down)
    ring.start(1)
    stays = [
        pltpu.make_async_copy(down_own, down_out.at[f], local.at[0]),
    ]
    for copy in stays:
        copy.start()

    def part(i):
        return dot_plain(heads[i * tokens : (i + 1) * tokens], proj[...])

    far_out[...] = part(3).astype(BF)
    pairs = [send(far_out, far, pair_sems, (0,), core)]
    near_out[...] = part(1).astype(BF)
    pairs.append(send(near_out, near, pair_sems, (1,), core))
    middle = part(2)
    pairs[0].wait()
    far_out[...] = (middle + far[...].astype(F32)).astype(BF)
    rows = tokens // 2
    halves = [pl.ds(i * rows, rows) for i in range(2)]
    across = [send(far_out.at[half], chip_in.at[half], chip_sems, (i,), chip) for i, half in enumerate(halves)]
    resid_out[...] = hidden[...].astype(F32) + part(0)
    pairs[1].wait()
    resid_out[...] += near[...].astype(F32)
    spread, spread_pair = [], []
    block = 64
    for i, half in enumerate(halves):
        across[i].wait_recv()
        for at in range(i * rows, (i + 1) * rows, block):
            here = slice(at, at + block)
            resid = resid_out[here] + chip_in[here].astype(F32)
            resid_out[here] = resid
            normed, _ = layer_norm(resid)
            mine[here] = (normed * vectors[0:1] + vectors[1:2]).astype(BF)
        spread.append(send(mine.at[half], mlp_out.at[2, half], spread_chip, (i,), chip))
        spread_pair.append(send(mine.at[half], mlp_out.at[1, half], spread_core, (i,), core))
        ring.arrived(i + 1)
        ring.start(i + 2)
    stays.append(pltpu.make_async_copy(mine, mlp_out.at[0], local.at[1]))
    stays[-1].start()
    for i, half in enumerate(halves):
        spread[i].wait_recv()
        spread_pair.append(send(mlp_out.at[2, half], mlp_out.at[3, half], spread_core, (2 + i,), core))
    for step in range(3, steps + 1):
        ring.arrived(step)
        if step < steps:
            ring.start(step + 1)
    ring.finish()
    for copy in across + spread:
        copy.wait_send()
    for copy in spread_pair + stays:
        copy.wait()


def bridge(heads, proj, hidden, vectors, down_own, fsdp_count):
    tokens, width = hidden.shape
    quarter = down_own.shape[0]
    dma = pltpu.SemaphoreType.DMA
    anywhere = pl.BlockSpec(memory_space=pltpu.HBM)
    inside = pl.BlockSpec(memory_space=pltpu.VMEM)
    wide = pltpu.VMEM((tokens, width), BF)
    return pl.pallas_call(
        functools.partial(bridge_kernel, count=fsdp_count),
        out_shape=(
            jax.ShapeDtypeStruct((4, tokens, width), BF),
            jax.ShapeDtypeStruct((tokens, width), F32),
            jax.ShapeDtypeStruct((fsdp_count, quarter, width), BF),
        ),
        in_specs=[inside] * 4 + [anywhere],
        out_specs=(anywhere, inside, anywhere),
        scratch_shapes=[wide] * 6
        + [
            dma((2, 2)),
            dma((2, 2)),
            dma((2, 2)),
            dma((2, 4)),
            dma((2, 2, fsdp_count // 2)),
            dma((4,)),
        ],
        compiler_params=pltpu.CompilerParams(
            collective_id=3, has_side_effects=True, vmem_limit_bytes=40 << 20
        ),
        cost_estimate=COST,
        name="bridge",
    )(heads, proj, hidden, vectors, down_own)


def feedback_kernel(
    parts,
    mlp_in,
    pre_grad,
    activ,
    cot,
    down_all,
    resid,
    gain,
    branch_out,
    result_out,
    resid_out,
    vectors_out,
    up_out,
    down_out,
    rest_out,
    mlp_here,
    pre_here,
    activ_here,
    cot_here,
    here,
    across_out,
    far,
    near,
    chip_in,
    branch,
    outs_first,
    ins_first,
    outs_next,
    ins_next,
    stage,
    down_here,
    low_here,
    low_far,
    low_near,
    low_chip,
    branch_low,
    pair_sems,
    chip_sems,
    spread_chip,
    spread_core,
    ring_sems,
    low_pair,
    low_across,
    local,
    *,
    count,
    shard,
    turned,
):
    s, f, owner, up, down, chip, core = neighbours(count)
    greet(up, down, chip, core)
    steps = count // 2
    tokens, width = resid.shape
    pairs = [send(parts.at[3], far, pair_sems, (0,), core), send(parts.at[1], near, pair_sems, (1,), core)]
    loads = [
        pltpu.make_async_copy(source, target, local.at[i])
        for i, (source, target) in enumerate(
            (
                (pre_grad, pre_here),
                (mlp_in, mlp_here),
                (parts.at[2], across_out),
                (cot, cot_here),
                (activ, activ_here),
                (parts.at[0], here),
            )
        )
    ]
    for copy in loads:
        copy.start()

    def product(left, right, place, out):
        start = pl.multiple_of(place * shard, shard)
        chosen = left[:, pl.ds(start, shard)] if turned else left[pl.ds(start, shard), :]
        for at in range(0, width, 512):
            cols = slice(at, at + 512)
            value = dot_rows(chosen, right[:, cols]) if turned else dot_plain(chosen, right[:, cols])
            out[:, cols] = value.astype(BF)

    def chunk(place, out):
        product(mlp_here, pre_here, place, out.at[pl.ds(0, shard)])
        product(activ_here, cot_here, place, out.at[pl.ds(shard, shard)])

    def low_part(j, down):
        lines = slice(j * tokens, (j + 1) * tokens)
        return dot_plain(activ_here[lines], down) if turned else dot_rows(activ_here[:, lines], down)

    upper, under = pl.ds(0, shard), pl.ds(shard, shard)
    devices = (up, down)
    side = width // 2
    sides = [
        pltpu.make_async_copy(down_all.at[:, :, pl.ds(i * side, side)], down_here, local.at[10 + i])
        for i in range(2)
    ]
    sides[0].start()
    loads[0].wait()
    loads[1].wait()
    product(mlp_here, pre_here, owner(steps), outs_first.at[upper])
    first = [send(outs_first.at[upper], ins_first.at[upper], ring_sems, (0, 0), up)]
    loads[2].wait()
    pairs[0].wait_recv()
    across_out[...] = (across_out[...].astype(F32) + far[...].astype(F32)).astype(BF)
    rows = tokens // 2
    halves = [pl.ds(i * rows, rows) for i in range(2)]
    across = [send(across_out.at[half], chip_in.at[half], chip_sems, (i,), chip) for i, half in enumerate(halves)]
    loads[3].wait()
    loads[4].wait()
    product(activ_here, cot_here, owner(steps), outs_first.at[under])
    first.append(send(outs_first.at[under], ins_first.at[under], ring_sems, (1, 0), down))
    chunk(owner(steps - 1), outs_next.at[0])
    chunk(owner(1 - steps), outs_next.at[1])
    second = []
    for way, part in enumerate((upper, under)):
        first[way].wait_recv()
        out = outs_next.at[way]
        out[part] = (out[part].astype(F32) + ins_first[part].astype(F32)).astype(BF)
        second.append(send(out, ins_next.at[way], ring_sems, (way, 1), devices[way]))

    loads[5].wait()
    pairs[1].wait_recv()
    gain_grad = jnp.zeros((1, width), F32)
    bias_grad = jnp.zeros((1, width), F32)
    spread, spread_pair = [], []
    block = 64
    for i, half in enumerate(halves):
        across[i].wait_recv()
        for at in range(i * rows, (i + 1) * rows, block):
            part = slice(at, at + block)
            grad = here[part].astype(F32) + near[part].astype(F32) + chip_in[part].astype(F32)
            normed, inverse = layer_norm(resid[part])
            gain_grad += jnp.sum(grad * normed, axis=0, keepdims=True)
            bias_grad += jnp.sum(grad, axis=0, keepdims=True)
            value = cot_here[part].astype(F32) + norm_back(grad * gain[...], normed, inverse)
            resid_out[part] = value
            branch[part] = value.astype(BF)
        spread.append(send(branch.at[half], branch_out.at[2, half], spread_chip, (i,), chip))
        spread_pair.append(send(branch.at[half], branch_out.at[1, half], spread_core, (i,), core))
    vectors_out[0:1] = gain_grad
    vectors_out[1:2] = bias_grad
    keep = pltpu.make_async_copy(branch, branch_out.at[0], local.at[6])
    keep.start()

    for copy in across:
        copy.wait_send()
    lows = (low_here, here, across_out, branch_low)
    for i in range(2):
        cols = pl.ds(i * side, side)
        sides[i].wait()
        down = down_here[...].reshape(-1, side)
        for j in (3, 1, 2, 0):
            value = low_part(j, down)
            lows[j][:, cols] = value if j == 0 else value.astype(BF)
        if i == 0:
            sides[1].start()
    low_sends = [send(lows[3], low_far, low_pair, (0,), core), send(lows[1], low_near, low_pair, (1,), core)]
    low_sends[0].wait()
    across_out[...] = (across_out[...].astype(F32) + low_far[...].astype(F32)).astype(BF)
    low_chip_copy = send(across_out, low_chip, low_across, (0,), chip)

    def rest(i, carry):
        back = lax.rem(i + 1, 2)
        n = (steps - (i + 1) // 2) * (1 - 2 * back)
        chunk(owner(n), stage)
        copy = pltpu.make_async_copy(stage, rest_out.at[i - 5], local.at[7])
        copy.start()
        copy.wait()
        return carry

    lax.fori_loop(5, count, rest, 0)
    for i, half in enumerate(halves):
        spread[i].wait_recv()
        spread_pair.append(send(branch_out.at[2, half], branch_out.at[3, half], spread_core, (2 + i,), core))
    leaving = []
    low_sends[1].wait()
    low_chip_copy.wait()
    for at in range(0, tokens, block):
        part = slice(at, at + block)
        value = resid[part] + low_here[part] + low_near[part].astype(F32) + low_chip[part].astype(F32)
        result_out[part] = value.astype(BF)
    for way, target in enumerate((up_out, down_out)):
        out = stage if way == 0 else outs_first
        if way:
            first[0].wait_send()
            first[1].wait_send()
        chunk(owner((steps - 2) * (1 - 2 * way)), out)
        second[way].wait_recv()
        out[...] = (out[...].astype(F32) + ins_next[way].astype(F32)).astype(BF)
        leaving.append(pltpu.make_async_copy(out, target, local.at[8 + way]))
        leaving[way].start()
    for copy in pairs + spread + second:
        copy.wait_send()
    for copy in spread_pair + leaving + [keep]:
        copy.wait()


def feedback(parts, mlp_in, pre_grad, activ, cot, down_all, resid, gain, fsdp_count, shard):
    tokens, width = resid.shape
    turned = shard % 128 == 0
    if not turned:
        mlp_in, activ = mlp_in.T, activ.T
    dma = pltpu.SemaphoreType.DMA
    anywhere = pl.BlockSpec(memory_space=pltpu.HBM)
    inside = pl.BlockSpec(memory_space=pltpu.VMEM)
    wide = pltpu.VMEM((tokens, width), BF)
    both = pltpu.VMEM((2 * shard, width), BF)
    quarter = down_all.shape[1]
    flow = jax.ShapeDtypeStruct((2 * shard, width), BF)
    return pl.pallas_call(
        functools.partial(feedback_kernel, count=fsdp_count, shard=shard, turned=turned),
        out_shape=(
            jax.ShapeDtypeStruct((4, tokens, width), BF),
            jax.ShapeDtypeStruct((tokens, width), BF),
            jax.ShapeDtypeStruct((tokens, width), F32),
            jax.ShapeDtypeStruct((2, width), F32),
            flow,
            flow,
            jax.ShapeDtypeStruct((fsdp_count - 5, 2 * shard, width), BF),
        ),
        in_specs=[anywhere] * 6 + [inside] * 2,
        out_specs=(anywhere, inside, inside, inside, anywhere, anywhere, anywhere),
        scratch_shapes=[pltpu.VMEM(value.shape, BF) for value in (mlp_in, pre_grad, activ, cot)]
        + [wide] * 6
        + [
            both,
            both,
            pltpu.VMEM((2, 2 * shard, width), BF),
            pltpu.VMEM((2, 2 * shard, width), BF),
            both,
            pltpu.VMEM((fsdp_count, quarter, width // 2), BF),
            pltpu.VMEM((tokens, width), F32),
            wide,
            wide,
            wide,
            wide,
            dma((2, 2)),
            dma((2, 2)),
            dma((2, 2)),
            dma((2, 4)),
            dma((2, 2, 2)),
            dma((2, 2)),
            dma((2, 1)),
            dma((12,)),
        ],
        compiler_params=pltpu.CompilerParams(
            collective_id=4, has_side_effects=True, vmem_limit_bytes=61 << 20
        ),
        cost_estimate=COST,
        name="feedback",
    )(parts, mlp_in, pre_grad, activ, cot, down_all, resid, gain)


class KernelScatter:
    def __init__(self, count, chunk, outs, ins, sems, up, down):
        self.steps, self.chunk, self.outs, self.ins, self.sems = count // 2, chunk, outs, ins, sems
        self.devices = (up, down)
        self.half = outs.shape[2] // 2
        self.copies = {}

    def start(self, step):
        half = self.half
        for way, sign in ((0, 1), (1, -1)):
            mine = self.chunk(sign * (self.steps - step))
            if step > 1:
                self.copies[way, step - 2].wait_send()
            out, into = self.outs.at[way, step % 2], self.ins.at[way, step]
            rows = slice(way * half, (way + 1) * half)
            rest = slice((1 - way) * half, (2 - way) * half)
            if step == 0:
                out, into = out.at[pl.ds(0, half)], into.at[pl.ds(0, half)]
                out[...] = mine[rows].astype(BF)
            elif step == 1:
                out[rows] = (mine[rows] + self.ins[way, 0, :half].astype(F32)).astype(BF)
                out[rest] = mine[rest].astype(BF)
            else:
                out[...] = (mine + self.ins[way, step - 1].astype(F32)).astype(BF)
            self.copies[way, step] = send(out, into, self.sems, (way, step), self.devices[way])

    def arrived(self, step):
        self.copies[0, step].wait_recv()
        self.copies[1, step].wait_recv()

    def total(self):
        last = self.steps - 1
        return self.chunk(0) + self.ins[0, last].astype(F32) + self.ins[1, last].astype(F32)

    def finish(self):
        for (_, step), copy in self.copies.items():
            if step >= self.steps - 2:
                copy.wait_send()


def closing_kernel(
    kv_parts,
    query_rows,
    q_weight,
    attn_parts,
    ff_up,
    ff_down,
    ff_rest,
    resid_grad,
    hidden,
    kv_weight,
    attn_in,
    mlp_vectors,
    grad_out,
    q_out,
    proj_out,
    ff_out,
    tail_out,
    kv_here,
    kv_near,
    kv_far,
    kv_chip_in,
    kv_outs,
    kv_ins,
    q_far_out,
    q_far,
    q_near,
    q_chip_in,
    q_here,
    attn_here,
    attn_own,
    proj_here,
    attn_outs,
    attn_ins,
    ff_here,
    ff_ins,
    ff_sum,
    kv_total,
    tail_here,
    tail_outs,
    tail_ins,
    swap_out,
    swap_in,
    local,
    kv_core_sems,
    kv_chip_sems,
    kv_sems,
    q_core_sems,
    q_chip_sems,
    attn_sems,
    ff_sems,
    ff_chip_sems,
    ff_core_sems,
    tail_sems,
    swap_sems,
    q_spread_sems,
    proj_spread_sems,
    move_sems,
    *,
    count,
    shard,
):
    s, f, owner, up, down, chip, core = neighbours(count)
    steps = count // 2
    order = [steps] + [sign * n for n in range(steps - 1, 0, -1) for sign in (1, -1)] + [0]
    other, sibling = lax.rem(s + 2, 4), core[0]
    far = lax.rem(sibling + 2, 4)
    tokens = hidden.shape[0]
    per = count // 4
    target = (lax.rem(f, 4), s * per + f // 4)
    source = (f // per, 4 * lax.rem(f, per) + s)
    greet_also((up, down, chip, core), (source,), met(target, s, f).astype(jnp.int32), s, f)

    kv_pair = [
        send(kv_parts.at[far], kv_far, kv_core_sems, (0,), core),
        send(kv_parts.at[sibling], kv_near, kv_core_sems, (1,), core),
    ]
    loads = [
        pltpu.make_async_copy(kv_parts.at[other], kv_here.at[1], local.at[0]),
        pltpu.make_async_copy(kv_parts.at[s], kv_here.at[0], local.at[1]),
        pltpu.make_async_copy(attn_parts, attn_here, local.at[2]),
        pltpu.make_async_copy(ff_rest.at[ff_rest.shape[0] - 1], ff_here, local.at[3]),
    ]
    for copy in loads:
        copy.start()
    ff_rows = ff_here.shape[0] // 2
    ff_parts = [pl.ds(i * ff_rows, ff_rows) for i in range(2)]
    ff_ring = []

    def ff_start(i):
        for way, (source, device) in enumerate(((ff_up, up), (ff_down, down))):
            copy = send(source.at[ff_parts[i]], ff_ins.at[way, ff_parts[i]], ff_sems, (way, i), device)
            ff_ring.append(copy)

    ff_start(0)

    def query_part(i):
        return dot_cols(query_rows[i * tokens : (i + 1) * tokens], q_weight[...])

    q_far_out[...] = query_part(3).astype(BF)
    q_pair = [send(q_far_out, q_far, q_core_sems, (0,), core)]
    grad_out[...] = query_part(1).astype(BF)
    loads[0].wait()
    kv_pair[0].wait_recv()
    kv_across = {}
    for i, n in enumerate(order):
        place = owner(n)
        kv_here[1, place] = (kv_here[1, place].astype(F32) + kv_far[place].astype(F32)).astype(BF)
        kv_across[n] = send(kv_here.at[1, place], kv_chip_in.at[i], kv_chip_sems, (i,), chip)
    part = query_part(2)
    q_pair[0].wait()
    q_chip_out = q_far_out
    q_chip_out[...] = (part + q_far[...].astype(F32)).astype(BF)
    rows = tokens // 2
    q_halves = [pl.ds(i * rows, rows) for i in range(2)]
    q_across = [
        send(q_chip_out.at[half], q_chip_in.at[half], q_chip_sems, (i,), chip) for i, half in enumerate(q_halves)
    ]
    q_pair.append(send(grad_out, q_near, q_core_sems, (1,), core))
    q_here[...] = query_part(0)
    loads[1].wait()
    kv_pair[1].wait_recv()

    def kv_chunk(n):
        n = steps if n == -steps else n
        place = owner(n)
        here = kv_here[0, place].astype(F32) + kv_near[place].astype(F32)
        return here + kv_chip_in[order.index(n)].astype(F32)

    loads[2].wait()

    def attn_chunk(n):
        return attn_here[order.index(steps if n == -steps else n)].astype(F32)

    kv = KernelScatter(count, kv_chunk, kv_outs, kv_ins, kv_sems, up, down)
    attn = KernelScatter(count, attn_chunk, attn_outs, attn_ins, attn_sems, up, down)
    for step in range(steps):
        for n in (steps - step, step - steps):
            if n in order:
                kv_across[n].wait_recv()
        if step:
            kv.arrived(step - 1)
        kv.start(step)
        if step:
            attn.arrived(step - 1)
        attn.start(step)
    ff_start(1)

    loads[3].wait()
    ff_pair, ff_across = [], []

    def ff_close(i):
        rows = ff_parts[i]
        for copy in ff_ring[2 * i : 2 * i + 2]:
            copy.wait_recv()
        arrived = ff_ins[0, rows].astype(F32) + ff_ins[1, rows].astype(F32)
        ff_sum[rows] = (ff_here[rows].astype(F32) + arrived).astype(BF)
        ff_across.append(send(ff_sum.at[rows], ff_out.at[2, rows], ff_chip_sems, (i,), chip))
        ff_pair.append(send(ff_sum.at[rows], ff_out.at[1, rows], ff_core_sems, (i,), core))

    ff_close(0)
    kv_across[0].wait_recv()
    kv.arrived(steps - 1)
    kv_total[...] = kv.total().astype(BF)

    attn.arrived(steps - 1)
    attn_own[...] = attn.total().astype(BF)
    part = proj_out.shape[1]
    lines = pl.ds(part, attn_own.shape[0] - part)
    q_lines = attn_own.at[lines]
    q_spread = [
        send(q_lines, q_out.at[2], q_spread_sems, (0,), chip),
        send(q_lines, q_out.at[1], q_spread_sems, (1,), core),
    ]
    q_keep = pltpu.make_async_copy(q_lines, q_out.at[0], local.at[5])
    q_keep.start()
    moved = Maybe(
        attn_own.at[pl.ds(0, part)],
        proj_here,
        proj_here,
        move_sems.at[0],
        move_sems.at[1],
        move_sems.at[1],
        move_sems.at[2],
        target,
        source,
        s,
        f,
    )

    q_pair[1].wait()
    for copy in q_across:
        copy.wait_recv()
    q_here[...] += q_near[...].astype(F32) + q_chip_in[...].astype(F32)
    for t in range(count):
        cols = slice(t * shard, (t + 1) * shard)
        q_here[:, cols] += dot_cols(kv_total[...], kv_weight[t, :shard, :])
    gain = jnp.concatenate([kv_weight[t, shard : shard + 1, :shard] for t in range(count)], axis=1).astype(F32)
    block = 64
    gain_grad = jnp.zeros((1, hidden.shape[1]), F32)
    bias_grad = jnp.zeros((1, hidden.shape[1]), F32)
    for at in range(0, tokens, block):
        here = slice(at, at + block)
        normed, inverse = layer_norm(hidden[here].astype(F32))
        grad = q_here[here]
        gain_grad += jnp.sum(grad * normed, axis=0, keepdims=True)
        bias_grad += jnp.sum(grad, axis=0, keepdims=True)
        grad_out[here] = (resid_grad[here] + norm_back(grad * gain, normed, inverse)).astype(BF)

    tail_here[...] = jnp.zeros_like(tail_here)
    vectors = (gain_grad, bias_grad, mlp_vectors[0:1], mlp_vectors[1:2])
    for t in range(count):
        cols = slice(t * shard, (t + 1) * shard)
        tail_here[t, :shard, :] = dot_rows(attn_in[:, cols], kv_total[...])
        for j, vector in enumerate(vectors):
            tail_here[t, shard + j : shard + j + 1, :shard] = vector[:, cols]
    tail = KernelScatter(count, lambda n: tail_here[owner(n)], tail_outs, tail_ins, tail_sems, up, down)
    for step in range(steps):
        if step:
            tail.arrived(step - 1)
        tail.start(step)
        if step == 0:
            ff_close(1)
            q_spread[0].wait_recv()
            q_spread.append(send(q_out.at[2], q_out.at[3], q_spread_sems, (2,), core))
            moved.arrived()
            moved.left()
            proj_spread = [
                send(proj_here, proj_out.at[2], proj_spread_sems, (0,), chip),
                send(proj_here, proj_out.at[1], proj_spread_sems, (1,), core),
            ]
            proj_keep = pltpu.make_async_copy(proj_here, proj_out.at[0], local.at[6])
            proj_keep.start()
    proj_spread[0].wait_recv()
    proj_spread.append(send(proj_out.at[2], proj_out.at[3], proj_spread_sems, (2,), core))
    tail.arrived(steps - 1)
    total = tail.total()
    swap_out[0] = total.astype(BF)
    swaps = [send(swap_out.at[0], swap_in.at[0], swap_sems, (0,), core)]
    for i, rows in enumerate(ff_parts):
        ff_across[i].wait_recv()
        ff_pair.append(send(ff_out.at[2, rows], ff_out.at[3, rows], ff_core_sems, (2 + i,), core))
    keep = pltpu.make_async_copy(ff_sum, ff_out.at[0], local.at[4])
    keep.start()
    swaps[0].wait_recv()
    swap_out[1] = (swap_out[0].astype(F32) + swap_in[0].astype(F32)).astype(BF)
    swaps.append(send(swap_out.at[1], swap_in.at[1], swap_sems, (1,), chip))
    swaps[1].wait_recv()
    tail_out[...] = swap_out[1].astype(F32) + swap_in[1].astype(F32)
    keep.wait()
    q_keep.wait()
    proj_keep.wait()
    q_spread[0].wait_send()
    proj_spread[0].wait_send()
    for copy in q_spread[1:] + proj_spread[1:]:
        copy.wait()
    for ring in (kv, attn, tail):
        ring.finish()
    for copy in kv_pair + q_across + list(kv_across.values()) + ff_ring + ff_across + swaps:
        copy.wait_send()
    for copy in ff_pair:
        copy.wait()


def closing(kv_parts, query_rows, q_weight, attn_parts, ff_flow, resid_grad, hidden, kv_weight, attn_in, mlp_vectors, shard):
    ff_up, ff_down, ff_rest = ff_flow
    fsdp_count, tokens, kv_cols = kv_parts.shape[1:]
    width = hidden.shape[1]
    steps = fsdp_count // 2
    dma = pltpu.SemaphoreType.DMA
    anywhere = pl.BlockSpec(memory_space=pltpu.HBM)
    inside = pl.BlockSpec(memory_space=pltpu.VMEM)
    attn_shape = attn_parts.shape[1:]
    part = shard // 4
    tail_shape = kv_weight.shape[1:]
    wide = pltpu.VMEM((tokens, width), BF)
    kv_all = pltpu.VMEM((fsdp_count, tokens, kv_cols), BF)

    def ring(shape):
        return pltpu.VMEM((2, steps) + tuple(shape), BF)

    def pair(shape):
        return pltpu.VMEM((2, 2) + tuple(shape), BF)

    ring_sems = dma((2, 2, steps))
    return pl.pallas_call(
        functools.partial(closing_kernel, count=fsdp_count, shard=shard),
        out_shape=(
            jax.ShapeDtypeStruct((tokens, width), BF),
            jax.ShapeDtypeStruct((4, attn_shape[0] - part, width), BF),
            jax.ShapeDtypeStruct((4, part, width), BF),
            jax.ShapeDtypeStruct((4,) + ff_up.shape, BF),
            jax.ShapeDtypeStruct(tail_shape, F32),
        ),
        in_specs=[anywhere, inside, inside, anywhere, anywhere, anywhere, anywhere] + [inside] * 5,
        out_specs=(inside, anywhere, anywhere, anywhere, inside),
        scratch_shapes=[
            pltpu.VMEM((2, fsdp_count, tokens, kv_cols), BF),
            kv_all,
            kv_all,
            kv_all,
            pair((tokens, kv_cols)),
            ring((tokens, kv_cols)),
            wide,
            wide,
            wide,
            wide,
            pltpu.VMEM((tokens, width), F32),
            pltpu.VMEM(attn_parts.shape, BF),
            pltpu.VMEM(attn_shape, BF),
            pltpu.VMEM((part, width), BF),
            pair(attn_shape),
            ring(attn_shape),
            pltpu.VMEM(ff_up.shape, BF),
            pltpu.VMEM((2,) + ff_up.shape, BF),
            pltpu.VMEM(ff_up.shape, BF),
            pltpu.VMEM((tokens, kv_cols), BF),
            pltpu.VMEM((fsdp_count,) + tail_shape, F32),
            pair(tail_shape),
            ring(tail_shape),
            pltpu.VMEM((2,) + tail_shape, BF),
            pltpu.VMEM((2,) + tail_shape, BF),
            dma((7,)),
            dma((2, 2)),
            dma((2, fsdp_count)),
            ring_sems,
            dma((2, 2)),
            dma((2, 2)),
            ring_sems,
            dma((2, 2, 2)),
            dma((2, 2)),
            dma((2, 4)),
            ring_sems,
            dma((2, 2)),
            dma((2, 3)),
            dma((2, 3)),
            dma((3,)),
        ],
        compiler_params=pltpu.CompilerParams(
            collective_id=2, has_side_effects=True, vmem_limit_bytes=61 << 20
        ),
        cost_estimate=COST,
        name="closing",
    )(
        kv_parts,
        query_rows,
        q_weight,
        attn_parts,
        ff_up,
        ff_down,
        ff_rest,
        resid_grad,
        hidden,
        kv_weight,
        attn_in,
        mlp_vectors,
    )


def attn_turned_kernel(order, rows_ref, query_ref, proj_ref, out_ref):
    part, cols = proj_ref.shape[0], query_ref.shape[1]
    grad = dot_rows(rows_ref[...], query_ref[...]).astype(BF)
    lines = out_ref.shape[1] - part
    out_ref[0, :part] = proj_ref[...]
    for k in range(grad.shape[0] // lines):
        out_ref[0, part:, k * cols : (k + 1) * cols] = grad[k * lines : (k + 1) * lines]


def attn_turned(order, rows, query_rows, proj_sum, shard):
    count, width = rows.shape
    cols = query_rows.shape[1]
    chunks = order.shape[0]
    part = proj_sum.shape[0] // chunks
    folds = width // cols
    lines = shard // folds
    if shard % 128:
        grad = dot_rows(rows, query_rows).astype(BF).reshape(chunks, folds, lines, cols)
        grad = grad.transpose(0, 2, 1, 3).reshape(chunks, lines, width)
        both = jnp.concatenate([proj_sum.reshape(chunks, part, width), grad], axis=1)
        return jnp.stack([lax.dynamic_index_in_dim(both, order[i], 0, False) for i in range(chunks)])
    return pl.pallas_call(
        attn_turned_kernel,
        out_shape=jax.ShapeDtypeStruct((chunks, part + lines, width), BF),
        grid_spec=pltpu.PrefetchScalarGridSpec(
            num_scalar_prefetch=1,
            grid=(chunks,),
            in_specs=[
                pl.BlockSpec((count, shard), lambda n, o: (0, o[n])),
                pl.BlockSpec((count, cols), lambda n, o: (0, 0)),
                pl.BlockSpec((part, width), lambda n, o: (o[n], 0)),
            ],
            out_specs=pl.BlockSpec((1, part + lines, width), lambda n, o: (n, 0, 0)),
        ),
        compiler_params=pltpu.CompilerParams(vmem_limit_bytes=30 << 20),
        cost_estimate=COST,
        name="attn_turned",
    )(order, rows, query_rows, proj_sum)


def rows_kernel(place, *refs):
    *ins, out = refs
    rows = ins[0].shape[0]
    for i, ref in enumerate(ins):
        out[pl.ds(pl.multiple_of((place[0] ^ i) * rows, rows), rows), :] = ref[...].astype(F32)


def stack_rows(place, pieces, tile):
    rows, width = pieces[0].shape
    return pl.pallas_call(
        rows_kernel,
        out_shape=jax.ShapeDtypeStruct((len(pieces) * rows, width), F32),
        grid_spec=pltpu.PrefetchScalarGridSpec(
            num_scalar_prefetch=1,
            grid=(width // tile,),
            in_specs=[pl.BlockSpec((rows, tile), lambda n, p: (0, n))] * len(pieces),
            out_specs=pl.BlockSpec((len(pieces) * rows, tile), lambda n, p: (0, n)),
        ),
        compiler_params=pltpu.CompilerParams(vmem_limit_bytes=40 << 20),
        cost_estimate=COST,
        name="stack_rows",
    )(place, *pieces)


def qkv_kernel(place, q_ref, tail_ref, out_ref):
    _, lines, width = q_ref.shape
    rows = out_ref.shape[0]
    folds = rows // lines
    cols = width // folds
    for i in range(q_ref.shape[0]):
        start = pl.multiple_of((place[0] ^ i) * cols, cols)
        for k in range(folds):
            part = q_ref[i, :, k * cols : (k + 1) * cols].astype(F32)
            out_ref[k * lines : (k + 1) * lines, pl.ds(start, cols)] = part
    out_ref[:, width:] = tail_ref[:rows, : out_ref.shape[1] - width]


def place_qkv(place, q_pieces, tail, rows, cols):
    return pl.pallas_call(
        qkv_kernel,
        out_shape=jax.ShapeDtypeStruct((rows, cols), F32),
        in_specs=[pl.BlockSpec(memory_space=pltpu.SMEM)] + [pl.BlockSpec(memory_space=pltpu.VMEM)] * 2,
        out_specs=pl.BlockSpec(memory_space=pltpu.VMEM),
        compiler_params=pltpu.CompilerParams(vmem_limit_bytes=30 << 20),
        cost_estimate=COST,
        name="place_qkv",
    )(place, q_pieces, tail)


def cols_kernel(place, *refs):
    *ins, out = refs
    cols = ins[0].shape[1]
    for i, ref in enumerate(ins):
        out[:, pl.ds(pl.multiple_of((place[0] ^ i) * cols, cols), cols)] = ref[...].astype(F32)


def stack_cols(place, pieces, cols):
    rows, width = pieces[0].shape
    count = len(pieces)
    if cols % 128:
        ordered = jnp.stack([lax.dynamic_index_in_dim(jnp.stack(pieces), place[0] ^ i, 0, False) for i in range(count)])
        ordered = ordered.reshape(count, rows, width // cols, cols).transpose(1, 2, 0, 3)
        return ordered.reshape(rows, count * width).astype(F32)
    return pl.pallas_call(
        cols_kernel,
        out_shape=jax.ShapeDtypeStruct((rows, count * width), F32),
        grid_spec=pltpu.PrefetchScalarGridSpec(
            num_scalar_prefetch=1,
            grid=(width // cols,),
            in_specs=[pl.BlockSpec((rows, cols), lambda n, p: (0, n))] * count,
            out_specs=pl.BlockSpec((rows, count * cols), lambda n, p: (0, n)),
        ),
        compiler_params=pltpu.CompilerParams(vmem_limit_bytes=40 << 20),
        cost_estimate=COST,
        name="stack_cols",
    )(place, *pieces)


def layer_norm(values):
    mean = jnp.mean(values, axis=-1, keepdims=True)
    center = values - mean
    inverse = lax.rsqrt(jnp.mean(center * center, axis=-1, keepdims=True) + EPS)
    return center * inverse, inverse


def norm_back(grad, normed, inverse):
    return inverse * (
        grad
        - jnp.mean(grad, axis=-1, keepdims=True)
        - normed * jnp.mean(grad * normed, axis=-1, keepdims=True)
    )


def gelu_tanh(values):
    return jax.nn.gelu(values, approximate=True)


def shards(
    hidden_in,
    out_cotangent,
    positions,
    block_mask,
    norm_gain,
    norm_bias,
    qkv_weight,
    proj_weight,
    mlp_gain,
    mlp_bias,
    fc_weight,
    down_weight,
):
    seq_count = lax.axis_size("seq")
    fsdp_count = lax.axis_size("fsdp")
    s = lax.axis_index("seq")
    f = lax.axis_index("fsdp")
    ring = Ring(fsdp_count)
    count = hidden_in.shape[1]
    width = hidden_in.shape[2]
    length = positions.shape[1]
    blocks = length // BLOCK
    shard = qkv_weight.shape[0]
    ff = fc_weight.shape[1]
    ff_shard = down_weight.shape[0]
    heads_here = HEADS // seq_count
    head_cols = heads_here * HD
    quarter = ff_shard // seq_count
    tokens_here = MB * count
    group = seq_count * tokens_here

    chunk_ids = jnp.stack([(s ^ i) * fsdp_count + f for i in range(seq_count)]).astype(jnp.int32)
    token_ids = chunk_ids[:, None] * count + jnp.arange(count, dtype=jnp.int32)[None]
    first = token_ids[:, None, :] - jnp.stack(
        [lax.dynamic_slice_in_dim(positions, chunk_ids[i] * count, count, 1) for i in range(seq_count)]
    )
    first = first[:, :, None, :]
    high_tiles = (chunk_ids * count + count - 1) // BLOCK + 1
    tables = jnp.concatenate(
        [
            jnp.broadcast_to(chunk_ids[None, :, None], (MB, seq_count, 1)),
            (first[:, :, 0, :1] // BLOCK).transpose(1, 0, 2),
            jnp.broadcast_to(high_tiles[None, :, None], (MB, seq_count, 1)),
            jnp.zeros((MB, seq_count, 1), jnp.int32),
            jnp.stack([block_mask[:, (chunk_ids[i] * count) // BLOCK] for i in range(seq_count)], axis=1),
        ],
        axis=2,
    ).reshape(-1)

    place = jnp.stack([s, f]).astype(jnp.int32)
    part = shard // seq_count
    down_own = lax.dynamic_slice_in_dim(down_weight, s * quarter, quarter, 0)
    if quarter % 128:
        fc_weight = lax.dynamic_slice_in_dim(
            fc_weight.reshape(shard, fsdp_count, seq_count, quarter), s, 1, 2
        ).reshape(shard, fsdp_count * quarter)

    span = 32
    vectors = jnp.stack([norm_gain, norm_bias, mlp_gain, mlp_bias])
    padded = jnp.pad(vectors, ((0, span - 4), (0, 2 * HD - shard)))
    own_kv = jnp.concatenate([qkv_weight[:, width:], padded], axis=0)
    hidden_own = hidden_in.reshape(tokens_here, width)
    cotangent = out_cotangent.reshape(tokens_here, width)
    hidden_all, kv_ring, q_ring, proj_ring, kv_all, fc_all, cotangent_all = opening(
        hidden_own, own_kv, qkv_weight, proj_weight, fc_weight, cotangent, fsdp_count, head_cols
    )
    cotangent_all = cotangent_all.reshape(group, width)
    kv_weight = kv_ring[:, :shard].reshape(width, 2 * HD)
    vectors = kv_ring[:, shard : shard + 4, :shard].transpose(1, 0, 2).reshape(4, width).astype(F32)
    gain_one, bias_one, gain_two, bias_two = vectors[0], vectors[1], vectors[2], vectors[3]
    q_weight = q_ring.reshape(width, head_cols)
    proj_full = proj_ring.reshape(head_cols, width)
    kv_all = kv_all.reshape(seq_count * fsdp_count, MB, count, 2 * HD)
    normed_all, _ = layer_norm(hidden_all.reshape(group, width).astype(F32))
    attn_in = (normed_all * gain_one + bias_one).astype(BF)
    own_attn_in = attn_in[:tokens_here]
    queries = dot_plain(attn_in, q_weight).astype(BF).reshape(seq_count, MB, count, head_cols)
    heads_out, logs = attend(tables, first, queries, kv_all, blocks)
    heads_rows = heads_out.reshape(group, head_cols)

    mlp_in, resid, down_all = bridge(
        heads_rows, proj_full, hidden_own, vectors[2:], down_own, fsdp_count
    )
    mlp_in = mlp_in.reshape(group, width)
    activ, pre_grad, mlp_in_parts = middle(mlp_in, cotangent_all, fc_all, down_all, 2 * BLOCK)
    branch, result, resid_grad, mlp_vectors, ff_up, ff_down, ff_rest = feedback(
        mlp_in_parts.reshape(seq_count, tokens_here, width),
        mlp_in,
        pre_grad,
        activ,
        cotangent_all,
        down_all,
        resid,
        gain_two[None],
        fsdp_count,
        shard,
    )
    branch = branch.reshape(group, width)
    steps = ring.steps()
    flow = Flow(ring, ring.scatter(ff_up, ff_down, lambda n: ff_rest[steps.index(n) - 5]))
    heads_grad = dot_cols(branch, proj_full).astype(BF).reshape(seq_count, MB, count, head_cols)
    query_grads, kv_grads = attend_back(
        tables, first, queries, kv_all, heads_out, logs, heads_grad, blocks
    )
    query_grads, kv_grads = flow.advance((query_grads, kv_grads))
    query_rows = query_grads.reshape(group, head_cols)

    proj_sum = dot_rows(heads_rows, branch).astype(BF)
    attn_parts = attn_turned(ring.order(), attn_in, query_rows, proj_sum, shard)
    ff_up, ff_down = flow.finish()
    grad_input, q_pieces, proj_pieces, ff_all, tail = closing(
        kv_grads.reshape(seq_count, fsdp_count, tokens_here, 2 * HD),
        query_rows,
        q_weight,
        attn_parts,
        (ff_up, ff_down, ff_rest),
        resid_grad,
        hidden_own,
        kv_ring,
        own_attn_in,
        mlp_vectors,
        shard,
    )
    vector_grads = tail[shard : shard + 4, :shard]
    ff_pieces = [ff_all[i] for i in range(seq_count)]
    grad_fc = stack_cols(place, [piece[:shard] for piece in ff_pieces], quarter)
    grad_down = stack_rows(place, [piece[shard:] for piece in ff_pieces], BLOCK)
    grad_proj = stack_rows(place, [proj_pieces[i] for i in range(seq_count)], width)
    grad_qkv = place_qkv(place, q_pieces, tail, shard, qkv_weight.shape[1])
    return (
        result.reshape(hidden_in.shape),
        grad_input.reshape(hidden_in.shape),
        vector_grads[0],
        vector_grads[1],
        grad_qkv,
        grad_proj,
        vector_grads[2],
        vector_grads[3],
        grad_fc,
        grad_down,
    )


def solution(mesh):
    rows = P(None, ("seq", "fsdp"), None)
    vector = P("fsdp")
    matrix = P("fsdp", None)
    in_specs = (rows, rows, P(), P(), vector, vector, matrix, matrix, vector, vector, matrix, matrix)
    out_specs = (rows, rows, vector, vector, matrix, matrix, vector, vector, matrix, matrix)
    return jax.shard_map(shards, mesh=mesh, in_specs=in_specs, out_specs=out_specs, check_vma=False)
```

```python
import functools
import math

import jax
import jax.numpy as jnp
from jax import lax
from jax.experimental import pallas as pl
from jax.experimental.pallas import tpu as pltpu
from jax.sharding import PartitionSpec as P

HEADS = 16
HD = 128
MB = 2
BLOCK = 256
EPS = 1e-05
NEG_FILL = -1e30
SCALE = HD ** (-0.5)
LOG2E = math.log2(math.e)
BF = jnp.bfloat16
COST = pl.CostEstimate(flops=0, bytes_accessed=0, transcendentals=0)
F32 = jnp.float32


def dot_rows(left, right):
    return lax.dot_general(left, right, (((0,), (0,)), ((), ())), preferred_element_type=F32)


def dot_cols(left, right):
    return lax.dot_general(left, right, (((1,), (1,)), ((), ())), preferred_element_type=F32)


def dot_plain(left, right):
    return lax.dot_general(left, right, (((1,), (0,)), ((), ())), preferred_element_type=F32)


def ring_order(count):
    return [2 * i for i in range(count // 2)] + [2 * i + 1 for i in reversed(range(count // 2))]


class Ring:
    def __init__(self, count):
        order = ring_order(count)
        self.count = count
        self.up = [(order[i], order[(i + 1) % count]) for i in range(count)]
        self.down = [(order[(i + 1) % count], order[i]) for i in range(count)]
        place = lax.axis_index("fsdp")
        half = count // 2
        self.place = place
        self.at = jnp.where(place % 2 == 0, place // 2, count - 1 - place // 2)

    def owner(self, step):
        count, half = self.count, self.count // 2
        at = lax.rem(self.at + (step + count), count)
        return jnp.where(at < half, 2 * at, 2 * (count - 1 - at) + 1)

    def steps(self):
        half = self.count // 2
        return [half] + [sign * n for n in range(half - 1, 0, -1) for sign in (1, -1)] + [0]

    def order(self):
        return jnp.stack([self.owner(n) for n in self.steps()]).astype(jnp.int32)

    def scatter(self, up, down, chunk):
        for step in range(self.count // 2 - 3, 0, -1):
            up = lax.ppermute(up, "fsdp", self.up)
            down = lax.ppermute(down, "fsdp", self.down)
            up, down = yield up, down
            up = (chunk(step).astype(F32) + up.astype(F32)).astype(BF)
            down = (chunk(-step).astype(F32) + down.astype(F32)).astype(BF)
        return up, down


class Flow:
    def __init__(self, ring, steps):
        self.ring, self.steps, self.result = ring, steps, None
        self.pending = next(steps)

    def advance(self, values=()):
        for _ in range(max(1, self.ring.count // 8)):
            if self.result is None:
                self.pending, values = lax.optimization_barrier((self.pending, values))
                try:
                    self.pending = self.steps.send(self.pending)
                except StopIteration as end:
                    self.result = end.value
        return values

    def finish(self):
        while self.result is None:
            self.advance()
        return self.result


def attend_kernel(tables, q_ref, kv_ref, first_ref, out_ref, log_ref, stack, high, total, result, *, heads, blocks):
    batch, piece = pl.program_id(0), pl.program_id(1)
    count = q_ref.shape[2]
    base = (batch * pl.num_programs(1) + piece) * (blocks + 4)
    chunk, low_tile, high_tile = tables[base], tables[base + 1], tables[base + 2]
    for h in range(heads):
        stack[h * count : (h + 1) * count, :] = q_ref[0, 0, :, h * HD : (h + 1) * HD]
    high[...] = jnp.full_like(high, NEG_FILL)
    total[...] = jnp.zeros_like(total)
    result[...] = jnp.zeros_like(result)
    tokens = chunk * count + lax.broadcasted_iota(jnp.int32, (1, count), 1)
    first = first_ref[0, 0]

    def step(tile, carry):
        @pl.when(tables[base + 4 + tile] != 0)
        def _():
            part = kv_ref[pl.ds(2 * tile, 2), 0].reshape(BLOCK, 2 * HD)
            keys, values = part[:, :HD], part[:, HD:]
            scores = dot_cols(keys, stack[...])
            index = tile * BLOCK + lax.broadcasted_iota(jnp.int32, (BLOCK, count), 0)
            allowed = (index <= tokens) & (index >= first)
            weights, scales = [], []
            for h in range(heads):
                lanes = slice(h * count, (h + 1) * count)
                score = jnp.where(allowed, scores[:, lanes] * (SCALE * LOG2E), NEG_FILL)
                old = high[:, lanes]
                new = jnp.maximum(old, jnp.max(score, axis=0, keepdims=True))
                weight = jnp.exp2(score - new)
                scale = jnp.exp2(old - new)
                high[:, lanes] = new
                total[:, lanes] = total[:, lanes] * scale + jnp.sum(weight, axis=0, keepdims=True)
                weights.append(weight.astype(BF))
                scales.append(scale)
            added = dot_rows(values, jnp.concatenate(weights, axis=1))
            result[...] = result[...] * jnp.concatenate(scales, axis=1) + added

        return carry

    lax.fori_loop(low_tile, high_tile, step, 0)
    final = result[...] / total[...]
    logs = high[...] + jnp.log2(total[...])
    for h in range(heads):
        lanes = slice(h * count, (h + 1) * count)
        out_ref[0, 0, :, h * HD : (h + 1) * HD] = final[:, lanes].T.astype(BF)
        log_ref[0, 0, h : h + 1, :] = logs[:, lanes]


def attend_back_kernel(
    tables,
    q_ref,
    kv_ref,
    first_ref,
    out_ref,
    log_ref,
    grad_ref,
    dq_ref,
    dkv_ref,
    stack,
    grads,
    logs,
    deltas,
    dq_sum,
    dkv_sum,
    *,
    heads,
    blocks,
):
    batch, piece = pl.program_id(0), pl.program_id(1)
    count = q_ref.shape[2]
    base = (batch * pl.num_programs(1) + piece) * (blocks + 4)
    chunk, low_tile, high_tile = tables[base], tables[base + 1], tables[base + 2]

    @pl.when(piece == 0)
    def _():
        dkv_sum[...] = jnp.zeros_like(dkv_sum)

    for h in range(heads):
        rows = slice(h * count, (h + 1) * count)
        cols = slice(h * HD, (h + 1) * HD)
        stack[rows, :] = q_ref[0, 0, :, cols]
        grad = grad_ref[0, 0, :, cols]
        grads[rows, :] = grad
        product = grad.astype(F32) * out_ref[0, 0, :, cols].astype(F32)
        deltas[:, rows] = jnp.sum(product.T, axis=0, keepdims=True)
        logs[:, rows] = log_ref[0, 0, h : h + 1, :]
    dq_sum[...] = jnp.zeros_like(dq_sum)
    tokens = chunk * count + lax.broadcasted_iota(jnp.int32, (1, count), 1)
    first = first_ref[0, 0]

    def step(tile, carry):
        @pl.when(tables[base + 4 + tile] != 0)
        def _():
            part = kv_ref[pl.ds(2 * tile, 2), 0].reshape(BLOCK, 2 * HD)
            keys, values = part[:, :HD], part[:, HD:]
            scores = dot_cols(keys, stack[...])
            pulls = dot_cols(values, grads[...])
            index = tile * BLOCK + lax.broadcasted_iota(jnp.int32, (BLOCK, count), 0)
            allowed = (index <= tokens) & (index >= first)
            weights, score_grads = [], []
            for h in range(heads):
                lanes = slice(h * count, (h + 1) * count)
                score = jnp.where(allowed, scores[:, lanes] * (SCALE * LOG2E), NEG_FILL)
                weight = jnp.exp2(score - logs[:, lanes])
                weights.append(weight.astype(BF))
                score_grads.append((weight * (pulls[:, lanes] - deltas[:, lanes])).astype(BF))
            weight = jnp.concatenate(weights, axis=1)
            score_grad = jnp.concatenate(score_grads, axis=1)
            dv = dot_plain(weight, grads[...])
            dk = dot_plain(score_grad, stack[...])
            dq_sum[...] += dot_rows(keys, score_grad)
            both = jnp.concatenate([dk, dv], axis=1).reshape(2, BLOCK // 2, 2 * HD)
            dkv_sum[pl.ds(2 * tile, 2)] += both

        return carry

    lax.fori_loop(low_tile, high_tile, step, 0)
    for h in range(heads):
        lanes = slice(h * count, (h + 1) * count)
        dq_ref[0, 0, :, h * HD : (h + 1) * HD] = (dq_sum[:, lanes] * SCALE).T.astype(BF)

    @pl.when(piece == pl.num_programs(1) - 1)
    def _():
        dkv_ref[:, 0, :, :HD] = (dkv_sum[:, :, :HD] * SCALE).astype(BF)
        dkv_ref[:, 0, :, HD:] = dkv_sum[:, :, HD:].astype(BF)


def attend(tables, first, queries, key_values, blocks):
    pieces, batches, count, width = queries.shape
    heads = width // HD
    chunks = key_values.shape[0]
    row_spec = pl.BlockSpec((1, 1, count, width), lambda b, i, t: (i, b, 0, 0))
    kv_spec = pl.BlockSpec((chunks, 1, count, 2 * HD), lambda b, i, t: (0, b, 0, 0))
    first_spec = pl.BlockSpec((1, 1, 1, count), lambda b, i, t: (i, b, 0, 0))
    log_spec = pl.BlockSpec((1, 1, heads, count), lambda b, i, t: (i, b, 0, 0))
    rows = heads * count
    return pl.pallas_call(
        functools.partial(attend_kernel, heads=heads, blocks=blocks),
        out_shape=(
            jax.ShapeDtypeStruct(queries.shape, BF),
            jax.ShapeDtypeStruct((pieces, batches, heads, count), F32),
        ),
        grid_spec=pltpu.PrefetchScalarGridSpec(
            num_scalar_prefetch=1,
            grid=(batches, pieces),
            in_specs=[row_spec, kv_spec, first_spec],
            out_specs=[row_spec, log_spec],
            scratch_shapes=[
                pltpu.VMEM((rows, HD), BF),
                pltpu.VMEM((1, rows), F32),
                pltpu.VMEM((1, rows), F32),
                pltpu.VMEM((HD, rows), F32),
            ],
        ),
        compiler_params=pltpu.CompilerParams(vmem_limit_bytes=40 << 20),
        cost_estimate=COST,
        name="attend",
    )(tables, queries, key_values, first)


def attend_back(tables, first, queries, key_values, out, logs, grads, blocks):
    pieces, batches, count, width = queries.shape
    heads = width // HD
    chunks = key_values.shape[0]
    row_spec = pl.BlockSpec((1, 1, count, width), lambda b, i, t: (i, b, 0, 0))
    kv_spec = pl.BlockSpec((chunks, 1, count, 2 * HD), lambda b, i, t: (0, b, 0, 0))
    first_spec = pl.BlockSpec((1, 1, 1, count), lambda b, i, t: (i, b, 0, 0))
    log_spec = pl.BlockSpec((1, 1, heads, count), lambda b, i, t: (i, b, 0, 0))
    rows = heads * count
    return pl.pallas_call(
        functools.partial(attend_back_kernel, heads=heads, blocks=blocks),
        out_shape=(
            jax.ShapeDtypeStruct(queries.shape, BF),
            jax.ShapeDtypeStruct(key_values.shape, BF),
        ),
        grid_spec=pltpu.PrefetchScalarGridSpec(
            num_scalar_prefetch=1,
            grid=(batches, pieces),
            in_specs=[row_spec, kv_spec, first_spec, row_spec, log_spec, row_spec],
            out_specs=[row_spec, kv_spec],
            scratch_shapes=[
                pltpu.VMEM((rows, HD), BF),
                pltpu.VMEM((rows, HD), BF),
                pltpu.VMEM((1, rows), F32),
                pltpu.VMEM((1, rows), F32),
                pltpu.VMEM((HD, rows), F32),
                pltpu.VMEM((chunks, count, 2 * HD), F32),
            ],
        ),
        compiler_params=pltpu.CompilerParams(vmem_limit_bytes=60 << 20),
        cost_estimate=COST,
        name="attend_back",
    )(tables, queries, key_values, first, out, logs, grads)


def neighbours(count):
    s, f = lax.axis_index("seq"), lax.axis_index("fsdp")
    half = count // 2
    at = jnp.where(lax.rem(f, 2) == 0, f // 2, count - 1 - f // 2)

    def owner(step):
        place = lax.rem(at + (step + count), count)
        return jnp.where(place < half, 2 * place, 2 * (count - 1 - place) + 1)

    chip = lax.rem(s + 2, 4)
    core = s + 1 - 2 * lax.rem(s, 2)
    return s, f, owner, (s, owner(1)), (s, owner(-1)), (chip, f), (core, f)


def greet(*devices):
    barrier = pltpu.get_barrier_semaphore()
    for device in devices:
        pl.semaphore_signal(barrier, inc=1, device_id=device, device_id_type=pl.DeviceIdType.MESH)
    pl.semaphore_wait(barrier, len(devices))


def met(device, s, f):
    return (device[0] == s) & (device[1] == f)


def greet_also(devices, sources, own, s, f):
    barrier = pltpu.get_barrier_semaphore()
    for device in devices:
        pl.semaphore_signal(barrier, inc=1, device_id=device, device_id_type=pl.DeviceIdType.MESH)
    for device in sources:

        @pl.when(jnp.logical_not(met(device, s, f)))
        def _():
            pl.semaphore_signal(barrier, inc=1, device_id=device, device_id_type=pl.DeviceIdType.MESH)

    pl.semaphore_wait(barrier, len(devices) + len(sources) - own)


class Maybe:
    def __init__(self, source, target, landing, send_sem, recv_sem, landing_sem, local_sem, device, sender, s, f):
        self.here, self.from_here = met(device, s, f), met(sender, s, f)
        kind = dict(device_id_type=pl.DeviceIdType.MESH)
        self.copy = pltpu.make_async_remote_copy(source, target, send_sem, recv_sem, device_id=device, **kind)
        self.into = pltpu.make_async_remote_copy(source, landing, send_sem, landing_sem, device_id=device, **kind)
        self.stay = pltpu.make_async_copy(source, target, local_sem)

        @pl.when(self.here)
        def _():
            self.stay.start()

        @pl.when(jnp.logical_not(self.here))
        def _():
            self.copy.start()

    def arrived(self):
        @pl.when(jnp.logical_not(self.from_here))
        def _():
            self.into.wait_recv()

    def left(self):
        @pl.when(self.here)
        def _():
            self.stay.wait()

        @pl.when(jnp.logical_not(self.here))
        def _():
            self.copy.wait_send()


def send(source, target, sems, index, device):
    copy = pltpu.make_async_remote_copy(
        src_ref=source,
        dst_ref=target,
        send_sem=sems.at[(0,) + index],
        recv_sem=sems.at[(1,) + index],
        device_id=device,
        device_id_type=pl.DeviceIdType.MESH,
    )
    copy.start()
    return copy


class KernelRing:
    def __init__(self, count, own, slots, sems, owner, up, down):
        self.count, self.own, self.slots, self.sems = count, own, slots, sems
        self.owner, self.up, self.down = owner, up, down
        self.copies = {}

    def start(self, step, given=None):
        half = self.slots.shape[1] // 2
        for way, device in enumerate((self.up, self.down)):
            slot = self.slots.at[self.owner((1 - step) if way == 0 else (step - 1))]
            source = self.own if step == 1 else slot
            if given is not None:
                source = given[way]
            if step == self.count // 2:
                rows = pl.ds(way * half, half)
                source, slot = source.at[rows], slot.at[rows]
            self.copies[way, step] = send(source, slot, self.sems, (way, step - 1), device)

    def arrived(self, step):
        self.copies[0, step].wait_recv()
        self.copies[1, step].wait_recv()

    def finish(self):
        for copy in self.copies.values():
            copy.wait_send()


def opening_kernel(
    hidden,
    kv_own,
    qkv_weight,
    proj_weight,
    fc_weight,
    cot,
    hidden_out,
    kvw_out,
    qw_out,
    proj_out,
    kv_out,
    fc_out,
    cot_out,
    weights,
    mine,
    q_own,
    fc_own,
    hid_chip,
    hid_core,
    kvw_sems,
    q_sems,
    proj_sems,
    kv_sems,
    kv_chip,
    kv_core,
    kv_far,
    fc_sems,
    cot_sems,
    move_sems,
    cut_sems,
    local,
    *,
    count,
    shard,
):
    s, f, owner, up, down, chip, core = neighbours(count)
    steps = count // 2
    per = count // 4
    target = (f // per, 4 * lax.rem(f, per) + s)
    source = (lax.rem(f, 4), s * per + f // 4)
    own_goes = met(target, s, f).astype(jnp.int32)
    greet_also((up, down, chip, core), (source,), own_goes, s, f)
    part = proj_out.shape[1]
    q_cols = qw_out.shape[2]
    q_cut = pltpu.make_async_copy(
        qkv_weight.at[:, pl.ds(pl.multiple_of(s * q_cols, q_cols), q_cols)], q_own, local.at[4]
    )
    q_cut.start()
    proj_own = proj_out.at[f]
    rings = [
        KernelRing(count, own, slots, sems, owner, up, down)
        for own, slots, sems in (
            (kv_own, kvw_out, kvw_sems),
            (q_own, qw_out, q_sems),
            (proj_own, proj_out, proj_sems),
            (fc_own, fc_out, fc_sems),
        )
    ]
    kvw, qw, proj, fc = rings
    kvw.start(1)
    moved = Maybe(
        proj_weight.at[pl.ds(pl.multiple_of(s * part, part), part)],
        proj_out.at[target[1]],
        proj_own,
        move_sems.at[0],
        move_sems.at[1],
        move_sems.at[1],
        move_sems.at[2],
        target,
        source,
        s,
        f,
    )
    if fc_weight.shape[1] == fc_out.shape[2]:
        cuts = [pltpu.make_async_copy(fc_weight, fc_own, cut_sems.at[0])]
    else:
        cols = fc_out.shape[2] // count
        cuts = [
            pltpu.make_async_copy(
                fc_weight.at[:, pl.ds(pl.multiple_of((g * 4 + s) * cols, cols), cols)],
                fc_own.at[:, pl.ds(g * cols, cols)],
                cut_sems.at[g],
            )
            for g in range(count)
        ]
    for copy in cuts:
        copy.start()
    rows = hidden.shape[0] // 2
    halves = [pl.ds(i * rows, rows) for i in range(2)]
    across = [send(hidden.at[half], hidden_out.at[2, half], hid_chip, (i,), chip) for i, half in enumerate(halves)]
    pair = [send(hidden, hidden_out.at[1], hid_core, (2,), core)]
    stays = [
        pltpu.make_async_copy(source, target, local.at[i])
        for i, (source, target) in enumerate(
            (
                (hidden, hidden_out.at[0]),
                (kv_own, kvw_out.at[f]),
                (cot, cot_out.at[0]),
            )
        )
    ]
    for copy in stays:
        copy.start()
    q_cut.wait()
    for copy in cuts:
        copy.wait()
    for i, (source, target) in enumerate(((q_own, qw_out.at[f]), (fc_own, fc_out.at[f]))):
        stays.append(pltpu.make_async_copy(source, target, local.at[3 if i == 0 else 5]))
        stays[-1].start()
    values = hidden[...].astype(F32)
    mean = jnp.mean(values, axis=-1, keepdims=True)
    center = values - mean
    inverse = lax.rsqrt(jnp.mean(center * center, axis=-1, keepdims=True) + EPS)
    for step in range(2, steps + 1):
        kvw.arrived(step - 1)
        kvw.start(step)
    qw.start(1)
    fc.start(1)
    kvw.arrived(steps)
    stays[1].wait()
    load = pltpu.make_async_copy(kvw_out, weights, local.at[6])
    load.start()
    load.wait()
    total = jnp.zeros((hidden.shape[0], kvw_out.shape[2]), F32)
    for t in range(count):
        cols = slice(t * shard, (t + 1) * shard)
        normed = (hidden[:, cols].astype(F32) - mean) * inverse
        gain = weights[t, shard : shard + 1, :shard].astype(F32)
        bias = weights[t, shard + 1 : shard + 2, :shard].astype(F32)
        total += dot_plain((normed * gain + bias).astype(BF), weights[t, :shard, :])
    mine[...] = total.astype(BF)

    spread = KernelRing(count, mine, kv_out.at[s], kv_sems, owner, up, down)
    spread.start(1)
    keep = pltpu.make_async_copy(mine, kv_out.at[s, f], local.at[7])
    keep.start()
    kv_across, kv_pair = [], []

    def pass_on(source, place):
        index = (len(kv_across),)
        kv_across.append((place, send(source, kv_out.at[s, place], kv_chip, index, chip)))
        kv_pair.append(send(source, kv_out.at[s, place], kv_core, index, core))

    pass_on(mine, f)
    for i, half in enumerate(halves):
        across[i].wait_recv()
        pair.append(send(hidden_out.at[2, half], hidden_out.at[2 + 1, half], hid_core, (i,), core))
    for step in range(1, steps + 1):
        spread.arrived(step)
        qw.arrived(step)
        if step < steps:
            spread.start(step + 1)
            qw.start(step + 1)
            for place in (owner(-step), owner(step)):
                pass_on(kv_out.at[s, place], place)
        else:
            pass_on(kv_out.at[s, owner(steps)], owner(steps))
        if step == 1:
            moved.arrived()
            moved.left()
            proj.start(1)
            cot_across = send(cot, cot_out.at[2], cot_sems, (0,), chip)
            cot_pair = send(cot, cot_out.at[1], cot_sems, (1,), core)
        else:
            proj.arrived(step - 1)
            proj.start(step)
        fc.arrived(step)
        if step < steps:
            fc.start(step + 1)
    other = lax.rem(s + 2, 4)
    far = []
    for i, (place, copy) in enumerate(kv_across):
        copy.wait_recv()
        slot = kv_out.at[other, place]
        far.append(send(slot, slot, kv_far, (i,), core))
    cot_across.wait()
    cot_far = send(cot_out.at[2], cot_out.at[3], cot_sems, (2,), core)
    proj.arrived(steps)
    for ring in rings + [spread]:
        ring.finish()
    for copy in [keep, cot_pair, cot_far, stays[0]] + stays[2:]:
        copy.wait()
    for copy in across + [copy for _, copy in kv_across]:
        copy.wait_send()
    for copy in pair + kv_pair + far:
        copy.wait()


def opening(hidden, kv_own, qkv_weight, proj_weight, fc_weight, cot, fsdp_count, q_cols):
    count, width = hidden.shape
    shard = qkv_weight.shape[0]
    dma = pltpu.SemaphoreType.DMA
    ring = dma((2, 2, fsdp_count // 2))
    anywhere = pl.BlockSpec(memory_space=pltpu.HBM)
    inside = pl.BlockSpec(memory_space=pltpu.VMEM)
    return pl.pallas_call(
        functools.partial(opening_kernel, count=fsdp_count, shard=shard),
        out_shape=(
            jax.ShapeDtypeStruct((4,) + hidden.shape, BF),
            jax.ShapeDtypeStruct((fsdp_count,) + kv_own.shape, BF),
            jax.ShapeDtypeStruct((fsdp_count, shard, q_cols), BF),
            jax.ShapeDtypeStruct((fsdp_count, shard // 4, width), BF),
            jax.ShapeDtypeStruct((4, fsdp_count, count, 2 * HD), BF),
            jax.ShapeDtypeStruct((fsdp_count, shard, width), BF),
            jax.ShapeDtypeStruct((4,) + hidden.shape, BF),
        ),
        in_specs=[inside, inside] + [anywhere] * 3 + [inside],
        out_specs=(anywhere,) * 7,
        scratch_shapes=[
            pltpu.VMEM((fsdp_count,) + kv_own.shape, BF),
            pltpu.VMEM((count, 2 * HD), BF),
            pltpu.VMEM((shard, q_cols), BF),
            pltpu.VMEM((shard, width), BF),
            dma((2, 2)),
            dma((2, 3)),
            ring,
            ring,
            ring,
            ring,
            dma((2, fsdp_count)),
            dma((2, fsdp_count)),
            dma((2, fsdp_count)),
            ring,
            dma((2, 3)),
            dma((3,)),
            dma((fsdp_count,)),
            dma((8,)),
        ],
        compiler_params=pltpu.CompilerParams(
            collective_id=1, has_side_effects=True, vmem_limit_bytes=40 << 20
        ),
        cost_estimate=COST,
        name="opening",
    )(hidden, kv_own, qkv_weight, proj_weight, fc_weight, cot)


GELU_A = math.sqrt(2 / math.pi)
GELU_B = 0.044715


def middle_kernel(rows_ref, cot_ref, fc_ref, down_ref, activ_ref, pre_ref, grad_ref, total, *, step):
    tile = pl.program_id(0)
    fc = fc_ref[...].reshape(-1, fc_ref.shape[2])
    down = down_ref[...].reshape(-1, down_ref.shape[2])

    @pl.when(tile == 0)
    def _():
        total[...] = jnp.zeros_like(total)

    for at in range(0, rows_ref.shape[0], step):
        part = slice(at, at + step)
        value = dot_plain(rows_ref[part], fc)
        pull = dot_cols(cot_ref[part], down)
        square = value * value
        bend = jnp.tanh(GELU_A * value * (1.0 + GELU_B * square))
        half = 0.5 * (1.0 + bend)
        activ_ref[part] = (value * half).astype(BF)
        slope = half + 0.5 * value * (1.0 - bend * bend) * (GELU_A * (1.0 + 3.0 * GELU_B * square))
        grad = (pull * slope).astype(BF)
        pre_ref[part] = grad
        total[part] += dot_cols(grad, fc)

    @pl.when(tile == pl.num_programs(0) - 1)
    def _():
        grad_ref[...] = total[...].astype(BF)


def middle(rows, cot, fc_all, down_all, tile):
    count, width = rows.shape
    parts, shard = fc_all.shape[:2]
    quarter = down_all.shape[1]
    hidden = parts * quarter
    per = tile // quarter
    whole = pl.BlockSpec((count, width), lambda n: (0, 0), pipeline_mode=pl.Buffered(1))
    cols = pl.BlockSpec((count, tile), lambda n: (0, n))
    return pl.pallas_call(
        functools.partial(middle_kernel, step=256),
        out_shape=(
            jax.ShapeDtypeStruct((count, hidden), BF),
            jax.ShapeDtypeStruct((count, hidden), BF),
            jax.ShapeDtypeStruct((count, width), BF),
        ),
        grid=(hidden // tile,),
        in_specs=[
            whole,
            whole,
            pl.BlockSpec((parts, shard, tile), lambda n: (0, 0, n)),
            pl.BlockSpec((per, quarter, width), lambda n: (n, 0, 0)),
        ],
        out_specs=(cols, cols, pl.BlockSpec((count, width), lambda n: (0, 0))),
        scratch_shapes=[pltpu.VMEM((count, width), F32)],
        compiler_params=pltpu.CompilerParams(vmem_limit_bytes=60 << 20),
        cost_estimate=COST,
        name="middle",
    )(rows, cot, fc_all, down_all)


def bridge_kernel(
    heads,
    proj,
    hidden,
    vectors,
    down_own,
    first_up,
    first_down,
    mlp_out,
    resid_out,
    down_out,
    far_out,
    far,
    near_out,
    near,
    chip_in,
    mine,
    pair_sems,
    chip_sems,
    spread_chip,
    spread_core,
    down_sems,
    local,
    *,
    count,
):
    s, f, owner, up, down, chip, core = neighbours(count)
    greet(up, down, chip, core)
    steps = count // 2
    tokens = hidden.shape[0]
    ring = KernelRing(count, down_own, down_out, down_sems, owner, up, down)
    ring.start(2, (first_up, first_down))
    stays = [
        pltpu.make_async_copy(down_own, down_out.at[f], local.at[0]),
        pltpu.make_async_copy(first_up, down_out.at[owner(-1)], local.at[2]),
        pltpu.make_async_copy(first_down, down_out.at[owner(1)], local.at[3]),
    ]
    for copy in stays:
        copy.start()

    def part(i):
        return dot_plain(heads[i * tokens : (i + 1) * tokens], proj[...])

    far_out[...] = part(3).astype(BF)
    pairs = [send(far_out, far, pair_sems, (0,), core)]
    near_out[...] = part(1).astype(BF)
    pairs.append(send(near_out, near, pair_sems, (1,), core))
    middle = part(2)
    pairs[0].wait()
    far_out[...] = (middle + far[...].astype(F32)).astype(BF)
    rows = tokens // 2
    halves = [pl.ds(i * rows, rows) for i in range(2)]
    across = [send(far_out.at[half], chip_in.at[half], chip_sems, (i,), chip) for i, half in enumerate(halves)]
    resid_out[...] = hidden[...].astype(F32) + part(0)
    pairs[1].wait()
    resid_out[...] += near[...].astype(F32)
    spread, spread_pair = [], []
    block = 64
    for i, half in enumerate(halves):
        across[i].wait_recv()
        for at in range(i * rows, (i + 1) * rows, block):
            here = slice(at, at + block)
            resid = resid_out[here] + chip_in[here].astype(F32)
            resid_out[here] = resid
            normed, _ = layer_norm(resid)
            mine[here] = (normed * vectors[0:1] + vectors[1:2]).astype(BF)
        spread.append(send(mine.at[half], mlp_out.at[2, half], spread_chip, (i,), chip))
        spread_pair.append(send(mine.at[half], mlp_out.at[1, half], spread_core, (i,), core))
        ring.arrived(i + 2)
        ring.start(i + 3)
    stays.append(pltpu.make_async_copy(mine, mlp_out.at[0], local.at[1]))
    stays[-1].start()
    for i, half in enumerate(halves):
        spread[i].wait_recv()
        spread_pair.append(send(mlp_out.at[2, half], mlp_out.at[3, half], spread_core, (2 + i,), core))
    for step in range(4, steps + 1):
        ring.arrived(step)
        if step < steps:
            ring.start(step + 1)
    ring.finish()
    for copy in across + spread:
        copy.wait_send()
    for copy in spread_pair + stays:
        copy.wait()


def bridge(heads, proj, hidden, vectors, down_own, first, fsdp_count):
    tokens, width = hidden.shape
    quarter = down_own.shape[0]
    dma = pltpu.SemaphoreType.DMA
    anywhere = pl.BlockSpec(memory_space=pltpu.HBM)
    inside = pl.BlockSpec(memory_space=pltpu.VMEM)
    wide = pltpu.VMEM((tokens, width), BF)
    return pl.pallas_call(
        functools.partial(bridge_kernel, count=fsdp_count),
        out_shape=(
            jax.ShapeDtypeStruct((4, tokens, width), BF),
            jax.ShapeDtypeStruct((tokens, width), F32),
            jax.ShapeDtypeStruct((fsdp_count, quarter, width), BF),
        ),
        in_specs=[inside] * 7,
        out_specs=(anywhere, inside, anywhere),
        scratch_shapes=[wide] * 6
        + [
            dma((2, 2)),
            dma((2, 2)),
            dma((2, 2)),
            dma((2, 4)),
            dma((2, 2, fsdp_count // 2)),
            dma((4,)),
        ],
        compiler_params=pltpu.CompilerParams(
            collective_id=3, has_side_effects=True, vmem_limit_bytes=40 << 20
        ),
        cost_estimate=COST,
        name="bridge",
    )(heads, proj, hidden, vectors, down_own, *first)


def feedback_kernel(
    parts,
    mlp_in,
    pre_grad,
    activ,
    cot,
    down_all,
    resid,
    gain,
    branch_out,
    result_out,
    resid_out,
    vectors_out,
    up_out,
    down_out,
    rest_out,
    mlp_here,
    pre_here,
    activ_here,
    cot_here,
    here,
    across_out,
    far,
    near,
    chip_in,
    branch,
    outs_first,
    ins_first,
    outs_next,
    ins_next,
    stage,
    down_here,
    low_here,
    low_far,
    low_near,
    low_chip,
    branch_low,
    pair_sems,
    chip_sems,
    spread_chip,
    spread_core,
    ring_sems,
    low_pair,
    low_across,
    local,
    *,
    count,
    shard,
    turned,
):
    s, f, owner, up, down, chip, core = neighbours(count)
    greet(up, down, chip, core)
    steps = count // 2
    tokens, width = resid.shape
    pairs = [send(parts.at[3], far, pair_sems, (0,), core), send(parts.at[1], near, pair_sems, (1,), core)]
    loads = [
        pltpu.make_async_copy(source, target, local.at[i])
        for i, (source, target) in enumerate(
            (
                (pre_grad, pre_here),
                (mlp_in, mlp_here),
                (parts.at[2], across_out),
                (cot, cot_here),
                (activ, activ_here),
                (parts.at[0], here),
            )
        )
    ]
    for copy in loads:
        copy.start()

    def product(left, right, place, out):
        start = pl.multiple_of(place * shard, shard)
        chosen = left[:, pl.ds(start, shard)] if turned else left[pl.ds(start, shard), :]
        for at in range(0, width, 512):
            cols = slice(at, at + 512)
            value = dot_rows(chosen, right[:, cols]) if turned else dot_plain(chosen, right[:, cols])
            out[:, cols] = value.astype(BF)

    def chunk(place, out):
        product(mlp_here, pre_here, place, out.at[pl.ds(0, shard)])
        product(activ_here, cot_here, place, out.at[pl.ds(shard, shard)])

    def low_part(j, down):
        lines = slice(j * tokens, (j + 1) * tokens)
        return dot_plain(activ_here[lines], down) if turned else dot_rows(activ_here[:, lines], down)

    upper, under = pl.ds(0, shard), pl.ds(shard, shard)
    devices = (up, down)
    side = width // 2
    sides = [
        pltpu.make_async_copy(down_all.at[:, :, pl.ds(i * side, side)], down_here, local.at[10 + i])
        for i in range(2)
    ]
    sides[0].start()
    loads[0].wait()
    loads[1].wait()
    product(mlp_here, pre_here, owner(steps), outs_first.at[upper])
    first = [send(outs_first.at[upper], ins_first.at[upper], ring_sems, (0, 0), up)]
    loads[2].wait()
    pairs[0].wait_recv()
    across_out[...] = (across_out[...].astype(F32) + far[...].astype(F32)).astype(BF)
    rows = tokens // 2
    halves = [pl.ds(i * rows, rows) for i in range(2)]
    across = [send(across_out.at[half], chip_in.at[half], chip_sems, (i,), chip) for i, half in enumerate(halves)]
    loads[3].wait()
    loads[4].wait()
    product(activ_here, cot_here, owner(steps), outs_first.at[under])
    first.append(send(outs_first.at[under], ins_first.at[under], ring_sems, (1, 0), down))
    chunk(owner(steps - 1), outs_next.at[0])
    chunk(owner(1 - steps), outs_next.at[1])
    second = []
    for way, part in enumerate((upper, under)):
        first[way].wait_recv()
        out = outs_next.at[way]
        out[part] = (out[part].astype(F32) + ins_first[part].astype(F32)).astype(BF)
        second.append(send(out, ins_next.at[way], ring_sems, (way, 1), devices[way]))

    loads[5].wait()
    pairs[1].wait_recv()
    gain_grad = jnp.zeros((1, width), F32)
    bias_grad = jnp.zeros((1, width), F32)
    spread, spread_pair = [], []
    block = 64
    for i, half in enumerate(halves):
        across[i].wait_recv()
        for at in range(i * rows, (i + 1) * rows, block):
            part = slice(at, at + block)
            grad = here[part].astype(F32) + near[part].astype(F32) + chip_in[part].astype(F32)
            normed, inverse = layer_norm(resid[part])
            gain_grad += jnp.sum(grad * normed, axis=0, keepdims=True)
            bias_grad += jnp.sum(grad, axis=0, keepdims=True)
            value = cot_here[part].astype(F32) + norm_back(grad * gain[...], normed, inverse)
            resid_out[part] = value
            branch[part] = value.astype(BF)
        spread.append(send(branch.at[half], branch_out.at[2, half], spread_chip, (i,), chip))
        spread_pair.append(send(branch.at[half], branch_out.at[1, half], spread_core, (i,), core))
    vectors_out[0:1] = gain_grad
    vectors_out[1:2] = bias_grad
    keep = pltpu.make_async_copy(branch, branch_out.at[0], local.at[6])
    keep.start()

    for copy in across:
        copy.wait_send()
    lows = (low_here, here, across_out, branch_low)
    for i in range(2):
        cols = pl.ds(i * side, side)
        sides[i].wait()
        down = down_here[...].reshape(-1, side)
        for j in (3, 1, 2, 0):
            value = low_part(j, down)
            lows[j][:, cols] = value if j == 0 else value.astype(BF)
        if i == 0:
            sides[1].start()
    low_sends = [send(lows[3], low_far, low_pair, (0,), core), send(lows[1], low_near, low_pair, (1,), core)]
    low_sends[0].wait()
    across_out[...] = (across_out[...].astype(F32) + low_far[...].astype(F32)).astype(BF)
    low_chip_copy = send(across_out, low_chip, low_across, (0,), chip)

    def rest(i, carry):
        back = lax.rem(i + 1, 2)
        n = (steps - (i + 1) // 2) * (1 - 2 * back)
        chunk(owner(n), stage)
        copy = pltpu.make_async_copy(stage, rest_out.at[i - 5], local.at[7])
        copy.start()
        copy.wait()
        return carry

    lax.fori_loop(5, count, rest, 0)
    for i, half in enumerate(halves):
        spread[i].wait_recv()
        spread_pair.append(send(branch_out.at[2, half], branch_out.at[3, half], spread_core, (2 + i,), core))
    leaving = []
    low_sends[1].wait()
    low_chip_copy.wait()
    for at in range(0, tokens, block):
        part = slice(at, at + block)
        value = resid[part] + low_here[part] + low_near[part].astype(F32) + low_chip[part].astype(F32)
        result_out[part] = value.astype(BF)
    for way, target in enumerate((up_out, down_out)):
        out = stage if way == 0 else outs_first
        if way:
            first[0].wait_send()
            first[1].wait_send()
        chunk(owner((steps - 2) * (1 - 2 * way)), out)
        second[way].wait_recv()
        out[...] = (out[...].astype(F32) + ins_next[way].astype(F32)).astype(BF)
        leaving.append(pltpu.make_async_copy(out, target, local.at[8 + way]))
        leaving[way].start()
    for copy in pairs + spread + second:
        copy.wait_send()
    for copy in spread_pair + leaving + [keep]:
        copy.wait()


def feedback(parts, mlp_in, pre_grad, activ, cot, down_all, resid, gain, fsdp_count, shard):
    tokens, width = resid.shape
    turned = shard % 128 == 0
    if not turned:
        mlp_in, activ = mlp_in.T, activ.T
    dma = pltpu.SemaphoreType.DMA
    anywhere = pl.BlockSpec(memory_space=pltpu.HBM)
    inside = pl.BlockSpec(memory_space=pltpu.VMEM)
    wide = pltpu.VMEM((tokens, width), BF)
    both = pltpu.VMEM((2 * shard, width), BF)
    quarter = down_all.shape[1]
    flow = jax.ShapeDtypeStruct((2 * shard, width), BF)
    return pl.pallas_call(
        functools.partial(feedback_kernel, count=fsdp_count, shard=shard, turned=turned),
        out_shape=(
            jax.ShapeDtypeStruct((4, tokens, width), BF),
            jax.ShapeDtypeStruct((tokens, width), BF),
            jax.ShapeDtypeStruct((tokens, width), F32),
            jax.ShapeDtypeStruct((2, width), F32),
            flow,
            flow,
            jax.ShapeDtypeStruct((fsdp_count - 5, 2 * shard, width), BF),
        ),
        in_specs=[anywhere] * 6 + [inside] * 2,
        out_specs=(anywhere, inside, inside, inside, anywhere, anywhere, anywhere),
        scratch_shapes=[pltpu.VMEM(value.shape, BF) for value in (mlp_in, pre_grad, activ, cot)]
        + [wide] * 6
        + [
            both,
            both,
            pltpu.VMEM((2, 2 * shard, width), BF),
            pltpu.VMEM((2, 2 * shard, width), BF),
            both,
            pltpu.VMEM((fsdp_count, quarter, width // 2), BF),
            pltpu.VMEM((tokens, width), F32),
            wide,
            wide,
            wide,
            wide,
            dma((2, 2)),
            dma((2, 2)),
            dma((2, 2)),
            dma((2, 4)),
            dma((2, 2, 2)),
            dma((2, 2)),
            dma((2, 1)),
            dma((12,)),
        ],
        compiler_params=pltpu.CompilerParams(
            collective_id=4, has_side_effects=True, vmem_limit_bytes=61 << 20
        ),
        cost_estimate=COST,
        name="feedback",
    )(parts, mlp_in, pre_grad, activ, cot, down_all, resid, gain)


class KernelScatter:
    def __init__(self, count, chunk, outs, ins, sems, up, down):
        self.steps, self.chunk, self.outs, self.ins, self.sems = count // 2, chunk, outs, ins, sems
        self.devices = (up, down)
        self.half = outs.shape[2] // 2
        self.copies = {}

    def start(self, step):
        half = self.half
        for way, sign in ((0, 1), (1, -1)):
            mine = self.chunk(sign * (self.steps - step))
            if step > 1:
                self.copies[way, step - 2].wait_send()
            out, into = self.outs.at[way, step % 2], self.ins.at[way, step]
            rows = slice(way * half, (way + 1) * half)
            rest = slice((1 - way) * half, (2 - way) * half)
            if step == 0:
                out, into = out.at[pl.ds(0, half)], into.at[pl.ds(0, half)]
                out[...] = mine[rows].astype(BF)
            elif step == 1:
                out[rows] = (mine[rows] + self.ins[way, 0, :half].astype(F32)).astype(BF)
                out[rest] = mine[rest].astype(BF)
            else:
                out[...] = (mine + self.ins[way, step - 1].astype(F32)).astype(BF)
            self.copies[way, step] = send(out, into, self.sems, (way, step), self.devices[way])

    def arrived(self, step):
        self.copies[0, step].wait_recv()
        self.copies[1, step].wait_recv()

    def total(self):
        last = self.steps - 1
        return self.chunk(0) + self.ins[0, last].astype(F32) + self.ins[1, last].astype(F32)

    def finish(self):
        for (_, step), copy in self.copies.items():
            if step >= self.steps - 2:
                copy.wait_send()


def closing_kernel(
    kv_parts,
    query_rows,
    q_weight,
    attn_parts,
    ff_up,
    ff_down,
    ff_rest,
    resid_grad,
    hidden,
    kv_weight,
    attn_in,
    mlp_vectors,
    grad_out,
    q_out,
    proj_out,
    ff_out,
    tail_out,
    kv_here,
    kv_near,
    kv_far,
    kv_chip_in,
    kv_outs,
    kv_ins,
    q_far_out,
    q_far,
    q_near,
    q_chip_in,
    q_here,
    attn_here,
    attn_own,
    proj_here,
    attn_outs,
    attn_ins,
    ff_here,
    ff_ins,
    ff_sum,
    kv_total,
    tail_here,
    tail_outs,
    tail_ins,
    swap_out,
    swap_in,
    local,
    kv_core_sems,
    kv_chip_sems,
    kv_sems,
    q_core_sems,
    q_chip_sems,
    attn_sems,
    ff_sems,
    ff_chip_sems,
    ff_core_sems,
    tail_sems,
    swap_sems,
    q_spread_sems,
    proj_spread_sems,
    move_sems,
    *,
    count,
    shard,
):
    s, f, owner, up, down, chip, core = neighbours(count)
    steps = count // 2
    order = [steps] + [sign * n for n in range(steps - 1, 0, -1) for sign in (1, -1)] + [0]
    other, sibling = lax.rem(s + 2, 4), core[0]
    far = lax.rem(sibling + 2, 4)
    tokens = hidden.shape[0]
    per = count // 4
    target = (lax.rem(f, 4), s * per + f // 4)
    source = (f // per, 4 * lax.rem(f, per) + s)
    greet_also((up, down, chip, core), (source,), met(target, s, f).astype(jnp.int32), s, f)

    kv_pair = [
        send(kv_parts.at[far], kv_far, kv_core_sems, (0,), core),
        send(kv_parts.at[sibling], kv_near, kv_core_sems, (1,), core),
    ]
    loads = [
        pltpu.make_async_copy(kv_parts.at[other], kv_here.at[1], local.at[0]),
        pltpu.make_async_copy(kv_parts.at[s], kv_here.at[0], local.at[1]),
        pltpu.make_async_copy(attn_parts, attn_here, local.at[2]),
        pltpu.make_async_copy(ff_rest.at[ff_rest.shape[0] - 1], ff_here, local.at[3]),
    ]
    for copy in loads:
        copy.start()
    ff_rows = ff_here.shape[0] // 2
    ff_parts = [pl.ds(i * ff_rows, ff_rows) for i in range(2)]
    ff_ring = []

    def ff_start(i):
        for way, (source, device) in enumerate(((ff_up, up), (ff_down, down))):
            copy = send(source.at[ff_parts[i]], ff_ins.at[way, ff_parts[i]], ff_sems, (way, i), device)
            ff_ring.append(copy)

    ff_start(0)

    def query_part(i):
        return dot_cols(query_rows[i * tokens : (i + 1) * tokens], q_weight[...])

    q_far_out[...] = query_part(3).astype(BF)
    q_pair = [send(q_far_out, q_far, q_core_sems, (0,), core)]
    grad_out[...] = query_part(1).astype(BF)
    loads[0].wait()
    kv_pair[0].wait_recv()
    kv_across = {}
    for i, n in enumerate(order):
        place = owner(n)
        kv_here[1, place] = (kv_here[1, place].astype(F32) + kv_far[place].astype(F32)).astype(BF)
        kv_across[n] = send(kv_here.at[1, place], kv_chip_in.at[i], kv_chip_sems, (i,), chip)
    part = query_part(2)
    q_pair[0].wait()
    q_chip_out = q_far_out
    q_chip_out[...] = (part + q_far[...].astype(F32)).astype(BF)
    rows = tokens // 2
    q_halves = [pl.ds(i * rows, rows) for i in range(2)]
    q_across = [
        send(q_chip_out.at[half], q_chip_in.at[half], q_chip_sems, (i,), chip) for i, half in enumerate(q_halves)
    ]
    q_pair.append(send(grad_out, q_near, q_core_sems, (1,), core))
    q_here[...] = query_part(0)
    loads[1].wait()
    kv_pair[1].wait_recv()

    def kv_chunk(n):
        n = steps if n == -steps else n
        place = owner(n)
        here = kv_here[0, place].astype(F32) + kv_near[place].astype(F32)
        return here + kv_chip_in[order.index(n)].astype(F32)

    loads[2].wait()

    def attn_chunk(n):
        return attn_here[order.index(steps if n == -steps else n)].astype(F32)

    kv = KernelScatter(count, kv_chunk, kv_outs, kv_ins, kv_sems, up, down)
    attn = KernelScatter(count, attn_chunk, attn_outs, attn_ins, attn_sems, up, down)
    for step in range(steps):
        for n in (steps - step, step - steps):
            if n in order:
                kv_across[n].wait_recv()
        if step:
            kv.arrived(step - 1)
        kv.start(step)
        if step:
            attn.arrived(step - 1)
        attn.start(step)
    ff_start(1)

    loads[3].wait()
    ff_pair, ff_across = [], []

    def ff_close(i):
        rows = ff_parts[i]
        for copy in ff_ring[2 * i : 2 * i + 2]:
            copy.wait_recv()
        arrived = ff_ins[0, rows].astype(F32) + ff_ins[1, rows].astype(F32)
        ff_sum[rows] = (ff_here[rows].astype(F32) + arrived).astype(BF)
        ff_across.append(send(ff_sum.at[rows], ff_out.at[2, rows], ff_chip_sems, (i,), chip))
        ff_pair.append(send(ff_sum.at[rows], ff_out.at[1, rows], ff_core_sems, (i,), core))

    ff_close(0)
    kv_across[0].wait_recv()
    kv.arrived(steps - 1)
    kv_total[...] = kv.total().astype(BF)

    attn.arrived(steps - 1)
    attn_own[...] = attn.total().astype(BF)
    part = proj_out.shape[1]
    lines = pl.ds(part, attn_own.shape[0] - part)
    q_lines = attn_own.at[lines]
    q_spread = [
        send(q_lines, q_out.at[2], q_spread_sems, (0,), chip),
        send(q_lines, q_out.at[1], q_spread_sems, (1,), core),
    ]
    q_keep = pltpu.make_async_copy(q_lines, q_out.at[0], local.at[5])
    q_keep.start()
    moved = Maybe(
        attn_own.at[pl.ds(0, part)],
        proj_here,
        proj_here,
        move_sems.at[0],
        move_sems.at[1],
        move_sems.at[1],
        move_sems.at[2],
        target,
        source,
        s,
        f,
    )

    q_pair[1].wait()
    for copy in q_across:
        copy.wait_recv()
    q_here[...] += q_near[...].astype(F32) + q_chip_in[...].astype(F32)
    for t in range(count):
        cols = slice(t * shard, (t + 1) * shard)
        q_here[:, cols] += dot_cols(kv_total[...], kv_weight[t, :shard, :])
    gain = jnp.concatenate([kv_weight[t, shard : shard + 1, :shard] for t in range(count)], axis=1).astype(F32)
    block = 64
    gain_grad = jnp.zeros((1, hidden.shape[1]), F32)
    bias_grad = jnp.zeros((1, hidden.shape[1]), F32)
    for at in range(0, tokens, block):
        here = slice(at, at + block)
        normed, inverse = layer_norm(hidden[here].astype(F32))
        grad = q_here[here]
        gain_grad += jnp.sum(grad * normed, axis=0, keepdims=True)
        bias_grad += jnp.sum(grad, axis=0, keepdims=True)
        grad_out[here] = (resid_grad[here] + norm_back(grad * gain, normed, inverse)).astype(BF)

    tail_here[...] = jnp.zeros_like(tail_here)
    vectors = (gain_grad, bias_grad, mlp_vectors[0:1], mlp_vectors[1:2])
    for t in range(count):
        cols = slice(t * shard, (t + 1) * shard)
        tail_here[t, :shard, :] = dot_rows(attn_in[:, cols], kv_total[...])
        for j, vector in enumerate(vectors):
            tail_here[t, shard + j : shard + j + 1, :shard] = vector[:, cols]
    tail = KernelScatter(count, lambda n: tail_here[owner(n)], tail_outs, tail_ins, tail_sems, up, down)
    for step in range(steps):
        if step:
            tail.arrived(step - 1)
        tail.start(step)
        if step == 0:
            ff_close(1)
            q_spread[0].wait_recv()
            q_spread.append(send(q_out.at[2], q_out.at[3], q_spread_sems, (2,), core))
            moved.arrived()
            moved.left()
            proj_spread = [
                send(proj_here, proj_out.at[2], proj_spread_sems, (0,), chip),
                send(proj_here, proj_out.at[1], proj_spread_sems, (1,), core),
            ]
            proj_keep = pltpu.make_async_copy(proj_here, proj_out.at[0], local.at[6])
            proj_keep.start()
    proj_spread[0].wait_recv()
    proj_spread.append(send(proj_out.at[2], proj_out.at[3], proj_spread_sems, (2,), core))
    tail.arrived(steps - 1)
    total = tail.total()
    swap_out[0] = total.astype(BF)
    swaps = [send(swap_out.at[0], swap_in.at[0], swap_sems, (0,), core)]
    for i, rows in enumerate(ff_parts):
        ff_across[i].wait_recv()
        ff_pair.append(send(ff_out.at[2, rows], ff_out.at[3, rows], ff_core_sems, (2 + i,), core))
    keep = pltpu.make_async_copy(ff_sum, ff_out.at[0], local.at[4])
    keep.start()
    swaps[0].wait_recv()
    swap_out[1] = (swap_out[0].astype(F32) + swap_in[0].astype(F32)).astype(BF)
    swaps.append(send(swap_out.at[1], swap_in.at[1], swap_sems, (1,), chip))
    swaps[1].wait_recv()
    tail_out[...] = swap_out[1].astype(F32) + swap_in[1].astype(F32)
    keep.wait()
    q_keep.wait()
    proj_keep.wait()
    q_spread[0].wait_send()
    proj_spread[0].wait_send()
    for copy in q_spread[1:] + proj_spread[1:]:
        copy.wait()
    for ring in (kv, attn, tail):
        ring.finish()
    for copy in kv_pair + q_across + list(kv_across.values()) + ff_ring + ff_across + swaps:
        copy.wait_send()
    for copy in ff_pair:
        copy.wait()


def closing(kv_parts, query_rows, q_weight, attn_parts, ff_flow, resid_grad, hidden, kv_weight, attn_in, mlp_vectors, shard):
    ff_up, ff_down, ff_rest = ff_flow
    fsdp_count, tokens, kv_cols = kv_parts.shape[1:]
    width = hidden.shape[1]
    steps = fsdp_count // 2
    dma = pltpu.SemaphoreType.DMA
    anywhere = pl.BlockSpec(memory_space=pltpu.HBM)
    inside = pl.BlockSpec(memory_space=pltpu.VMEM)
    attn_shape = attn_parts.shape[1:]
    part = shard // 4
    tail_shape = kv_weight.shape[1:]
    wide = pltpu.VMEM((tokens, width), BF)
    kv_all = pltpu.VMEM((fsdp_count, tokens, kv_cols), BF)

    def ring(shape):
        return pltpu.VMEM((2, steps) + tuple(shape), BF)

    def pair(shape):
        return pltpu.VMEM((2, 2) + tuple(shape), BF)

    ring_sems = dma((2, 2, steps))
    return pl.pallas_call(
        functools.partial(closing_kernel, count=fsdp_count, shard=shard),
        out_shape=(
            jax.ShapeDtypeStruct((tokens, width), BF),
            jax.ShapeDtypeStruct((4, attn_shape[0] - part, width), BF),
            jax.ShapeDtypeStruct((4, part, width), BF),
            jax.ShapeDtypeStruct((4,) + ff_up.shape, BF),
            jax.ShapeDtypeStruct(tail_shape, F32),
        ),
        in_specs=[anywhere, inside, inside, anywhere, anywhere, anywhere, anywhere] + [inside] * 5,
        out_specs=(inside, anywhere, anywhere, anywhere, inside),
        scratch_shapes=[
            pltpu.VMEM((2, fsdp_count, tokens, kv_cols), BF),
            kv_all,
            kv_all,
            kv_all,
            pair((tokens, kv_cols)),
            ring((tokens, kv_cols)),
            wide,
            wide,
            wide,
            wide,
            pltpu.VMEM((tokens, width), F32),
            pltpu.VMEM(attn_parts.shape, BF),
            pltpu.VMEM(attn_shape, BF),
            pltpu.VMEM((part, width), BF),
            pair(attn_shape),
            ring(attn_shape),
            pltpu.VMEM(ff_up.shape, BF),
            pltpu.VMEM((2,) + ff_up.shape, BF),
            pltpu.VMEM(ff_up.shape, BF),
            pltpu.VMEM((tokens, kv_cols), BF),
            pltpu.VMEM((fsdp_count,) + tail_shape, F32),
            pair(tail_shape),
            ring(tail_shape),
            pltpu.VMEM((2,) + tail_shape, BF),
            pltpu.VMEM((2,) + tail_shape, BF),
            dma((7,)),
            dma((2, 2)),
            dma((2, fsdp_count)),
            ring_sems,
            dma((2, 2)),
            dma((2, 2)),
            ring_sems,
            dma((2, 2, 2)),
            dma((2, 2)),
            dma((2, 4)),
            ring_sems,
            dma((2, 2)),
            dma((2, 3)),
            dma((2, 3)),
            dma((3,)),
        ],
        compiler_params=pltpu.CompilerParams(
            collective_id=2, has_side_effects=True, vmem_limit_bytes=61 << 20
        ),
        cost_estimate=COST,
        name="closing",
    )(
        kv_parts,
        query_rows,
        q_weight,
        attn_parts,
        ff_up,
        ff_down,
        ff_rest,
        resid_grad,
        hidden,
        kv_weight,
        attn_in,
        mlp_vectors,
    )


def attn_turned_kernel(order, rows_ref, query_ref, proj_ref, out_ref):
    part, cols = proj_ref.shape[0], query_ref.shape[1]
    grad = dot_rows(rows_ref[...], query_ref[...]).astype(BF)
    lines = out_ref.shape[1] - part
    out_ref[0, :part] = proj_ref[...]
    for k in range(grad.shape[0] // lines):
        out_ref[0, part:, k * cols : (k + 1) * cols] = grad[k * lines : (k + 1) * lines]


def attn_turned(order, rows, query_rows, proj_sum, shard):
    count, width = rows.shape
    cols = query_rows.shape[1]
    chunks = order.shape[0]
    part = proj_sum.shape[0] // chunks
    folds = width // cols
    lines = shard // folds
    if shard % 128:
        grad = dot_rows(rows, query_rows).astype(BF).reshape(chunks, folds, lines, cols)
        grad = grad.transpose(0, 2, 1, 3).reshape(chunks, lines, width)
        both = jnp.concatenate([proj_sum.reshape(chunks, part, width), grad], axis=1)
        return jnp.stack([lax.dynamic_index_in_dim(both, order[i], 0, False) for i in range(chunks)])
    return pl.pallas_call(
        attn_turned_kernel,
        out_shape=jax.ShapeDtypeStruct((chunks, part + lines, width), BF),
        grid_spec=pltpu.PrefetchScalarGridSpec(
            num_scalar_prefetch=1,
            grid=(chunks,),
            in_specs=[
                pl.BlockSpec((count, shard), lambda n, o: (0, o[n])),
                pl.BlockSpec((count, cols), lambda n, o: (0, 0)),
                pl.BlockSpec((part, width), lambda n, o: (o[n], 0)),
            ],
            out_specs=pl.BlockSpec((1, part + lines, width), lambda n, o: (n, 0, 0)),
        ),
        compiler_params=pltpu.CompilerParams(vmem_limit_bytes=30 << 20),
        cost_estimate=COST,
        name="attn_turned",
    )(order, rows, query_rows, proj_sum)


def rows_kernel(place, *refs):
    *ins, out = refs
    rows = ins[0].shape[0]
    for i, ref in enumerate(ins):
        out[pl.ds(pl.multiple_of((place[0] ^ i) * rows, rows), rows), :] = ref[...].astype(F32)


def stack_rows(place, pieces, tile):
    rows, width = pieces[0].shape
    return pl.pallas_call(
        rows_kernel,
        out_shape=jax.ShapeDtypeStruct((len(pieces) * rows, width), F32),
        grid_spec=pltpu.PrefetchScalarGridSpec(
            num_scalar_prefetch=1,
            grid=(width // tile,),
            in_specs=[pl.BlockSpec((rows, tile), lambda n, p: (0, n))] * len(pieces),
            out_specs=pl.BlockSpec((len(pieces) * rows, tile), lambda n, p: (0, n)),
        ),
        compiler_params=pltpu.CompilerParams(vmem_limit_bytes=40 << 20),
        cost_estimate=COST,
        name="stack_rows",
    )(place, *pieces)


def qkv_kernel(place, q_ref, tail_ref, out_ref):
    _, lines, width = q_ref.shape
    rows = out_ref.shape[0]
    folds = rows // lines
    cols = width // folds
    for i in range(q_ref.shape[0]):
        start = pl.multiple_of((place[0] ^ i) * cols, cols)
        for k in range(folds):
            part = q_ref[i, :, k * cols : (k + 1) * cols].astype(F32)
            out_ref[k * lines : (k + 1) * lines, pl.ds(start, cols)] = part
    out_ref[:, width:] = tail_ref[:rows, : out_ref.shape[1] - width]


def place_qkv(place, q_pieces, tail, rows, cols):
    return pl.pallas_call(
        qkv_kernel,
        out_shape=jax.ShapeDtypeStruct((rows, cols), F32),
        in_specs=[pl.BlockSpec(memory_space=pltpu.SMEM)] + [pl.BlockSpec(memory_space=pltpu.VMEM)] * 2,
        out_specs=pl.BlockSpec(memory_space=pltpu.VMEM),
        compiler_params=pltpu.CompilerParams(vmem_limit_bytes=30 << 20),
        cost_estimate=COST,
        name="place_qkv",
    )(place, q_pieces, tail)


def cols_kernel(place, *refs):
    *ins, out = refs
    cols = ins[0].shape[1]
    for i, ref in enumerate(ins):
        out[:, pl.ds(pl.multiple_of((place[0] ^ i) * cols, cols), cols)] = ref[...].astype(F32)


def stack_cols(place, pieces, cols):
    rows, width = pieces[0].shape
    count = len(pieces)
    if cols % 128:
        ordered = jnp.stack([lax.dynamic_index_in_dim(jnp.stack(pieces), place[0] ^ i, 0, False) for i in range(count)])
        ordered = ordered.reshape(count, rows, width // cols, cols).transpose(1, 2, 0, 3)
        return ordered.reshape(rows, count * width).astype(F32)
    return pl.pallas_call(
        cols_kernel,
        out_shape=jax.ShapeDtypeStruct((rows, count * width), F32),
        grid_spec=pltpu.PrefetchScalarGridSpec(
            num_scalar_prefetch=1,
            grid=(width // cols,),
            in_specs=[pl.BlockSpec((rows, cols), lambda n, p: (0, n))] * count,
            out_specs=pl.BlockSpec((rows, count * cols), lambda n, p: (0, n)),
        ),
        compiler_params=pltpu.CompilerParams(vmem_limit_bytes=40 << 20),
        cost_estimate=COST,
        name="stack_cols",
    )(place, *pieces)


def layer_norm(values):
    mean = jnp.mean(values, axis=-1, keepdims=True)
    center = values - mean
    inverse = lax.rsqrt(jnp.mean(center * center, axis=-1, keepdims=True) + EPS)
    return center * inverse, inverse


def norm_back(grad, normed, inverse):
    return inverse * (
        grad
        - jnp.mean(grad, axis=-1, keepdims=True)
        - normed * jnp.mean(grad * normed, axis=-1, keepdims=True)
    )


def gelu_tanh(values):
    return jax.nn.gelu(values, approximate=True)


def shards(
    hidden_in,
    out_cotangent,
    positions,
    block_mask,
    norm_gain,
    norm_bias,
    qkv_weight,
    proj_weight,
    mlp_gain,
    mlp_bias,
    fc_weight,
    down_weight,
):
    seq_count = lax.axis_size("seq")
    fsdp_count = lax.axis_size("fsdp")
    s = lax.axis_index("seq")
    f = lax.axis_index("fsdp")
    ring = Ring(fsdp_count)
    count = hidden_in.shape[1]
    width = hidden_in.shape[2]
    length = positions.shape[1]
    blocks = length // BLOCK
    shard = qkv_weight.shape[0]
    ff = fc_weight.shape[1]
    ff_shard = down_weight.shape[0]
    heads_here = HEADS // seq_count
    head_cols = heads_here * HD
    quarter = ff_shard // seq_count
    tokens_here = MB * count
    group = seq_count * tokens_here

    chunk_ids = jnp.stack([(s ^ i) * fsdp_count + f for i in range(seq_count)]).astype(jnp.int32)
    token_ids = chunk_ids[:, None] * count + jnp.arange(count, dtype=jnp.int32)[None]
    first = token_ids[:, None, :] - jnp.stack(
        [lax.dynamic_slice_in_dim(positions, chunk_ids[i] * count, count, 1) for i in range(seq_count)]
    )
    first = first[:, :, None, :]
    high_tiles = (chunk_ids * count + count - 1) // BLOCK + 1
    tables = jnp.concatenate(
        [
            jnp.broadcast_to(chunk_ids[None, :, None], (MB, seq_count, 1)),
            (first[:, :, 0, :1] // BLOCK).transpose(1, 0, 2),
            jnp.broadcast_to(high_tiles[None, :, None], (MB, seq_count, 1)),
            jnp.zeros((MB, seq_count, 1), jnp.int32),
            jnp.stack([block_mask[:, (chunk_ids[i] * count) // BLOCK] for i in range(seq_count)], axis=1),
        ],
        axis=2,
    ).reshape(-1)

    place = jnp.stack([s, f]).astype(jnp.int32)
    part = shard // seq_count
    down_own = lax.dynamic_slice_in_dim(down_weight, s * quarter, quarter, 0)
    if quarter % 128:
        fc_weight = lax.dynamic_slice_in_dim(
            fc_weight.reshape(shard, fsdp_count, seq_count, quarter), s, 1, 2
        ).reshape(shard, fsdp_count * quarter)

    span = 32
    vectors = jnp.stack([norm_gain, norm_bias, mlp_gain, mlp_bias])
    padded = jnp.pad(vectors, ((0, span - 4), (0, 2 * HD - shard)))
    own_kv = jnp.concatenate([qkv_weight[:, width:], padded], axis=0)
    hidden_own = hidden_in.reshape(tokens_here, width)
    cotangent = out_cotangent.reshape(tokens_here, width)
    hidden_all, kv_ring, q_ring, proj_ring, kv_all, fc_all, cotangent_all = opening(
        hidden_own, own_kv, qkv_weight, proj_weight, fc_weight, cotangent, fsdp_count, head_cols
    )
    cotangent_all = cotangent_all.reshape(group, width)
    down_first, kv_all = lax.optimization_barrier((down_own, kv_all))
    down_given = (lax.ppermute(down_first, "fsdp", ring.up), lax.ppermute(down_first, "fsdp", ring.down))
    kv_weight = kv_ring[:, :shard].reshape(width, 2 * HD)
    vectors = kv_ring[:, shard : shard + 4, :shard].transpose(1, 0, 2).reshape(4, width).astype(F32)
    gain_one, bias_one, gain_two, bias_two = vectors[0], vectors[1], vectors[2], vectors[3]
    q_weight = q_ring.reshape(width, head_cols)
    proj_full = proj_ring.reshape(head_cols, width)
    kv_all = kv_all.reshape(seq_count * fsdp_count, MB, count, 2 * HD)
    normed_all, _ = layer_norm(hidden_all.reshape(group, width).astype(F32))
    attn_in = (normed_all * gain_one + bias_one).astype(BF)
    own_attn_in = attn_in[:tokens_here]
    queries = dot_plain(attn_in, q_weight).astype(BF).reshape(seq_count, MB, count, head_cols)
    heads_out, logs = attend(tables, first, queries, kv_all, blocks)
    heads_rows = heads_out.reshape(group, head_cols)

    mlp_in, resid, down_all = bridge(
        heads_rows, proj_full, hidden_own, vectors[2:], down_own, down_given, fsdp_count
    )
    mlp_in = mlp_in.reshape(group, width)
    activ, pre_grad, mlp_in_parts = middle(mlp_in, cotangent_all, fc_all, down_all, 2 * BLOCK)
    branch, result, resid_grad, mlp_vectors, ff_up, ff_down, ff_rest = feedback(
        mlp_in_parts.reshape(seq_count, tokens_here, width),
        mlp_in,
        pre_grad,
        activ,
        cotangent_all,
        down_all,
        resid,
        gain_two[None],
        fsdp_count,
        shard,
    )
    branch = branch.reshape(group, width)
    steps = ring.steps()
    flow = Flow(ring, ring.scatter(ff_up, ff_down, lambda n: ff_rest[steps.index(n) - 5]))
    heads_grad = dot_cols(branch, proj_full).astype(BF).reshape(seq_count, MB, count, head_cols)
    query_grads, kv_grads = attend_back(
        tables, first, queries, kv_all, heads_out, logs, heads_grad, blocks
    )
    query_grads, kv_grads = flow.advance((query_grads, kv_grads))
    query_rows = query_grads.reshape(group, head_cols)

    proj_sum = dot_rows(heads_rows, branch).astype(BF)
    attn_parts = attn_turned(ring.order(), attn_in, query_rows, proj_sum, shard)
    ff_up, ff_down = flow.finish()
    grad_input, q_pieces, proj_pieces, ff_all, tail = closing(
        kv_grads.reshape(seq_count, fsdp_count, tokens_here, 2 * HD),
        query_rows,
        q_weight,
        attn_parts,
        (ff_up, ff_down, ff_rest),
        resid_grad,
        hidden_own,
        kv_ring,
        own_attn_in,
        mlp_vectors,
        shard,
    )
    vector_grads = tail[shard : shard + 4, :shard]
    ff_pieces = [ff_all[i] for i in range(seq_count)]
    grad_fc = stack_cols(place, [piece[:shard] for piece in ff_pieces], quarter)
    grad_down = stack_rows(place, [piece[shard:] for piece in ff_pieces], BLOCK)
    grad_proj = stack_rows(place, [proj_pieces[i] for i in range(seq_count)], width)
    grad_qkv = place_qkv(place, q_pieces, tail, shard, qkv_weight.shape[1])
    return (
        result.reshape(hidden_in.shape),
        grad_input.reshape(hidden_in.shape),
        vector_grads[0],
        vector_grads[1],
        grad_qkv,
        grad_proj,
        vector_grads[2],
        vector_grads[3],
        grad_fc,
        grad_down,
    )


def solution(mesh):
    rows = P(None, ("seq", "fsdp"), None)
    vector = P("fsdp")
    matrix = P("fsdp", None)
    in_specs = (rows, rows, P(), P(), vector, vector, matrix, matrix, vector, vector, matrix, matrix)
    out_specs = (rows, rows, vector, vector, matrix, matrix, vector, vector, matrix, matrix)
    return jax.shard_map(shards, mesh=mesh, in_specs=in_specs, out_specs=out_specs, check_vma=False)
```

```python
import functools
import math

import jax
import jax.numpy as jnp
from jax import lax
from jax.experimental import pallas as pl
from jax.experimental.pallas import tpu as pltpu
from jax.sharding import PartitionSpec as P

HEADS = 16
HD = 128
MB = 2
BLOCK = 256
EPS = 1e-05
NEG_FILL = -1e30
SCALE = HD ** (-0.5)
LOG2E = math.log2(math.e)
BF = jnp.bfloat16
COST = pl.CostEstimate(flops=0, bytes_accessed=0, transcendentals=0)
F32 = jnp.float32


def dot_rows(left, right):
    return lax.dot_general(left, right, (((0,), (0,)), ((), ())), preferred_element_type=F32)


def dot_cols(left, right):
    return lax.dot_general(left, right, (((1,), (1,)), ((), ())), preferred_element_type=F32)


def dot_plain(left, right):
    return lax.dot_general(left, right, (((1,), (0,)), ((), ())), preferred_element_type=F32)


def ring_order(count):
    return [2 * i for i in range(count // 2)] + [2 * i + 1 for i in reversed(range(count // 2))]


class Ring:
    def __init__(self, count):
        order = ring_order(count)
        self.count = count
        self.up = [(order[i], order[(i + 1) % count]) for i in range(count)]
        self.down = [(order[(i + 1) % count], order[i]) for i in range(count)]
        place = lax.axis_index("fsdp")
        half = count // 2
        self.place = place
        self.at = jnp.where(place % 2 == 0, place // 2, count - 1 - place // 2)

    def owner(self, step):
        count, half = self.count, self.count // 2
        at = lax.rem(self.at + (step + count), count)
        return jnp.where(at < half, 2 * at, 2 * (count - 1 - at) + 1)

    def steps(self):
        half = self.count // 2
        return [half] + [sign * n for n in range(half - 1, 0, -1) for sign in (1, -1)] + [0]

    def order(self):
        return jnp.stack([self.owner(n) for n in self.steps()]).astype(jnp.int32)

    def scatter(self, up, down, chunk):
        for step in range(self.count // 2 - 3, 0, -1):
            up = lax.ppermute(up, "fsdp", self.up)
            down = lax.ppermute(down, "fsdp", self.down)
            up, down = yield up, down
            up = (chunk(step).astype(F32) + up.astype(F32)).astype(BF)
            down = (chunk(-step).astype(F32) + down.astype(F32)).astype(BF)
        return up, down


class Flow:
    def __init__(self, ring, steps):
        self.ring, self.steps, self.result = ring, steps, None
        self.pending = next(steps)

    def advance(self, values=()):
        for _ in range(max(1, self.ring.count // 8)):
            if self.result is None:
                self.pending, values = lax.optimization_barrier((self.pending, values))
                try:
                    self.pending = self.steps.send(self.pending)
                except StopIteration as end:
                    self.result = end.value
        return values

    def finish(self):
        while self.result is None:
            self.advance()
        return self.result


def attend_kernel(tables, q_ref, kv_ref, first_ref, out_ref, log_ref, stack, high, total, result, *, heads, blocks):
    batch, piece = pl.program_id(0), pl.program_id(1)
    count = q_ref.shape[2]
    base = (batch * pl.num_programs(1) + piece) * (blocks + 4)
    chunk, low_tile, high_tile = tables[base], tables[base + 1], tables[base + 2]
    for h in range(heads):
        stack[h * count : (h + 1) * count, :] = q_ref[0, 0, :, h * HD : (h + 1) * HD]
    high[...] = jnp.full_like(high, NEG_FILL)
    total[...] = jnp.zeros_like(total)
    result[...] = jnp.zeros_like(result)
    tokens = chunk * count + lax.broadcasted_iota(jnp.int32, (1, count), 1)
    first = first_ref[0, 0]

    def step(tile, carry):
        @pl.when(tables[base + 4 + tile] != 0)
        def _():
            part = kv_ref[pl.ds(2 * tile, 2), 0].reshape(BLOCK, 2 * HD)
            keys, values = part[:, :HD], part[:, HD:]
            scores = dot_cols(keys, stack[...])
            index = tile * BLOCK + lax.broadcasted_iota(jnp.int32, (BLOCK, count), 0)
            allowed = (index <= tokens) & (index >= first)
            weights, scales = [], []
            for h in range(heads):
                lanes = slice(h * count, (h + 1) * count)
                score = jnp.where(allowed, scores[:, lanes] * (SCALE * LOG2E), NEG_FILL)
                old = high[:, lanes]
                new = jnp.maximum(old, jnp.max(score, axis=0, keepdims=True))
                weight = jnp.exp2(score - new)
                scale = jnp.exp2(old - new)
                high[:, lanes] = new
                total[:, lanes] = total[:, lanes] * scale + jnp.sum(weight, axis=0, keepdims=True)
                weights.append(weight.astype(BF))
                scales.append(scale)
            added = dot_rows(values, jnp.concatenate(weights, axis=1))
            result[...] = result[...] * jnp.concatenate(scales, axis=1) + added

        return carry

    lax.fori_loop(low_tile, high_tile, step, 0)
    final = result[...] / total[...]
    logs = high[...] + jnp.log2(total[...])
    for h in range(heads):
        lanes = slice(h * count, (h + 1) * count)
        out_ref[0, 0, :, h * HD : (h + 1) * HD] = final[:, lanes].T.astype(BF)
        log_ref[0, 0, h : h + 1, :] = logs[:, lanes]


def attend_back_kernel(
    tables,
    q_ref,
    kv_ref,
    first_ref,
    out_ref,
    log_ref,
    grad_ref,
    dq_ref,
    dkv_ref,
    stack,
    grads,
    logs,
    deltas,
    dq_sum,
    dkv_sum,
    *,
    heads,
    blocks,
):
    batch, piece = pl.program_id(0), pl.program_id(1)
    count = q_ref.shape[2]
    base = (batch * pl.num_programs(1) + piece) * (blocks + 4)
    chunk, low_tile, high_tile = tables[base], tables[base + 1], tables[base + 2]

    @pl.when(piece == 0)
    def _():
        dkv_sum[...] = jnp.zeros_like(dkv_sum)

    for h in range(heads):
        rows = slice(h * count, (h + 1) * count)
        cols = slice(h * HD, (h + 1) * HD)
        stack[rows, :] = q_ref[0, 0, :, cols]
        grad = grad_ref[0, 0, :, cols]
        grads[rows, :] = grad
        product = grad.astype(F32) * out_ref[0, 0, :, cols].astype(F32)
        deltas[:, rows] = jnp.sum(product.T, axis=0, keepdims=True)
        logs[:, rows] = log_ref[0, 0, h : h + 1, :]
    dq_sum[...] = jnp.zeros_like(dq_sum)
    tokens = chunk * count + lax.broadcasted_iota(jnp.int32, (1, count), 1)
    first = first_ref[0, 0]

    def step(tile, carry):
        @pl.when(tables[base + 4 + tile] != 0)
        def _():
            part = kv_ref[pl.ds(2 * tile, 2), 0].reshape(BLOCK, 2 * HD)
            keys, values = part[:, :HD], part[:, HD:]
            scores = dot_cols(keys, stack[...])
            pulls = dot_cols(values, grads[...])
            index = tile * BLOCK + lax.broadcasted_iota(jnp.int32, (BLOCK, count), 0)
            allowed = (index <= tokens) & (index >= first)
            weights, score_grads = [], []
            for h in range(heads):
                lanes = slice(h * count, (h + 1) * count)
                score = jnp.where(allowed, scores[:, lanes] * (SCALE * LOG2E), NEG_FILL)
                weight = jnp.exp2(score - logs[:, lanes])
                weights.append(weight.astype(BF))
                score_grads.append((weight * (pulls[:, lanes] - deltas[:, lanes])).astype(BF))
            weight = jnp.concatenate(weights, axis=1)
            score_grad = jnp.concatenate(score_grads, axis=1)
            dv = dot_plain(weight, grads[...])
            dk = dot_plain(score_grad, stack[...])
            dq_sum[...] += dot_rows(keys, score_grad)
            both = jnp.concatenate([dk, dv], axis=1).reshape(2, BLOCK // 2, 2 * HD)
            dkv_sum[pl.ds(2 * tile, 2)] += both

        return carry

    lax.fori_loop(low_tile, high_tile, step, 0)
    for h in range(heads):
        lanes = slice(h * count, (h + 1) * count)
        dq_ref[0, 0, :, h * HD : (h + 1) * HD] = (dq_sum[:, lanes] * SCALE).T.astype(BF)

    @pl.when(piece == pl.num_programs(1) - 1)
    def _():
        dkv_ref[:, 0, :, :HD] = (dkv_sum[:, :, :HD] * SCALE).astype(BF)
        dkv_ref[:, 0, :, HD:] = dkv_sum[:, :, HD:].astype(BF)


def attend(tables, first, queries, key_values, blocks):
    pieces, batches, count, width = queries.shape
    heads = width // HD
    chunks = key_values.shape[0]
    row_spec = pl.BlockSpec((1, 1, count, width), lambda b, i, t: (i, b, 0, 0))
    kv_spec = pl.BlockSpec((chunks, 1, count, 2 * HD), lambda b, i, t: (0, b, 0, 0))
    first_spec = pl.BlockSpec((1, 1, 1, count), lambda b, i, t: (i, b, 0, 0))
    log_spec = pl.BlockSpec((1, 1, heads, count), lambda b, i, t: (i, b, 0, 0))
    rows = heads * count
    return pl.pallas_call(
        functools.partial(attend_kernel, heads=heads, blocks=blocks),
        out_shape=(
            jax.ShapeDtypeStruct(queries.shape, BF),
            jax.ShapeDtypeStruct((pieces, batches, heads, count), F32),
        ),
        grid_spec=pltpu.PrefetchScalarGridSpec(
            num_scalar_prefetch=1,
            grid=(batches, pieces),
            in_specs=[row_spec, kv_spec, first_spec],
            out_specs=[row_spec, log_spec],
            scratch_shapes=[
                pltpu.VMEM((rows, HD), BF),
                pltpu.VMEM((1, rows), F32),
                pltpu.VMEM((1, rows), F32),
                pltpu.VMEM((HD, rows), F32),
            ],
        ),
        compiler_params=pltpu.CompilerParams(vmem_limit_bytes=40 << 20),
        cost_estimate=COST,
        name="attend",
    )(tables, queries, key_values, first)


def attend_back(tables, first, queries, key_values, out, logs, grads, blocks):
    pieces, batches, count, width = queries.shape
    heads = width // HD
    chunks = key_values.shape[0]
    row_spec = pl.BlockSpec((1, 1, count, width), lambda b, i, t: (i, b, 0, 0))
    kv_spec = pl.BlockSpec((chunks, 1, count, 2 * HD), lambda b, i, t: (0, b, 0, 0))
    first_spec = pl.BlockSpec((1, 1, 1, count), lambda b, i, t: (i, b, 0, 0))
    log_spec = pl.BlockSpec((1, 1, heads, count), lambda b, i, t: (i, b, 0, 0))
    rows = heads * count
    return pl.pallas_call(
        functools.partial(attend_back_kernel, heads=heads, blocks=blocks),
        out_shape=(
            jax.ShapeDtypeStruct(queries.shape, BF),
            jax.ShapeDtypeStruct(key_values.shape, BF),
        ),
        grid_spec=pltpu.PrefetchScalarGridSpec(
            num_scalar_prefetch=1,
            grid=(batches, pieces),
            in_specs=[row_spec, kv_spec, first_spec, row_spec, log_spec, row_spec],
            out_specs=[row_spec, kv_spec],
            scratch_shapes=[
                pltpu.VMEM((rows, HD), BF),
                pltpu.VMEM((rows, HD), BF),
                pltpu.VMEM((1, rows), F32),
                pltpu.VMEM((1, rows), F32),
                pltpu.VMEM((HD, rows), F32),
                pltpu.VMEM((chunks, count, 2 * HD), F32),
            ],
        ),
        compiler_params=pltpu.CompilerParams(vmem_limit_bytes=60 << 20),
        cost_estimate=COST,
        name="attend_back",
    )(tables, queries, key_values, first, out, logs, grads)


def neighbours(count):
    s, f = lax.axis_index("seq"), lax.axis_index("fsdp")
    half = count // 2
    at = jnp.where(lax.rem(f, 2) == 0, f // 2, count - 1 - f // 2)

    def owner(step):
        place = lax.rem(at + (step + count), count)
        return jnp.where(place < half, 2 * place, 2 * (count - 1 - place) + 1)

    chip = lax.rem(s + 2, 4)
    core = s + 1 - 2 * lax.rem(s, 2)
    return s, f, owner, (s, owner(1)), (s, owner(-1)), (chip, f), (core, f)


def greet(*devices):
    barrier = pltpu.get_barrier_semaphore()
    for device in devices:
        pl.semaphore_signal(barrier, inc=1, device_id=device, device_id_type=pl.DeviceIdType.MESH)
    pl.semaphore_wait(barrier, len(devices))


def met(device, s, f):
    return (device[0] == s) & (device[1] == f)


def greet_also(devices, sources, own, s, f):
    barrier = pltpu.get_barrier_semaphore()
    for device in devices:
        pl.semaphore_signal(barrier, inc=1, device_id=device, device_id_type=pl.DeviceIdType.MESH)
    for device in sources:

        @pl.when(jnp.logical_not(met(device, s, f)))
        def _():
            pl.semaphore_signal(barrier, inc=1, device_id=device, device_id_type=pl.DeviceIdType.MESH)

    pl.semaphore_wait(barrier, len(devices) + len(sources) - own)


class Maybe:
    def __init__(self, source, target, landing, send_sem, recv_sem, landing_sem, local_sem, device, sender, s, f):
        self.here, self.from_here = met(device, s, f), met(sender, s, f)
        kind = dict(device_id_type=pl.DeviceIdType.MESH)
        self.copy = pltpu.make_async_remote_copy(source, target, send_sem, recv_sem, device_id=device, **kind)
        self.into = pltpu.make_async_remote_copy(source, landing, send_sem, landing_sem, device_id=device, **kind)
        self.stay = pltpu.make_async_copy(source, target, local_sem)

        @pl.when(self.here)
        def _():
            self.stay.start()

        @pl.when(jnp.logical_not(self.here))
        def _():
            self.copy.start()

    def arrived(self):
        @pl.when(jnp.logical_not(self.from_here))
        def _():
            self.into.wait_recv()

    def left(self):
        @pl.when(self.here)
        def _():
            self.stay.wait()

        @pl.when(jnp.logical_not(self.here))
        def _():
            self.copy.wait_send()


def send(source, target, sems, index, device):
    copy = pltpu.make_async_remote_copy(
        src_ref=source,
        dst_ref=target,
        send_sem=sems.at[(0,) + index],
        recv_sem=sems.at[(1,) + index],
        device_id=device,
        device_id_type=pl.DeviceIdType.MESH,
    )
    copy.start()
    return copy


class KernelRing:
    def __init__(self, count, own, slots, sems, owner, up, down):
        self.count, self.own, self.slots, self.sems = count, own, slots, sems
        self.owner, self.up, self.down = owner, up, down
        self.copies = {}

    def start(self, step, given=None):
        half = self.slots.shape[1] // 2
        for way, device in enumerate((self.up, self.down)):
            slot = self.slots.at[self.owner((1 - step) if way == 0 else (step - 1))]
            source = self.own if step == 1 else slot
            if given is not None:
                source = given[way]
            if step == self.count // 2:
                rows = pl.ds(way * half, half)
                source, slot = source.at[rows], slot.at[rows]
            self.copies[way, step] = send(source, slot, self.sems, (way, step - 1), device)

    def arrived(self, step):
        self.copies[0, step].wait_recv()
        self.copies[1, step].wait_recv()

    def finish(self):
        for copy in self.copies.values():
            copy.wait_send()


def opening_kernel(
    hidden,
    kv_own,
    qkv_weight,
    proj_weight,
    fc_weight,
    cot,
    hidden_out,
    kvw_out,
    qw_out,
    proj_out,
    kv_out,
    fc_out,
    cot_out,
    weights,
    mine,
    q_own,
    fc_own,
    hid_chip,
    hid_core,
    kvw_sems,
    q_sems,
    proj_sems,
    kv_sems,
    kv_chip,
    kv_core,
    kv_far,
    fc_sems,
    cot_sems,
    move_sems,
    cut_sems,
    local,
    *,
    count,
    shard,
):
    s, f, owner, up, down, chip, core = neighbours(count)
    steps = count // 2
    per = count // 4
    target = (f // per, 4 * lax.rem(f, per) + s)
    source = (lax.rem(f, 4), s * per + f // 4)
    own_goes = met(target, s, f).astype(jnp.int32)
    greet_also((up, down, chip, core), (source,), own_goes, s, f)
    part = proj_out.shape[1]
    q_cols = qw_out.shape[2]
    q_cut = pltpu.make_async_copy(
        qkv_weight.at[:, pl.ds(pl.multiple_of(s * q_cols, q_cols), q_cols)], q_own, local.at[4]
    )
    q_cut.start()
    proj_own = proj_out.at[f]
    rings = [
        KernelRing(count, own, slots, sems, owner, up, down)
        for own, slots, sems in (
            (kv_own, kvw_out, kvw_sems),
            (q_own, qw_out, q_sems),
            (proj_own, proj_out, proj_sems),
            (fc_own, fc_out, fc_sems),
        )
    ]
    kvw, qw, proj, fc = rings
    kvw.start(1)
    moved = Maybe(
        proj_weight.at[pl.ds(pl.multiple_of(s * part, part), part)],
        proj_out.at[target[1]],
        proj_own,
        move_sems.at[0],
        move_sems.at[1],
        move_sems.at[1],
        move_sems.at[2],
        target,
        source,
        s,
        f,
    )
    if fc_weight.shape[1] == fc_out.shape[2]:
        cuts = [pltpu.make_async_copy(fc_weight, fc_own, cut_sems.at[0])]
    else:
        cols = fc_out.shape[2] // count
        cuts = [
            pltpu.make_async_copy(
                fc_weight.at[:, pl.ds(pl.multiple_of((g * 4 + s) * cols, cols), cols)],
                fc_own.at[:, pl.ds(g * cols, cols)],
                cut_sems.at[g],
            )
            for g in range(count)
        ]
    for copy in cuts:
        copy.start()
    rows = hidden.shape[0] // 2
    halves = [pl.ds(i * rows, rows) for i in range(2)]
    across = [send(hidden.at[half], hidden_out.at[2, half], hid_chip, (i,), chip) for i, half in enumerate(halves)]
    pair = [send(hidden, hidden_out.at[1], hid_core, (2,), core)]
    stays = [
        pltpu.make_async_copy(source, target, local.at[i])
        for i, (source, target) in enumerate(
            (
                (hidden, hidden_out.at[0]),
                (kv_own, kvw_out.at[f]),
                (cot, cot_out.at[0]),
            )
        )
    ]
    for copy in stays:
        copy.start()
    q_cut.wait()
    for copy in cuts:
        copy.wait()
    for i, (source, target) in enumerate(((q_own, qw_out.at[f]), (fc_own, fc_out.at[f]))):
        stays.append(pltpu.make_async_copy(source, target, local.at[3 if i == 0 else 5]))
        stays[-1].start()
    values = hidden[...].astype(F32)
    mean = jnp.mean(values, axis=-1, keepdims=True)
    center = values - mean
    inverse = lax.rsqrt(jnp.mean(center * center, axis=-1, keepdims=True) + EPS)
    for step in range(2, steps + 1):
        kvw.arrived(step - 1)
        kvw.start(step)
    qw.start(1)
    fc.start(1)
    kvw.arrived(steps)
    stays[1].wait()
    load = pltpu.make_async_copy(kvw_out, weights, local.at[6])
    load.start()
    load.wait()
    total = jnp.zeros((hidden.shape[0], kvw_out.shape[2]), F32)
    for t in range(count):
        cols = slice(t * shard, (t + 1) * shard)
        normed = (hidden[:, cols].astype(F32) - mean) * inverse
        gain = weights[t, shard : shard + 1, :shard].astype(F32)
        bias = weights[t, shard + 1 : shard + 2, :shard].astype(F32)
        total += dot_plain((normed * gain + bias).astype(BF), weights[t, :shard, :])
    mine[...] = total.astype(BF)

    spread = KernelRing(count, mine, kv_out.at[s], kv_sems, owner, up, down)
    spread.start(1)
    keep = pltpu.make_async_copy(mine, kv_out.at[s, f], local.at[7])
    keep.start()
    kv_across, kv_pair = [], []

    def pass_on(source, place):
        index = (len(kv_across),)
        kv_across.append((place, send(source, kv_out.at[s, place], kv_chip, index, chip)))
        kv_pair.append(send(source, kv_out.at[s, place], kv_core, index, core))

    pass_on(mine, f)
    for i, half in enumerate(halves):
        across[i].wait_recv()
        pair.append(send(hidden_out.at[2, half], hidden_out.at[2 + 1, half], hid_core, (i,), core))
    for step in range(1, steps + 1):
        spread.arrived(step)
        qw.arrived(step)
        if step < steps:
            spread.start(step + 1)
            qw.start(step + 1)
            for place in (owner(-step), owner(step)):
                pass_on(kv_out.at[s, place], place)
        else:
            pass_on(kv_out.at[s, owner(steps)], owner(steps))
        if step == 1:
            moved.arrived()
            moved.left()
            proj.start(1)
            cot_across = send(cot, cot_out.at[2], cot_sems, (0,), chip)
            cot_pair = send(cot, cot_out.at[1], cot_sems, (1,), core)
        else:
            proj.arrived(step - 1)
            proj.start(step)
        if step < steps - 1:
            fc.arrived(step)
        if step < steps - 2:
            fc.start(step + 1)
    other = lax.rem(s + 2, 4)
    far = []
    for i, (place, copy) in enumerate(kv_across):
        copy.wait_recv()
        slot = kv_out.at[other, place]
        far.append(send(slot, slot, kv_far, (i,), core))
    cot_across.wait()
    cot_far = send(cot_out.at[2], cot_out.at[3], cot_sems, (2,), core)
    proj.arrived(steps)
    for ring in rings + [spread]:
        ring.finish()
    for copy in [keep, cot_pair, cot_far, stays[0]] + stays[2:]:
        copy.wait()
    for copy in across + [copy for _, copy in kv_across]:
        copy.wait_send()
    for copy in pair + kv_pair + far:
        copy.wait()


def opening(hidden, kv_own, qkv_weight, proj_weight, fc_weight, cot, fsdp_count, q_cols):
    count, width = hidden.shape
    shard = qkv_weight.shape[0]
    dma = pltpu.SemaphoreType.DMA
    ring = dma((2, 2, fsdp_count // 2))
    anywhere = pl.BlockSpec(memory_space=pltpu.HBM)
    inside = pl.BlockSpec(memory_space=pltpu.VMEM)
    return pl.pallas_call(
        functools.partial(opening_kernel, count=fsdp_count, shard=shard),
        out_shape=(
            jax.ShapeDtypeStruct((4,) + hidden.shape, BF),
            jax.ShapeDtypeStruct((fsdp_count,) + kv_own.shape, BF),
            jax.ShapeDtypeStruct((fsdp_count, shard, q_cols), BF),
            jax.ShapeDtypeStruct((fsdp_count, shard // 4, width), BF),
            jax.ShapeDtypeStruct((4, fsdp_count, count, 2 * HD), BF),
            jax.ShapeDtypeStruct((fsdp_count, shard, width), BF),
            jax.ShapeDtypeStruct((4,) + hidden.shape, BF),
        ),
        in_specs=[inside, inside] + [anywhere] * 3 + [inside],
        out_specs=(anywhere,) * 7,
        scratch_shapes=[
            pltpu.VMEM((fsdp_count,) + kv_own.shape, BF),
            pltpu.VMEM((count, 2 * HD), BF),
            pltpu.VMEM((shard, q_cols), BF),
            pltpu.VMEM((shard, width), BF),
            dma((2, 2)),
            dma((2, 3)),
            ring,
            ring,
            ring,
            ring,
            dma((2, fsdp_count)),
            dma((2, fsdp_count)),
            dma((2, fsdp_count)),
            ring,
            dma((2, 3)),
            dma((3,)),
            dma((fsdp_count,)),
            dma((8,)),
        ],
        compiler_params=pltpu.CompilerParams(
            collective_id=1, has_side_effects=True, vmem_limit_bytes=40 << 20
        ),
        cost_estimate=COST,
        name="opening",
    )(hidden, kv_own, qkv_weight, proj_weight, fc_weight, cot)


GELU_A = math.sqrt(2 / math.pi)
GELU_B = 0.044715


def middle_kernel(rows_ref, cot_ref, fc_ref, down_ref, activ_ref, pre_ref, grad_ref, total, *, step):
    tile = pl.program_id(0)
    fc = fc_ref[...].reshape(-1, fc_ref.shape[2])
    down = down_ref[...].reshape(-1, down_ref.shape[2])

    @pl.when(tile == 0)
    def _():
        total[...] = jnp.zeros_like(total)

    for at in range(0, rows_ref.shape[0], step):
        part = slice(at, at + step)
        value = dot_plain(rows_ref[part], fc)
        pull = dot_cols(cot_ref[part], down)
        square = value * value
        bend = jnp.tanh(GELU_A * value * (1.0 + GELU_B * square))
        half = 0.5 * (1.0 + bend)
        activ_ref[part] = (value * half).astype(BF)
        slope = half + 0.5 * value * (1.0 - bend * bend) * (GELU_A * (1.0 + 3.0 * GELU_B * square))
        grad = (pull * slope).astype(BF)
        pre_ref[part] = grad
        total[part] += dot_cols(grad, fc)

    @pl.when(tile == pl.num_programs(0) - 1)
    def _():
        grad_ref[...] = total[...].astype(BF)


def middle(rows, cot, fc_all, down_all, tile):
    count, width = rows.shape
    parts, shard = fc_all.shape[:2]
    quarter = down_all.shape[1]
    hidden = parts * quarter
    per = tile // quarter
    whole = pl.BlockSpec((count, width), lambda n: (0, 0), pipeline_mode=pl.Buffered(1))
    cols = pl.BlockSpec((count, tile), lambda n: (0, n))
    return pl.pallas_call(
        functools.partial(middle_kernel, step=256),
        out_shape=(
            jax.ShapeDtypeStruct((count, hidden), BF),
            jax.ShapeDtypeStruct((count, hidden), BF),
            jax.ShapeDtypeStruct((count, width), BF),
        ),
        grid=(hidden // tile,),
        in_specs=[
            whole,
            whole,
            pl.BlockSpec((parts, shard, tile), lambda n: (0, 0, n)),
            pl.BlockSpec((per, quarter, width), lambda n: (n, 0, 0)),
        ],
        out_specs=(cols, cols, pl.BlockSpec((count, width), lambda n: (0, 0))),
        scratch_shapes=[pltpu.VMEM((count, width), F32)],
        compiler_params=pltpu.CompilerParams(vmem_limit_bytes=60 << 20),
        cost_estimate=COST,
        name="middle",
    )(rows, cot, fc_all, down_all)


def bridge_kernel(
    heads,
    proj,
    hidden,
    vectors,
    down_own,
    first_up,
    first_down,
    mlp_out,
    resid_out,
    down_out,
    far_out,
    far,
    near_out,
    near,
    chip_in,
    mine,
    pair_sems,
    chip_sems,
    spread_chip,
    spread_core,
    down_sems,
    local,
    *,
    count,
):
    s, f, owner, up, down, chip, core = neighbours(count)
    greet(up, down, chip, core)
    steps = count // 2
    tokens = hidden.shape[0]
    ring = KernelRing(count, down_own, down_out, down_sems, owner, up, down)
    ring.start(2, (first_up, first_down))
    stays = [
        pltpu.make_async_copy(down_own, down_out.at[f], local.at[0]),
        pltpu.make_async_copy(first_up, down_out.at[owner(-1)], local.at[2]),
        pltpu.make_async_copy(first_down, down_out.at[owner(1)], local.at[3]),
    ]
    for copy in stays:
        copy.start()

    def part(i):
        return dot_plain(heads[i * tokens : (i + 1) * tokens], proj[...])

    far_out[...] = part(3).astype(BF)
    pairs = [send(far_out, far, pair_sems, (0,), core)]
    near_out[...] = part(1).astype(BF)
    pairs.append(send(near_out, near, pair_sems, (1,), core))
    middle = part(2)
    pairs[0].wait()
    far_out[...] = (middle + far[...].astype(F32)).astype(BF)
    rows = tokens // 2
    halves = [pl.ds(i * rows, rows) for i in range(2)]
    across = [send(far_out.at[half], chip_in.at[half], chip_sems, (i,), chip) for i, half in enumerate(halves)]
    resid_out[...] = hidden[...].astype(F32) + part(0)
    pairs[1].wait()
    resid_out[...] += near[...].astype(F32)
    spread, spread_pair = [], []
    block = 64
    for i, half in enumerate(halves):
        across[i].wait_recv()
        for at in range(i * rows, (i + 1) * rows, block):
            here = slice(at, at + block)
            resid = resid_out[here] + chip_in[here].astype(F32)
            resid_out[here] = resid
            normed, _ = layer_norm(resid)
            mine[here] = (normed * vectors[0:1] + vectors[1:2]).astype(BF)
        spread.append(send(mine.at[half], mlp_out.at[2, half], spread_chip, (i,), chip))
        spread_pair.append(send(mine.at[half], mlp_out.at[1, half], spread_core, (i,), core))
        ring.arrived(i + 2)
        ring.start(i + 3)
    stays.append(pltpu.make_async_copy(mine, mlp_out.at[0], local.at[1]))
    stays[-1].start()
    for i, half in enumerate(halves):
        spread[i].wait_recv()
        spread_pair.append(send(mlp_out.at[2, half], mlp_out.at[3, half], spread_core, (2 + i,), core))
    for step in range(4, steps + 1):
        ring.arrived(step)
        if step < steps:
            ring.start(step + 1)
    ring.finish()
    for copy in across + spread:
        copy.wait_send()
    for copy in spread_pair + stays:
        copy.wait()


def bridge(heads, proj, hidden, vectors, down_own, first, fsdp_count):
    tokens, width = hidden.shape
    quarter = down_own.shape[0]
    dma = pltpu.SemaphoreType.DMA
    anywhere = pl.BlockSpec(memory_space=pltpu.HBM)
    inside = pl.BlockSpec(memory_space=pltpu.VMEM)
    wide = pltpu.VMEM((tokens, width), BF)
    return pl.pallas_call(
        functools.partial(bridge_kernel, count=fsdp_count),
        out_shape=(
            jax.ShapeDtypeStruct((4, tokens, width), BF),
            jax.ShapeDtypeStruct((tokens, width), F32),
            jax.ShapeDtypeStruct((fsdp_count, quarter, width), BF),
        ),
        in_specs=[inside] * 7,
        out_specs=(anywhere, inside, anywhere),
        scratch_shapes=[wide] * 6
        + [
            dma((2, 2)),
            dma((2, 2)),
            dma((2, 2)),
            dma((2, 4)),
            dma((2, 2, fsdp_count // 2)),
            dma((4,)),
        ],
        compiler_params=pltpu.CompilerParams(
            collective_id=3, has_side_effects=True, vmem_limit_bytes=40 << 20
        ),
        cost_estimate=COST,
        name="bridge",
    )(heads, proj, hidden, vectors, down_own, *first)


def feedback_kernel(
    parts,
    mlp_in,
    pre_grad,
    activ,
    cot,
    down_all,
    resid,
    gain,
    branch_out,
    result_out,
    resid_out,
    vectors_out,
    up_out,
    down_out,
    rest_out,
    mlp_here,
    pre_here,
    activ_here,
    cot_here,
    here,
    across_out,
    far,
    near,
    chip_in,
    branch,
    outs_first,
    ins_first,
    outs_next,
    ins_next,
    stage,
    down_here,
    low_here,
    low_far,
    low_near,
    low_chip,
    branch_low,
    pair_sems,
    chip_sems,
    spread_chip,
    spread_core,
    ring_sems,
    low_pair,
    low_across,
    local,
    *,
    count,
    shard,
    turned,
):
    s, f, owner, up, down, chip, core = neighbours(count)
    greet(up, down, chip, core)
    steps = count // 2
    tokens, width = resid.shape
    pairs = [send(parts.at[3], far, pair_sems, (0,), core), send(parts.at[1], near, pair_sems, (1,), core)]
    loads = [
        pltpu.make_async_copy(source, target, local.at[i])
        for i, (source, target) in enumerate(
            (
                (pre_grad, pre_here),
                (mlp_in, mlp_here),
                (parts.at[2], across_out),
                (cot, cot_here),
                (activ, activ_here),
                (parts.at[0], here),
            )
        )
    ]
    for copy in loads:
        copy.start()

    def product(left, right, place, out):
        start = pl.multiple_of(place * shard, shard)
        chosen = left[:, pl.ds(start, shard)] if turned else left[pl.ds(start, shard), :]
        for at in range(0, width, 512):
            cols = slice(at, at + 512)
            value = dot_rows(chosen, right[:, cols]) if turned else dot_plain(chosen, right[:, cols])
            out[:, cols] = value.astype(BF)

    def chunk(place, out):
        product(mlp_here, pre_here, place, out.at[pl.ds(0, shard)])
        product(activ_here, cot_here, place, out.at[pl.ds(shard, shard)])

    def low_part(j, down):
        lines = slice(j * tokens, (j + 1) * tokens)
        return dot_plain(activ_here[lines], down) if turned else dot_rows(activ_here[:, lines], down)

    upper, under = pl.ds(0, shard), pl.ds(shard, shard)
    devices = (up, down)
    side = width // 2
    sides = [
        pltpu.make_async_copy(down_all.at[:, :, pl.ds(i * side, side)], down_here, local.at[10 + i])
        for i in range(2)
    ]
    sides[0].start()
    loads[0].wait()
    loads[1].wait()
    product(mlp_here, pre_here, owner(steps), outs_first.at[upper])
    first = [send(outs_first.at[upper], ins_first.at[upper], ring_sems, (0, 0), up)]
    loads[2].wait()
    pairs[0].wait_recv()
    across_out[...] = (across_out[...].astype(F32) + far[...].astype(F32)).astype(BF)
    rows = tokens // 2
    halves = [pl.ds(i * rows, rows) for i in range(2)]
    across = [send(across_out.at[half], chip_in.at[half], chip_sems, (i,), chip) for i, half in enumerate(halves)]
    loads[3].wait()
    loads[4].wait()
    product(activ_here, cot_here, owner(steps), outs_first.at[under])
    first.append(send(outs_first.at[under], ins_first.at[under], ring_sems, (1, 0), down))
    chunk(owner(steps - 1), outs_next.at[0])
    chunk(owner(1 - steps), outs_next.at[1])
    second = []
    for way, part in enumerate((upper, under)):
        first[way].wait_recv()
        out = outs_next.at[way]
        out[part] = (out[part].astype(F32) + ins_first[part].astype(F32)).astype(BF)
        second.append(send(out, ins_next.at[way], ring_sems, (way, 1), devices[way]))

    loads[5].wait()
    pairs[1].wait_recv()
    gain_grad = jnp.zeros((1, width), F32)
    bias_grad = jnp.zeros((1, width), F32)
    spread, spread_pair = [], []
    block = 64
    for i, half in enumerate(halves):
        across[i].wait_recv()
        for at in range(i * rows, (i + 1) * rows, block):
            part = slice(at, at + block)
            grad = here[part].astype(F32) + near[part].astype(F32) + chip_in[part].astype(F32)
            normed, inverse = layer_norm(resid[part])
            gain_grad += jnp.sum(grad * normed, axis=0, keepdims=True)
            bias_grad += jnp.sum(grad, axis=0, keepdims=True)
            value = cot_here[part].astype(F32) + norm_back(grad * gain[...], normed, inverse)
            resid_out[part] = value
            branch[part] = value.astype(BF)
        spread.append(send(branch.at[half], branch_out.at[2, half], spread_chip, (i,), chip))
        spread_pair.append(send(branch.at[half], branch_out.at[1, half], spread_core, (i,), core))
    vectors_out[0:1] = gain_grad
    vectors_out[1:2] = bias_grad
    keep = pltpu.make_async_copy(branch, branch_out.at[0], local.at[6])
    keep.start()

    for copy in across:
        copy.wait_send()
    lows = (low_here, here, across_out, branch_low)
    for i in range(2):
        cols = pl.ds(i * side, side)
        sides[i].wait()
        down = down_here[...].reshape(-1, side)
        for j in (3, 1, 2, 0):
            value = low_part(j, down)
            lows[j][:, cols] = value if j == 0 else value.astype(BF)
        if i == 0:
            sides[1].start()
    low_sends = [send(lows[3], low_far, low_pair, (0,), core), send(lows[1], low_near, low_pair, (1,), core)]
    low_sends[0].wait()
    across_out[...] = (across_out[...].astype(F32) + low_far[...].astype(F32)).astype(BF)
    low_chip_copy = send(across_out, low_chip, low_across, (0,), chip)

    def rest(i, carry):
        back = lax.rem(i + 1, 2)
        n = (steps - (i + 1) // 2) * (1 - 2 * back)
        chunk(owner(n), stage)
        copy = pltpu.make_async_copy(stage, rest_out.at[i - 5], local.at[7])
        copy.start()
        copy.wait()
        return carry

    lax.fori_loop(5, count, rest, 0)
    for i, half in enumerate(halves):
        spread[i].wait_recv()
        spread_pair.append(send(branch_out.at[2, half], branch_out.at[3, half], spread_core, (2 + i,), core))
    leaving = []
    low_sends[1].wait()
    low_chip_copy.wait()
    for at in range(0, tokens, block):
        part = slice(at, at + block)
        value = resid[part] + low_here[part] + low_near[part].astype(F32) + low_chip[part].astype(F32)
        result_out[part] = value.astype(BF)
    for way, target in enumerate((up_out, down_out)):
        out = stage if way == 0 else outs_first
        if way:
            first[0].wait_send()
            first[1].wait_send()
        chunk(owner((steps - 2) * (1 - 2 * way)), out)
        second[way].wait_recv()
        out[...] = (out[...].astype(F32) + ins_next[way].astype(F32)).astype(BF)
        leaving.append(pltpu.make_async_copy(out, target, local.at[8 + way]))
        leaving[way].start()
    for copy in pairs + spread + second:
        copy.wait_send()
    for copy in spread_pair + leaving + [keep]:
        copy.wait()


def feedback(parts, mlp_in, pre_grad, activ, cot, down_all, resid, gain, fsdp_count, shard):
    tokens, width = resid.shape
    turned = shard % 128 == 0
    if not turned:
        mlp_in, activ = mlp_in.T, activ.T
    dma = pltpu.SemaphoreType.DMA
    anywhere = pl.BlockSpec(memory_space=pltpu.HBM)
    inside = pl.BlockSpec(memory_space=pltpu.VMEM)
    wide = pltpu.VMEM((tokens, width), BF)
    both = pltpu.VMEM((2 * shard, width), BF)
    quarter = down_all.shape[1]
    flow = jax.ShapeDtypeStruct((2 * shard, width), BF)
    return pl.pallas_call(
        functools.partial(feedback_kernel, count=fsdp_count, shard=shard, turned=turned),
        out_shape=(
            jax.ShapeDtypeStruct((4, tokens, width), BF),
            jax.ShapeDtypeStruct((tokens, width), BF),
            jax.ShapeDtypeStruct((tokens, width), F32),
            jax.ShapeDtypeStruct((2, width), F32),
            flow,
            flow,
            jax.ShapeDtypeStruct((fsdp_count - 5, 2 * shard, width), BF),
        ),
        in_specs=[anywhere] * 6 + [inside] * 2,
        out_specs=(anywhere, inside, inside, inside, anywhere, anywhere, anywhere),
        scratch_shapes=[pltpu.VMEM(value.shape, BF) for value in (mlp_in, pre_grad, activ, cot)]
        + [wide] * 6
        + [
            both,
            both,
            pltpu.VMEM((2, 2 * shard, width), BF),
            pltpu.VMEM((2, 2 * shard, width), BF),
            both,
            pltpu.VMEM((fsdp_count, quarter, width // 2), BF),
            pltpu.VMEM((tokens, width), F32),
            wide,
            wide,
            wide,
            wide,
            dma((2, 2)),
            dma((2, 2)),
            dma((2, 2)),
            dma((2, 4)),
            dma((2, 2, 2)),
            dma((2, 2)),
            dma((2, 1)),
            dma((12,)),
        ],
        compiler_params=pltpu.CompilerParams(
            collective_id=4, has_side_effects=True, vmem_limit_bytes=61 << 20
        ),
        cost_estimate=COST,
        name="feedback",
    )(parts, mlp_in, pre_grad, activ, cot, down_all, resid, gain)


class KernelScatter:
    def __init__(self, count, chunk, outs, ins, sems, up, down):
        self.steps, self.chunk, self.outs, self.ins, self.sems = count // 2, chunk, outs, ins, sems
        self.devices = (up, down)
        self.half = outs.shape[2] // 2
        self.copies = {}

    def start(self, step):
        half = self.half
        for way, sign in ((0, 1), (1, -1)):
            mine = self.chunk(sign * (self.steps - step))
            if step > 1:
                self.copies[way, step - 2].wait_send()
            out, into = self.outs.at[way, step % 2], self.ins.at[way, step]
            rows = slice(way * half, (way + 1) * half)
            rest = slice((1 - way) * half, (2 - way) * half)
            if step == 0:
                out, into = out.at[pl.ds(0, half)], into.at[pl.ds(0, half)]
                out[...] = mine[rows].astype(BF)
            elif step == 1:
                out[rows] = (mine[rows] + self.ins[way, 0, :half].astype(F32)).astype(BF)
                out[rest] = mine[rest].astype(BF)
            else:
                out[...] = (mine + self.ins[way, step - 1].astype(F32)).astype(BF)
            self.copies[way, step] = send(out, into, self.sems, (way, step), self.devices[way])

    def arrived(self, step):
        self.copies[0, step].wait_recv()
        self.copies[1, step].wait_recv()

    def total(self):
        last = self.steps - 1
        return self.chunk(0) + self.ins[0, last].astype(F32) + self.ins[1, last].astype(F32)

    def finish(self):
        for (_, step), copy in self.copies.items():
            if step >= self.steps - 2:
                copy.wait_send()


def closing_kernel(
    kv_parts,
    query_rows,
    q_weight,
    attn_parts,
    ff_up,
    ff_down,
    ff_rest,
    resid_grad,
    hidden,
    kv_weight,
    attn_in,
    mlp_vectors,
    grad_out,
    q_out,
    proj_out,
    ff_out,
    tail_out,
    kv_here,
    kv_near,
    kv_far,
    kv_chip_in,
    kv_outs,
    kv_ins,
    q_far_out,
    q_far,
    q_near,
    q_chip_in,
    q_here,
    attn_here,
    attn_own,
    proj_here,
    attn_outs,
    attn_ins,
    ff_here,
    ff_ins,
    ff_sum,
    kv_total,
    tail_here,
    tail_outs,
    tail_ins,
    swap_out,
    swap_in,
    local,
    kv_core_sems,
    kv_chip_sems,
    kv_sems,
    q_core_sems,
    q_chip_sems,
    attn_sems,
    ff_sems,
    ff_chip_sems,
    ff_core_sems,
    tail_sems,
    swap_sems,
    q_spread_sems,
    proj_spread_sems,
    move_sems,
    *,
    count,
    shard,
):
    s, f, owner, up, down, chip, core = neighbours(count)
    steps = count // 2
    order = [steps] + [sign * n for n in range(steps - 1, 0, -1) for sign in (1, -1)] + [0]
    other, sibling = lax.rem(s + 2, 4), core[0]
    far = lax.rem(sibling + 2, 4)
    tokens = hidden.shape[0]
    per = count // 4
    target = (lax.rem(f, 4), s * per + f // 4)
    source = (f // per, 4 * lax.rem(f, per) + s)
    greet_also((up, down, chip, core), (source,), met(target, s, f).astype(jnp.int32), s, f)

    kv_pair = [
        send(kv_parts.at[far], kv_far, kv_core_sems, (0,), core),
        send(kv_parts.at[sibling], kv_near, kv_core_sems, (1,), core),
    ]
    loads = [
        pltpu.make_async_copy(kv_parts.at[other], kv_here.at[1], local.at[0]),
        pltpu.make_async_copy(kv_parts.at[s], kv_here.at[0], local.at[1]),
        pltpu.make_async_copy(attn_parts, attn_here, local.at[2]),
        pltpu.make_async_copy(ff_rest.at[ff_rest.shape[0] - 1], ff_here, local.at[3]),
    ]
    for copy in loads:
        copy.start()
    ff_rows = ff_here.shape[0] // 2
    ff_parts = [pl.ds(i * ff_rows, ff_rows) for i in range(2)]
    ff_ring = []

    def ff_start(i):
        for way, (source, device) in enumerate(((ff_up, up), (ff_down, down))):
            copy = send(source.at[ff_parts[i]], ff_ins.at[way, ff_parts[i]], ff_sems, (way, i), device)
            ff_ring.append(copy)

    ff_start(0)

    def query_part(i):
        return dot_cols(query_rows[i * tokens : (i + 1) * tokens], q_weight[...])

    q_far_out[...] = query_part(3).astype(BF)
    q_pair = [send(q_far_out, q_far, q_core_sems, (0,), core)]
    grad_out[...] = query_part(1).astype(BF)
    loads[0].wait()
    kv_pair[0].wait_recv()
    kv_across = {}
    for i, n in enumerate(order):
        place = owner(n)
        kv_here[1, place] = (kv_here[1, place].astype(F32) + kv_far[place].astype(F32)).astype(BF)
        kv_across[n] = send(kv_here.at[1, place], kv_chip_in.at[i], kv_chip_sems, (i,), chip)
    part = query_part(2)
    q_pair[0].wait()
    q_chip_out = q_far_out
    q_chip_out[...] = (part + q_far[...].astype(F32)).astype(BF)
    rows = tokens // 2
    q_halves = [pl.ds(i * rows, rows) for i in range(2)]
    q_across = [
        send(q_chip_out.at[half], q_chip_in.at[half], q_chip_sems, (i,), chip) for i, half in enumerate(q_halves)
    ]
    q_pair.append(send(grad_out, q_near, q_core_sems, (1,), core))
    q_here[...] = query_part(0)
    loads[1].wait()
    kv_pair[1].wait_recv()

    def kv_chunk(n):
        n = steps if n == -steps else n
        place = owner(n)
        here = kv_here[0, place].astype(F32) + kv_near[place].astype(F32)
        return here + kv_chip_in[order.index(n)].astype(F32)

    loads[2].wait()

    def attn_chunk(n):
        return attn_here[order.index(steps if n == -steps else n)].astype(F32)

    kv = KernelScatter(count, kv_chunk, kv_outs, kv_ins, kv_sems, up, down)
    attn = KernelScatter(count, attn_chunk, attn_outs, attn_ins, attn_sems, up, down)
    for step in range(steps):
        for n in (steps - step, step - steps):
            if n in order:
                kv_across[n].wait_recv()
        if step:
            kv.arrived(step - 1)
        kv.start(step)
        if step:
            attn.arrived(step - 1)
        attn.start(step)
    ff_start(1)

    loads[3].wait()
    ff_pair, ff_across = [], []

    def ff_close(i):
        rows = ff_parts[i]
        for copy in ff_ring[2 * i : 2 * i + 2]:
            copy.wait_recv()
        arrived = ff_ins[0, rows].astype(F32) + ff_ins[1, rows].astype(F32)
        ff_sum[rows] = (ff_here[rows].astype(F32) + arrived).astype(BF)
        ff_across.append(send(ff_sum.at[rows], ff_out.at[2, rows], ff_chip_sems, (i,), chip))
        ff_pair.append(send(ff_sum.at[rows], ff_out.at[1, rows], ff_core_sems, (i,), core))

    ff_close(0)
    kv_across[0].wait_recv()
    kv.arrived(steps - 1)
    kv_total[...] = kv.total().astype(BF)

    attn.arrived(steps - 1)
    attn_own[...] = attn.total().astype(BF)
    part = proj_out.shape[1]
    lines = pl.ds(part, attn_own.shape[0] - part)
    q_lines = attn_own.at[lines]
    q_spread = [
        send(q_lines, q_out.at[2], q_spread_sems, (0,), chip),
        send(q_lines, q_out.at[1], q_spread_sems, (1,), core),
    ]
    q_keep = pltpu.make_async_copy(q_lines, q_out.at[0], local.at[5])
    q_keep.start()
    moved = Maybe(
        attn_own.at[pl.ds(0, part)],
        proj_here,
        proj_here,
        move_sems.at[0],
        move_sems.at[1],
        move_sems.at[1],
        move_sems.at[2],
        target,
        source,
        s,
        f,
    )

    q_pair[1].wait()
    for copy in q_across:
        copy.wait_recv()
    q_here[...] += q_near[...].astype(F32) + q_chip_in[...].astype(F32)
    for t in range(count):
        cols = slice(t * shard, (t + 1) * shard)
        q_here[:, cols] += dot_cols(kv_total[...], kv_weight[t, :shard, :])
    gain = jnp.concatenate([kv_weight[t, shard : shard + 1, :shard] for t in range(count)], axis=1).astype(F32)
    block = 64
    gain_grad = jnp.zeros((1, hidden.shape[1]), F32)
    bias_grad = jnp.zeros((1, hidden.shape[1]), F32)
    for at in range(0, tokens, block):
        here = slice(at, at + block)
        normed, inverse = layer_norm(hidden[here].astype(F32))
        grad = q_here[here]
        gain_grad += jnp.sum(grad * normed, axis=0, keepdims=True)
        bias_grad += jnp.sum(grad, axis=0, keepdims=True)
        grad_out[here] = (resid_grad[here] + norm_back(grad * gain, normed, inverse)).astype(BF)

    tail_here[...] = jnp.zeros_like(tail_here)
    vectors = (gain_grad, bias_grad, mlp_vectors[0:1], mlp_vectors[1:2])
    for t in range(count):
        cols = slice(t * shard, (t + 1) * shard)
        tail_here[t, :shard, :] = dot_rows(attn_in[:, cols], kv_total[...])
        for j, vector in enumerate(vectors):
            tail_here[t, shard + j : shard + j + 1, :shard] = vector[:, cols]
    tail = KernelScatter(count, lambda n: tail_here[owner(n)], tail_outs, tail_ins, tail_sems, up, down)
    for step in range(steps):
        if step:
            tail.arrived(step - 1)
        tail.start(step)
        if step == 0:
            ff_close(1)
            q_spread[0].wait_recv()
            q_spread.append(send(q_out.at[2], q_out.at[3], q_spread_sems, (2,), core))
            moved.arrived()
            moved.left()
            proj_spread = [
                send(proj_here, proj_out.at[2], proj_spread_sems, (0,), chip),
                send(proj_here, proj_out.at[1], proj_spread_sems, (1,), core),
            ]
            proj_keep = pltpu.make_async_copy(proj_here, proj_out.at[0], local.at[6])
            proj_keep.start()
    proj_spread[0].wait_recv()
    proj_spread.append(send(proj_out.at[2], proj_out.at[3], proj_spread_sems, (2,), core))
    tail.arrived(steps - 1)
    total = tail.total()
    swap_out[0] = total.astype(BF)
    swaps = [send(swap_out.at[0], swap_in.at[0], swap_sems, (0,), core)]
    for i, rows in enumerate(ff_parts):
        ff_across[i].wait_recv()
        ff_pair.append(send(ff_out.at[2, rows], ff_out.at[3, rows], ff_core_sems, (2 + i,), core))
    keep = pltpu.make_async_copy(ff_sum, ff_out.at[0], local.at[4])
    keep.start()
    swaps[0].wait_recv()
    swap_out[1] = (swap_out[0].astype(F32) + swap_in[0].astype(F32)).astype(BF)
    swaps.append(send(swap_out.at[1], swap_in.at[1], swap_sems, (1,), chip))
    swaps[1].wait_recv()
    tail_out[...] = swap_out[1].astype(F32) + swap_in[1].astype(F32)
    keep.wait()
    q_keep.wait()
    proj_keep.wait()
    q_spread[0].wait_send()
    proj_spread[0].wait_send()
    for copy in q_spread[1:] + proj_spread[1:]:
        copy.wait()
    for ring in (kv, attn, tail):
        ring.finish()
    for copy in kv_pair + q_across + list(kv_across.values()) + ff_ring + ff_across + swaps:
        copy.wait_send()
    for copy in ff_pair:
        copy.wait()


def closing(kv_parts, query_rows, q_weight, attn_parts, ff_flow, resid_grad, hidden, kv_weight, attn_in, mlp_vectors, shard):
    ff_up, ff_down, ff_rest = ff_flow
    fsdp_count, tokens, kv_cols = kv_parts.shape[1:]
    width = hidden.shape[1]
    steps = fsdp_count // 2
    dma = pltpu.SemaphoreType.DMA
    anywhere = pl.BlockSpec(memory_space=pltpu.HBM)
    inside = pl.BlockSpec(memory_space=pltpu.VMEM)
    attn_shape = attn_parts.shape[1:]
    part = shard // 4
    tail_shape = kv_weight.shape[1:]
    wide = pltpu.VMEM((tokens, width), BF)
    kv_all = pltpu.VMEM((fsdp_count, tokens, kv_cols), BF)

    def ring(shape):
        return pltpu.VMEM((2, steps) + tuple(shape), BF)

    def pair(shape):
        return pltpu.VMEM((2, 2) + tuple(shape), BF)

    ring_sems = dma((2, 2, steps))
    return pl.pallas_call(
        functools.partial(closing_kernel, count=fsdp_count, shard=shard),
        out_shape=(
            jax.ShapeDtypeStruct((tokens, width), BF),
            jax.ShapeDtypeStruct((4, attn_shape[0] - part, width), BF),
            jax.ShapeDtypeStruct((4, part, width), BF),
            jax.ShapeDtypeStruct((4,) + ff_up.shape, BF),
            jax.ShapeDtypeStruct(tail_shape, F32),
        ),
        in_specs=[anywhere, inside, inside, anywhere, anywhere, anywhere, anywhere] + [inside] * 5,
        out_specs=(inside, anywhere, anywhere, anywhere, inside),
        scratch_shapes=[
            pltpu.VMEM((2, fsdp_count, tokens, kv_cols), BF),
            kv_all,
            kv_all,
            kv_all,
            pair((tokens, kv_cols)),
            ring((tokens, kv_cols)),
            wide,
            wide,
            wide,
            wide,
            pltpu.VMEM((tokens, width), F32),
            pltpu.VMEM(attn_parts.shape, BF),
            pltpu.VMEM(attn_shape, BF),
            pltpu.VMEM((part, width), BF),
            pair(attn_shape),
            ring(attn_shape),
            pltpu.VMEM(ff_up.shape, BF),
            pltpu.VMEM((2,) + ff_up.shape, BF),
            pltpu.VMEM(ff_up.shape, BF),
            pltpu.VMEM((tokens, kv_cols), BF),
            pltpu.VMEM((fsdp_count,) + tail_shape, F32),
            pair(tail_shape),
            ring(tail_shape),
            pltpu.VMEM((2,) + tail_shape, BF),
            pltpu.VMEM((2,) + tail_shape, BF),
            dma((7,)),
            dma((2, 2)),
            dma((2, fsdp_count)),
            ring_sems,
            dma((2, 2)),
            dma((2, 2)),
            ring_sems,
            dma((2, 2, 2)),
            dma((2, 2)),
            dma((2, 4)),
            ring_sems,
            dma((2, 2)),
            dma((2, 3)),
            dma((2, 3)),
            dma((3,)),
        ],
        compiler_params=pltpu.CompilerParams(
            collective_id=2, has_side_effects=True, vmem_limit_bytes=61 << 20
        ),
        cost_estimate=COST,
        name="closing",
    )(
        kv_parts,
        query_rows,
        q_weight,
        attn_parts,
        ff_up,
        ff_down,
        ff_rest,
        resid_grad,
        hidden,
        kv_weight,
        attn_in,
        mlp_vectors,
    )


def attn_turned_kernel(order, rows_ref, query_ref, proj_ref, out_ref):
    part, cols = proj_ref.shape[0], query_ref.shape[1]
    grad = dot_rows(rows_ref[...], query_ref[...]).astype(BF)
    lines = out_ref.shape[1] - part
    out_ref[0, :part] = proj_ref[...]
    for k in range(grad.shape[0] // lines):
        out_ref[0, part:, k * cols : (k + 1) * cols] = grad[k * lines : (k + 1) * lines]


def attn_turned(order, rows, query_rows, proj_sum, shard):
    count, width = rows.shape
    cols = query_rows.shape[1]
    chunks = order.shape[0]
    part = proj_sum.shape[0] // chunks
    folds = width // cols
    lines = shard // folds
    if shard % 128:
        grad = dot_rows(rows, query_rows).astype(BF).reshape(chunks, folds, lines, cols)
        grad = grad.transpose(0, 2, 1, 3).reshape(chunks, lines, width)
        both = jnp.concatenate([proj_sum.reshape(chunks, part, width), grad], axis=1)
        return jnp.stack([lax.dynamic_index_in_dim(both, order[i], 0, False) for i in range(chunks)])
    return pl.pallas_call(
        attn_turned_kernel,
        out_shape=jax.ShapeDtypeStruct((chunks, part + lines, width), BF),
        grid_spec=pltpu.PrefetchScalarGridSpec(
            num_scalar_prefetch=1,
            grid=(chunks,),
            in_specs=[
                pl.BlockSpec((count, shard), lambda n, o: (0, o[n])),
                pl.BlockSpec((count, cols), lambda n, o: (0, 0)),
                pl.BlockSpec((part, width), lambda n, o: (o[n], 0)),
            ],
            out_specs=pl.BlockSpec((1, part + lines, width), lambda n, o: (n, 0, 0)),
        ),
        compiler_params=pltpu.CompilerParams(vmem_limit_bytes=30 << 20),
        cost_estimate=COST,
        name="attn_turned",
    )(order, rows, query_rows, proj_sum)


def rows_kernel(place, *refs):
    *ins, out = refs
    rows = ins[0].shape[0]
    for i, ref in enumerate(ins):
        out[pl.ds(pl.multiple_of((place[0] ^ i) * rows, rows), rows), :] = ref[...].astype(F32)


def stack_rows(place, pieces, tile):
    rows, width = pieces[0].shape
    return pl.pallas_call(
        rows_kernel,
        out_shape=jax.ShapeDtypeStruct((len(pieces) * rows, width), F32),
        grid_spec=pltpu.PrefetchScalarGridSpec(
            num_scalar_prefetch=1,
            grid=(width // tile,),
            in_specs=[pl.BlockSpec((rows, tile), lambda n, p: (0, n))] * len(pieces),
            out_specs=pl.BlockSpec((len(pieces) * rows, tile), lambda n, p: (0, n)),
        ),
        compiler_params=pltpu.CompilerParams(vmem_limit_bytes=40 << 20),
        cost_estimate=COST,
        name="stack_rows",
    )(place, *pieces)


def qkv_kernel(place, q_ref, tail_ref, out_ref):
    _, lines, width = q_ref.shape
    rows = out_ref.shape[0]
    folds = rows // lines
    cols = width // folds
    for i in range(q_ref.shape[0]):
        start = pl.multiple_of((place[0] ^ i) * cols, cols)
        for k in range(folds):
            part = q_ref[i, :, k * cols : (k + 1) * cols].astype(F32)
            out_ref[k * lines : (k + 1) * lines, pl.ds(start, cols)] = part
    out_ref[:, width:] = tail_ref[:rows, : out_ref.shape[1] - width]


def place_qkv(place, q_pieces, tail, rows, cols):
    return pl.pallas_call(
        qkv_kernel,
        out_shape=jax.ShapeDtypeStruct((rows, cols), F32),
        in_specs=[pl.BlockSpec(memory_space=pltpu.SMEM)] + [pl.BlockSpec(memory_space=pltpu.VMEM)] * 2,
        out_specs=pl.BlockSpec(memory_space=pltpu.VMEM),
        compiler_params=pltpu.CompilerParams(vmem_limit_bytes=30 << 20),
        cost_estimate=COST,
        name="place_qkv",
    )(place, q_pieces, tail)


def cols_kernel(place, *refs):
    *ins, out = refs
    cols = ins[0].shape[1]
    for i, ref in enumerate(ins):
        out[:, pl.ds(pl.multiple_of((place[0] ^ i) * cols, cols), cols)] = ref[...].astype(F32)


def stack_cols(place, pieces, cols):
    rows, width = pieces[0].shape
    count = len(pieces)
    if cols % 128:
        ordered = jnp.stack([lax.dynamic_index_in_dim(jnp.stack(pieces), place[0] ^ i, 0, False) for i in range(count)])
        ordered = ordered.reshape(count, rows, width // cols, cols).transpose(1, 2, 0, 3)
        return ordered.reshape(rows, count * width).astype(F32)
    return pl.pallas_call(
        cols_kernel,
        out_shape=jax.ShapeDtypeStruct((rows, count * width), F32),
        grid_spec=pltpu.PrefetchScalarGridSpec(
            num_scalar_prefetch=1,
            grid=(width // cols,),
            in_specs=[pl.BlockSpec((rows, cols), lambda n, p: (0, n))] * count,
            out_specs=pl.BlockSpec((rows, count * cols), lambda n, p: (0, n)),
        ),
        compiler_params=pltpu.CompilerParams(vmem_limit_bytes=40 << 20),
        cost_estimate=COST,
        name="stack_cols",
    )(place, *pieces)


def layer_norm(values):
    mean = jnp.mean(values, axis=-1, keepdims=True)
    center = values - mean
    inverse = lax.rsqrt(jnp.mean(center * center, axis=-1, keepdims=True) + EPS)
    return center * inverse, inverse


def norm_back(grad, normed, inverse):
    return inverse * (
        grad
        - jnp.mean(grad, axis=-1, keepdims=True)
        - normed * jnp.mean(grad * normed, axis=-1, keepdims=True)
    )


def gelu_tanh(values):
    return jax.nn.gelu(values, approximate=True)


def shards(
    hidden_in,
    out_cotangent,
    positions,
    block_mask,
    norm_gain,
    norm_bias,
    qkv_weight,
    proj_weight,
    mlp_gain,
    mlp_bias,
    fc_weight,
    down_weight,
):
    seq_count = lax.axis_size("seq")
    fsdp_count = lax.axis_size("fsdp")
    s = lax.axis_index("seq")
    f = lax.axis_index("fsdp")
    ring = Ring(fsdp_count)
    count = hidden_in.shape[1]
    width = hidden_in.shape[2]
    length = positions.shape[1]
    blocks = length // BLOCK
    shard = qkv_weight.shape[0]
    ff = fc_weight.shape[1]
    ff_shard = down_weight.shape[0]
    heads_here = HEADS // seq_count
    head_cols = heads_here * HD
    quarter = ff_shard // seq_count
    tokens_here = MB * count
    group = seq_count * tokens_here

    chunk_ids = jnp.stack([(s ^ i) * fsdp_count + f for i in range(seq_count)]).astype(jnp.int32)
    token_ids = chunk_ids[:, None] * count + jnp.arange(count, dtype=jnp.int32)[None]
    first = token_ids[:, None, :] - jnp.stack(
        [lax.dynamic_slice_in_dim(positions, chunk_ids[i] * count, count, 1) for i in range(seq_count)]
    )
    first = first[:, :, None, :]
    high_tiles = (chunk_ids * count + count - 1) // BLOCK + 1
    tables = jnp.concatenate(
        [
            jnp.broadcast_to(chunk_ids[None, :, None], (MB, seq_count, 1)),
            (first[:, :, 0, :1] // BLOCK).transpose(1, 0, 2),
            jnp.broadcast_to(high_tiles[None, :, None], (MB, seq_count, 1)),
            jnp.zeros((MB, seq_count, 1), jnp.int32),
            jnp.stack([block_mask[:, (chunk_ids[i] * count) // BLOCK] for i in range(seq_count)], axis=1),
        ],
        axis=2,
    ).reshape(-1)

    place = jnp.stack([s, f]).astype(jnp.int32)
    part = shard // seq_count
    down_own = lax.dynamic_slice_in_dim(down_weight, s * quarter, quarter, 0)
    if quarter % 128:
        fc_weight = lax.dynamic_slice_in_dim(
            fc_weight.reshape(shard, fsdp_count, seq_count, quarter), s, 1, 2
        ).reshape(shard, fsdp_count * quarter)

    span = 32
    vectors = jnp.stack([norm_gain, norm_bias, mlp_gain, mlp_bias])
    padded = jnp.pad(vectors, ((0, span - 4), (0, 2 * HD - shard)))
    own_kv = jnp.concatenate([qkv_weight[:, width:], padded], axis=0)
    hidden_own = hidden_in.reshape(tokens_here, width)
    cotangent = out_cotangent.reshape(tokens_here, width)
    hidden_all, kv_ring, q_ring, proj_ring, kv_all, fc_all, cotangent_all = opening(
        hidden_own, own_kv, qkv_weight, proj_weight, fc_weight, cotangent, fsdp_count, head_cols
    )
    cotangent_all = cotangent_all.reshape(group, width)
    down_first, kv_all = lax.optimization_barrier((down_own, kv_all))
    down_given = (lax.ppermute(down_first, "fsdp", ring.up), lax.ppermute(down_first, "fsdp", ring.down))
    kv_weight = kv_ring[:, :shard].reshape(width, 2 * HD)
    vectors = kv_ring[:, shard : shard + 4, :shard].transpose(1, 0, 2).reshape(4, width).astype(F32)
    gain_one, bias_one, gain_two, bias_two = vectors[0], vectors[1], vectors[2], vectors[3]
    q_weight = q_ring.reshape(width, head_cols)
    proj_full = proj_ring.reshape(head_cols, width)
    kv_all = kv_all.reshape(seq_count * fsdp_count, MB, count, 2 * HD)
    normed_all, _ = layer_norm(hidden_all.reshape(group, width).astype(F32))
    attn_in = (normed_all * gain_one + bias_one).astype(BF)
    attn_in = lax.optimization_barrier(attn_in)
    own_attn_in = attn_in[:tokens_here]
    queries = dot_plain(attn_in, q_weight).astype(BF).reshape(seq_count, MB, count, head_cols)
    heads_out, logs = attend(tables, first, queries, kv_all, blocks)
    heads_rows = heads_out.reshape(group, head_cols)

    far = fsdp_count // 2 - 1
    low = lax.dynamic_index_in_dim(fc_all, ring.owner(1 - far), 0, keepdims=False)
    high = lax.dynamic_index_in_dim(fc_all, ring.owner(far - 1), 0, keepdims=False)
    low, high = lax.ppermute(low, "fsdp", ring.up), lax.ppermute(high, "fsdp", ring.down)
    low, high, heads_rows = lax.optimization_barrier((low, high, heads_rows))
    last_low = lax.ppermute(low[: shard // 2], "fsdp", ring.up)
    last_high = lax.ppermute(high[shard // 2 :], "fsdp", ring.down)
    for piece, step, row in ((low, -far, 0), (high, far, 0), (last_low, far + 1, 0), (last_high, far + 1, shard // 2)):
        fc_all = lax.dynamic_update_slice(fc_all, piece[None], (ring.owner(step), row, 0))

    mlp_in, resid, down_all = bridge(
        heads_rows, proj_full, hidden_own, vectors[2:], down_own, down_given, fsdp_count
    )
    mlp_in = mlp_in.reshape(group, width)
    activ, pre_grad, mlp_in_parts = middle(mlp_in, cotangent_all, fc_all, down_all, 2 * BLOCK)
    branch, result, resid_grad, mlp_vectors, ff_up, ff_down, ff_rest = feedback(
        mlp_in_parts.reshape(seq_count, tokens_here, width),
        mlp_in,
        pre_grad,
        activ,
        cotangent_all,
        down_all,
        resid,
        gain_two[None],
        fsdp_count,
        shard,
    )
    branch = branch.reshape(group, width)
    steps = ring.steps()
    flow = Flow(ring, ring.scatter(ff_up, ff_down, lambda n: ff_rest[steps.index(n) - 5]))
    heads_grad = dot_cols(branch, proj_full).astype(BF).reshape(seq_count, MB, count, head_cols)
    query_grads, kv_grads = attend_back(
        tables, first, queries, kv_all, heads_out, logs, heads_grad, blocks
    )
    query_grads, kv_grads = flow.advance((query_grads, kv_grads))
    query_rows = query_grads.reshape(group, head_cols)

    proj_sum = dot_rows(heads_rows, branch).astype(BF)
    attn_parts = attn_turned(ring.order(), attn_in, query_rows, proj_sum, shard)
    ff_up, ff_down = flow.finish()
    grad_input, q_pieces, proj_pieces, ff_all, tail = closing(
        kv_grads.reshape(seq_count, fsdp_count, tokens_here, 2 * HD),
        query_rows,
        q_weight,
        attn_parts,
        (ff_up, ff_down, ff_rest),
        resid_grad,
        hidden_own,
        kv_ring,
        own_attn_in,
        mlp_vectors,
        shard,
    )
    vector_grads = tail[shard : shard + 4, :shard]
    ff_pieces = [ff_all[i] for i in range(seq_count)]
    grad_fc = stack_cols(place, [piece[:shard] for piece in ff_pieces], quarter)
    grad_down = stack_rows(place, [piece[shard:] for piece in ff_pieces], BLOCK)
    grad_proj = stack_rows(place, [proj_pieces[i] for i in range(seq_count)], width)
    grad_qkv = place_qkv(place, q_pieces, tail, shard, qkv_weight.shape[1])
    return (
        result.reshape(hidden_in.shape),
        grad_input.reshape(hidden_in.shape),
        vector_grads[0],
        vector_grads[1],
        grad_qkv,
        grad_proj,
        vector_grads[2],
        vector_grads[3],
        grad_fc,
        grad_down,
    )


def solution(mesh):
    rows = P(None, ("seq", "fsdp"), None)
    vector = P("fsdp")
    matrix = P("fsdp", None)
    in_specs = (rows, rows, P(), P(), vector, vector, matrix, matrix, vector, vector, matrix, matrix)
    out_specs = (rows, rows, vector, vector, matrix, matrix, vector, vector, matrix, matrix)
    return jax.shard_map(shards, mesh=mesh, in_specs=in_specs, out_specs=out_specs, check_vma=False)
```

```python
import functools
import math

import jax
import jax.numpy as jnp
from jax import lax
from jax.experimental import pallas as pl
from jax.experimental.pallas import tpu as pltpu
from jax.sharding import PartitionSpec as P

HEADS = 16
HD = 128
MB = 2
BLOCK = 256
EPS = 1e-05
NEG_FILL = -1e30
SCALE = HD ** (-0.5)
LOG2E = math.log2(math.e)
BF = jnp.bfloat16
COST = pl.CostEstimate(flops=0, bytes_accessed=0, transcendentals=0)
F32 = jnp.float32


def dot_rows(left, right):
    return lax.dot_general(left, right, (((0,), (0,)), ((), ())), preferred_element_type=F32)


def dot_cols(left, right):
    return lax.dot_general(left, right, (((1,), (1,)), ((), ())), preferred_element_type=F32)


def dot_plain(left, right):
    return lax.dot_general(left, right, (((1,), (0,)), ((), ())), preferred_element_type=F32)


def ring_order(count):
    return [2 * i for i in range(count // 2)] + [2 * i + 1 for i in reversed(range(count // 2))]


class Ring:
    def __init__(self, count):
        order = ring_order(count)
        self.count = count
        self.up = [(order[i], order[(i + 1) % count]) for i in range(count)]
        self.down = [(order[(i + 1) % count], order[i]) for i in range(count)]
        place = lax.axis_index("fsdp")
        half = count // 2
        self.place = place
        self.at = jnp.where(place % 2 == 0, place // 2, count - 1 - place // 2)

    def owner(self, step):
        count, half = self.count, self.count // 2
        at = lax.rem(self.at + (step + count), count)
        return jnp.where(at < half, 2 * at, 2 * (count - 1 - at) + 1)

    def steps(self):
        half = self.count // 2
        return [half] + [sign * n for n in range(half - 1, 0, -1) for sign in (1, -1)] + [0]

    def order(self):
        return jnp.stack([self.owner(n) for n in self.steps()]).astype(jnp.int32)

    def scatter(self, up, down, chunk):
        for step in range(self.count // 2 - 3, 0, -1):
            up = lax.ppermute(up, "fsdp", self.up)
            down = lax.ppermute(down, "fsdp", self.down)
            up, down = yield up, down
            up = (chunk(step).astype(F32) + up.astype(F32)).astype(BF)
            down = (chunk(-step).astype(F32) + down.astype(F32)).astype(BF)
        return up, down


class Flow:
    def __init__(self, ring, steps):
        self.ring, self.steps, self.result = ring, steps, None
        self.pending = next(steps)

    def advance(self, values=()):
        for _ in range(max(1, self.ring.count // 8)):
            if self.result is None:
                self.pending, values = lax.optimization_barrier((self.pending, values))
                try:
                    self.pending = self.steps.send(self.pending)
                except StopIteration as end:
                    self.result = end.value
        return values

    def finish(self):
        while self.result is None:
            self.advance()
        return self.result


def attend_kernel(tables, q_ref, kv_ref, first_ref, out_ref, log_ref, stack, high, total, result, *, heads, blocks):
    batch, piece = pl.program_id(0), pl.program_id(1)
    count = q_ref.shape[2]
    base = (batch * pl.num_programs(1) + piece) * (blocks + 4)
    chunk, low_tile, high_tile = tables[base], tables[base + 1], tables[base + 2]
    for h in range(heads):
        stack[h * count : (h + 1) * count, :] = q_ref[0, 0, :, h * HD : (h + 1) * HD]
    high[...] = jnp.full_like(high, NEG_FILL)
    total[...] = jnp.zeros_like(total)
    result[...] = jnp.zeros_like(result)
    tokens = chunk * count + lax.broadcasted_iota(jnp.int32, (1, count), 1)
    first = first_ref[0, 0]

    def step(tile, carry):
        @pl.when(tables[base + 4 + tile] != 0)
        def _():
            part = kv_ref[pl.ds(2 * tile, 2), 0].reshape(BLOCK, 2 * HD)
            keys, values = part[:, :HD], part[:, HD:]
            scores = dot_cols(keys, stack[...])
            index = tile * BLOCK + lax.broadcasted_iota(jnp.int32, (BLOCK, count), 0)
            allowed = (index <= tokens) & (index >= first)
            weights, scales = [], []
            for h in range(heads):
                lanes = slice(h * count, (h + 1) * count)
                score = jnp.where(allowed, scores[:, lanes] * (SCALE * LOG2E), NEG_FILL)
                old = high[:, lanes]
                new = jnp.maximum(old, jnp.max(score, axis=0, keepdims=True))
                weight = jnp.exp2(score - new)
                scale = jnp.exp2(old - new)
                high[:, lanes] = new
                total[:, lanes] = total[:, lanes] * scale + jnp.sum(weight, axis=0, keepdims=True)
                weights.append(weight.astype(BF))
                scales.append(scale)
            added = dot_rows(values, jnp.concatenate(weights, axis=1))
            result[...] = result[...] * jnp.concatenate(scales, axis=1) + added

        return carry

    lax.fori_loop(low_tile, high_tile, step, 0)
    final = result[...] / total[...]
    logs = high[...] + jnp.log2(total[...])
    for h in range(heads):
        lanes = slice(h * count, (h + 1) * count)
        out_ref[0, 0, :, h * HD : (h + 1) * HD] = final[:, lanes].T.astype(BF)
        log_ref[0, 0, h : h + 1, :] = logs[:, lanes]


def attend_back_kernel(
    tables,
    q_ref,
    kv_ref,
    first_ref,
    out_ref,
    log_ref,
    grad_ref,
    dq_ref,
    dkv_ref,
    stack,
    grads,
    logs,
    deltas,
    dq_sum,
    dkv_sum,
    *,
    heads,
    blocks,
):
    batch, piece = pl.program_id(0), pl.program_id(1)
    count = q_ref.shape[2]
    base = (batch * pl.num_programs(1) + piece) * (blocks + 4)
    chunk, low_tile, high_tile = tables[base], tables[base + 1], tables[base + 2]

    @pl.when(piece == 0)
    def _():
        dkv_sum[...] = jnp.zeros_like(dkv_sum)

    for h in range(heads):
        rows = slice(h * count, (h + 1) * count)
        cols = slice(h * HD, (h + 1) * HD)
        stack[rows, :] = q_ref[0, 0, :, cols]
        grad = grad_ref[0, 0, :, cols]
        grads[rows, :] = grad
        product = grad.astype(F32) * out_ref[0, 0, :, cols].astype(F32)
        deltas[:, rows] = jnp.sum(product.T, axis=0, keepdims=True)
        logs[:, rows] = log_ref[0, 0, h : h + 1, :]
    dq_sum[...] = jnp.zeros_like(dq_sum)
    tokens = chunk * count + lax.broadcasted_iota(jnp.int32, (1, count), 1)
    first = first_ref[0, 0]

    def step(tile, carry):
        @pl.when(tables[base + 4 + tile] != 0)
        def _():
            part = kv_ref[pl.ds(2 * tile, 2), 0].reshape(BLOCK, 2 * HD)
            keys, values = part[:, :HD], part[:, HD:]
            scores = dot_cols(keys, stack[...])
            pulls = dot_cols(values, grads[...])
            index = tile * BLOCK + lax.broadcasted_iota(jnp.int32, (BLOCK, count), 0)
            allowed = (index <= tokens) & (index >= first)
            weights, score_grads = [], []
            for h in range(heads):
                lanes = slice(h * count, (h + 1) * count)
                score = jnp.where(allowed, scores[:, lanes] * (SCALE * LOG2E), NEG_FILL)
                weight = jnp.exp2(score - logs[:, lanes])
                weights.append(weight.astype(BF))
                score_grads.append((weight * (pulls[:, lanes] - deltas[:, lanes])).astype(BF))
            weight = jnp.concatenate(weights, axis=1)
            score_grad = jnp.concatenate(score_grads, axis=1)
            dv = dot_plain(weight, grads[...])
            dk = dot_plain(score_grad, stack[...])
            dq_sum[...] += dot_rows(keys, score_grad)
            both = jnp.concatenate([dk, dv], axis=1).reshape(2, BLOCK // 2, 2 * HD)
            dkv_sum[pl.ds(2 * tile, 2)] += both

        return carry

    lax.fori_loop(low_tile, high_tile, step, 0)
    for h in range(heads):
        lanes = slice(h * count, (h + 1) * count)
        dq_ref[0, 0, :, h * HD : (h + 1) * HD] = (dq_sum[:, lanes] * SCALE).T.astype(BF)

    @pl.when(piece == pl.num_programs(1) - 1)
    def _():
        dkv_ref[:, 0, :, :HD] = (dkv_sum[:, :, :HD] * SCALE).astype(BF)
        dkv_ref[:, 0, :, HD:] = dkv_sum[:, :, HD:].astype(BF)


def attend(tables, first, queries, key_values, blocks):
    pieces, batches, count, width = queries.shape
    heads = width // HD
    chunks = key_values.shape[0]
    row_spec = pl.BlockSpec((1, 1, count, width), lambda b, i, t: (i, b, 0, 0))
    kv_spec = pl.BlockSpec((chunks, 1, count, 2 * HD), lambda b, i, t: (0, b, 0, 0))
    first_spec = pl.BlockSpec((1, 1, 1, count), lambda b, i, t: (i, b, 0, 0))
    log_spec = pl.BlockSpec((1, 1, heads, count), lambda b, i, t: (i, b, 0, 0))
    rows = heads * count
    return pl.pallas_call(
        functools.partial(attend_kernel, heads=heads, blocks=blocks),
        out_shape=(
            jax.ShapeDtypeStruct(queries.shape, BF),
            jax.ShapeDtypeStruct((pieces, batches, heads, count), F32),
        ),
        grid_spec=pltpu.PrefetchScalarGridSpec(
            num_scalar_prefetch=1,
            grid=(batches, pieces),
            in_specs=[row_spec, kv_spec, first_spec],
            out_specs=[row_spec, log_spec],
            scratch_shapes=[
                pltpu.VMEM((rows, HD), BF),
                pltpu.VMEM((1, rows), F32),
                pltpu.VMEM((1, rows), F32),
                pltpu.VMEM((HD, rows), F32),
            ],
        ),
        compiler_params=pltpu.CompilerParams(vmem_limit_bytes=40 << 20),
        cost_estimate=COST,
        name="attend",
    )(tables, queries, key_values, first)


def attend_back(tables, first, queries, key_values, out, logs, grads, blocks):
    pieces, batches, count, width = queries.shape
    heads = width // HD
    chunks = key_values.shape[0]
    row_spec = pl.BlockSpec((1, 1, count, width), lambda b, i, t: (i, b, 0, 0))
    kv_spec = pl.BlockSpec((chunks, 1, count, 2 * HD), lambda b, i, t: (0, b, 0, 0))
    first_spec = pl.BlockSpec((1, 1, 1, count), lambda b, i, t: (i, b, 0, 0))
    log_spec = pl.BlockSpec((1, 1, heads, count), lambda b, i, t: (i, b, 0, 0))
    rows = heads * count
    return pl.pallas_call(
        functools.partial(attend_back_kernel, heads=heads, blocks=blocks),
        out_shape=(
            jax.ShapeDtypeStruct(queries.shape, BF),
            jax.ShapeDtypeStruct(key_values.shape, BF),
        ),
        grid_spec=pltpu.PrefetchScalarGridSpec(
            num_scalar_prefetch=1,
            grid=(batches, pieces),
            in_specs=[row_spec, kv_spec, first_spec, row_spec, log_spec, row_spec],
            out_specs=[row_spec, kv_spec],
            scratch_shapes=[
                pltpu.VMEM((rows, HD), BF),
                pltpu.VMEM((rows, HD), BF),
                pltpu.VMEM((1, rows), F32),
                pltpu.VMEM((1, rows), F32),
                pltpu.VMEM((HD, rows), F32),
                pltpu.VMEM((chunks, count, 2 * HD), F32),
            ],
        ),
        compiler_params=pltpu.CompilerParams(vmem_limit_bytes=60 << 20),
        cost_estimate=COST,
        name="attend_back",
    )(tables, queries, key_values, first, out, logs, grads)


def neighbours(count):
    s, f = lax.axis_index("seq"), lax.axis_index("fsdp")
    half = count // 2
    at = jnp.where(lax.rem(f, 2) == 0, f // 2, count - 1 - f // 2)

    def owner(step):
        place = lax.rem(at + (step + count), count)
        return jnp.where(place < half, 2 * place, 2 * (count - 1 - place) + 1)

    chip = lax.rem(s + 2, 4)
    core = s + 1 - 2 * lax.rem(s, 2)
    return s, f, owner, (s, owner(1)), (s, owner(-1)), (chip, f), (core, f)


def greet(*devices):
    barrier = pltpu.get_barrier_semaphore()
    for device in devices:
        pl.semaphore_signal(barrier, inc=1, device_id=device, device_id_type=pl.DeviceIdType.MESH)
    pl.semaphore_wait(barrier, len(devices))


def met(device, s, f):
    return (device[0] == s) & (device[1] == f)


def greet_also(devices, sources, own, s, f):
    barrier = pltpu.get_barrier_semaphore()
    for device in devices:
        pl.semaphore_signal(barrier, inc=1, device_id=device, device_id_type=pl.DeviceIdType.MESH)
    for device in sources:

        @pl.when(jnp.logical_not(met(device, s, f)))
        def _():
            pl.semaphore_signal(barrier, inc=1, device_id=device, device_id_type=pl.DeviceIdType.MESH)

    pl.semaphore_wait(barrier, len(devices) + len(sources) - own)


class Maybe:
    def __init__(self, source, target, landing, send_sem, recv_sem, landing_sem, local_sem, device, sender, s, f):
        self.here, self.from_here = met(device, s, f), met(sender, s, f)
        kind = dict(device_id_type=pl.DeviceIdType.MESH)
        self.copy = pltpu.make_async_remote_copy(source, target, send_sem, recv_sem, device_id=device, **kind)
        self.into = pltpu.make_async_remote_copy(source, landing, send_sem, landing_sem, device_id=device, **kind)
        self.stay = pltpu.make_async_copy(source, target, local_sem)

        @pl.when(self.here)
        def _():
            self.stay.start()

        @pl.when(jnp.logical_not(self.here))
        def _():
            self.copy.start()

    def arrived(self):
        @pl.when(jnp.logical_not(self.from_here))
        def _():
            self.into.wait_recv()

    def left(self):
        @pl.when(self.here)
        def _():
            self.stay.wait()

        @pl.when(jnp.logical_not(self.here))
        def _():
            self.copy.wait_send()


def send(source, target, sems, index, device):
    copy = pltpu.make_async_remote_copy(
        src_ref=source,
        dst_ref=target,
        send_sem=sems.at[(0,) + index],
        recv_sem=sems.at[(1,) + index],
        device_id=device,
        device_id_type=pl.DeviceIdType.MESH,
    )
    copy.start()
    return copy


class KernelRing:
    def __init__(self, count, own, slots, sems, owner, up, down):
        self.count, self.own, self.slots, self.sems = count, own, slots, sems
        self.owner, self.up, self.down = owner, up, down
        self.copies = {}

    def start(self, step, given=None):
        half = self.slots.shape[1] // 2
        for way, device in enumerate((self.up, self.down)):
            slot = self.slots.at[self.owner((1 - step) if way == 0 else (step - 1))]
            source = self.own if step == 1 else slot
            if given is not None:
                source = given[way]
            if step == self.count // 2:
                rows = pl.ds(way * half, half)
                source, slot = source.at[rows], slot.at[rows]
            self.copies[way, step] = send(source, slot, self.sems, (way, step - 1), device)

    def arrived(self, step):
        self.copies[0, step].wait_recv()
        self.copies[1, step].wait_recv()

    def finish(self):
        for copy in self.copies.values():
            copy.wait_send()


def opening_kernel(
    hidden,
    kv_own,
    qkv_weight,
    proj_weight,
    fc_weight,
    cot,
    hidden_out,
    kvw_out,
    qw_out,
    proj_out,
    kv_out,
    fc_out,
    cot_out,
    weights,
    mine,
    q_own,
    fc_own,
    hid_chip,
    hid_core,
    kvw_sems,
    q_sems,
    proj_sems,
    kv_sems,
    kv_chip,
    kv_core,
    kv_far,
    fc_sems,
    cot_sems,
    move_sems,
    cut_sems,
    local,
    *,
    count,
    shard,
):
    s, f, owner, up, down, chip, core = neighbours(count)
    steps = count // 2
    per = count // 4
    target = (f // per, 4 * lax.rem(f, per) + s)
    source = (lax.rem(f, 4), s * per + f // 4)
    own_goes = met(target, s, f).astype(jnp.int32)
    greet_also((up, down, chip, core), (source,), own_goes, s, f)
    part = proj_out.shape[1]
    q_cols = qw_out.shape[2]
    q_cut = pltpu.make_async_copy(
        qkv_weight.at[:, pl.ds(pl.multiple_of(s * q_cols, q_cols), q_cols)], q_own, local.at[4]
    )
    q_cut.start()
    proj_own = proj_out.at[f]
    rings = [
        KernelRing(count, own, slots, sems, owner, up, down)
        for own, slots, sems in (
            (kv_own, kvw_out, kvw_sems),
            (q_own, qw_out, q_sems),
            (proj_own, proj_out, proj_sems),
            (fc_own, fc_out, fc_sems),
        )
    ]
    kvw, qw, proj, fc = rings
    kvw.start(1)
    moved = Maybe(
        proj_weight.at[pl.ds(pl.multiple_of(s * part, part), part)],
        proj_out.at[target[1]],
        proj_own,
        move_sems.at[0],
        move_sems.at[1],
        move_sems.at[1],
        move_sems.at[2],
        target,
        source,
        s,
        f,
    )
    if fc_weight.shape[1] == fc_out.shape[2]:
        cuts = [pltpu.make_async_copy(fc_weight, fc_own, cut_sems.at[0])]
    else:
        cols = fc_out.shape[2] // count
        cuts = [
            pltpu.make_async_copy(
                fc_weight.at[:, pl.ds(pl.multiple_of((g * 4 + s) * cols, cols), cols)],
                fc_own.at[:, pl.ds(g * cols, cols)],
                cut_sems.at[g],
            )
            for g in range(count)
        ]
    for copy in cuts:
        copy.start()
    rows = hidden.shape[0] // 2
    halves = [pl.ds(i * rows, rows) for i in range(2)]
    across = [send(hidden.at[half], hidden_out.at[2, half], hid_chip, (i,), chip) for i, half in enumerate(halves)]
    pair = [send(hidden, hidden_out.at[1], hid_core, (2,), core)]
    stays = [
        pltpu.make_async_copy(source, target, local.at[i])
        for i, (source, target) in enumerate(
            (
                (hidden, hidden_out.at[0]),
                (kv_own, kvw_out.at[f]),
                (cot, cot_out.at[0]),
            )
        )
    ]
    for copy in stays:
        copy.start()
    q_cut.wait()
    for copy in cuts:
        copy.wait()
    for i, (source, target) in enumerate(((q_own, qw_out.at[f]), (fc_own, fc_out.at[f]))):
        stays.append(pltpu.make_async_copy(source, target, local.at[3 if i == 0 else 5]))
        stays[-1].start()
    values = hidden[...].astype(F32)
    mean = jnp.mean(values, axis=-1, keepdims=True)
    center = values - mean
    inverse = lax.rsqrt(jnp.mean(center * center, axis=-1, keepdims=True) + EPS)
    for step in range(2, steps + 1):
        kvw.arrived(step - 1)
        kvw.start(step)
    qw.start(1)
    fc.start(1)
    kvw.arrived(steps)
    stays[1].wait()
    load = pltpu.make_async_copy(kvw_out, weights, local.at[6])
    load.start()
    load.wait()
    total = jnp.zeros((hidden.shape[0], kvw_out.shape[2]), F32)
    for t in range(count):
        cols = slice(t * shard, (t + 1) * shard)
        normed = (hidden[:, cols].astype(F32) - mean) * inverse
        gain = weights[t, shard : shard + 1, :shard].astype(F32)
        bias = weights[t, shard + 1 : shard + 2, :shard].astype(F32)
        total += dot_plain((normed * gain + bias).astype(BF), weights[t, :shard, :])
    mine[...] = total.astype(BF)

    spread = KernelRing(count, mine, kv_out.at[s], kv_sems, owner, up, down)
    spread.start(1)
    keep = pltpu.make_async_copy(mine, kv_out.at[s, f], local.at[7])
    keep.start()
    kv_across, kv_pair = [], []

    def pass_on(source, place):
        index = (len(kv_across),)
        kv_across.append((place, send(source, kv_out.at[s, place], kv_chip, index, chip)))
        kv_pair.append(send(source, kv_out.at[s, place], kv_core, index, core))

    pass_on(mine, f)
    for i, half in enumerate(halves):
        across[i].wait_recv()
        pair.append(send(hidden_out.at[2, half], hidden_out.at[2 + 1, half], hid_core, (i,), core))
    for step in range(1, steps + 1):
        spread.arrived(step)
        qw.arrived(step)
        if step < steps:
            spread.start(step + 1)
            qw.start(step + 1)
            for place in (owner(-step), owner(step)):
                pass_on(kv_out.at[s, place], place)
        else:
            pass_on(kv_out.at[s, owner(steps)], owner(steps))
        if step == 1:
            moved.arrived()
            moved.left()
            proj.start(1)
            cot_across = send(cot, cot_out.at[2], cot_sems, (0,), chip)
            cot_pair = send(cot, cot_out.at[1], cot_sems, (1,), core)
        else:
            proj.arrived(step - 1)
            proj.start(step)
        if step < steps - 1:
            fc.arrived(step)
        if step < steps - 2:
            fc.start(step + 1)
    other = lax.rem(s + 2, 4)
    far = []
    for i, (place, copy) in enumerate(kv_across):
        copy.wait_recv()
        slot = kv_out.at[other, place]
        far.append(send(slot, slot, kv_far, (i,), core))
    cot_across.wait()
    cot_far = send(cot_out.at[2], cot_out.at[3], cot_sems, (2,), core)
    proj.arrived(steps)
    for ring in rings + [spread]:
        ring.finish()
    for copy in [keep, cot_pair, cot_far, stays[0]] + stays[2:]:
        copy.wait()
    for copy in across + [copy for _, copy in kv_across]:
        copy.wait_send()
    for copy in pair + kv_pair + far:
        copy.wait()


def opening(hidden, kv_own, qkv_weight, proj_weight, fc_weight, cot, fsdp_count, q_cols):
    count, width = hidden.shape
    shard = qkv_weight.shape[0]
    dma = pltpu.SemaphoreType.DMA
    ring = dma((2, 2, fsdp_count // 2))
    anywhere = pl.BlockSpec(memory_space=pltpu.HBM)
    inside = pl.BlockSpec(memory_space=pltpu.VMEM)
    return pl.pallas_call(
        functools.partial(opening_kernel, count=fsdp_count, shard=shard),
        out_shape=(
            jax.ShapeDtypeStruct((4,) + hidden.shape, BF),
            jax.ShapeDtypeStruct((fsdp_count,) + kv_own.shape, BF),
            jax.ShapeDtypeStruct((fsdp_count, shard, q_cols), BF),
            jax.ShapeDtypeStruct((fsdp_count, shard // 4, width), BF),
            jax.ShapeDtypeStruct((4, fsdp_count, count, 2 * HD), BF),
            jax.ShapeDtypeStruct((fsdp_count, shard, width), BF),
            jax.ShapeDtypeStruct((4,) + hidden.shape, BF),
        ),
        in_specs=[inside, inside] + [anywhere] * 3 + [inside],
        out_specs=(anywhere,) * 7,
        scratch_shapes=[
            pltpu.VMEM((fsdp_count,) + kv_own.shape, BF),
            pltpu.VMEM((count, 2 * HD), BF),
            pltpu.VMEM((shard, q_cols), BF),
            pltpu.VMEM((shard, width), BF),
            dma((2, 2)),
            dma((2, 3)),
            ring,
            ring,
            ring,
            ring,
            dma((2, fsdp_count)),
            dma((2, fsdp_count)),
            dma((2, fsdp_count)),
            ring,
            dma((2, 3)),
            dma((3,)),
            dma((fsdp_count,)),
            dma((8,)),
        ],
        compiler_params=pltpu.CompilerParams(
            collective_id=1, has_side_effects=True, vmem_limit_bytes=40 << 20
        ),
        cost_estimate=COST,
        name="opening",
    )(hidden, kv_own, qkv_weight, proj_weight, fc_weight, cot)


GELU_A = math.sqrt(2 / math.pi)
GELU_B = 0.044715


def middle_kernel(rows_ref, cot_ref, fc_ref, down_ref, activ_ref, pre_ref, grad_ref, total, *, step):
    tile = pl.program_id(0)
    fc = fc_ref[...].reshape(-1, fc_ref.shape[2])
    down = down_ref[...].reshape(-1, down_ref.shape[2])

    @pl.when(tile == 0)
    def _():
        total[...] = jnp.zeros_like(total)

    for at in range(0, rows_ref.shape[0], step):
        part = slice(at, at + step)
        value = dot_plain(rows_ref[part], fc)
        pull = dot_cols(cot_ref[part], down)
        square = value * value
        bend = jnp.tanh(GELU_A * value * (1.0 + GELU_B * square))
        half = 0.5 * (1.0 + bend)
        activ_ref[part] = (value * half).astype(BF)
        slope = half + 0.5 * value * (1.0 - bend * bend) * (GELU_A * (1.0 + 3.0 * GELU_B * square))
        grad = (pull * slope).astype(BF)
        pre_ref[part] = grad
        total[part] += dot_cols(grad, fc)

    @pl.when(tile == pl.num_programs(0) - 1)
    def _():
        grad_ref[...] = total[...].astype(BF)


def middle(rows, cot, fc_all, down_all, tile):
    count, width = rows.shape
    parts, shard = fc_all.shape[:2]
    quarter = down_all.shape[1]
    hidden = parts * quarter
    per = tile // quarter
    whole = pl.BlockSpec((count, width), lambda n: (0, 0), pipeline_mode=pl.Buffered(1))
    cols = pl.BlockSpec((count, tile), lambda n: (0, n))
    return pl.pallas_call(
        functools.partial(middle_kernel, step=256),
        out_shape=(
            jax.ShapeDtypeStruct((count, hidden), BF),
            jax.ShapeDtypeStruct((count, hidden), BF),
            jax.ShapeDtypeStruct((count, width), BF),
        ),
        grid=(hidden // tile,),
        in_specs=[
            whole,
            whole,
            pl.BlockSpec((parts, shard, tile), lambda n: (0, 0, n)),
            pl.BlockSpec((per, quarter, width), lambda n: (n, 0, 0)),
        ],
        out_specs=(cols, cols, pl.BlockSpec((count, width), lambda n: (0, 0))),
        scratch_shapes=[pltpu.VMEM((count, width), F32)],
        compiler_params=pltpu.CompilerParams(vmem_limit_bytes=60 << 20),
        cost_estimate=COST,
        name="middle",
    )(rows, cot, fc_all, down_all)


def bridge_kernel(
    heads,
    proj,
    hidden,
    vectors,
    down_own,
    first_up,
    first_down,
    mlp_out,
    resid_out,
    down_out,
    far_out,
    far,
    near_out,
    near,
    chip_in,
    mine,
    pair_sems,
    chip_sems,
    spread_chip,
    spread_core,
    down_sems,
    local,
    *,
    count,
):
    s, f, owner, up, down, chip, core = neighbours(count)
    greet(up, down, chip, core)
    steps = count // 2
    tokens = hidden.shape[0]
    ring = KernelRing(count, down_own, down_out, down_sems, owner, up, down)
    ring.start(2, (first_up, first_down))
    stays = [
        pltpu.make_async_copy(down_own, down_out.at[f], local.at[0]),
        pltpu.make_async_copy(first_up, down_out.at[owner(-1)], local.at[2]),
        pltpu.make_async_copy(first_down, down_out.at[owner(1)], local.at[3]),
    ]
    for copy in stays:
        copy.start()

    def part(i):
        return dot_plain(heads[i * tokens : (i + 1) * tokens], proj[...])

    far_out[...] = part(3).astype(BF)
    pairs = [send(far_out, far, pair_sems, (0,), core)]
    near_out[...] = part(1).astype(BF)
    pairs.append(send(near_out, near, pair_sems, (1,), core))
    middle = part(2)
    pairs[0].wait()
    far_out[...] = (middle + far[...].astype(F32)).astype(BF)
    rows = tokens // 2
    halves = [pl.ds(i * rows, rows) for i in range(2)]
    across = [send(far_out.at[half], chip_in.at[half], chip_sems, (i,), chip) for i, half in enumerate(halves)]
    resid_out[...] = hidden[...].astype(F32) + part(0)
    pairs[1].wait()
    resid_out[...] += near[...].astype(F32)
    spread, spread_pair = [], []
    block = 64
    for i, half in enumerate(halves):
        across[i].wait_recv()
        for at in range(i * rows, (i + 1) * rows, block):
            here = slice(at, at + block)
            resid = resid_out[here] + chip_in[here].astype(F32)
            resid_out[here] = resid
            normed, _ = layer_norm(resid)
            mine[here] = (normed * vectors[0:1] + vectors[1:2]).astype(BF)
        spread.append(send(mine.at[half], mlp_out.at[2, half], spread_chip, (i,), chip))
        spread_pair.append(send(mine.at[half], mlp_out.at[1, half], spread_core, (i,), core))
        ring.arrived(i + 2)
        ring.start(i + 3)
    stays.append(pltpu.make_async_copy(mine, mlp_out.at[0], local.at[1]))
    stays[-1].start()
    for i, half in enumerate(halves):
        spread[i].wait_recv()
        spread_pair.append(send(mlp_out.at[2, half], mlp_out.at[3, half], spread_core, (2 + i,), core))
    for step in range(4, steps + 1):
        ring.arrived(step)
        if step < steps:
            ring.start(step + 1)
    ring.finish()
    for copy in across + spread:
        copy.wait_send()
    for copy in spread_pair + stays:
        copy.wait()


def bridge(heads, proj, hidden, vectors, down_own, first, fsdp_count):
    tokens, width = hidden.shape
    quarter = down_own.shape[0]
    dma = pltpu.SemaphoreType.DMA
    anywhere = pl.BlockSpec(memory_space=pltpu.HBM)
    inside = pl.BlockSpec(memory_space=pltpu.VMEM)
    wide = pltpu.VMEM((tokens, width), BF)
    return pl.pallas_call(
        functools.partial(bridge_kernel, count=fsdp_count),
        out_shape=(
            jax.ShapeDtypeStruct((4, tokens, width), BF),
            jax.ShapeDtypeStruct((tokens, width), F32),
            jax.ShapeDtypeStruct((fsdp_count, quarter, width), BF),
        ),
        in_specs=[inside] * 7,
        out_specs=(anywhere, inside, anywhere),
        scratch_shapes=[wide] * 6
        + [
            dma((2, 2)),
            dma((2, 2)),
            dma((2, 2)),
            dma((2, 4)),
            dma((2, 2, fsdp_count // 2)),
            dma((4,)),
        ],
        compiler_params=pltpu.CompilerParams(
            collective_id=3, has_side_effects=True, vmem_limit_bytes=40 << 20
        ),
        cost_estimate=COST,
        name="bridge",
    )(heads, proj, hidden, vectors, down_own, *first)


def feedback_kernel(
    parts,
    mlp_in,
    pre_grad,
    activ,
    cot,
    down_all,
    resid,
    gain,
    branch_out,
    result_out,
    resid_out,
    vectors_out,
    up_out,
    down_out,
    rest_out,
    mlp_here,
    pre_here,
    activ_here,
    cot_here,
    here,
    across_out,
    far,
    near,
    chip_in,
    branch,
    outs_first,
    ins_first,
    outs_next,
    ins_next,
    stage,
    down_here,
    low_here,
    low_far,
    low_near,
    low_chip,
    branch_low,
    pair_sems,
    chip_sems,
    spread_chip,
    spread_core,
    ring_sems,
    low_pair,
    low_across,
    local,
    *,
    count,
    shard,
    turned,
):
    s, f, owner, up, down, chip, core = neighbours(count)
    greet(up, down, chip, core)
    steps = count // 2
    tokens, width = resid.shape
    pairs = [send(parts.at[3], far, pair_sems, (0,), core), send(parts.at[1], near, pair_sems, (1,), core)]
    loads = [
        pltpu.make_async_copy(source, target, local.at[i])
        for i, (source, target) in enumerate(
            (
                (pre_grad, pre_here),
                (mlp_in, mlp_here),
                (parts.at[2], across_out),
                (cot, cot_here),
                (activ, activ_here),
                (parts.at[0], here),
            )
        )
    ]
    for copy in loads:
        copy.start()

    def product(left, right, place, out):
        start = pl.multiple_of(place * shard, shard)
        chosen = left[:, pl.ds(start, shard)] if turned else left[pl.ds(start, shard), :]
        for at in range(0, width, 512):
            cols = slice(at, at + 512)
            value = dot_rows(chosen, right[:, cols]) if turned else dot_plain(chosen, right[:, cols])
            out[:, cols] = value.astype(BF)

    def chunk(place, out):
        product(mlp_here, pre_here, place, out.at[pl.ds(0, shard)])
        product(activ_here, cot_here, place, out.at[pl.ds(shard, shard)])

    def low_part(j, down):
        lines = slice(j * tokens, (j + 1) * tokens)
        return dot_plain(activ_here[lines], down) if turned else dot_rows(activ_here[:, lines], down)

    upper, under = pl.ds(0, shard), pl.ds(shard, shard)
    devices = (up, down)
    side = width // 2
    sides = [
        pltpu.make_async_copy(down_all.at[:, :, pl.ds(i * side, side)], down_here, local.at[10 + i])
        for i in range(2)
    ]
    sides[0].start()
    loads[0].wait()
    loads[1].wait()
    product(mlp_here, pre_here, owner(steps), outs_first.at[upper])
    first = [send(outs_first.at[upper], ins_first.at[upper], ring_sems, (0, 0), up)]
    loads[2].wait()
    pairs[0].wait_recv()
    across_out[...] = (across_out[...].astype(F32) + far[...].astype(F32)).astype(BF)
    rows = tokens // 2
    halves = [pl.ds(i * rows, rows) for i in range(2)]
    across = [send(across_out.at[half], chip_in.at[half], chip_sems, (i,), chip) for i, half in enumerate(halves)]
    loads[3].wait()
    loads[4].wait()
    product(activ_here, cot_here, owner(steps), outs_first.at[under])
    first.append(send(outs_first.at[under], ins_first.at[under], ring_sems, (1, 0), down))
    chunk(owner(steps - 1), outs_next.at[0])
    chunk(owner(1 - steps), outs_next.at[1])
    second = []
    for way, part in enumerate((upper, under)):
        first[way].wait_recv()
        out = outs_next.at[way]
        out[part] = (out[part].astype(F32) + ins_first[part].astype(F32)).astype(BF)
        second.append(send(out, ins_next.at[way], ring_sems, (way, 1), devices[way]))

    loads[5].wait()
    pairs[1].wait_recv()
    gain_grad = jnp.zeros((1, width), F32)
    bias_grad = jnp.zeros((1, width), F32)
    spread, spread_pair = [], []
    block = 64
    for i, half in enumerate(halves):
        across[i].wait_recv()
        for at in range(i * rows, (i + 1) * rows, block):
            part = slice(at, at + block)
            grad = here[part].astype(F32) + near[part].astype(F32) + chip_in[part].astype(F32)
            normed, inverse = layer_norm(resid[part])
            gain_grad += jnp.sum(grad * normed, axis=0, keepdims=True)
            bias_grad += jnp.sum(grad, axis=0, keepdims=True)
            value = cot_here[part].astype(F32) + norm_back(grad * gain[...], normed, inverse)
            resid_out[part] = value
            branch[part] = value.astype(BF)
        spread.append(send(branch.at[half], branch_out.at[2, half], spread_chip, (i,), chip))
        spread_pair.append(send(branch.at[half], branch_out.at[1, half], spread_core, (i,), core))
    vectors_out[0:1] = gain_grad
    vectors_out[1:2] = bias_grad
    keep = pltpu.make_async_copy(branch, branch_out.at[0], local.at[6])
    keep.start()

    for copy in across:
        copy.wait_send()
    lows = (low_here, here, across_out, branch_low)
    for i in range(2):
        cols = pl.ds(i * side, side)
        sides[i].wait()
        down = down_here[...].reshape(-1, side)
        for j in (3, 1, 2, 0):
            value = low_part(j, down)
            lows[j][:, cols] = value if j == 0 else value.astype(BF)
        if i == 0:
            sides[1].start()
    low_sends = [send(lows[3], low_far, low_pair, (0,), core), send(lows[1], low_near, low_pair, (1,), core)]
    low_sends[0].wait()
    across_out[...] = (across_out[...].astype(F32) + low_far[...].astype(F32)).astype(BF)
    low_chip_copy = send(across_out, low_chip, low_across, (0,), chip)

    def rest(i, carry):
        back = lax.rem(i + 1, 2)
        n = (steps - (i + 1) // 2) * (1 - 2 * back)
        chunk(owner(n), stage)
        copy = pltpu.make_async_copy(stage, rest_out.at[i - 5], local.at[7])
        copy.start()
        copy.wait()
        return carry

    lax.fori_loop(5, count, rest, 0)
    for i, half in enumerate(halves):
        spread[i].wait_recv()
        spread_pair.append(send(branch_out.at[2, half], branch_out.at[3, half], spread_core, (2 + i,), core))
    leaving = []
    low_sends[1].wait()
    low_chip_copy.wait()
    for at in range(0, tokens, block):
        part = slice(at, at + block)
        value = resid[part] + low_here[part] + low_near[part].astype(F32) + low_chip[part].astype(F32)
        result_out[part] = value.astype(BF)
    for way, target in enumerate((up_out, down_out)):
        out = stage if way == 0 else outs_first
        if way:
            first[0].wait_send()
            first[1].wait_send()
        chunk(owner((steps - 2) * (1 - 2 * way)), out)
        second[way].wait_recv()
        out[...] = (out[...].astype(F32) + ins_next[way].astype(F32)).astype(BF)
        leaving.append(pltpu.make_async_copy(out, target, local.at[8 + way]))
        leaving[way].start()
    for copy in pairs + spread + second:
        copy.wait_send()
    for copy in spread_pair + leaving + [keep]:
        copy.wait()


def feedback(parts, mlp_in, pre_grad, activ, cot, down_all, resid, gain, fsdp_count, shard):
    tokens, width = resid.shape
    turned = shard % 128 == 0
    if not turned:
        mlp_in, activ = mlp_in.T, activ.T
    dma = pltpu.SemaphoreType.DMA
    anywhere = pl.BlockSpec(memory_space=pltpu.HBM)
    inside = pl.BlockSpec(memory_space=pltpu.VMEM)
    wide = pltpu.VMEM((tokens, width), BF)
    both = pltpu.VMEM((2 * shard, width), BF)
    quarter = down_all.shape[1]
    flow = jax.ShapeDtypeStruct((2 * shard, width), BF)
    return pl.pallas_call(
        functools.partial(feedback_kernel, count=fsdp_count, shard=shard, turned=turned),
        out_shape=(
            jax.ShapeDtypeStruct((4, tokens, width), BF),
            jax.ShapeDtypeStruct((tokens, width), BF),
            jax.ShapeDtypeStruct((tokens, width), F32),
            jax.ShapeDtypeStruct((2, width), F32),
            flow,
            flow,
            jax.ShapeDtypeStruct((fsdp_count - 5, 2 * shard, width), BF),
        ),
        in_specs=[anywhere] * 6 + [inside] * 2,
        out_specs=(anywhere, inside, inside, inside, anywhere, anywhere, anywhere),
        scratch_shapes=[pltpu.VMEM(value.shape, BF) for value in (mlp_in, pre_grad, activ, cot)]
        + [wide] * 6
        + [
            both,
            both,
            pltpu.VMEM((2, 2 * shard, width), BF),
            pltpu.VMEM((2, 2 * shard, width), BF),
            both,
            pltpu.VMEM((fsdp_count, quarter, width // 2), BF),
            pltpu.VMEM((tokens, width), F32),
            wide,
            wide,
            wide,
            wide,
            dma((2, 2)),
            dma((2, 2)),
            dma((2, 2)),
            dma((2, 4)),
            dma((2, 2, 2)),
            dma((2, 2)),
            dma((2, 1)),
            dma((12,)),
        ],
        compiler_params=pltpu.CompilerParams(
            collective_id=4, has_side_effects=True, vmem_limit_bytes=61 << 20
        ),
        cost_estimate=COST,
        name="feedback",
    )(parts, mlp_in, pre_grad, activ, cot, down_all, resid, gain)


class KernelScatter:
    def __init__(self, count, chunk, outs, ins, sems, up, down):
        self.steps, self.chunk, self.outs, self.ins, self.sems = count // 2, chunk, outs, ins, sems
        self.devices = (up, down)
        self.half = outs.shape[2] // 2
        self.copies = {}

    def start(self, step):
        half = self.half
        for way, sign in ((0, 1), (1, -1)):
            mine = self.chunk(sign * (self.steps - step))
            if step > 1:
                self.copies[way, step - 2].wait_send()
            out, into = self.outs.at[way, step % 2], self.ins.at[way, step]
            rows = slice(way * half, (way + 1) * half)
            rest = slice((1 - way) * half, (2 - way) * half)
            if step == 0:
                out, into = out.at[pl.ds(0, half)], into.at[pl.ds(0, half)]
                out[...] = mine[rows].astype(BF)
            elif step == 1:
                out[rows] = (mine[rows] + self.ins[way, 0, :half].astype(F32)).astype(BF)
                out[rest] = mine[rest].astype(BF)
            else:
                out[...] = (mine + self.ins[way, step - 1].astype(F32)).astype(BF)
            self.copies[way, step] = send(out, into, self.sems, (way, step), self.devices[way])

    def arrived(self, step):
        self.copies[0, step].wait_recv()
        self.copies[1, step].wait_recv()

    def total(self):
        last = self.steps - 1
        return self.chunk(0) + self.ins[0, last].astype(F32) + self.ins[1, last].astype(F32)

    def finish(self):
        for (_, step), copy in self.copies.items():
            if step >= self.steps - 2:
                copy.wait_send()


def closing_kernel(
    kv_parts,
    query_rows,
    q_weight,
    attn_parts,
    ff_up,
    ff_down,
    ff_rest,
    resid_grad,
    hidden,
    kv_weight,
    attn_in,
    mlp_vectors,
    grad_out,
    q_out,
    proj_out,
    ff_out,
    tail_out,
    kv_here,
    kv_near,
    kv_far,
    kv_chip_in,
    kv_outs,
    kv_ins,
    q_far_out,
    q_far,
    q_near,
    q_chip_in,
    q_here,
    attn_here,
    attn_own,
    proj_here,
    attn_outs,
    attn_ins,
    ff_here,
    ff_ins,
    ff_sum,
    kv_total,
    tail_here,
    tail_outs,
    tail_ins,
    swap_out,
    swap_in,
    local,
    kv_core_sems,
    kv_chip_sems,
    kv_sems,
    q_core_sems,
    q_chip_sems,
    attn_sems,
    ff_sems,
    ff_chip_sems,
    ff_core_sems,
    tail_sems,
    swap_sems,
    q_spread_sems,
    proj_spread_sems,
    move_sems,
    *,
    count,
    shard,
):
    s, f, owner, up, down, chip, core = neighbours(count)
    steps = count // 2
    order = [steps] + [sign * n for n in range(steps - 1, 0, -1) for sign in (1, -1)] + [0]
    other, sibling = lax.rem(s + 2, 4), core[0]
    far = lax.rem(sibling + 2, 4)
    tokens = hidden.shape[0]
    per = count // 4
    target = (lax.rem(f, 4), s * per + f // 4)
    source = (f // per, 4 * lax.rem(f, per) + s)
    greet_also((up, down, chip, core), (source,), met(target, s, f).astype(jnp.int32), s, f)

    kv_pair = [
        send(kv_parts.at[far], kv_far, kv_core_sems, (0,), core),
        send(kv_parts.at[sibling], kv_near, kv_core_sems, (1,), core),
    ]
    loads = [
        pltpu.make_async_copy(kv_parts.at[other], kv_here.at[1], local.at[0]),
        pltpu.make_async_copy(kv_parts.at[s], kv_here.at[0], local.at[1]),
        pltpu.make_async_copy(attn_parts, attn_here, local.at[2]),
        pltpu.make_async_copy(ff_rest.at[ff_rest.shape[0] - 1], ff_here, local.at[3]),
    ]
    for copy in loads:
        copy.start()
    ff_rows = ff_here.shape[0] // 2
    ff_parts = [pl.ds(i * ff_rows, ff_rows) for i in range(2)]
    ff_ring = []

    def ff_start(i):
        for way, (source, device) in enumerate(((ff_up, up), (ff_down, down))):
            copy = send(source.at[ff_parts[i]], ff_ins.at[way, ff_parts[i]], ff_sems, (way, i), device)
            ff_ring.append(copy)

    ff_start(0)

    def query_part(i):
        return dot_cols(query_rows[i * tokens : (i + 1) * tokens], q_weight[...])

    q_far_out[...] = query_part(3).astype(BF)
    q_pair = [send(q_far_out, q_far, q_core_sems, (0,), core)]
    grad_out[...] = query_part(1).astype(BF)
    loads[0].wait()
    kv_pair[0].wait_recv()
    kv_across = {}
    for i, n in enumerate(order):
        place = owner(n)
        kv_here[1, place] = (kv_here[1, place].astype(F32) + kv_far[place].astype(F32)).astype(BF)
        kv_across[n] = send(kv_here.at[1, place], kv_chip_in.at[i], kv_chip_sems, (i,), chip)
    part = query_part(2)
    q_pair[0].wait()
    q_chip_out = q_far_out
    q_chip_out[...] = (part + q_far[...].astype(F32)).astype(BF)
    rows = tokens // 2
    q_halves = [pl.ds(i * rows, rows) for i in range(2)]
    q_across = [
        send(q_chip_out.at[half], q_chip_in.at[half], q_chip_sems, (i,), chip) for i, half in enumerate(q_halves)
    ]
    q_pair.append(send(grad_out, q_near, q_core_sems, (1,), core))
    q_here[...] = query_part(0)
    loads[1].wait()
    kv_pair[1].wait_recv()

    def kv_chunk(n):
        n = steps if n == -steps else n
        place = owner(n)
        here = kv_here[0, place].astype(F32) + kv_near[place].astype(F32)
        return here + kv_chip_in[order.index(n)].astype(F32)

    loads[2].wait()

    def attn_chunk(n):
        return attn_here[order.index(steps if n == -steps else n)].astype(F32)

    kv = KernelScatter(count, kv_chunk, kv_outs, kv_ins, kv_sems, up, down)
    attn = KernelScatter(count, attn_chunk, attn_outs, attn_ins, attn_sems, up, down)
    for step in range(steps):
        for n in (steps - step, step - steps):
            if n in order:
                kv_across[n].wait_recv()
        if step:
            kv.arrived(step - 1)
        kv.start(step)
        if step:
            attn.arrived(step - 1)
        attn.start(step)
    ff_start(1)

    loads[3].wait()
    ff_pair, ff_across = [], []

    def ff_close(i):
        rows = ff_parts[i]
        for copy in ff_ring[2 * i : 2 * i + 2]:
            copy.wait_recv()
        arrived = ff_ins[0, rows].astype(F32) + ff_ins[1, rows].astype(F32)
        ff_sum[rows] = (ff_here[rows].astype(F32) + arrived).astype(BF)
        ff_across.append(send(ff_sum.at[rows], ff_out.at[2, rows], ff_chip_sems, (i,), chip))
        ff_pair.append(send(ff_sum.at[rows], ff_out.at[1, rows], ff_core_sems, (i,), core))

    ff_close(0)
    kv_across[0].wait_recv()
    kv.arrived(steps - 1)
    kv_total[...] = kv.total().astype(BF)

    attn.arrived(steps - 1)
    attn_own[...] = attn.total().astype(BF)
    part = proj_out.shape[1]
    lines = pl.ds(part, attn_own.shape[0] - part)
    q_lines = attn_own.at[lines]
    q_spread = [
        send(q_lines, q_out.at[2], q_spread_sems, (0,), chip),
        send(q_lines, q_out.at[1], q_spread_sems, (1,), core),
    ]
    q_keep = pltpu.make_async_copy(q_lines, q_out.at[0], local.at[5])
    q_keep.start()
    moved = Maybe(
        attn_own.at[pl.ds(0, part)],
        proj_here,
        proj_here,
        move_sems.at[0],
        move_sems.at[1],
        move_sems.at[1],
        move_sems.at[2],
        target,
        source,
        s,
        f,
    )

    q_pair[1].wait()
    for copy in q_across:
        copy.wait_recv()
    q_here[...] += q_near[...].astype(F32) + q_chip_in[...].astype(F32)
    for t in range(count):
        cols = slice(t * shard, (t + 1) * shard)
        q_here[:, cols] += dot_cols(kv_total[...], kv_weight[t, :shard, :])
    gain = jnp.concatenate([kv_weight[t, shard : shard + 1, :shard] for t in range(count)], axis=1).astype(F32)
    block = 64
    gain_grad = jnp.zeros((1, hidden.shape[1]), F32)
    bias_grad = jnp.zeros((1, hidden.shape[1]), F32)
    for at in range(0, tokens, block):
        here = slice(at, at + block)
        normed, inverse = layer_norm(hidden[here].astype(F32))
        grad = q_here[here]
        gain_grad += jnp.sum(grad * normed, axis=0, keepdims=True)
        bias_grad += jnp.sum(grad, axis=0, keepdims=True)
        grad_out[here] = (resid_grad[here] + norm_back(grad * gain, normed, inverse)).astype(BF)

    tail_here[...] = jnp.zeros_like(tail_here)
    vectors = (gain_grad, bias_grad, mlp_vectors[0:1], mlp_vectors[1:2])
    for t in range(count):
        cols = slice(t * shard, (t + 1) * shard)
        tail_here[t, :shard, :] = dot_rows(attn_in[:, cols], kv_total[...])
        for j, vector in enumerate(vectors):
            tail_here[t, shard + j : shard + j + 1, :shard] = vector[:, cols]
    tail = KernelScatter(count, lambda n: tail_here[owner(n)], tail_outs, tail_ins, tail_sems, up, down)
    for step in range(steps):
        if step:
            tail.arrived(step - 1)
        tail.start(step)
        if step == 0:
            ff_close(1)
            q_spread[0].wait_recv()
            q_spread.append(send(q_out.at[2], q_out.at[3], q_spread_sems, (2,), core))
            moved.arrived()
            moved.left()
            proj_spread = [
                send(proj_here, proj_out.at[2], proj_spread_sems, (0,), chip),
                send(proj_here, proj_out.at[1], proj_spread_sems, (1,), core),
            ]
            proj_keep = pltpu.make_async_copy(proj_here, proj_out.at[0], local.at[6])
            proj_keep.start()
    proj_spread[0].wait_recv()
    proj_spread.append(send(proj_out.at[2], proj_out.at[3], proj_spread_sems, (2,), core))
    tail.arrived(steps - 1)
    total = tail.total()
    swap_out[0] = total.astype(BF)
    swaps = [send(swap_out.at[0], swap_in.at[0], swap_sems, (0,), core)]
    for i, rows in enumerate(ff_parts):
        ff_across[i].wait_recv()
        ff_pair.append(send(ff_out.at[2, rows], ff_out.at[3, rows], ff_core_sems, (2 + i,), core))
    keep = pltpu.make_async_copy(ff_sum, ff_out.at[0], local.at[4])
    keep.start()
    swaps[0].wait_recv()
    swap_out[1] = (swap_out[0].astype(F32) + swap_in[0].astype(F32)).astype(BF)
    swaps.append(send(swap_out.at[1], swap_in.at[1], swap_sems, (1,), chip))
    swaps[1].wait_recv()
    tail_out[...] = swap_out[1].astype(F32) + swap_in[1].astype(F32)
    keep.wait()
    q_keep.wait()
    proj_keep.wait()
    q_spread[0].wait_send()
    proj_spread[0].wait_send()
    for copy in q_spread[1:] + proj_spread[1:]:
        copy.wait()
    for ring in (kv, attn, tail):
        ring.finish()
    for copy in kv_pair + q_across + list(kv_across.values()) + ff_ring + ff_across + swaps:
        copy.wait_send()
    for copy in ff_pair:
        copy.wait()


def closing(kv_parts, query_rows, q_weight, attn_parts, ff_flow, resid_grad, hidden, kv_weight, attn_in, mlp_vectors, shard):
    ff_up, ff_down, ff_rest = ff_flow
    fsdp_count, tokens, kv_cols = kv_parts.shape[1:]
    width = hidden.shape[1]
    steps = fsdp_count // 2
    dma = pltpu.SemaphoreType.DMA
    anywhere = pl.BlockSpec(memory_space=pltpu.HBM)
    inside = pl.BlockSpec(memory_space=pltpu.VMEM)
    attn_shape = attn_parts.shape[1:]
    part = shard // 4
    tail_shape = kv_weight.shape[1:]
    wide = pltpu.VMEM((tokens, width), BF)
    kv_all = pltpu.VMEM((fsdp_count, tokens, kv_cols), BF)

    def ring(shape):
        return pltpu.VMEM((2, steps) + tuple(shape), BF)

    def pair(shape):
        return pltpu.VMEM((2, 2) + tuple(shape), BF)

    ring_sems = dma((2, 2, steps))
    return pl.pallas_call(
        functools.partial(closing_kernel, count=fsdp_count, shard=shard),
        out_shape=(
            jax.ShapeDtypeStruct((tokens, width), BF),
            jax.ShapeDtypeStruct((4, attn_shape[0] - part, width), BF),
            jax.ShapeDtypeStruct((4, part, width), BF),
            jax.ShapeDtypeStruct((4,) + ff_up.shape, BF),
            jax.ShapeDtypeStruct(tail_shape, F32),
        ),
        in_specs=[anywhere, inside, inside, anywhere, anywhere, anywhere, anywhere] + [inside] * 5,
        out_specs=(inside, anywhere, anywhere, anywhere, inside),
        scratch_shapes=[
            pltpu.VMEM((2, fsdp_count, tokens, kv_cols), BF),
            kv_all,
            kv_all,
            kv_all,
            pair((tokens, kv_cols)),
            ring((tokens, kv_cols)),
            wide,
            wide,
            wide,
            wide,
            pltpu.VMEM((tokens, width), F32),
            pltpu.VMEM(attn_parts.shape, BF),
            pltpu.VMEM(attn_shape, BF),
            pltpu.VMEM((part, width), BF),
            pair(attn_shape),
            ring(attn_shape),
            pltpu.VMEM(ff_up.shape, BF),
            pltpu.VMEM((2,) + ff_up.shape, BF),
            pltpu.VMEM(ff_up.shape, BF),
            pltpu.VMEM((tokens, kv_cols), BF),
            pltpu.VMEM((fsdp_count,) + tail_shape, F32),
            pair(tail_shape),
            ring(tail_shape),
            pltpu.VMEM((2,) + tail_shape, BF),
            pltpu.VMEM((2,) + tail_shape, BF),
            dma((7,)),
            dma((2, 2)),
            dma((2, fsdp_count)),
            ring_sems,
            dma((2, 2)),
            dma((2, 2)),
            ring_sems,
            dma((2, 2, 2)),
            dma((2, 2)),
            dma((2, 4)),
            ring_sems,
            dma((2, 2)),
            dma((2, 3)),
            dma((2, 3)),
            dma((3,)),
        ],
        compiler_params=pltpu.CompilerParams(
            collective_id=2, has_side_effects=True, vmem_limit_bytes=61 << 20
        ),
        cost_estimate=COST,
        name="closing",
    )(
        kv_parts,
        query_rows,
        q_weight,
        attn_parts,
        ff_up,
        ff_down,
        ff_rest,
        resid_grad,
        hidden,
        kv_weight,
        attn_in,
        mlp_vectors,
    )


def attn_turned_kernel(order, rows_ref, query_ref, proj_ref, out_ref):
    part, cols = proj_ref.shape[0], query_ref.shape[1]
    grad = dot_rows(rows_ref[...], query_ref[...]).astype(BF)
    lines = out_ref.shape[1] - part
    out_ref[0, :part] = proj_ref[...]
    for k in range(grad.shape[0] // lines):
        out_ref[0, part:, k * cols : (k + 1) * cols] = grad[k * lines : (k + 1) * lines]


def attn_turned(order, rows, query_rows, proj_sum, shard):
    count, width = rows.shape
    cols = query_rows.shape[1]
    chunks = order.shape[0]
    part = proj_sum.shape[0] // chunks
    folds = width // cols
    lines = shard // folds
    if shard % 128:
        grad = dot_rows(rows, query_rows).astype(BF).reshape(chunks, folds, lines, cols)
        grad = grad.transpose(0, 2, 1, 3).reshape(chunks, lines, width)
        both = jnp.concatenate([proj_sum.reshape(chunks, part, width), grad], axis=1)
        return jnp.stack([lax.dynamic_index_in_dim(both, order[i], 0, False) for i in range(chunks)])
    return pl.pallas_call(
        attn_turned_kernel,
        out_shape=jax.ShapeDtypeStruct((chunks, part + lines, width), BF),
        grid_spec=pltpu.PrefetchScalarGridSpec(
            num_scalar_prefetch=1,
            grid=(chunks,),
            in_specs=[
                pl.BlockSpec((count, shard), lambda n, o: (0, o[n])),
                pl.BlockSpec((count, cols), lambda n, o: (0, 0)),
                pl.BlockSpec((part, width), lambda n, o: (o[n], 0)),
            ],
            out_specs=pl.BlockSpec((1, part + lines, width), lambda n, o: (n, 0, 0)),
        ),
        compiler_params=pltpu.CompilerParams(vmem_limit_bytes=30 << 20),
        cost_estimate=COST,
        name="attn_turned",
    )(order, rows, query_rows, proj_sum)


def rows_kernel(place, *refs):
    *ins, out = refs
    rows = ins[0].shape[0]
    for i, ref in enumerate(ins):
        out[pl.ds(pl.multiple_of((place[0] ^ i) * rows, rows), rows), :] = ref[...].astype(F32)


def stack_rows(place, pieces, tile):
    rows, width = pieces[0].shape
    return pl.pallas_call(
        rows_kernel,
        out_shape=jax.ShapeDtypeStruct((len(pieces) * rows, width), F32),
        grid_spec=pltpu.PrefetchScalarGridSpec(
            num_scalar_prefetch=1,
            grid=(width // tile,),
            in_specs=[pl.BlockSpec((rows, tile), lambda n, p: (0, n))] * len(pieces),
            out_specs=pl.BlockSpec((len(pieces) * rows, tile), lambda n, p: (0, n)),
        ),
        compiler_params=pltpu.CompilerParams(vmem_limit_bytes=40 << 20),
        cost_estimate=COST,
        name="stack_rows",
    )(place, *pieces)


def qkv_kernel(place, q_ref, tail_ref, out_ref):
    _, lines, width = q_ref.shape
    rows = out_ref.shape[0]
    folds = rows // lines
    cols = width // folds
    for i in range(q_ref.shape[0]):
        start = pl.multiple_of((place[0] ^ i) * cols, cols)
        for k in range(folds):
            part = q_ref[i, :, k * cols : (k + 1) * cols].astype(F32)
            out_ref[k * lines : (k + 1) * lines, pl.ds(start, cols)] = part
    out_ref[:, width:] = tail_ref[:rows, : out_ref.shape[1] - width]


def place_qkv(place, q_pieces, tail, rows, cols):
    return pl.pallas_call(
        qkv_kernel,
        out_shape=jax.ShapeDtypeStruct((rows, cols), F32),
        in_specs=[pl.BlockSpec(memory_space=pltpu.SMEM)] + [pl.BlockSpec(memory_space=pltpu.VMEM)] * 2,
        out_specs=pl.BlockSpec(memory_space=pltpu.VMEM),
        compiler_params=pltpu.CompilerParams(vmem_limit_bytes=30 << 20),
        cost_estimate=COST,
        name="place_qkv",
    )(place, q_pieces, tail)


def cols_kernel(place, *refs):
    *ins, out = refs
    cols = ins[0].shape[1]
    for i, ref in enumerate(ins):
        out[:, pl.ds(pl.multiple_of((place[0] ^ i) * cols, cols), cols)] = ref[...].astype(F32)


def stack_cols(place, pieces, cols):
    rows, width = pieces[0].shape
    count = len(pieces)
    if cols % 128:
        ordered = jnp.stack([lax.dynamic_index_in_dim(jnp.stack(pieces), place[0] ^ i, 0, False) for i in range(count)])
        ordered = ordered.reshape(count, rows, width // cols, cols).transpose(1, 2, 0, 3)
        return ordered.reshape(rows, count * width).astype(F32)
    return pl.pallas_call(
        cols_kernel,
        out_shape=jax.ShapeDtypeStruct((rows, count * width), F32),
        grid_spec=pltpu.PrefetchScalarGridSpec(
            num_scalar_prefetch=1,
            grid=(width // cols,),
            in_specs=[pl.BlockSpec((rows, cols), lambda n, p: (0, n))] * count,
            out_specs=pl.BlockSpec((rows, count * cols), lambda n, p: (0, n)),
        ),
        compiler_params=pltpu.CompilerParams(vmem_limit_bytes=40 << 20),
        cost_estimate=COST,
        name="stack_cols",
    )(place, *pieces)


def layer_norm(values):
    mean = jnp.mean(values, axis=-1, keepdims=True)
    center = values - mean
    inverse = lax.rsqrt(jnp.mean(center * center, axis=-1, keepdims=True) + EPS)
    return center * inverse, inverse


def norm_back(grad, normed, inverse):
    return inverse * (
        grad
        - jnp.mean(grad, axis=-1, keepdims=True)
        - normed * jnp.mean(grad * normed, axis=-1, keepdims=True)
    )


def gelu_tanh(values):
    return jax.nn.gelu(values, approximate=True)


def shards(
    hidden_in,
    out_cotangent,
    positions,
    block_mask,
    norm_gain,
    norm_bias,
    qkv_weight,
    proj_weight,
    mlp_gain,
    mlp_bias,
    fc_weight,
    down_weight,
):
    seq_count = lax.axis_size("seq")
    fsdp_count = lax.axis_size("fsdp")
    s = lax.axis_index("seq")
    f = lax.axis_index("fsdp")
    ring = Ring(fsdp_count)
    count = hidden_in.shape[1]
    width = hidden_in.shape[2]
    length = positions.shape[1]
    blocks = length // BLOCK
    shard = qkv_weight.shape[0]
    ff = fc_weight.shape[1]
    ff_shard = down_weight.shape[0]
    heads_here = HEADS // seq_count
    head_cols = heads_here * HD
    quarter = ff_shard // seq_count
    tokens_here = MB * count
    group = seq_count * tokens_here

    chunk_ids = jnp.stack([(s ^ i) * fsdp_count + f for i in range(seq_count)]).astype(jnp.int32)
    token_ids = chunk_ids[:, None] * count + jnp.arange(count, dtype=jnp.int32)[None]
    first = token_ids[:, None, :] - jnp.stack(
        [lax.dynamic_slice_in_dim(positions, chunk_ids[i] * count, count, 1) for i in range(seq_count)]
    )
    first = first[:, :, None, :]
    high_tiles = (chunk_ids * count + count - 1) // BLOCK + 1
    tables = jnp.concatenate(
        [
            jnp.broadcast_to(chunk_ids[None, :, None], (MB, seq_count, 1)),
            (first[:, :, 0, :1] // BLOCK).transpose(1, 0, 2),
            jnp.broadcast_to(high_tiles[None, :, None], (MB, seq_count, 1)),
            jnp.zeros((MB, seq_count, 1), jnp.int32),
            jnp.stack([block_mask[:, (chunk_ids[i] * count) // BLOCK] for i in range(seq_count)], axis=1),
        ],
        axis=2,
    ).reshape(-1)

    place = jnp.stack([s, f]).astype(jnp.int32)
    part = shard // seq_count
    down_own = lax.dynamic_slice_in_dim(down_weight, s * quarter, quarter, 0)
    if quarter % 128:
        fc_weight = lax.dynamic_slice_in_dim(
            fc_weight.reshape(shard, fsdp_count, seq_count, quarter), s, 1, 2
        ).reshape(shard, fsdp_count * quarter)

    span = 32
    vectors = jnp.stack([norm_gain, norm_bias, mlp_gain, mlp_bias])
    padded = jnp.pad(vectors, ((0, span - 4), (0, 2 * HD - shard)))
    own_kv = jnp.concatenate([qkv_weight[:, width:], padded], axis=0)
    hidden_own = hidden_in.reshape(tokens_here, width)
    cotangent = out_cotangent.reshape(tokens_here, width)
    hidden_all, kv_ring, q_ring, proj_ring, kv_all, fc_all, cotangent_all = opening(
        hidden_own, own_kv, qkv_weight, proj_weight, fc_weight, cotangent, fsdp_count, head_cols
    )
    cotangent_all = cotangent_all.reshape(group, width)
    down_first, kv_all = lax.optimization_barrier((down_own, kv_all))
    down_given = (lax.ppermute(down_first, "fsdp", ring.up), lax.ppermute(down_first, "fsdp", ring.down))
    kv_weight = kv_ring[:, :shard].reshape(width, 2 * HD)
    vectors = kv_ring[:, shard : shard + 4, :shard].transpose(1, 0, 2).reshape(4, width).astype(F32)
    gain_one, bias_one, gain_two, bias_two = vectors[0], vectors[1], vectors[2], vectors[3]
    q_weight = q_ring.reshape(width, head_cols)
    proj_full = proj_ring.reshape(head_cols, width)
    kv_all = kv_all.reshape(seq_count * fsdp_count, MB, count, 2 * HD)
    normed_all, _ = layer_norm(hidden_all.reshape(group, width).astype(F32))
    attn_in = (normed_all * gain_one + bias_one).astype(BF)
    attn_in = lax.optimization_barrier(attn_in)
    own_attn_in = attn_in[:tokens_here]
    queries = dot_plain(attn_in, q_weight).astype(BF).reshape(seq_count, MB, count, head_cols)
    heads_out, logs = attend(tables, first, queries, kv_all, blocks)
    heads_rows = heads_out.reshape(group, head_cols)

    far = fsdp_count // 2 - 1
    low = lax.dynamic_index_in_dim(fc_all, ring.owner(1 - far), 0, keepdims=False)
    high = lax.dynamic_index_in_dim(fc_all, ring.owner(far - 1), 0, keepdims=False)
    low, high = lax.ppermute(low, "fsdp", ring.up), lax.ppermute(high, "fsdp", ring.down)
    low, high, heads_rows = lax.optimization_barrier((low, high, heads_rows))
    last_low = lax.ppermute(low[: shard // 2], "fsdp", ring.up)
    last_high = lax.ppermute(high[shard // 2 :], "fsdp", ring.down)
    for piece, step, row in ((low, -far, 0), (high, far, 0), (last_low, far + 1, 0), (last_high, far + 1, shard // 2)):
        fc_all = lax.dynamic_update_slice(fc_all, piece[None], (ring.owner(step), row, 0))

    mlp_in, resid, down_all = bridge(
        heads_rows, proj_full, hidden_own, vectors[2:], down_own, down_given, fsdp_count
    )
    mlp_in = mlp_in.reshape(group, width)
    activ, pre_grad, mlp_in_parts = middle(mlp_in, cotangent_all, fc_all, down_all, 4 * BLOCK)
    branch, result, resid_grad, mlp_vectors, ff_up, ff_down, ff_rest = feedback(
        mlp_in_parts.reshape(seq_count, tokens_here, width),
        mlp_in,
        pre_grad,
        activ,
        cotangent_all,
        down_all,
        resid,
        gain_two[None],
        fsdp_count,
        shard,
    )
    branch = branch.reshape(group, width)
    steps = ring.steps()
    flow = Flow(ring, ring.scatter(ff_up, ff_down, lambda n: ff_rest[steps.index(n) - 5]))
    heads_grad = dot_cols(branch, proj_full).astype(BF).reshape(seq_count, MB, count, head_cols)
    query_grads, kv_grads = attend_back(
        tables, first, queries, kv_all, heads_out, logs, heads_grad, blocks
    )
    query_grads, kv_grads = flow.advance((query_grads, kv_grads))
    query_rows = query_grads.reshape(group, head_cols)

    proj_sum = dot_rows(heads_rows, branch).astype(BF)
    attn_parts = attn_turned(ring.order(), attn_in, query_rows, proj_sum, shard)
    ff_up, ff_down = flow.finish()
    grad_input, q_pieces, proj_pieces, ff_all, tail = closing(
        kv_grads.reshape(seq_count, fsdp_count, tokens_here, 2 * HD),
        query_rows,
        q_weight,
        attn_parts,
        (ff_up, ff_down, ff_rest),
        resid_grad,
        hidden_own,
        kv_ring,
        own_attn_in,
        mlp_vectors,
        shard,
    )
    vector_grads = tail[shard : shard + 4, :shard]
    ff_pieces = [ff_all[i] for i in range(seq_count)]
    grad_fc = stack_cols(place, [piece[:shard] for piece in ff_pieces], quarter)
    grad_down = stack_rows(place, [piece[shard:] for piece in ff_pieces], BLOCK)
    grad_proj = stack_rows(place, [proj_pieces[i] for i in range(seq_count)], width)
    grad_qkv = place_qkv(place, q_pieces, tail, shard, qkv_weight.shape[1])
    return (
        result.reshape(hidden_in.shape),
        grad_input.reshape(hidden_in.shape),
        vector_grads[0],
        vector_grads[1],
        grad_qkv,
        grad_proj,
        vector_grads[2],
        vector_grads[3],
        grad_fc,
        grad_down,
    )


def solution(mesh):
    rows = P(None, ("seq", "fsdp"), None)
    vector = P("fsdp")
    matrix = P("fsdp", None)
    in_specs = (rows, rows, P(), P(), vector, vector, matrix, matrix, vector, vector, matrix, matrix)
    out_specs = (rows, rows, vector, vector, matrix, matrix, vector, vector, matrix, matrix)
    return jax.shard_map(shards, mesh=mesh, in_specs=in_specs, out_specs=out_specs, check_vma=False)
```
